32 devices in a mesh: scen: 2 (over y), lon: 4 (over z), lat: 2 (over x), gau: 2 (over core).
Axes of the slice: x: 2, y: 2, z: 4, core: 2. Of those that a mesh axis runs over, the one named last changes fastest.
Arguments:
- depth: float32 [512, 2048], P(('lat', 'gau'), 'lon'), may hold values from 3 to 6
- surface: float32 [1024, 2048], P(('scen', 'lat', 'gau'), 'lon'), parts along dimension 0, may hold values from -3 to 3
- friction: float32 [512, 2048], P(('lat', 'gau'), 'lon'), may hold values from 0.002 to 0.06
- wet: int32 [512, 2048], P(('lat', 'gau'), 'lon'), may hold values 0 or 1
- coastal_tiles: int32 [8], replicated, may hold values from 0 to 15, as said below
- gauge_route: int32 [512, 1], P(('scen', 'lon', 'lat', 'gau')), parts along dimension 0, may hold values from 0 to 7; in each aligned block of 16 rows (0 to 15, 16 to 31, ...) at most 2 rows name the same one
- gauge_cell: int32 [512], P(('scen', 'lon', 'lat', 'gau')), parts along dimension 0, may hold values from 0 to 65535
- gauge_times: int32 [512, 2, 4], P(('scen', 'lon', 'lat', 'gau')), parts along dimension 0, may hold values from 0 to 7
- gauge_resid: float32 [512, 2, 4], P(('scen', 'lon', 'lat', 'gau')), parts along dimension 0, may hold values from -6 to 6
Outputs:
- smoothed_grad: float32 [1024, 2048], P(('scen', 'lat', 'gau'), 'lon'), parts along dimension 0
The draws below stay inside these ranges and needn't reach their ends.
There are 2 independent parts, one for each index of `scen`. The reference program is written for one: setup_inputs(seed, part) draws one part's arguments, and reference() takes and returns one part's arrays. A program takes and returns all parts, laid end to end along the dimension named above; an argument that names none is the same for every part. Nothing has to cross between parts.
Inputs may be any that keep to these rules, and one draw needn't show every extreme that they name: `coastal_tiles`: 8 distinct tile numbers. `gauge_route`: among the 16 gauges of one owner (aligned blocks of rows) no entry is named more than 2 times; in every draw some owner names one entry exactly 2 times.
All inputs are finite; a program needn't handle non-finite values. No bound on the sum of `wet` on one device may be relied on, other than what follows from the above.
Results may differ from the reference program's by a relative error of at most 0.00022.
Values sent between devices are 32-bit elements; how exact they have to be, the bound alone decides.
No kernel may reach another device: no remote copies, remote signals or barrier semaphores. Data moves between devices by JAX's collectives and lax.ppermute only.
A program may use at most 64 MiB of HBM per device.

```python
import math
import jax
import jax.numpy as jnp
import numpy as np
from jax import lax

CX = 512
CY = 128
STEPS_BLOCK = 8
BLOCKS = 2
SAMP = 4
CAP = 2
TILES = 16
GPD = 16
NCOAST = 8
GAUGES = 256
NX = 2048
NY = 512
N_LON = 4
N_LAT = 2
N_GAU = 2


def draw_coastal_tiles(key, part):
    key = jax.random.fold_in(key, 5)
    return jax.random.permutation(key, TILES)[:NCOAST].astype(jnp.int32)


def plant(array, key, low, largest):
    extent = array.shape
    spot = [jax.random.randint(jax.random.fold_in(key, axis), (), 0, extent[axis]) for axis in range(len(extent))]
    array = array.at[tuple(spot)].set(low)
    longest = extent.index(max(extent))
    spot[longest] = (spot[longest] + 1) % extent[longest]
    return array.at[tuple(spot)].set(largest)


def block_scale(stream_key, extent, pieces, smallest, largest):
    gain, own = 1.0, jax.random.fold_in(stream_key, 6)
    for axis_at, blocks in pieces:
        heights = jnp.exp(jax.random.uniform(jax.random.fold_in(own, axis_at), (blocks,), jnp.float32, smallest / len(pieces), largest / len(pieces)))
        gain = gain * jnp.repeat(heights, extent[axis_at] // blocks).reshape([-1 if axis == axis_at else 1 for axis in range(len(extent))])
    return gain


def routed_block(rng, own, number, rows, count, top, bound, slope):
    order = jax.random.permutation(rng, count)
    packed, common = portions_of(count, rows * top, bound, slope, True), portions_of(count, rows * top, bound, slope, False)
    places = jnp.arange(count)

    def named(tallies, turn):
        used = int((tallies > 0).sum())
        fixed = max(1, used // 4)
        moved = fixed + (places - fixed + turn * (used - fixed)) % max(1, count - fixed)
        return jnp.zeros((count,), jnp.int32).at[order[jnp.where(places < fixed, places, moved)]].set(jnp.asarray(tallies, jnp.int32))

    tallies = jnp.where(number % 4 == 0, named(packed, number // 4), named(common, number - number // 4 - 1))
    mixed = jax.random.permutation(jax.random.fold_in(own, 3), count)
    donor, taker = mixed[0:count // 2 * 2:2], mixed[1:count // 2 * 2:2]
    slack = jnp.minimum(tallies[donor] - 1, bound - tallies[taker]) // 2
    slack = jnp.where((donor == order[0]) | (taker == order[0]) | (tallies[taker] == 0), 0, jnp.maximum(slack, 0))
    moved = jax.random.randint(jax.random.fold_in(own, 4), (count // 2,), 0, 1 << 20) % (slack + 1)
    tallies = tallies.at[donor].add(-moved).at[taker].add(moved)
    members = jnp.searchsorted(jnp.cumsum(tallies), jnp.arange(rows * top), side="right").astype(jnp.int32)
    grid = members.reshape(top, rows).T
    grid = grid[jax.random.permutation(jax.random.fold_in(own, 1), rows)]
    turn = jax.random.randint(jax.random.fold_in(own, 2), (rows, 1), 0, top)
    return jnp.take_along_axis(grid, (jnp.arange(top)[None, :] + turn) % top, axis=1)


def portions_of(number_of, total, reach, lean, full):
    weights = [(1 << 20) // math.isqrt(grade ** lean) + 1 for grade in range(1, number_of + 1)]
    largest = reach if full else min(reach, max(-(-total // number_of), total * weights[0] // sum(weights)))
    least = 1 if total - largest >= number_of - 1 else 0
    given, rest = [largest] + [least] * (number_of - 1), total - largest - least * (number_of - 1)
    while rest > 0:
        free = [i for i in range(1, number_of) if given[i] < largest] or [i for i in range(1, number_of) if given[i] < reach]
        whole, budget = sum([weights[i] for i in free]), rest
        for i in free:
            addition = min(reach - given[i], max(1, budget * weights[i] // whole), rest)
            given[i] = given[i] + addition
            rest = rest - addition
    return np.array(given)


def scatter_about(stream_key, dims, deviation, reach, pieces=(), kind=jnp.bfloat16):
    array = deviation * jax.random.normal(stream_key, dims, jnp.float32)
    if pieces:
        array = array * block_scale(stream_key, dims, pieces, -0.22, 0.18)
    return jnp.clip(array, -reach, reach).astype(kind)


def setup_inputs(seed: int = 0, part: int = 0) -> dict:
    key_list = jax.random.split(jax.random.key(seed), 10)
    own_keys = jax.random.split(jax.random.fold_in(key_list[9], part), 10)
    depth = jnp.clip(jnp.exp(math.log(6.0) - 0.6931472 * jax.random.uniform(key_list[0], (NY, NX), jnp.float32) ** block_scale(key_list[0], (NY, NX), ((0, 4), (1, 4)), -0.2, 0.2)), 3.0, 6.0)
    surface = scatter_about(own_keys[1], (NY, NX), 0.8, 3.0, ((0, 4), (1, 4)), jnp.float32)
    friction = jnp.clip(jnp.exp(math.log(0.06) - 3.4011973 * jax.random.uniform(key_list[2], (NY, NX), jnp.float32) ** block_scale(key_list[2], (NY, NX), ((0, 4), (1, 4)), -0.2, 0.2)), 0.002, 0.06)
    wet = plant((jax.random.randint(key_list[3], (NY, NX), 0, 4) < 3).astype(jnp.int32), jax.random.fold_in(key_list[3], 1), 0, 1)
    coastal_tiles = draw_coastal_tiles(jax.random.fold_in(key_list[9], 71), part)
    gauge_route_keys = jax.random.split(jax.random.fold_in(own_keys[5], 1), GAUGES // GPD)
    gauge_route_turns = jax.random.permutation(jax.random.fold_in(own_keys[5], 3), GAUGES // GPD)
    gauge_route = jax.vmap(lambda own, number: routed_block(jax.random.fold_in(own_keys[5], 2), own, number, GPD, NCOAST, 1, CAP, 2))(gauge_route_keys, gauge_route_turns).reshape((GAUGES, 1))
    gauge_cell = plant(jax.random.randint(own_keys[6], (GAUGES,), 0, CY * CX), jax.random.fold_in(own_keys[6], 1), 0, (CY * CX) - 1).astype(jnp.int32)
    gauge_times = plant(jax.random.randint(own_keys[7], (GAUGES, BLOCKS, SAMP), 0, STEPS_BLOCK), jax.random.fold_in(own_keys[7], 1), 0, STEPS_BLOCK - 1).astype(jnp.int32)
    gauge_resid = scatter_about(own_keys[8], (GAUGES, BLOCKS, SAMP), 1.0, 6.0, ((0, 16),), jnp.float32)
    return dict(depth=depth, surface=surface, friction=friction, wet=wet, coastal_tiles=coastal_tiles, gauge_route=gauge_route, gauge_cell=gauge_cell, gauge_times=gauge_times, gauge_resid=gauge_resid)


courant = 0.45
depth_floor = 0.1


def adjoint_step(surface_adj, flux_x, flux_y, total_depth, strength):
    padded = jnp.pad(surface_adj, 1)
    east_west = (padded[1:-1, 2:] - padded[1:-1, :-2]) * 0.5
    north_south = (padded[2:, 1:-1] - padded[:-2, 1:-1]) * 0.5
    new_x = strength * (flux_x + courant * east_west)
    new_y = strength * (flux_y + courant * north_south)
    carried_x = jnp.pad(total_depth * new_x, 1)
    carried_y = jnp.pad(total_depth * new_y, 1)
    spread_term = (carried_x[1:-1, 2:] - carried_x[1:-1, :-2]) * 0.5 + (carried_y[2:, 1:-1] - carried_y[:-2, 1:-1]) * 0.5
    return surface_adj + courant * spread_term, new_x, new_y


def reference(depth, surface, friction, wet, coastal_tiles, gauge_route, gauge_cell, gauge_times, gauge_resid):
    wet_float = wet.astype(jnp.float32)
    total_depth = jnp.maximum(depth + surface, depth_floor)
    strength = (1.0 - friction) * wet_float
    route = gauge_route[:, 0]
    target = coastal_tiles[route]
    row_blocks = N_LAT * N_GAU
    rows_at = (target % row_blocks) * CY + gauge_cell // CX
    cols_at = (target // row_blocks) * CX + gauge_cell % CX
    levels = jnp.arange(STEPS_BLOCK, dtype=jnp.int32)
    series = jnp.sum(gauge_resid[..., None] * (gauge_times[..., None] == levels).astype(jnp.float32), axis=2)
    surface_adj = jnp.zeros(depth.shape, jnp.float32)
    flux_x = jnp.zeros(depth.shape, jnp.float32)
    flux_y = jnp.zeros(depth.shape, jnp.float32)
    for block in reversed(range(BLOCKS)):
        for level in reversed(range(STEPS_BLOCK)):
            surface_adj = surface_adj.at[rows_at, cols_at].add(series[:, block, level])
            surface_adj, flux_x, flux_y = adjoint_step(surface_adj, flux_x, flux_y, total_depth, strength)
    grad = surface_adj * wet_float
    length = 2.0 * CX
    columns = jnp.arange(NX, dtype=jnp.int32)

    def strip(index):
        outputs = index * CX + jnp.arange(CX, dtype=jnp.int32)
        kernel = jnp.exp(-jnp.abs(columns[:, None] - outputs[None, :]).astype(jnp.float32) / length)
        return jnp.dot(grad, kernel, precision=lax.Precision.HIGHEST, preferred_element_type=jnp.float32)

    strips = lax.map(strip, jnp.arange(N_LON, dtype=jnp.int32))
    return jnp.transpose(strips, (1, 0, 2)).reshape(NY, NX)
```

```python
import functools
import math

import jax
import jax.numpy as jnp
from jax import lax
from jax.experimental import pallas as pl
from jax.experimental.pallas import tpu as pltpu
from jax.sharding import PartitionSpec as P

STEPS_BLOCK = 8
LANES = 128
PAD = 8
SEG = 32

courant = 0.45
depth_floor = 0.1

GRID_AXES = ("lon", "lat", "gau")
ROW_AXES = ("lat", "gau")
VMEM_LIMIT = 48 * 1024 * 1024


def roll_lanes(x, shift):
    shift = shift % LANES
    return x if shift == 0 else pltpu.roll(x, shift, 1)


def lane_iota(rows):
    return lax.broadcasted_iota(jnp.int32, (rows, LANES), 1)


def pack_lanes(pieces):
    rows = pieces[0][0].shape[0]
    segment = lane_iota(rows) // SEG
    packed = jnp.zeros((rows, LANES), jnp.float32)
    for place, (array, first) in enumerate(pieces):
        packed = jnp.where(segment == place, roll_lanes(array, place * SEG - first), packed)
    return packed


def gauge_place(owned):
    if owned <= LANES - 2 * SEG:
        return 0, 2 * SEG, SEG
    assert owned <= LANES
    return SEG, 0, SEG + 24


def prepare(
    halo, depth_ref, surface_ref, friction_ref, wet_ref, coast_ref, route_ref, cell_ref, times_ref, resid_ref,
    keep_ref, gain_ref, parcel_ref, south_ref, north_ref, east_ref, west_ref, block_ref,
):
    height, width = depth_ref.shape
    scale = (courant * 0.5) ** 2
    depth = jnp.maximum(depth_ref[...] + surface_ref[...], depth_floor)
    keep = (1.0 - friction_ref[...]) * wet_ref[...].astype(jnp.float32)
    gain = (scale * depth) * keep
    keep_ref[...] = keep
    gain_ref[...] = gain
    south_ref[0] = keep[height - halo :]
    south_ref[1] = gain[height - halo :]
    north_ref[0] = keep[:halo]
    north_ref[1] = gain[:halo]
    half = height // 2
    first, last = slice(0, LANES), slice(width - LANES, width)
    end = LANES - halo
    east_ref[...] = pack_lanes(
        [(keep[:half, last], end), (gain[:half, last], end), (keep[half:, last], end), (gain[half:, last], end)]
    )
    west_ref[...] = pack_lanes(
        [(keep[:half, first], 0), (gain[:half, first], 0), (keep[half:, first], 0), (gain[half:, first], 0)]
    )

    row_tiles = lax.axis_size("lat") * lax.axis_size("gau")
    owned = route_ref.shape[1]
    blocks, samples = times_ref.shape[:2]
    route = route_ref[...]
    target = jnp.zeros_like(route)
    for entry in range(coast_ref.shape[0]):
        target = jnp.where(route == entry, coast_ref[entry], target)
    cell = cell_ref[...]
    row_bits, width_bits = int(math.log2(row_tiles)), int(math.log2(width))
    assert row_tiles == 1 << row_bits and width == 1 << width_bits
    grid_row = (target & (row_tiles - 1)) * height + (cell >> width_bits)
    grid_col = (target >> row_bits) * width + (cell & (width - 1))
    block_ref[...] = jnp.zeros_like(block_ref)
    levels = lax.broadcasted_iota(jnp.int32, (STEPS_BLOCK, owned), 0)
    for block in range(blocks):
        times, resid = times_ref[block], resid_ref[block]
        series = jnp.zeros((STEPS_BLOCK, owned), jnp.float32)
        for sample in range(samples):
            series = series + jnp.where(times[sample : sample + 1] == levels, resid[sample : sample + 1], 0.0)
        block_ref[block * STEPS_BLOCK : (block + 1) * STEPS_BLOCK, :owned] = series
    at = blocks * STEPS_BLOCK
    block_ref[at : at + 1, :owned] = grid_row.astype(jnp.float32)
    block_ref[at + 1 : at + 2, :owned] = grid_col.astype(jnp.float32)
    top, lane, _ = gauge_place(owned)
    gauges = roll_lanes(block_ref[...], lane)
    tiles = parcel_ref.shape[0]

    def put(tile, carry):
        parcel_ref[tile, top : top + 24, :] = gauges
        return carry

    lax.fori_loop(0, tiles, put, 0, unroll=tiles <= 16)

    my_lon = lax.axis_index("lon")
    my_row = lax.axis_index("lat") * lax.axis_size("gau") + lax.axis_index("gau")
    lons = lax.axis_size("lon")
    full = jnp.zeros((SEG, LANES), jnp.float32)
    if top == 0:
        full = jnp.concatenate([gauges, jnp.zeros((SEG - 24, LANES), jnp.float32)], axis=0)
    segment = lane_iota(SEG) // SEG
    for d_row in (-1, 1):
        rows = slice(0, halo) if d_row < 0 else slice(height - halo, height)
        for d_lon in (-1, 1):
            cols, start = (first, 0) if d_lon < 0 else (last, end)
            corner = jnp.where(segment == 0, roll_lanes(keep[rows, cols], -start), full)
            corner = jnp.where(segment == 1, roll_lanes(gain[rows, cols], SEG - start), corner)
            to_row, to_lon = my_row + d_row, my_lon + d_lon
            there = (to_row >= 0) & (to_row < row_tiles) & (to_lon >= 0) & (to_lon < lons)

            @pl.when(there)
            def _():
                parcel_ref[to_lon * row_tiles + to_row, 0:SEG, :] = corner


def shift_from(planes, shift, lanes):
    count = len(planes)
    rolled = [roll_lanes(plane, -shift) for plane in planes]
    if shift > 0:
        return [jnp.where(lanes >= LANES - shift, rolled[(c + 1) % count], rolled[c]) for c in range(count)]
    return [jnp.where(lanes < -shift, rolled[(c - 1) % count], rolled[c]) for c in range(count)]


def sweep(
    steps, owned, keep_ref, gain_ref, top_ref, bottom_ref, left_ref, right_ref, parcel_ref,
    grad_ref, sums_ref,
    a, fx, fy, keep_x, gain_x, keep_y, gain_y, keep_all, gain_all, force, series_ref, rows_hot, cols_hot,
):
    height, width = keep_ref.shape
    halo = 2 * steps
    inner = width // LANES
    planes = inner + 1
    rows_all = a.shape[1]
    base = PAD + halo
    row_tiles = lax.axis_size("lat") * lax.axis_size("gau")
    lons = lax.axis_size("lon")
    my_lon = lax.axis_index("lon")
    my_row = lax.axis_index("lat") * lax.axis_size("gau") + lax.axis_index("gau")
    end = LANES - halo

    for ref in (a, fx, fy):
        ref[...] = jnp.zeros_like(ref)

    half = height // 2
    segment = lane_iota(half) // SEG
    for kind, (source, whole) in enumerate(((keep_ref, keep_all), (gain_ref, gain_all))):
        for c in range(planes):
            whole[c, 0:PAD, :] = jnp.zeros((PAD, LANES), jnp.float32)
            whole[c, rows_all - PAD :, :] = jnp.zeros((PAD, LANES), jnp.float32)
        for c in range(inner):
            cols = slice(c * LANES, (c + 1) * LANES)
            whole[c, base : base + height, :] = source[:, cols]
            whole[c, PAD:base, :] = top_ref[kind, :, cols]
            whole[c, base + height : base + height + halo, :] = bottom_ref[kind, :, cols]
        for part in range(2):
            piece = 2 * part + kind
            from_left = roll_lanes(left_ref[...], end - piece * SEG)
            from_right = roll_lanes(right_ref[...], -piece * SEG)
            both = jnp.where(segment == 0, from_right, jnp.where(segment == LANES // SEG - 1, from_left, 0.0))
            whole[inner, base + part * half : base + (part + 1) * half, :] = both
        corner_segment = lane_iota(SEG) // SEG
        for d_row, at in ((-1, PAD), (1, base + height)):
            found = jnp.zeros((SEG, LANES), jnp.float32)
            for d_lon in (-1, 1):
                row, lon = my_row + d_row, my_lon + d_lon
                there = (row >= 0) & (row < row_tiles) & (lon >= 0) & (lon < lons)
                source_tile = jnp.where(there, lon * row_tiles + row, 0)
                block = parcel_ref[source_tile, 0:SEG, :]
                goal = 0 if d_lon > 0 else end
                block = roll_lanes(block, goal - kind * SEG)
                there_scale = jnp.where(there, 1, 0)
                found = jnp.where((corner_segment == goal // SEG) & (there_scale == 1), block, found)
            whole[inner, at : at + halo, :] = found

    lanes8 = lane_iota(8)
    for whole, by_x, by_y in ((keep_all, keep_x, keep_y), (gain_all, gain_x, gain_y)):
        for r in range(PAD, rows_all - PAD, 8):
            shifted = shift_from([whole[c, r : r + 8, :] for c in range(planes)], 1, lanes8)
            for c in range(planes):
                by_x[c, r : r + 8, :] = shifted[c]
                by_y[c, r : r + 8, :] = whole[c, r + 1 : r + 9, :]

    top, lane, _ = gauge_place(owned)
    group = rows_hot.shape[1] // owned
    wide = group * owned
    sources = parcel_ref.shape[0]
    groups = sources // group
    per_plane = LANES // owned
    row_shift = (base - my_row * height).astype(jnp.float32)
    col_shift = (-my_lon * width).astype(jnp.float32)

    def gather_gauges(index):
        for part in range(wide // LANES):
            total = jnp.zeros((24, LANES), jnp.float32)
            lanes24 = lane_iota(24)
            for i in range(per_plane):
                source = index * group + part * per_plane + i
                block = roll_lanes(parcel_ref[source, top : top + 24, :], i * owned - lane)
                total = jnp.where((lanes24 >= i * owned) & (lanes24 < (i + 1) * owned), block, total)
            cols = slice(part * LANES, (part + 1) * LANES)
            series_ref[:, cols] = total[:steps]
            row = total[steps : steps + 1] + row_shift
            col = total[steps + 1 : steps + 2] + col_shift
            col = jnp.where((col >= -halo) & (col < 0), col + float(planes * LANES), jnp.where(col < width + halo, col, -1.0))
            at = lax.broadcasted_iota(jnp.int32, (rows_all, LANES), 0).astype(jnp.float32)
            rows_hot[:, cols] = (at == row).astype(jnp.float32)
            by_gauge = jnp.transpose(jnp.broadcast_to(col, (LANES, LANES)))
            for c in range(planes):
                place = (lane_iota(LANES) + c * LANES).astype(jnp.float32)
                cols_hot[part * LANES : (part + 1) * LANES, c * LANES : (c + 1) * LANES] = (
                    (by_gauge == place).astype(jnp.float32).astype(jnp.bfloat16)
                )

    def forcing(level, lo, hi):
        def product():
            value = series_ref[pl.ds(level, 1), :]
            high = value.astype(jnp.bfloat16).astype(jnp.float32)
            low = value - high
            hot = rows_hot[lo:hi, :]
            return jnp.dot(
                (hot * high).astype(jnp.bfloat16), cols_hot[...], preferred_element_type=jnp.float32
            ) + jnp.dot((hot * low).astype(jnp.bfloat16), cols_hot[...], preferred_element_type=jnp.float32)

        def store(total, add):
            for c in range(planes):
                piece = total[:, c * LANES : (c + 1) * LANES]
                force[c, lo:hi, :] = force[c, lo:hi, :] + piece if add else piece

        if groups == 1:
            store(product(), False)
        else:
            force[...] = jnp.zeros_like(force)

            def more(index, carry):
                gather_gauges(index)
                store(product(), True)
                return carry

            lax.fori_loop(0, groups, more, 0)

    if groups == 1:
        gather_gauges(0)

    col_valid = jnp.where(lanes8 < LANES // 2, jnp.where(my_lon < lons - 1, 1.0, 0.0), jnp.where(my_lon > 0, 1.0, 0.0))
    col_mask = jnp.where((lanes8 < halo) | (lanes8 >= end), col_valid, 0.0)
    above = jnp.where(my_row > 0, 1.0, 0.0)
    below = jnp.where(my_row < row_tiles - 1, 1.0, 0.0)

    def advance(lo, hi, forced):
        for r in range(lo, hi, 8):
            here = [a[c, r : r + 8, :] for c in range(planes)]
            ahead = shift_from(here, 2, lanes8)
            new_x = [
                keep_x[c, r : r + 8, :] * fx[c, r : r + 8, :] + gain_x[c, r : r + 8, :] * (ahead[c] - here[c])
                for c in range(planes)
            ]
            behind = shift_from(new_x, -2, lanes8)
            for c in range(planes):
                new_y = keep_y[c, r : r + 8, :] * fy[c, r : r + 8, :] + gain_y[c, r : r + 8, :] * (
                    a[c, r + 2 : r + 10, :] - here[c]
                )
                fx[c, r : r + 8, :] = new_x[c]
                fy[c, r : r + 8, :] = new_y
                value = here[c] + (new_x[c] - behind[c]) + (new_y - fy[c, r - 2 : r + 6, :])
                if c == inner:
                    value = value * col_mask
                if r == base - 8:
                    value = value * above
                if r == base + height:
                    value = value * below
                if forced:
                    value = value + force[c, r : r + 8, :]
                a[c, r : r + 8, :] = value

    lo, hi = PAD, rows_all - PAD
    forcing(steps - 1, lo, hi)
    for c in range(planes):
        a[c, lo:hi, :] = force[c, lo:hi, :]
    done = 0
    while done < steps - 1:
        spare = (2 * done) // 8 * 8
        bounds = (PAD + spare, rows_all - PAD - spare)
        until = min(done + 4, steps - 1)

        def body(step, carry, bounds=bounds):
            forcing(steps - 2 - step, *bounds)
            advance(*bounds, True)
            return carry

        lax.fori_loop(done, until, body, 0)
        done = until
    spare = (2 * done) // 8 * 8
    advance(PAD + spare, rows_all - PAD - spare, False)

    for c in range(inner):
        cols = slice(c * LANES, (c + 1) * LANES)
        grad_ref[:, cols] = a[c, base : base + height, :]


def weigh(grad_in, wet_ref, grad_ref, sums_ref):
    height, width = grad_in.shape
    length = 2.0 * width
    grad = grad_in[...] * wet_ref[...].astype(jnp.float32)
    grad_ref[...] = grad
    kind = lax.broadcasted_iota(jnp.int32, (8, width), 0)
    column = lax.broadcasted_iota(jnp.int32, (8, width), 1)
    steps_off = jnp.where(kind == 0, column, width - 1 - column).astype(jnp.float32)
    weights = jnp.where(kind < 2, jnp.exp(-steps_off / length), 0.0)
    sums = lax.dot_general(
        weights, grad, (((1,), (1,)), ((), ())), precision=lax.Precision.HIGHEST, preferred_element_type=jnp.float32
    )
    for i in range(sums_ref.shape[0]):
        sums_ref[i] = sums


def smooth(grad_ref, out_ref):
    width = grad_ref.shape[1]
    length = 2.0 * width
    row = lax.broadcasted_iota(jnp.int32, (width, width), 0)
    column = lax.broadcasted_iota(jnp.int32, (width, width), 1)
    kernel = jnp.exp(-jnp.abs(row - column).astype(jnp.float32) / length)
    out_ref[...] = jnp.dot(
        grad_ref[...], kernel, precision=lax.Precision.HIGHEST, preferred_element_type=jnp.float32
    )


def finish(own_ref, sums_ref, out_ref):
    width = own_ref.shape[1]
    length = 2.0 * width
    count = sums_ref.shape[0]
    me = lax.axis_index("lon")
    row = lax.broadcasted_iota(jnp.int32, (count, width), 0)
    column = lax.broadcasted_iota(jnp.int32, (count, width), 1)
    strip, kind = row >> 3, row & 7
    left = (kind == 0) & (strip > me)
    right = (kind == 1) & (strip < me)
    away = jnp.where(left, (strip - me) * width - column, (me - strip - 1) * width + column + 1)
    weights = jnp.where(left | right, jnp.exp(-jnp.maximum(away, 0).astype(jnp.float32) / length), 0.0)
    out_ref[...] = own_ref[...] + lax.dot_general(
        sums_ref[...], weights, (((0,), (0,)), ((), ())), precision=lax.Precision.HIGHEST,
        preferred_element_type=jnp.float32,
    )


def f32(*shape):
    return jax.ShapeDtypeStruct(shape, jnp.float32)


def vmem(count):
    return [pl.BlockSpec(memory_space=pltpu.VMEM)] * count


def local(depth, surface, friction, wet, coastal_tiles, gauge_route, gauge_cell, gauge_times, gauge_resid):
    height, width = depth.shape
    owned = gauge_route.shape[0]
    blocks = gauge_resid.shape[1]
    steps = blocks * STEPS_BLOCK
    halo = 2 * steps
    assert halo == SEG and height == LANES
    tiles = lax.axis_size(GRID_AXES)
    lons = lax.axis_size("lon")
    row_tiles = lax.axis_size(ROW_AXES)
    _, _, parcel_rows = gauge_place(owned)
    params = pltpu.CompilerParams(vmem_limit_bytes=VMEM_LIMIT)

    keep, gain, parcel, south, north, east, west = pl.pallas_call(
        functools.partial(prepare, halo),
        out_shape=(
            f32(height, width), f32(height, width), f32(tiles, parcel_rows, LANES),
            f32(2, halo, width), f32(2, halo, width), f32(height // 2, LANES), f32(height // 2, LANES),
        ),
        in_specs=vmem(4) + [pl.BlockSpec(memory_space=pltpu.SMEM)] + vmem(4),
        out_specs=tuple(vmem(7)),
        scratch_shapes=[pltpu.VMEM((24, LANES), jnp.float32)],
        compiler_params=params,
        name="prepare",
    )(
        depth, surface, friction, wet, coastal_tiles, gauge_route.reshape(1, owned), gauge_cell.reshape(1, owned),
        jnp.transpose(gauge_times, (1, 2, 0)), jnp.transpose(gauge_resid, (1, 2, 0)),
    )

    parcel = lax.all_to_all(parcel, GRID_AXES, split_axis=0, concat_axis=0, tiled=True)
    down = [(i, i + 1) for i in range(row_tiles - 1)]
    up = [(i + 1, i) for i in range(row_tiles - 1)]
    top = lax.ppermute(south, ROW_AXES, down)
    bottom = lax.ppermute(north, ROW_AXES, up)
    left = lax.ppermute(east, "lon", [(i, i + 1) for i in range(lons - 1)])
    right = lax.ppermute(west, "lon", [(i + 1, i) for i in range(lons - 1)])

    planes = width // LANES + 1
    rows_all = height + 2 * halo + 2 * PAD
    wide = max(2 * LANES, owned)
    plane = pltpu.VMEM((planes, rows_all, LANES), jnp.float32)
    grad = pl.pallas_call(
        functools.partial(sweep_call, steps, owned),
        out_shape=f32(height, width),
        in_specs=vmem(7),
        out_specs=vmem(1)[0],
        scratch_shapes=[plane] * 10 + [
            pltpu.VMEM((steps, wide), jnp.float32),
            pltpu.VMEM((rows_all, wide), jnp.float32),
            pltpu.VMEM((wide, planes * LANES), jnp.bfloat16),
        ],
        compiler_params=params,
        name="sweep",
    )(keep, gain, top, bottom, left, right, parcel)

    grad, sums = pl.pallas_call(
        weigh,
        out_shape=(f32(height, width), f32(lons, 8, height)),
        in_specs=vmem(2),
        out_specs=tuple(vmem(2)),
        compiler_params=params,
        name="weigh",
    )(grad, wet)
    sums = lax.all_to_all(sums, "lon", split_axis=0, concat_axis=0, tiled=True)
    own = pl.pallas_call(
        smooth, out_shape=f32(height, width), in_specs=vmem(1), out_specs=vmem(1)[0], compiler_params=params,
        cost_estimate=pl.CostEstimate(flops=6 * 2 * height * width * width, bytes_accessed=2 * 4 * height * width, transcendentals=width * width),
        name="smooth",
    )(grad)
    return pl.pallas_call(
        finish, out_shape=f32(height, width), in_specs=vmem(2), out_specs=vmem(1)[0], compiler_params=params, name="finish",
    )(own, sums.reshape(lons * 8, height))


def sweep_call(steps, owned, *refs):
    ins, grad_ref, scratch = refs[:7], refs[7], refs[8:]
    sweep(steps, owned, *ins, grad_ref, None, *scratch)


def solution(mesh):
    in_specs = (
        P(("lat", "gau"), "lon"),
        P(("scen", "lat", "gau"), "lon"),
        P(("lat", "gau"), "lon"),
        P(("lat", "gau"), "lon"),
        P(),
        P(("scen", "lon", "lat", "gau"), None),
        P(("scen", "lon", "lat", "gau")),
        P(("scen", "lon", "lat", "gau"), None, None),
        P(("scen", "lon", "lat", "gau"), None, None),
    )
    out_specs = P(("scen", "lat", "gau"), "lon")
    return jax.shard_map(local, mesh=mesh, in_specs=in_specs, out_specs=out_specs, check_vma=False)
```

```python
import functools
import math

import jax
import jax.numpy as jnp
from jax import lax
from jax.experimental import pallas as pl
from jax.experimental.pallas import tpu as pltpu
from jax.sharding import PartitionSpec as P

STEPS_BLOCK = 8
LANES = 128
PAD = 16
SEG = 32

courant = 0.45
depth_floor = 0.1

GRID_AXES = ("lon", "lat", "gau")
ROW_AXES = ("lat", "gau")
VMEM_LIMIT = 48 * 1024 * 1024


def roll_lanes(x, shift):
    shift = shift % LANES
    return x if shift == 0 else pltpu.roll(x, shift, 1)


def lane_iota(rows):
    return lax.broadcasted_iota(jnp.int32, (rows, LANES), 1)


def pack_lanes(pieces):
    rows = pieces[0][0].shape[0]
    segment = lane_iota(rows) // SEG
    packed = jnp.zeros((rows, LANES), jnp.float32)
    for place, (array, first) in enumerate(pieces):
        packed = jnp.where(segment == place, roll_lanes(array, place * SEG - first), packed)
    return packed


def gauge_rows(owned):
    if 3 * owned <= LANES:
        return STEPS_BLOCK, owned
    assert owned <= LANES
    return 3 * STEPS_BLOCK, 0


def my_place():
    row = lax.axis_index("lat") * lax.axis_size("gau") + lax.axis_index("gau")
    return row, lax.axis_index("lon"), lax.axis_size("lat") * lax.axis_size("gau"), lax.axis_size("lon")


def prepare(
    halo, keep_ref, gain_ref, coast_ref, route_ref, cell_ref, times_ref, resid_ref,
    parcel_ref, rows_ref, strips_ref, block_ref,
):
    height, width = keep_ref.shape
    my_row, my_lon, row_tiles, lons = my_place()
    keep, gain = keep_ref[...], gain_ref[...]
    half = height // 2
    first, last = slice(0, LANES), slice(width - LANES, width)
    end = LANES - halo

    owned = route_ref.shape[1]
    blocks, samples = times_ref.shape[:2]
    assert blocks == 2
    route, coast = route_ref[...], coast_ref[...]
    target = jnp.zeros_like(route)
    for entry in range(coast.shape[1]):
        target = jnp.where(route == entry, jnp.broadcast_to(coast[:, entry : entry + 1], route.shape), target)
    cell = cell_ref[...]
    row_bits, width_bits = int(math.log2(row_tiles)), int(math.log2(width))
    assert row_tiles == 1 << row_bits and width == 1 << width_bits
    grid_row = (target & (row_tiles - 1)) * height + (cell >> width_bits)
    grid_col = (target >> row_bits) * width + (cell & (width - 1))
    block_ref[...] = jnp.zeros_like(block_ref)
    levels = lax.broadcasted_iota(jnp.int32, (STEPS_BLOCK, owned), 0)
    for block in range(blocks):
        times, resid = times_ref[block], resid_ref[block]
        series = jnp.zeros((STEPS_BLOCK, owned), jnp.float32)
        for sample in range(samples):
            series = series + jnp.where(times[sample : sample + 1] == levels, resid[sample : sample + 1], 0.0)
        block_ref[block * STEPS_BLOCK : (block + 1) * STEPS_BLOCK, :owned] = series
    at = blocks * STEPS_BLOCK
    block_ref[at : at + 1, :owned] = grid_row.astype(jnp.float32)
    block_ref[at + 1 : at + 2, :owned] = grid_col.astype(jnp.float32)
    size, apart = gauge_rows(owned)
    gauges = block_ref[...]
    if size == STEPS_BLOCK:
        gauges = sum(
            roll_lanes(gauges[i * STEPS_BLOCK : (i + 1) * STEPS_BLOCK], i * apart) for i in range(3)
        )
    tiles = parcel_ref.shape[0]

    def put(tile, carry):
        parcel_ref[tile, 0:size, :] = gauges
        return carry

    lax.fori_loop(0, tiles, put, 0, unroll=tiles <= 16)

    for d_row in (-1, 1):
        top = 0 if d_row < 0 else height - halo
        for d_lon in (-1, 1):
            cols, start = (first, 0) if d_lon < 0 else (last, end)
            to_row, to_lon = my_row + d_row, my_lon + d_lon
            there = (to_row >= 0) & (to_row < row_tiles) & (to_lon >= 0) & (to_lon < lons)

            @pl.when(there)
            def _():
                for kind, source in enumerate((keep, gain)):
                    corner = pack_lanes([(source[top + 8 * i : top + 8 * i + 8, cols], start) for i in range(4)])
                    parcel_ref[to_lon * row_tiles + to_row, size + 8 * kind : size + 8 * kind + 8, :] = corner

        there = (my_row + d_row >= 0) & (my_row + d_row < row_tiles)

        @pl.when(there)
        def _():
            rows_ref[my_row + d_row, 0] = keep[top : top + halo]
            rows_ref[my_row + d_row, 1] = gain[top : top + halo]

    for d_lon in (-1, 1):
        cols, start = (first, 0) if d_lon < 0 else (last, end)
        there = (my_lon + d_lon >= 0) & (my_lon + d_lon < lons)

        @pl.when(there)
        def _():
            strips_ref[my_lon + d_lon] = pack_lanes(
                [(keep[:half, cols], start), (gain[:half, cols], start), (keep[half:, cols], start), (gain[half:, cols], start)]
            )


def shift_from(planes, shift, lanes):
    count = len(planes)
    rolled = [roll_lanes(plane, -shift) for plane in planes]
    if shift > 0:
        return [jnp.where(lanes >= LANES - shift, rolled[(c + 1) % count], rolled[c]) for c in range(count)]
    return [jnp.where(lanes < -shift, rolled[(c - 1) % count], rolled[c]) for c in range(count)]


def sweep(
    steps, owned, keep_ref, gain_ref, rows_ref, strips_ref, parcel_ref,
    grad_ref, sums_ref,
    a, fx, fy, keep_x, gain_x, keep_all, gain_all, force0, force1, series_ref, rows_hot, cols_hot,
):
    height, width = keep_ref.shape
    halo = 2 * steps
    inner = width // LANES
    planes = inner + 1
    rows_all = a.shape[1]
    base = PAD + halo
    my_row, my_lon, row_tiles, lons = my_place()
    end = LANES - halo
    size, apart = gauge_rows(owned)

    for ref in (a, fx, fy):
        ref[...] = jnp.zeros_like(ref)

    def known(condition, value):
        return jnp.where(jnp.where(condition, 1, 0) == 1, value, 0.0)

    half = height // 2
    has_top, has_bottom = my_row > 0, my_row < row_tiles - 1
    has_left, has_right = my_lon > 0, my_lon < lons - 1
    above, below = jnp.maximum(my_row - 1, 0), jnp.minimum(my_row + 1, row_tiles - 1)
    left, right = jnp.maximum(my_lon - 1, 0), jnp.minimum(my_lon + 1, lons - 1)
    for kind, (source, whole) in enumerate(((keep_ref, keep_all), (gain_ref, gain_all))):
        for c in range(planes):
            whole[c, 0:PAD, :] = jnp.zeros((PAD, LANES), jnp.float32)
            whole[c, rows_all - PAD :, :] = jnp.zeros((PAD, LANES), jnp.float32)
        for c in range(inner):
            cols = slice(c * LANES, (c + 1) * LANES)
            whole[c, base : base + height, :] = source[:, cols]
            whole[c, PAD:base, :] = known(has_top, rows_ref[above, kind, :, cols])
            whole[c, base + height : base + height + halo, :] = known(has_bottom, rows_ref[below, kind, :, cols])
        segment = lane_iota(half) // SEG
        from_left, from_right = strips_ref[left], strips_ref[right]
        for part in range(2):
            piece = 2 * part + kind
            by_left = known(has_left, roll_lanes(from_left, end - piece * SEG))
            by_right = known(has_right, roll_lanes(from_right, -piece * SEG))
            both = jnp.where(segment == 0, by_right, jnp.where(segment == LANES // SEG - 1, by_left, 0.0))
            whole[inner, base + part * half : base + (part + 1) * half, :] = both
        segment = lane_iota(8) // SEG
        for has_row, row, at in ((has_top, above, PAD), (has_bottom, below, base + height)):
            by_left = known(has_row & has_left, parcel_ref[left * row_tiles + row, size + 8 * kind : size + 8 * kind + 8, :])
            by_right = known(has_row & has_right, parcel_ref[right * row_tiles + row, size + 8 * kind : size + 8 * kind + 8, :])
            for i in range(4):
                both = jnp.where(
                    segment == 0, roll_lanes(by_right, -i * SEG),
                    jnp.where(segment == LANES // SEG - 1, roll_lanes(by_left, end - i * SEG), 0.0),
                )
                whole[inner, at + 8 * i : at + 8 * i + 8, :] = both

    lanes8 = lane_iota(8)
    for whole, by_x in ((keep_all, keep_x), (gain_all, gain_x)):
        for r in range(PAD, rows_all - PAD, 8):
            shifted = shift_from([whole[c, r : r + 8, :] for c in range(planes)], 1, lanes8)
            for c in range(planes):
                by_x[c, r : r + 8, :] = shifted[c]

    group = rows_hot.shape[1] // owned
    wide = group * owned
    groups = parcel_ref.shape[0] // group
    per_plane = LANES // owned
    row_shift = (base - my_row * height).astype(jnp.float32)
    col_shift = (-my_lon * width).astype(jnp.float32)

    def gather_gauges(index):
        lanes = lane_iota(STEPS_BLOCK)
        for part in range(wide // LANES):
            cols = slice(part * LANES, (part + 1) * LANES)
            fields = []
            for field in range(3):
                total = jnp.zeros((STEPS_BLOCK, LANES), jnp.float32)
                rows = slice(0, 8) if apart else slice(8 * field, 8 * field + 8)
                for i in range(per_plane):
                    source = index * group + part * per_plane + i
                    block = roll_lanes(parcel_ref[source, rows, :], i * owned - field * apart)
                    total = jnp.where((lanes >= i * owned) & (lanes < (i + 1) * owned), block, total)
                fields.append(total)
            series_ref[0:8, cols] = fields[0]
            series_ref[8:16, cols] = fields[1]
            row = fields[2][0:1] + row_shift
            col = fields[2][1:2] + col_shift
            col = jnp.where((col >= -halo) & (col < 0), col + float(planes * LANES), jnp.where(col < width + halo, col, -1.0))
            at = lax.broadcasted_iota(jnp.int32, (rows_all, LANES), 0).astype(jnp.float32)
            rows_hot[:, cols] = (at == row).astype(jnp.float32).astype(jnp.bfloat16)
            by_gauge = jnp.transpose(jnp.broadcast_to(col, (LANES, LANES)))
            for c in range(planes):
                place = (lane_iota(LANES) + c * LANES).astype(jnp.float32)
                cols_hot[part * LANES : (part + 1) * LANES, c * LANES : (c + 1) * LANES] = (
                    (by_gauge == place).astype(jnp.float32).astype(jnp.bfloat16)
                )

    def pieces_of(level, lo, hi, goal, add=False):
        lo, hi = lo // 16 * 16, -(-hi // 16) * 16
        value = series_ref[pl.ds(level, 1), :]
        high = value.astype(jnp.bfloat16)
        low = (value - high.astype(jnp.float32)).astype(jnp.bfloat16)
        hot = rows_hot[lo:hi, :]
        both = jnp.concatenate([hot * high, hot * low], axis=0)

        def piece(first, count):
            total = jnp.dot(
                both, cols_hot[:, first * LANES : (first + count) * LANES], preferred_element_type=jnp.float32
            )
            total = total[: hi - lo] + total[hi - lo :]
            for c in range(count):
                part = total[:, c * LANES : (c + 1) * LANES]
                goal[first + c, lo:hi, :] = goal[first + c, lo:hi, :] + part if add else part

        return [functools.partial(piece, first, min(2, planes - first)) for first in range(0, planes, 2)]

    def pieces_for(level, lo, hi, goal):
        if groups == 1:
            return pieces_of(level, lo, hi, goal)

        def whole():
            goal[...] = jnp.zeros_like(goal)

            def more(index, carry):
                gather_gauges(index)
                for piece in pieces_of(level, lo, hi, goal, True):
                    piece()
                return carry

            lax.fori_loop(0, groups, more, 0)

        return [whole]

    if groups == 1:
        gather_gauges(0)

    col_valid = jnp.where(lanes8 < LANES // 2, jnp.where(has_right, 1.0, 0.0), jnp.where(has_left, 1.0, 0.0))
    col_mask = jnp.where((lanes8 < halo) | (lanes8 >= end), col_valid, 0.0)
    row_above, row_below = jnp.where(has_top, 1.0, 0.0), jnp.where(has_bottom, 1.0, 0.0)

    def advance(step, force, pieces):
        spare = 2 * step // 8 * 8
        lo, hi = PAD + spare, rows_all - PAD - spare
        every = (hi - lo) // 8 // max(1, len(pieces))
        pieces = list(pieces)
        for r in range(lo, hi, 8):
            if pieces and (r - lo) // 8 % every == 0:
                pieces.pop(0)()
            here = [a[c, r : r + 8, :] for c in range(planes)]
            ahead = shift_from(here, 2, lanes8)
            new_x = [
                keep_x[c, r : r + 8, :] * fx[c, r : r + 8, :] + gain_x[c, r : r + 8, :] * (ahead[c] - here[c])
                for c in range(planes)
            ]
            behind = shift_from(new_x, -2, lanes8)
            for c in range(planes):
                new_y = keep_all[c, r + 1 : r + 9, :] * fy[c, r : r + 8, :] + gain_all[c, r + 1 : r + 9, :] * (
                    a[c, r + 2 : r + 10, :] - here[c]
                )
                fx[c, r : r + 8, :] = new_x[c]
                fy[c, r : r + 8, :] = new_y
                value = here[c] + (new_x[c] - behind[c]) + (new_y - fy[c, r - 2 : r + 6, :])
                if c == inner:
                    value = value * col_mask
                if r == base - 8:
                    value = value * row_above
                if r == base + height:
                    value = value * row_below
                if force is not None:
                    value = value + force[c, r : r + 8, :]
                a[c, r : r + 8, :] = value
        assert not pieces

    last = steps - 1
    for order, goal in ((0, a), (1, force1)):
        for piece in pieces_for(last - order, PAD, rows_all - PAD, goal):
            piece()

    def pair(step, like):
        for odd in range(2):
            spare = 2 * like // 8 * 8
            uses, makes = (force1, force0) if odd == 0 else (force0, force1)
            pieces = pieces_for(last - 2 - step - odd, PAD + spare, rows_all - PAD - spare, makes)
            advance(like, uses, pieces)

    for start in range(0, steps, 4):
        if start + 4 < steps:

            def body(index, carry, start=start):
                pair(start + 2 * index, start)
                return carry

            lax.fori_loop(0, 2, body, 0)
        else:
            pair(start, start)
            advance(start, force1, [])
            advance(start, None, [])

    grad = jnp.concatenate([a[c, base : base + height, :] for c in range(inner)], axis=1)
    grad = jnp.where(keep_ref[...] > 0.0, grad, 0.0)
    grad_ref[...] = grad
    length = 2.0 * width
    kind = lax.broadcasted_iota(jnp.int32, (8, width), 0)
    column = lax.broadcasted_iota(jnp.int32, (8, width), 1)
    steps_off = jnp.where(kind == 0, column, width - 1 - column).astype(jnp.float32)
    weights = jnp.where(kind < 2, jnp.exp(-steps_off / length), 0.0)
    sums = lax.dot_general(
        weights, grad, (((1,), (1,)), ((), ())), precision=lax.Precision.HIGHEST, preferred_element_type=jnp.float32
    )
    for i in range(sums_ref.shape[0]):
        sums_ref[i] = sums


def smooth(grad_ref, out_ref):
    width = grad_ref.shape[1]
    length = 2.0 * width
    row = lax.broadcasted_iota(jnp.int32, (width, width), 0)
    column = lax.broadcasted_iota(jnp.int32, (width, width), 1)
    kernel = jnp.exp(-jnp.abs(row - column).astype(jnp.float32) / length)
    out_ref[...] = jnp.dot(
        grad_ref[...], kernel, precision=lax.Precision.HIGHEST, preferred_element_type=jnp.float32
    )


def finish(own_ref, sums_ref, out_ref):
    width = own_ref.shape[1]
    length = 2.0 * width
    count = sums_ref.shape[0]
    me = lax.axis_index("lon")
    row = lax.broadcasted_iota(jnp.int32, (count, width), 0)
    column = lax.broadcasted_iota(jnp.int32, (count, width), 1)
    strip, kind = row >> 3, row & 7
    left = (kind == 0) & (strip > me)
    right = (kind == 1) & (strip < me)
    away = jnp.where(left, (strip - me) * width - column, (me - strip - 1) * width + column + 1)
    weights = jnp.where(left | right, jnp.exp(-jnp.maximum(away, 0).astype(jnp.float32) / length), 0.0)
    out_ref[...] = own_ref[...] + lax.dot_general(
        sums_ref[...], weights, (((0,), (0,)), ((), ())), precision=lax.Precision.HIGHEST,
        preferred_element_type=jnp.float32,
    )


def f32(*shape):
    return jax.ShapeDtypeStruct(shape, jnp.float32)


def vmem(count):
    return [pl.BlockSpec(memory_space=pltpu.VMEM)] * count


def local(depth, surface, friction, wet, coastal_tiles, gauge_route, gauge_cell, gauge_times, gauge_resid):
    height, width = depth.shape
    owned = gauge_route.shape[0]
    blocks = gauge_resid.shape[1]
    steps = blocks * STEPS_BLOCK
    halo = 2 * steps
    assert halo == SEG and height == LANES
    tiles = lax.axis_size(GRID_AXES)
    lons = lax.axis_size("lon")
    row_tiles = lax.axis_size(ROW_AXES)
    parcel_rows = gauge_rows(owned)[0] + 16
    params = pltpu.CompilerParams(vmem_limit_bytes=VMEM_LIMIT)

    keep = (1.0 - friction) * wet.astype(jnp.float32)
    gain = ((courant * 0.5) ** 2 * jnp.maximum(depth + surface, depth_floor)) * keep
    parcel, rows, strips = pl.pallas_call(
        functools.partial(prepare, halo),
        out_shape=(
            f32(tiles, parcel_rows, LANES), f32(row_tiles, 2, halo, width), f32(lons, height // 2, LANES),
        ),
        in_specs=vmem(7),
        out_specs=tuple(vmem(3)),
        scratch_shapes=[pltpu.VMEM((24, LANES), jnp.float32)],
        compiler_params=params,
        name="prepare",
    )(
        keep, gain, coastal_tiles.reshape(1, -1), gauge_route.reshape(1, owned), gauge_cell.reshape(1, owned),
        jnp.transpose(gauge_times, (1, 2, 0)), jnp.transpose(gauge_resid, (1, 2, 0)),
    )

    def exchange(array, axes):
        return lax.all_to_all(array, axes, split_axis=0, concat_axis=0, tiled=True)

    rows = exchange(rows, ROW_AXES)
    strips = exchange(strips, "lon")
    parcel = exchange(parcel, GRID_AXES)

    planes = width // LANES + 1
    rows_all = height + 2 * halo + 2 * PAD
    wide = max(2 * LANES, owned)
    plane = pltpu.VMEM((planes, rows_all, LANES), jnp.float32)
    grad, sums = pl.pallas_call(
        functools.partial(sweep, steps, owned),
        out_shape=(f32(height, width), f32(lons, 8, height)),
        in_specs=vmem(5),
        out_specs=tuple(vmem(2)),
        scratch_shapes=[plane] * 9 + [
            pltpu.VMEM((steps, wide), jnp.float32),
            pltpu.VMEM((rows_all, wide), jnp.bfloat16),
            pltpu.VMEM((wide, planes * LANES), jnp.bfloat16),
        ],
        compiler_params=params,
        name="sweep",
    )(keep, gain, rows, strips, parcel)

    sums = exchange(sums, "lon")
    own = pl.pallas_call(
        smooth, out_shape=f32(height, width), in_specs=vmem(1), out_specs=vmem(1)[0], compiler_params=params,
        cost_estimate=pl.CostEstimate(
            flops=6 * 2 * height * width * width, bytes_accessed=2 * 4 * height * width, transcendentals=width * width
        ),
        name="smooth",
    )(grad)
    return pl.pallas_call(
        finish, out_shape=f32(height, width), in_specs=vmem(2), out_specs=vmem(1)[0], compiler_params=params, name="finish",
    )(own, sums.reshape(lons * 8, height))


def solution(mesh):
    in_specs = (
        P(("lat", "gau"), "lon"),
        P(("scen", "lat", "gau"), "lon"),
        P(("lat", "gau"), "lon"),
        P(("lat", "gau"), "lon"),
        P(),
        P(("scen", "lon", "lat", "gau"), None),
        P(("scen", "lon", "lat", "gau")),
        P(("scen", "lon", "lat", "gau"), None, None),
        P(("scen", "lon", "lat", "gau"), None, None),
    )
    out_specs = P(("scen", "lat", "gau"), "lon")
    return jax.shard_map(local, mesh=mesh, in_specs=in_specs, out_specs=out_specs, check_vma=False)
```

```python
import functools
import math

import jax
import jax.numpy as jnp
from jax import lax
from jax.experimental import pallas as pl
from jax.experimental.pallas import tpu as pltpu
from jax.sharding import PartitionSpec as P

STEPS_BLOCK = 8
LANES = 128
SEG = 32

courant = 0.45
depth_floor = 0.1

GRID_AXES = ("lon", "lat", "gau")
ROW_AXES = ("lat", "gau")
VMEM_LIMIT = 16 * 1024 * 1024


def roll_lanes(x, shift):
    shift = shift % LANES
    return x if shift == 0 else pltpu.roll(x, shift, 1)


def lane_iota(rows):
    return lax.broadcasted_iota(jnp.int32, (rows, LANES), 1)


def pack_lanes(pieces):
    rows = pieces[0][0].shape[0]
    segment = lane_iota(rows) // SEG
    packed = jnp.zeros((rows, LANES), jnp.float32)
    for place, (array, first) in enumerate(pieces):
        packed = jnp.where(segment == place, roll_lanes(array, place * SEG - first), packed)
    return packed


def gauge_rows(owned):
    if 3 * owned <= LANES:
        return STEPS_BLOCK, owned
    assert owned <= LANES
    return 3 * STEPS_BLOCK, 0


def my_place():
    row = lax.axis_index("lat") * lax.axis_size("gau") + lax.axis_index("gau")
    return row, lax.axis_index("lon"), lax.axis_size("lat") * lax.axis_size("gau"), lax.axis_size("lon")


def prepare(
    halo, keep_ref, gain_ref, coast_ref, route_ref, cell_ref, times_ref, resid_ref,
    parcel_ref, south_ref, north_ref, east_ref, west_ref, block_ref,
):
    height, width = keep_ref.shape
    my_row, my_lon, row_tiles, lons = my_place()
    keep, gain = keep_ref[...], gain_ref[...]
    half = height // 2
    first, last = slice(0, LANES), slice(width - LANES, width)
    end = LANES - halo

    owned = route_ref.shape[1]
    blocks, samples = times_ref.shape[:2]
    assert blocks == 2
    route, coast = route_ref[...], coast_ref[...]
    target = jnp.zeros_like(route)
    for entry in range(coast.shape[1]):
        target = jnp.where(route == entry, jnp.broadcast_to(coast[:, entry : entry + 1], route.shape), target)
    cell = cell_ref[...]
    row_bits, width_bits = int(math.log2(row_tiles)), int(math.log2(width))
    assert row_tiles == 1 << row_bits and width == 1 << width_bits
    grid_row = (target & (row_tiles - 1)) * height + (cell >> width_bits)
    grid_col = (target >> row_bits) * width + (cell & (width - 1))
    block_ref[...] = jnp.zeros_like(block_ref)
    levels = lax.broadcasted_iota(jnp.int32, (STEPS_BLOCK, owned), 0)
    for block in range(blocks):
        times, resid = times_ref[block], resid_ref[block]
        series = jnp.zeros((STEPS_BLOCK, owned), jnp.float32)
        for sample in range(samples):
            series = series + jnp.where(times[sample : sample + 1] == levels, resid[sample : sample + 1], 0.0)
        block_ref[block * STEPS_BLOCK : (block + 1) * STEPS_BLOCK, :owned] = series
    at = blocks * STEPS_BLOCK
    block_ref[at : at + 1, :owned] = grid_row.astype(jnp.float32)
    block_ref[at + 1 : at + 2, :owned] = grid_col.astype(jnp.float32)
    size, apart = gauge_rows(owned)
    gauges = block_ref[...]
    if size == STEPS_BLOCK:
        gauges = sum(
            roll_lanes(gauges[i * STEPS_BLOCK : (i + 1) * STEPS_BLOCK], i * apart) for i in range(3)
        )
    tiles = parcel_ref.shape[0]

    def put(tile, carry):
        parcel_ref[tile, 0:size, :] = gauges
        return carry

    lax.fori_loop(0, tiles, put, 0, unroll=tiles <= 16)

    for d_row in (-1, 1):
        top = 0 if d_row < 0 else height - halo
        for d_lon in (-1, 1):
            cols, start = (first, 0) if d_lon < 0 else (last, end)
            to_row, to_lon = my_row + d_row, my_lon + d_lon
            there = (to_row >= 0) & (to_row < row_tiles) & (to_lon >= 0) & (to_lon < lons)

            @pl.when(there)
            def _():
                for kind, source in enumerate((keep, gain)):
                    corner = pack_lanes([(source[top + 8 * i : top + 8 * i + 8, cols], start) for i in range(4)])
                    parcel_ref[to_lon * row_tiles + to_row, size + 8 * kind : size + 8 * kind + 8, :] = corner

    south_ref[0], south_ref[1] = keep[height - halo :], gain[height - halo :]
    north_ref[0], north_ref[1] = keep[:halo], gain[:halo]
    for goal, cols, start in ((east_ref, last, end), (west_ref, first, 0)):
        goal[...] = pack_lanes(
            [(keep[:half, cols], start), (gain[:half, cols], start), (keep[half:, cols], start), (gain[half:, cols], start)]
        )


def shift_from(planes, shift, lanes):
    count = len(planes)
    rolled = [roll_lanes(plane, -shift) for plane in planes]
    if shift > 0:
        return [jnp.where(lanes >= LANES - shift, rolled[(c + 1) % count], rolled[c]) for c in range(count)]
    return [jnp.where(lanes < -shift, rolled[(c - 1) % count], rolled[c]) for c in range(count)]


def force(steps, halo, height, width, parcel_ref, force_ref, series_ref, rows_hot, cols_hot):
    planes, rows_all = force_ref.shape[1:3]
    my_row, my_lon, row_tiles, lons = my_place()
    wide = rows_hot.shape[1]
    tiles, parcel_rows = parcel_ref.shape[:2]
    size = parcel_rows - 16
    apart = wide // tiles if size == STEPS_BLOCK else 0
    owned = apart if apart else LANES
    group = wide // owned
    groups = tiles // group
    per_plane = LANES // owned
    blocks = rows_all // 8
    row_shift = (halo - my_row * height).astype(jnp.float32)
    col_shift = (-my_lon * width).astype(jnp.float32)
    place = lax.broadcasted_iota(jnp.int32, (rows_all, LANES), 0)
    at = ((place & 7) * blocks + (place >> 3)).astype(jnp.float32)

    def gather_gauges(index):
        lanes = lane_iota(STEPS_BLOCK)
        for part in range(wide // LANES):
            cols = slice(part * LANES, (part + 1) * LANES)
            fields = []
            for field in range(3):
                total = jnp.zeros((STEPS_BLOCK, LANES), jnp.float32)
                rows = slice(0, 8) if apart else slice(8 * field, 8 * field + 8)
                for i in range(per_plane):
                    source = index * group + part * per_plane + i
                    block = roll_lanes(parcel_ref[source, rows, :], i * owned - field * apart)
                    total = jnp.where((lanes >= i * owned) & (lanes < (i + 1) * owned), block, total)
                fields.append(total)
            series_ref[0:8, cols] = fields[0]
            series_ref[8:16, cols] = fields[1]
            row = fields[2][0:1] + row_shift
            col = fields[2][1:2] + col_shift
            col = jnp.where((col >= -halo) & (col < 0), col + float(planes * LANES), jnp.where(col < width + halo, col, -1.0))
            rows_hot[:, cols] = (at == row).astype(jnp.float32).astype(jnp.bfloat16)
            by_gauge = jnp.transpose(jnp.broadcast_to(col, (LANES, LANES)))
            for c in range(planes):
                spot = (lane_iota(LANES) + c * LANES).astype(jnp.float32)
                hot = (by_gauge == spot).astype(jnp.float32).astype(jnp.bfloat16)
                cols_hot[part * LANES : (part + 1) * LANES, c * LANES : (c + 1) * LANES] = hot
                cols_hot[wide + part * LANES : wide + (part + 1) * LANES, c * LANES : (c + 1) * LANES] = hot

    def level_of(level, add):
        value = series_ref[pl.ds(level, 1), :]
        high = value.astype(jnp.bfloat16)
        low = (value - high.astype(jnp.float32)).astype(jnp.bfloat16)
        hot = rows_hot[...]
        both = jnp.concatenate([hot * high, hot * low], axis=1)
        for first in range(0, planes, 2):
            count = min(2, planes - first)
            total = jnp.dot(
                both, cols_hot[:, first * LANES : (first + count) * LANES], preferred_element_type=jnp.float32
            )
            for c in range(count):
                part = total[:, c * LANES : (c + 1) * LANES]
                force_ref[level, first + c] = force_ref[level, first + c] + part if add else part

    def levels(add):
        def one(level, carry):
            level_of(level, add)
            return carry

        lax.fori_loop(0, steps, one, 0)

    gather_gauges(0)
    levels(False)
    if groups > 1:

        def more(index, carry):
            gather_gauges(index)
            levels(True)
            return carry

        lax.fori_loop(1, groups, more, 0)


def sweep(
    steps, keep_ref, gain_ref, top_ref, bottom_ref, left_ref, right_ref, parcel_ref, force_ref,
    grad_ref, sums_ref,
    a, fx, fy, keep_x, gain_x, keep_y, gain_y, plain,
):
    height, width = keep_ref.shape
    halo = 2 * steps
    inner = width // LANES
    planes = inner + 1
    rows_all = a.shape[1]
    blocks = rows_all // 8
    my_row, my_lon, row_tiles, lons = my_place()
    end = LANES - halo
    size = parcel_ref.shape[1] - 16
    has_top, has_bottom = my_row > 0, my_row < row_tiles - 1
    has_left, has_right = my_lon > 0, my_lon < lons - 1
    above, below = jnp.maximum(my_row - 1, 0), jnp.minimum(my_row + 1, row_tiles - 1)
    left, right = jnp.maximum(my_lon - 1, 0), jnp.minimum(my_lon + 1, lons - 1)
    lanes8 = lane_iota(8)

    def known(condition, value):
        return jnp.where(jnp.where(condition, 1, 0) == 1, value, 0.0)

    def up(value):
        return pltpu.roll(value, 7, 0)

    def down(value):
        return pltpu.roll(value, 1, 0)

    half = height // 2
    for kind, (source, by_x, by_y) in enumerate(((keep_ref, keep_x, keep_y), (gain_ref, gain_x, gain_y))):
        for c in range(inner):
            cols = slice(c * LANES, (c + 1) * LANES)
            plain[c, halo : halo + height, :] = source[:, cols]
            plain[c, 0:halo, :] = top_ref[kind, :, cols]
            plain[c, halo + height :, :] = bottom_ref[kind, :, cols]
        segment = lane_iota(half) // SEG
        for part in range(2):
            piece = 2 * part + kind
            by_left = roll_lanes(left_ref[...], end - piece * SEG)
            by_right = roll_lanes(right_ref[...], -piece * SEG)
            both = jnp.where(segment == 0, by_right, jnp.where(segment == LANES // SEG - 1, by_left, 0.0))
            plain[inner, halo + part * half : halo + (part + 1) * half, :] = both
        segment = lane_iota(8) // SEG
        for has_row, row, at in ((has_top, above, 0), (has_bottom, below, halo + height)):
            by_left = known(has_row & has_left, parcel_ref[left * row_tiles + row, size + 8 * kind : size + 8 * kind + 8, :])
            by_right = known(has_row & has_right, parcel_ref[right * row_tiles + row, size + 8 * kind : size + 8 * kind + 8, :])
            for i in range(4):
                both = jnp.where(
                    segment == 0, roll_lanes(by_right, -i * SEG),
                    jnp.where(segment == LANES // SEG - 1, roll_lanes(by_left, end - i * SEG), 0.0),
                )
                plain[inner, at + 8 * i : at + 8 * i + 8, :] = both
        for q in range(blocks):
            values = [plain[c, pl.ds(q, 8, stride=blocks), :] for c in range(planes)]
            shifted = shift_from(values, 1, lanes8)
            to = (q - 1) % blocks * 8
            for c in range(planes):
                by_x[c, 8 * q : 8 * q + 8, :] = shifted[c]
                by_y[c, to : to + 8, :] = up(values[c]) if q == 0 else values[c]

    for ref in (a, fx, fy):
        ref[...] = jnp.zeros_like(ref)

    col_valid = jnp.where(lanes8 < LANES // 2, jnp.where(has_right, 1.0, 0.0), jnp.where(has_left, 1.0, 0.0))
    col_mask = jnp.where((lanes8 < halo) | (lanes8 >= end), col_valid, 0.0)
    sublane = lax.broadcasted_iota(jnp.int32, (8, LANES), 0)
    row_mask = {}
    for row, there in ((halo - 1, has_top), (halo + height, has_bottom)):
        row_mask[row % blocks] = jnp.where(sublane == row // blocks, jnp.where(there, 1.0, 0.0), 1.0)
    every = range(planes)

    def step(index, carry):
        level = steps - 1 - index
        current, new_y = {}, {}

        def here(q):
            if q not in current:
                current[q] = [a[c, 8 * q : 8 * q + 8, :] + force_ref[level, c, 8 * q : 8 * q + 8, :] for c in every]
            return current[q]

        def move_y(q):
            near = here(q)
            ahead = here(q + 2) if q + 2 < blocks else [up(value) for value in here(q + 2 - blocks)]
            rows = slice(8 * q, 8 * q + 8)
            new_y[q] = [keep_y[c, rows, :] * fy[c, rows, :] + gain_y[c, rows, :] * (ahead[c] - near[c]) for c in every]
            for c in every:
                fy[c, rows, :] = new_y[q][c]

        def move(q):
            near = here(q)
            rows = slice(8 * q, 8 * q + 8)
            ahead = shift_from(near, 2, lanes8)
            new_x = [keep_x[c, rows, :] * fx[c, rows, :] + gain_x[c, rows, :] * (ahead[c] - near[c]) for c in every]
            behind = shift_from(new_x, -2, lanes8)
            before = new_y[q - 2] if q >= 2 else [down(value) for value in new_y[q - 2 + blocks]]
            for c in every:
                fx[c, rows, :] = new_x[c]
                value = near[c] + (new_x[c] - behind[c]) + (new_y[q][c] - before[c])
                if c == inner:
                    value = value * col_mask
                if q in row_mask:
                    value = value * row_mask[q]
                a[c, rows, :] = value

        move_y(0)
        move_y(1)
        for q in range(2, blocks):
            move_y(q)
            move(q)
        move(0)
        move(1)
        return carry

    lax.fori_loop(0, steps, step, 0)

    for r in range(0, height, 8):
        s, q = divmod(halo + r, blocks)
        for c in range(inner):
            cols = slice(c * LANES, (c + 1) * LANES)
            value = a[c, pl.ds(8 * q + s, 8, stride=8), :]
            grad_ref[r : r + 8, cols] = jnp.where(keep_ref[r : r + 8, cols] > 0.0, value, 0.0)
    length = 2.0 * width
    kind = lax.broadcasted_iota(jnp.int32, (8, width), 0)
    column = lax.broadcasted_iota(jnp.int32, (8, width), 1)
    steps_off = jnp.where(kind == 0, column, width - 1 - column).astype(jnp.float32)
    weights = jnp.where(kind < 2, jnp.exp(-steps_off / length), 0.0)
    sums = lax.dot_general(
        weights, grad_ref[...], (((1,), (1,)), ((), ())), precision=lax.Precision.HIGHEST,
        preferred_element_type=jnp.float32,
    )
    for i in range(sums_ref.shape[0]):
        sums_ref[i] = sums


def smooth(grad_ref, out_ref):
    width = grad_ref.shape[1]
    length = 2.0 * width
    row = lax.broadcasted_iota(jnp.int32, (width, width), 0)
    column = lax.broadcasted_iota(jnp.int32, (width, width), 1)
    kernel = jnp.exp(-jnp.abs(row - column).astype(jnp.float32) / length)
    out_ref[...] = jnp.dot(
        grad_ref[...], kernel, precision=lax.Precision.HIGHEST, preferred_element_type=jnp.float32
    )


def finish(own_ref, sums_ref, out_ref):
    width = own_ref.shape[1]
    length = 2.0 * width
    count = sums_ref.shape[0]
    me = lax.axis_index("lon")
    row = lax.broadcasted_iota(jnp.int32, (count, width), 0)
    column = lax.broadcasted_iota(jnp.int32, (count, width), 1)
    strip, kind = row >> 3, row & 7
    left = (kind == 0) & (strip > me)
    right = (kind == 1) & (strip < me)
    away = jnp.where(left, (strip - me) * width - column, (me - strip - 1) * width + column + 1)
    weights = jnp.where(left | right, jnp.exp(-jnp.maximum(away, 0).astype(jnp.float32) / length), 0.0)
    out_ref[...] = own_ref[...] + lax.dot_general(
        sums_ref[...], weights, (((0,), (0,)), ((), ())), precision=lax.Precision.HIGHEST,
        preferred_element_type=jnp.float32,
    )


def f32(*shape):
    return jax.ShapeDtypeStruct(shape, jnp.float32)


def vmem(count):
    return [pl.BlockSpec(memory_space=pltpu.VMEM)] * count


def local(depth, surface, friction, wet, coastal_tiles, gauge_route, gauge_cell, gauge_times, gauge_resid):
    height, width = depth.shape
    owned = gauge_route.shape[0]
    blocks = gauge_resid.shape[1]
    steps = blocks * STEPS_BLOCK
    halo = 2 * steps
    assert halo == SEG and height == LANES
    tiles = lax.axis_size(GRID_AXES)
    lons = lax.axis_size("lon")
    row_tiles = lax.axis_size(ROW_AXES)
    parcel_rows = gauge_rows(owned)[0] + 16
    params = pltpu.CompilerParams(vmem_limit_bytes=VMEM_LIMIT)

    keep = (1.0 - friction) * wet.astype(jnp.float32)
    gain = ((courant * 0.5) ** 2 * jnp.maximum(depth + surface, depth_floor)) * keep
    parcel, south, north, east, west = pl.pallas_call(
        functools.partial(prepare, halo),
        out_shape=(
            f32(tiles, parcel_rows, LANES), f32(2, halo, width), f32(2, halo, width),
            f32(height // 2, LANES), f32(height // 2, LANES),
        ),
        in_specs=vmem(7),
        out_specs=tuple(vmem(5)),
        scratch_shapes=[pltpu.VMEM((24, LANES), jnp.float32)],
        compiler_params=params,
        name="prepare",
    )(
        keep, gain, coastal_tiles.reshape(1, -1), gauge_route.reshape(1, owned), gauge_cell.reshape(1, owned),
        jnp.transpose(gauge_times, (1, 2, 0)), jnp.transpose(gauge_resid, (1, 2, 0)),
    )

    def exchange(array, axes):
        return lax.all_to_all(array, axes, split_axis=0, concat_axis=0, tiled=True)

    parcel = exchange(parcel, GRID_AXES)
    down = [(i, i + 1) for i in range(row_tiles - 1)]
    up = [(i + 1, i) for i in range(row_tiles - 1)]
    top = lax.ppermute(south, ROW_AXES, down)
    bottom = lax.ppermute(north, ROW_AXES, up)
    left = lax.ppermute(east, "lon", [(i, i + 1) for i in range(lons - 1)])
    right = lax.ppermute(west, "lon", [(i + 1, i) for i in range(lons - 1)])

    planes = width // LANES + 1
    rows_all = height + 2 * halo
    wide = max(2 * LANES, owned)
    pushes = pl.pallas_call(
        functools.partial(force, steps, halo, height, width),
        out_shape=f32(steps, planes, rows_all, LANES),
        in_specs=vmem(1),
        out_specs=vmem(1)[0],
        scratch_shapes=[
            pltpu.VMEM((steps, wide), jnp.float32),
            pltpu.VMEM((rows_all, wide), jnp.bfloat16),
            pltpu.VMEM((2 * wide, planes * LANES), jnp.bfloat16),
        ],
        compiler_params=params,
        cost_estimate=pl.CostEstimate(
            flops=4 * steps * rows_all * wide * planes * LANES, bytes_accessed=4 * steps * planes * rows_all * LANES,
            transcendentals=0,
        ),
        name="force",
    )(parcel)

    plane = pltpu.VMEM((planes, rows_all, LANES), jnp.float32)
    grad, sums = pl.pallas_call(
        functools.partial(sweep, steps),
        out_shape=(f32(height, width), f32(lons, 8, height)),
        in_specs=vmem(8),
        out_specs=tuple(vmem(2)),
        scratch_shapes=[plane] * 8,
        compiler_params=params,
        name="sweep",
    )(keep, gain, top, bottom, left, right, parcel, pushes)

    sums = exchange(sums, "lon")
    own = pl.pallas_call(
        smooth, out_shape=f32(height, width), in_specs=vmem(1), out_specs=vmem(1)[0], compiler_params=params,
        cost_estimate=pl.CostEstimate(
            flops=6 * 2 * height * width * width, bytes_accessed=2 * 4 * height * width, transcendentals=width * width
        ),
        name="smooth",
    )(grad)
    return pl.pallas_call(
        finish, out_shape=f32(height, width), in_specs=vmem(2), out_specs=vmem(1)[0], compiler_params=params, name="finish",
    )(own, sums.reshape(lons * 8, height))


def solution(mesh):
    in_specs = (
        P(("lat", "gau"), "lon"),
        P(("scen", "lat", "gau"), "lon"),
        P(("lat", "gau"), "lon"),
        P(("lat", "gau"), "lon"),
        P(),
        P(("scen", "lon", "lat", "gau"), None),
        P(("scen", "lon", "lat", "gau")),
        P(("scen", "lon", "lat", "gau"), None, None),
        P(("scen", "lon", "lat", "gau"), None, None),
    )
    out_specs = P(("scen", "lat", "gau"), "lon")
    return jax.shard_map(local, mesh=mesh, in_specs=in_specs, out_specs=out_specs, check_vma=False)
```

```python
import functools
import math

import jax
import jax.numpy as jnp
from jax import lax
from jax.experimental import pallas as pl
from jax.experimental.pallas import tpu as pltpu
from jax.sharding import PartitionSpec as P

STEPS_BLOCK = 8
LANES = 128
SEG = 32
LEVELS = 4
CHUNK = 4

courant = 0.45
depth_floor = 0.1

GRID_AXES = ("lon", "lat", "gau")
ROW_AXES = ("lat", "gau")
VMEM_LIMIT = 16 * 1024 * 1024


def roll_lanes(x, shift):
    shift = shift % LANES
    return x if shift == 0 else pltpu.roll(x, shift, 1)


def lane_iota(rows):
    return lax.broadcasted_iota(jnp.int32, (rows, LANES), 1)


def pack_lanes(pieces):
    rows = pieces[0][0].shape[0]
    segment = lane_iota(rows) // SEG
    packed = jnp.zeros((rows, LANES), jnp.float32)
    for place, (array, first) in enumerate(pieces):
        packed = jnp.where(segment == place, roll_lanes(array, place * SEG - first), packed)
    return packed


def gauge_rows(owned):
    if 3 * owned <= LANES:
        return STEPS_BLOCK, owned
    assert owned <= LANES
    return 3 * STEPS_BLOCK, 0


def my_place():
    row = lax.axis_index("lat") * lax.axis_size("gau") + lax.axis_index("gau")
    return row, lax.axis_index("lon"), lax.axis_size("lat") * lax.axis_size("gau"), lax.axis_size("lon")


def prepare(
    halo, blocks, samples, coast_count, keep_ref, gain_ref, gauge_ref,
    parcel_ref, south_ref, north_ref, east_ref, west_ref, block_ref,
):
    height, width = keep_ref.shape
    my_row, my_lon, row_tiles, lons = my_place()
    keep, gain = keep_ref[...], gain_ref[...]
    half = height // 2
    first, last = slice(0, LANES), slice(width - LANES, width)
    end = LANES - halo

    owned = gauge_ref.shape[1]
    assert blocks == 2
    count = blocks * samples
    route, cell, coast = (gauge_ref[2 * count + i : 2 * count + i + 1, :].astype(jnp.int32) for i in range(3))
    target = jnp.zeros_like(route)
    for entry in range(coast_count):
        target = jnp.where(route == entry, jnp.broadcast_to(coast[:, entry : entry + 1], route.shape), target)
    row_bits, width_bits = int(math.log2(row_tiles)), int(math.log2(width))
    assert row_tiles == 1 << row_bits and width == 1 << width_bits
    grid_row = (target & (row_tiles - 1)) * height + (cell >> width_bits)
    grid_col = (target >> row_bits) * width + (cell & (width - 1))
    block_ref[...] = jnp.zeros_like(block_ref)
    levels = lax.broadcasted_iota(jnp.int32, (STEPS_BLOCK, owned), 0).astype(jnp.float32)
    for block in range(blocks):
        series = jnp.zeros((STEPS_BLOCK, owned), jnp.float32)
        for sample in range(block * samples, (block + 1) * samples):
            times, resid = gauge_ref[sample : sample + 1, :], gauge_ref[count + sample : count + sample + 1, :]
            series = series + jnp.where(times == levels, resid, 0.0)
        block_ref[block * STEPS_BLOCK : (block + 1) * STEPS_BLOCK, :owned] = series
    at = blocks * STEPS_BLOCK
    block_ref[at : at + 1, :owned] = grid_row.astype(jnp.float32)
    block_ref[at + 1 : at + 2, :owned] = grid_col.astype(jnp.float32)
    size, apart = gauge_rows(owned)
    gauges = block_ref[...]
    if size == STEPS_BLOCK:
        gauges = sum(
            roll_lanes(gauges[i * STEPS_BLOCK : (i + 1) * STEPS_BLOCK], i * apart) for i in range(3)
        )
    tiles = parcel_ref.shape[0]

    def put(tile, carry):
        parcel_ref[tile, 0:size, :] = gauges
        return carry

    lax.fori_loop(0, tiles, put, 0, unroll=tiles <= 16)

    for d_row in (-1, 1):
        top = 0 if d_row < 0 else height - halo
        for d_lon in (-1, 1):
            cols, start = (first, 0) if d_lon < 0 else (last, end)
            to_row, to_lon = my_row + d_row, my_lon + d_lon
            there = (to_row >= 0) & (to_row < row_tiles) & (to_lon >= 0) & (to_lon < lons)

            @pl.when(there)
            def _():
                for kind, source in enumerate((keep, gain)):
                    corner = pack_lanes([(source[top + 8 * i : top + 8 * i + 8, cols], start) for i in range(4)])
                    parcel_ref[to_lon * row_tiles + to_row, size + 8 * kind : size + 8 * kind + 8, :] = corner

    south_ref[0], south_ref[1] = keep[height - halo :], gain[height - halo :]
    north_ref[0], north_ref[1] = keep[:halo], gain[:halo]
    for goal, cols, start in ((east_ref, last, end), (west_ref, first, 0)):
        goal[...] = pack_lanes(
            [(keep[:half, cols], start), (gain[:half, cols], start), (keep[half:, cols], start), (gain[half:, cols], start)]
        )


def shift_from(planes, shift, lanes):
    count = len(planes)
    rolled = [roll_lanes(plane, -shift) for plane in planes]
    if shift > 0:
        return [jnp.where(lanes >= LANES - shift, rolled[(c + 1) % count], rolled[c]) for c in range(count)]
    return [jnp.where(lanes < -shift, rolled[(c - 1) % count], rolled[c]) for c in range(count)]


def force(steps, halo, height, width, parcel_ref, force_ref, series_ref, rows_hot, cols_hot):
    planes, rows_all = force_ref.shape[1:3]
    my_row, my_lon, row_tiles, lons = my_place()
    wide = rows_hot.shape[1]
    tiles, parcel_rows = parcel_ref.shape[:2]
    size = parcel_rows - 16
    apart = wide // tiles if size == STEPS_BLOCK else 0
    owned = apart if apart else LANES
    group = wide // owned
    groups = tiles // group
    per_plane = LANES // owned
    blocks = rows_all // 8
    row_shift = (halo - my_row * height).astype(jnp.float32)
    col_shift = (-my_lon * width).astype(jnp.float32)
    place = lax.broadcasted_iota(jnp.int32, (rows_all, LANES), 0)
    at = ((place & 7) * blocks + (place >> 3)).astype(jnp.float32)

    def gather_gauges(index):
        lanes = lane_iota(STEPS_BLOCK)
        for part in range(wide // LANES):
            cols = slice(part * LANES, (part + 1) * LANES)
            fields = []
            for field in range(3):
                total = jnp.zeros((STEPS_BLOCK, LANES), jnp.float32)
                rows = slice(0, 8) if apart else slice(8 * field, 8 * field + 8)
                for i in range(per_plane):
                    source = index * group + part * per_plane + i
                    block = roll_lanes(parcel_ref[source, rows, :], i * owned - field * apart)
                    total = jnp.where((lanes >= i * owned) & (lanes < (i + 1) * owned), block, total)
                fields.append(total)
            series_ref[0:8, cols] = fields[0]
            series_ref[8:16, cols] = fields[1]
            row = fields[2][0:1] + row_shift
            col = fields[2][1:2] + col_shift
            col = jnp.where((col >= -halo) & (col < 0), col + float(planes * LANES), jnp.where(col < width + halo, col, -1.0))
            rows_hot[:, cols] = (at == row).astype(jnp.float32).astype(jnp.bfloat16)
            by_gauge = jnp.transpose(jnp.broadcast_to(col, (LANES, LANES)))
            for c in range(planes):
                spot = (lane_iota(LANES) + c * LANES).astype(jnp.float32)
                hot = (by_gauge == spot).astype(jnp.float32).astype(jnp.bfloat16)
                cols_hot[part * LANES : (part + 1) * LANES, c * LANES : (c + 1) * LANES] = hot
                cols_hot[wide + part * LANES : wide + (part + 1) * LANES, c * LANES : (c + 1) * LANES] = hot

    def levels_of(start, add):
        hot = rows_hot[...]
        both = []
        for level in range(LEVELS):
            value = series_ref[pl.ds(start + level, 1), :]
            high = value.astype(jnp.bfloat16)
            low = (value - high.astype(jnp.float32)).astype(jnp.bfloat16)
            both.append(jnp.concatenate([hot * high, hot * low], axis=1))
        both = jnp.concatenate(both, axis=0)
        for first in range(0, planes, 2):
            count = min(2, planes - first)
            total = jnp.dot(
                both, cols_hot[:, first * LANES : (first + count) * LANES], preferred_element_type=jnp.float32
            )
            for level in range(LEVELS):
                for c in range(count):
                    part = total[level * rows_all : (level + 1) * rows_all, c * LANES : (c + 1) * LANES]
                    goal = (start + level, first + c)
                    force_ref[goal] = force_ref[goal] + part if add else part

    def levels(add):
        def one(index, carry):
            levels_of(index * LEVELS, add)
            return carry

        lax.fori_loop(0, steps // LEVELS, one, 0)

    force_ref[steps] = jnp.zeros_like(force_ref[steps])
    gather_gauges(0)
    levels(False)
    if groups > 1:

        def more(index, carry):
            gather_gauges(index)
            levels(True)
            return carry

        lax.fori_loop(1, groups, more, 0)


def sweep(
    steps, keep_ref, gain_ref, top_ref, bottom_ref, left_ref, right_ref, parcel_ref, force_ref,
    grad_ref, sums_ref,
    a, fx, fy, keep_x, gain_x, keep_y, gain_y, plain,
):
    height, width = keep_ref.shape
    halo = 2 * steps
    inner = width // LANES
    planes = inner + 1
    rows_all = plain.shape[1]
    blocks = rows_all // 8
    my_row, my_lon, row_tiles, lons = my_place()
    end = LANES - halo
    size = parcel_ref.shape[1] - 16
    has_top, has_bottom = my_row > 0, my_row < row_tiles - 1
    has_left, has_right = my_lon > 0, my_lon < lons - 1
    above, below = jnp.maximum(my_row - 1, 0), jnp.minimum(my_row + 1, row_tiles - 1)
    left, right = jnp.maximum(my_lon - 1, 0), jnp.minimum(my_lon + 1, lons - 1)
    lanes8 = lane_iota(8)

    def known(condition, value):
        return jnp.where(jnp.where(condition, 1, 0) == 1, value, 0.0)

    def up(value):
        return pltpu.roll(value, 7, 0)

    def down(value):
        return pltpu.roll(value, 1, 0)

    half = height // 2
    for kind, (source, by_x, by_y) in enumerate(((keep_ref, keep_x, keep_y), (gain_ref, gain_x, gain_y))):
        for c in range(inner):
            cols = slice(c * LANES, (c + 1) * LANES)
            plain[c, halo : halo + height, :] = source[:, cols]
            plain[c, 0:halo, :] = top_ref[kind, :, cols]
            plain[c, halo + height :, :] = bottom_ref[kind, :, cols]
        segment = lane_iota(half) // SEG
        for part in range(2):
            piece = 2 * part + kind
            by_left = roll_lanes(left_ref[...], end - piece * SEG)
            by_right = roll_lanes(right_ref[...], -piece * SEG)
            both = jnp.where(segment == 0, by_right, jnp.where(segment == LANES // SEG - 1, by_left, 0.0))
            plain[inner, halo + part * half : halo + (part + 1) * half, :] = both
        segment = lane_iota(8) // SEG
        for has_row, row, at in ((has_top, above, 0), (has_bottom, below, halo + height)):
            by_left = known(has_row & has_left, parcel_ref[left * row_tiles + row, size + 8 * kind : size + 8 * kind + 8, :])
            by_right = known(has_row & has_right, parcel_ref[right * row_tiles + row, size + 8 * kind : size + 8 * kind + 8, :])
            for i in range(4):
                both = jnp.where(
                    segment == 0, roll_lanes(by_right, -i * SEG),
                    jnp.where(segment == LANES // SEG - 1, roll_lanes(by_left, end - i * SEG), 0.0),
                )
                plain[inner, at + 8 * i : at + 8 * i + 8, :] = both
        for q in range(blocks):
            values = [plain[c, pl.ds(q, 8, stride=blocks), :] for c in range(planes)]
            shifted = shift_from(values, 1, lanes8)
            to = (q - 1) % blocks * 8
            for c in range(planes):
                by_x[c, 8 * q : 8 * q + 8, :] = shifted[c]
                by_y[c, to : to + 8, :] = up(values[c]) if q == 0 else values[c]

    fx[...] = jnp.zeros_like(fx)
    fy[...] = jnp.zeros_like(fy)
    a[:, 0:rows_all, :] = force_ref[steps - 1]

    col_valid = jnp.where(lanes8 < LANES // 2, jnp.where(has_right, 1.0, 0.0), jnp.where(has_left, 1.0, 0.0))
    col_mask = jnp.where((lanes8 < halo) | (lanes8 >= end), col_valid, 0.0)
    sublane = lax.broadcasted_iota(jnp.int32, (8, LANES), 0)
    top_mask = jnp.where(sublane == (halo - 1) // blocks, jnp.where(has_top, 1.0, 0.0), 1.0)
    bottom_mask = jnp.where(sublane == (halo + height) // blocks, jnp.where(has_bottom, 1.0, 0.0), 1.0)
    every = range(planes)

    def step(index, carry):
        after = jnp.where(index == steps - 1, steps, steps - 2 - index)
        for q in range(2):
            for c in every:
                a[c, rows_all + 8 * q : rows_all + 8 * q + 8, :] = up(a[c, 8 * q : 8 * q + 8, :])

        def chunk(number, inner_carry):
            start = pl.multiple_of(number * (8 * CHUNK), 8 * CHUNK)

            def at(q):
                return pl.ds(start + 8 * q, 8)

            near = [[a[c, at(q), :] for c in every] for q in range(CHUNK + 2)]
            new_y = [[fy[c, at(q), :] for c in every] for q in range(2)]
            total, new_x = [], []
            for q in range(CHUNK):
                new_y.append(
                    [
                        keep_y[c, at(q), :] * fy[c, at(q + 2), :] + gain_y[c, at(q), :] * (near[q + 2][c] - near[q][c])
                        for c in every
                    ]
                )
                ahead = shift_from(near[q], 2, lanes8)
                new_x.append(
                    [keep_x[c, at(q), :] * fx[c, at(q), :] + gain_x[c, at(q), :] * (ahead[c] - near[q][c]) for c in every]
                )
                total.append([near[q][c] + (new_y[q + 2][c] - new_y[q][c]) for c in every])
            behind = [shift_from(new_x[q], -2, lanes8) for q in range(CHUNK)]
            for q in range(CHUNK):
                for c in every:
                    value = total[q][c] + (new_x[q][c] - behind[q][c])
                    if c == inner:
                        value = value * col_mask
                    total[q][c] = value + force_ref[after, c, at(q), :]
            for q in range(CHUNK):
                for c in every:
                    fx[c, at(q), :] = new_x[q][c]
                    fy[c, at(q + 2), :] = new_y[q + 2][c]
                    a[c, at(q), :] = total[q][c]
            return inner_carry

        fy[:, 0:16, :] = jnp.zeros((planes, 16, LANES), jnp.float32)
        lax.fori_loop(0, blocks // CHUNK, chunk, 0)
        for q in range(2):
            for c in every:
                rows = slice(8 * q, 8 * q + 8)
                past = down(fy[c, rows_all + 8 * q : rows_all + 8 * q + 8, :])
                a[c, rows, :] = a[c, rows, :] - (past * col_mask if c == inner else past)
        for row, mask in ((halo - 1, top_mask), (halo + height, bottom_mask)):
            rows = slice(row % blocks * 8, row % blocks * 8 + 8)
            for c in every:
                a[c, rows, :] = a[c, rows, :] * mask
        return carry

    lax.fori_loop(0, steps, step, 0)

    for r in range(0, height, 8):
        s, q = divmod(halo + r, blocks)
        for c in range(inner):
            cols = slice(c * LANES, (c + 1) * LANES)
            value = a[c, pl.ds(8 * q + s, 8, stride=8), :]
            grad_ref[r : r + 8, cols] = jnp.where(keep_ref[r : r + 8, cols] > 0.0, value, 0.0)
    length = 2.0 * width
    kind = lax.broadcasted_iota(jnp.int32, (8, width), 0)
    column = lax.broadcasted_iota(jnp.int32, (8, width), 1)
    steps_off = jnp.where(kind == 0, column, width - 1 - column).astype(jnp.float32)
    weights = jnp.where(kind < 2, jnp.exp(-steps_off / length), 0.0)
    sums = lax.dot_general(
        weights, grad_ref[...], (((1,), (1,)), ((), ())), precision=lax.Precision.HIGHEST,
        preferred_element_type=jnp.float32,
    )
    for i in range(sums_ref.shape[0]):
        sums_ref[i] = sums


def smooth(grad_ref, out_ref):
    width = grad_ref.shape[1]
    length = 2.0 * width
    row = lax.broadcasted_iota(jnp.int32, (width, width), 0)
    column = lax.broadcasted_iota(jnp.int32, (width, width), 1)
    kernel = jnp.exp(-jnp.abs(row - column).astype(jnp.float32) / length)
    out_ref[...] = jnp.dot(
        grad_ref[...], kernel, precision=lax.Precision.HIGHEST, preferred_element_type=jnp.float32
    )


def finish(own_ref, sums_ref, out_ref):
    width = own_ref.shape[1]
    length = 2.0 * width
    count = sums_ref.shape[0]
    me = lax.axis_index("lon")
    row = lax.broadcasted_iota(jnp.int32, (count, width), 0)
    column = lax.broadcasted_iota(jnp.int32, (count, width), 1)
    strip, kind = row >> 3, row & 7
    left = (kind == 0) & (strip > me)
    right = (kind == 1) & (strip < me)
    away = jnp.where(left, (strip - me) * width - column, (me - strip - 1) * width + column + 1)
    weights = jnp.where(left | right, jnp.exp(-jnp.maximum(away, 0).astype(jnp.float32) / length), 0.0)
    out_ref[...] = own_ref[...] + lax.dot_general(
        sums_ref[...], weights, (((0,), (0,)), ((), ())), precision=lax.Precision.HIGHEST,
        preferred_element_type=jnp.float32,
    )


def f32(*shape):
    return jax.ShapeDtypeStruct(shape, jnp.float32)


def vmem(count):
    return [pl.BlockSpec(memory_space=pltpu.VMEM)] * count


def local(depth, surface, friction, wet, coastal_tiles, gauge_route, gauge_cell, gauge_times, gauge_resid):
    height, width = depth.shape
    owned = gauge_route.shape[0]
    blocks = gauge_resid.shape[1]
    steps = blocks * STEPS_BLOCK
    halo = 2 * steps
    assert halo == SEG and height == LANES
    tiles = lax.axis_size(GRID_AXES)
    lons = lax.axis_size("lon")
    row_tiles = lax.axis_size(ROW_AXES)
    parcel_rows = gauge_rows(owned)[0] + 16
    params = pltpu.CompilerParams(vmem_limit_bytes=VMEM_LIMIT)

    keep = (1.0 - friction) * wet.astype(jnp.float32)
    gain = ((courant * 0.5) ** 2 * jnp.maximum(depth + surface, depth_floor)) * keep
    samples, coast_count = gauge_resid.shape[2], coastal_tiles.shape[0]
    assert coast_count <= owned

    def by_gauge(array):
        return jnp.transpose(array, (1, 2, 0)).reshape(blocks * samples, owned)

    gauges = jnp.concatenate(
        [
            by_gauge(gauge_times).astype(jnp.float32), by_gauge(gauge_resid),
            gauge_route.reshape(1, owned).astype(jnp.float32), gauge_cell.reshape(1, owned).astype(jnp.float32),
            jnp.pad(coastal_tiles, (0, owned - coast_count)).reshape(1, owned).astype(jnp.float32),
        ],
        axis=0,
    )
    parcel, south, north, east, west = pl.pallas_call(
        functools.partial(prepare, halo, blocks, samples, coast_count),
        out_shape=(
            f32(tiles, parcel_rows, LANES), f32(2, halo, width), f32(2, halo, width),
            f32(height // 2, LANES), f32(height // 2, LANES),
        ),
        in_specs=vmem(3),
        out_specs=tuple(vmem(5)),
        scratch_shapes=[pltpu.VMEM((24, LANES), jnp.float32)],
        compiler_params=params,
        name="prepare",
    )(keep, gain, gauges)

    def exchange(array, axes):
        return lax.all_to_all(array, axes, split_axis=0, concat_axis=0, tiled=True)

    parcel = exchange(parcel, GRID_AXES)
    down = [(i, i + 1) for i in range(row_tiles - 1)]
    up = [(i + 1, i) for i in range(row_tiles - 1)]
    top = lax.ppermute(south, ROW_AXES, down)
    bottom = lax.ppermute(north, ROW_AXES, up)
    left = lax.ppermute(east, "lon", [(i, i + 1) for i in range(lons - 1)])
    right = lax.ppermute(west, "lon", [(i + 1, i) for i in range(lons - 1)])

    planes = width // LANES + 1
    rows_all = height + 2 * halo
    wide = max(2 * LANES, owned)
    pushes = pl.pallas_call(
        functools.partial(force, steps, halo, height, width),
        out_shape=f32(steps + 1, planes, rows_all, LANES),
        in_specs=vmem(1),
        out_specs=vmem(1)[0],
        scratch_shapes=[
            pltpu.VMEM((steps, wide), jnp.float32),
            pltpu.VMEM((rows_all, wide), jnp.bfloat16),
            pltpu.VMEM((2 * wide, planes * LANES), jnp.bfloat16),
        ],
        compiler_params=params,
        cost_estimate=pl.CostEstimate(
            flops=4 * steps * rows_all * wide * planes * LANES, bytes_accessed=4 * steps * planes * rows_all * LANES,
            transcendentals=0,
        ),
        name="force",
    )(parcel)

    plane = pltpu.VMEM((planes, rows_all, LANES), jnp.float32)
    longer = pltpu.VMEM((planes, rows_all + 16, LANES), jnp.float32)
    grad, sums = pl.pallas_call(
        functools.partial(sweep, steps),
        out_shape=(f32(height, width), f32(lons, 8, height)),
        in_specs=vmem(8),
        out_specs=tuple(vmem(2)),
        scratch_shapes=[longer, plane, longer] + [plane] * 5,
        compiler_params=params,
        name="sweep",
    )(keep, gain, top, bottom, left, right, parcel, pushes)

    sums = exchange(sums, "lon")
    own = pl.pallas_call(
        smooth, out_shape=f32(height, width), in_specs=vmem(1), out_specs=vmem(1)[0], compiler_params=params,
        cost_estimate=pl.CostEstimate(
            flops=6 * 2 * height * width * width, bytes_accessed=2 * 4 * height * width, transcendentals=width * width
        ),
        name="smooth",
    )(grad)
    return pl.pallas_call(
        finish, out_shape=f32(height, width), in_specs=vmem(2), out_specs=vmem(1)[0], compiler_params=params, name="finish",
    )(own, sums.reshape(lons * 8, height))


def solution(mesh):
    in_specs = (
        P(("lat", "gau"), "lon"),
        P(("scen", "lat", "gau"), "lon"),
        P(("lat", "gau"), "lon"),
        P(("lat", "gau"), "lon"),
        P(),
        P(("scen", "lon", "lat", "gau"), None),
        P(("scen", "lon", "lat", "gau")),
        P(("scen", "lon", "lat", "gau"), None, None),
        P(("scen", "lon", "lat", "gau"), None, None),
    )
    out_specs = P(("scen", "lat", "gau"), "lon")
    return jax.shard_map(local, mesh=mesh, in_specs=in_specs, out_specs=out_specs, check_vma=False)
```

```python
import functools
import math

import jax
import jax.numpy as jnp
from jax import lax
from jax.experimental import pallas as pl
from jax.experimental.pallas import tpu as pltpu
from jax.sharding import PartitionSpec as P

STEPS_BLOCK = 8
LANES = 128
SEG = 32
LEVELS = 4
CHUNK = 4

courant = 0.45
depth_floor = 0.1

GRID_AXES = ("lon", "lat", "gau")
ROW_AXES = ("lat", "gau")
VMEM_LIMIT = 16 * 1024 * 1024


def roll_lanes(x, shift):
    shift = shift % LANES
    return x if shift == 0 else pltpu.roll(x, shift, 1)


def lane_iota(rows):
    return lax.broadcasted_iota(jnp.int32, (rows, LANES), 1)


def pack_lanes(pieces):
    rows = pieces[0][0].shape[0]
    segment = lane_iota(rows) // SEG
    packed = jnp.zeros((rows, LANES), jnp.float32)
    for place, (array, first) in enumerate(pieces):
        packed = jnp.where(segment == place, roll_lanes(array, place * SEG - first), packed)
    return packed


def gauge_rows(owned):
    if 3 * owned <= LANES:
        return STEPS_BLOCK, owned
    assert owned <= LANES
    return 3 * STEPS_BLOCK, 0


def my_place():
    row = lax.axis_index("lat") * lax.axis_size("gau") + lax.axis_index("gau")
    return row, lax.axis_index("lon"), lax.axis_size("lat") * lax.axis_size("gau"), lax.axis_size("lon")


def prepare(
    halo, blocks, samples, coast_count, keep_ref, gain_ref, gauge_ref, resid_ref,
    parcel_ref, south_ref, north_ref, east_ref, west_ref, block_ref,
):
    height, width = keep_ref.shape
    my_row, my_lon, row_tiles, lons = my_place()
    keep, gain = keep_ref[...], gain_ref[...]
    half = height // 2
    first, last = slice(0, LANES), slice(width - LANES, width)
    end = LANES - halo

    owned = gauge_ref.shape[2]
    assert blocks == 2
    route, cell, coast = (gauge_ref[blocks, i : i + 1, :] for i in range(3))
    target = jnp.zeros_like(route)
    for entry in range(coast_count):
        target = jnp.where(route == entry, jnp.broadcast_to(coast[:, entry : entry + 1], route.shape), target)
    row_bits, width_bits = int(math.log2(row_tiles)), int(math.log2(width))
    assert row_tiles == 1 << row_bits and width == 1 << width_bits
    grid_row = (target & (row_tiles - 1)) * height + (cell >> width_bits)
    grid_col = (target >> row_bits) * width + (cell & (width - 1))
    block_ref[...] = jnp.zeros_like(block_ref)
    levels = lax.broadcasted_iota(jnp.int32, (STEPS_BLOCK, owned), 0)
    for block in range(blocks):
        series = jnp.zeros((STEPS_BLOCK, owned), jnp.float32)
        for sample in range(samples):
            times = gauge_ref[block, sample : sample + 1, :]
            resid = resid_ref[block, sample : sample + 1, :]
            series = series + jnp.where(times == levels, resid, 0.0)
        block_ref[block * STEPS_BLOCK : (block + 1) * STEPS_BLOCK, :owned] = series
    at = blocks * STEPS_BLOCK
    block_ref[at : at + 1, :owned] = grid_row.astype(jnp.float32)
    block_ref[at + 1 : at + 2, :owned] = grid_col.astype(jnp.float32)
    size, apart = gauge_rows(owned)
    gauges = block_ref[...]
    if size == STEPS_BLOCK:
        gauges = sum(
            roll_lanes(gauges[i * STEPS_BLOCK : (i + 1) * STEPS_BLOCK], i * apart) for i in range(3)
        )
    tiles = parcel_ref.shape[0]

    def put(tile, carry):
        parcel_ref[tile, 0:size, :] = gauges
        return carry

    lax.fori_loop(0, tiles, put, 0, unroll=tiles <= 16)

    for d_row in (-1, 1):
        top = 0 if d_row < 0 else height - halo
        for d_lon in (-1, 1):
            cols, start = (first, 0) if d_lon < 0 else (last, end)
            to_row, to_lon = my_row + d_row, my_lon + d_lon
            there = (to_row >= 0) & (to_row < row_tiles) & (to_lon >= 0) & (to_lon < lons)

            @pl.when(there)
            def _():
                for kind, source in enumerate((keep, gain)):
                    corner = pack_lanes([(source[top + 8 * i : top + 8 * i + 8, cols], start) for i in range(4)])
                    parcel_ref[to_lon * row_tiles + to_row, size + 8 * kind : size + 8 * kind + 8, :] = corner

    south_ref[0], south_ref[1] = keep[height - halo :], gain[height - halo :]
    north_ref[0], north_ref[1] = keep[:halo], gain[:halo]
    for goal, cols, start in ((east_ref, last, end), (west_ref, first, 0)):
        goal[...] = pack_lanes(
            [(keep[:half, cols], start), (gain[:half, cols], start), (keep[half:, cols], start), (gain[half:, cols], start)]
        )


def shift_from(planes, shift, lanes):
    count = len(planes)
    rolled = [roll_lanes(plane, -shift) for plane in planes]
    if shift > 0:
        return [jnp.where(lanes >= LANES - shift, rolled[(c + 1) % count], rolled[c]) for c in range(count)]
    return [jnp.where(lanes < -shift, rolled[(c - 1) % count], rolled[c]) for c in range(count)]


def force(steps, halo, height, width, parcel_ref, force_ref, series_ref, rows_hot, cols_hot):
    planes, rows_all = force_ref.shape[1], height + 2 * halo
    my_row, my_lon, row_tiles, lons = my_place()
    wide = rows_hot.shape[1]
    tiles, parcel_rows = parcel_ref.shape[:2]
    size = parcel_rows - 16
    apart = wide // tiles if size == STEPS_BLOCK else 0
    owned = apart if apart else LANES
    group = wide // owned
    groups = tiles // group
    per_plane = LANES // owned
    blocks = rows_all // 8
    row_shift = (halo - my_row * height).astype(jnp.float32)
    col_shift = (-my_lon * width).astype(jnp.float32)
    place = lax.broadcasted_iota(jnp.int32, (rows_all, LANES), 0)
    at = ((place & 7) * blocks + (place >> 3)).astype(jnp.float32)

    def gather_gauges(index):
        lanes = lane_iota(STEPS_BLOCK)
        for part in range(wide // LANES):
            cols = slice(part * LANES, (part + 1) * LANES)
            fields = []
            for field in range(3):
                total = jnp.zeros((STEPS_BLOCK, LANES), jnp.float32)
                rows = slice(0, 8) if apart else slice(8 * field, 8 * field + 8)
                for i in range(per_plane):
                    source = index * group + part * per_plane + i
                    block = roll_lanes(parcel_ref[source, rows, :], i * owned - field * apart)
                    total = jnp.where((lanes >= i * owned) & (lanes < (i + 1) * owned), block, total)
                fields.append(total)
            series_ref[0:8, cols] = fields[0]
            series_ref[8:16, cols] = fields[1]
            row = fields[2][0:1] + row_shift
            col = fields[2][1:2] + col_shift
            col = jnp.where((col >= -halo) & (col < 0), col + float(planes * LANES), jnp.where(col < width + halo, col, -1.0))
            rows_hot[:, cols] = (at == row).astype(jnp.float32).astype(jnp.bfloat16)
            by_gauge = jnp.transpose(jnp.broadcast_to(col, (LANES, LANES)))
            for c in range(planes):
                spot = (lane_iota(LANES) + c * LANES).astype(jnp.float32)
                hot = (by_gauge == spot).astype(jnp.float32).astype(jnp.bfloat16)
                cols_hot[part * LANES : (part + 1) * LANES, c * LANES : (c + 1) * LANES] = hot
                cols_hot[wide + part * LANES : wide + (part + 1) * LANES, c * LANES : (c + 1) * LANES] = hot

    def levels_of(start, add):
        hot = rows_hot[...]
        both = []
        for level in range(LEVELS):
            value = series_ref[pl.ds(start + level, 1), :]
            high = value.astype(jnp.bfloat16)
            low = (value - high.astype(jnp.float32)).astype(jnp.bfloat16)
            both.append(jnp.concatenate([hot * high, hot * low], axis=1))
        both = jnp.concatenate(both, axis=0)
        for first in range(0, planes, 2):
            count = min(2, planes - first)
            total = jnp.dot(
                both, cols_hot[:, first * LANES : (first + count) * LANES], preferred_element_type=jnp.float32
            )
            for level in range(LEVELS):
                for c in range(count):
                    part = total[level * rows_all : (level + 1) * rows_all, c * LANES : (c + 1) * LANES]
                    goal = (start + level, first + c, slice(0, rows_all))
                    force_ref[goal] = force_ref[goal] + part if add else part

    def levels(add):
        def one(index, carry):
            levels_of(index * LEVELS, add)
            return carry

        lax.fori_loop(0, steps // LEVELS, one, 0)

    force_ref[steps] = jnp.zeros_like(force_ref[steps])
    gather_gauges(0)
    levels(False)
    if groups > 1:

        def more(index, carry):
            gather_gauges(index)
            levels(True)
            return carry

        lax.fori_loop(1, groups, more, 0)


def sweep(
    steps, keep_ref, gain_ref, top_ref, bottom_ref, left_ref, right_ref, parcel_ref, force_ref,
    grad_ref, sums_ref,
    a, fx, fy, keep_x, gain_x, keep_y, gain_y, plain,
):
    height, width = keep_ref.shape
    halo = 2 * steps
    inner = width // LANES
    planes = inner + 1
    rows_all = height + 2 * halo
    blocks = rows_all // 8
    my_row, my_lon, row_tiles, lons = my_place()
    end = LANES - halo
    size = parcel_ref.shape[1] - 16
    has_top, has_bottom = my_row > 0, my_row < row_tiles - 1
    has_left, has_right = my_lon > 0, my_lon < lons - 1
    above, below = jnp.maximum(my_row - 1, 0), jnp.minimum(my_row + 1, row_tiles - 1)
    left, right = jnp.maximum(my_lon - 1, 0), jnp.minimum(my_lon + 1, lons - 1)
    lanes8 = lane_iota(8)

    def known(condition, value):
        return jnp.where(jnp.where(condition, 1, 0) == 1, value, 0.0)

    def up(value):
        return pltpu.roll(value, 7, 0)

    def down(value):
        return pltpu.roll(value, 1, 0)

    half = height // 2
    for kind, (source, by_x, by_y) in enumerate(((keep_ref, keep_x, keep_y), (gain_ref, gain_x, gain_y))):
        for c in range(inner):
            cols = slice(c * LANES, (c + 1) * LANES)
            plain[c, halo : halo + height, :] = source[:, cols]
            plain[c, 0:halo, :] = top_ref[kind, :, cols]
            plain[c, halo + height : rows_all, :] = bottom_ref[kind, :, cols]
        segment = lane_iota(half) // SEG
        for part in range(2):
            piece = 2 * part + kind
            by_left = roll_lanes(left_ref[...], end - piece * SEG)
            by_right = roll_lanes(right_ref[...], -piece * SEG)
            both = jnp.where(segment == 0, by_right, jnp.where(segment == LANES // SEG - 1, by_left, 0.0))
            plain[inner, halo + part * half : halo + (part + 1) * half, :] = both
        segment = lane_iota(8) // SEG
        for has_row, row, at in ((has_top, above, 0), (has_bottom, below, halo + height)):
            by_left = known(has_row & has_left, parcel_ref[left * row_tiles + row, size + 8 * kind : size + 8 * kind + 8, :])
            by_right = known(has_row & has_right, parcel_ref[right * row_tiles + row, size + 8 * kind : size + 8 * kind + 8, :])
            for i in range(4):
                both = jnp.where(
                    segment == 0, roll_lanes(by_right, -i * SEG),
                    jnp.where(segment == LANES // SEG - 1, roll_lanes(by_left, end - i * SEG), 0.0),
                )
                plain[inner, at + 8 * i : at + 8 * i + 8, :] = both
        for q in range(blocks):
            values = [plain[c, pl.ds(q, 8, stride=blocks), :] for c in range(planes)]
            shifted = shift_from(values, 1, lanes8)
            to = (q - 1) % blocks * 8
            for c in range(planes):
                by_x[c, 8 * q : 8 * q + 8, :] = shifted[c]
                by_y[c, to : to + 8, :] = up(values[c]) if q == 0 else values[c]

    fx[...] = jnp.zeros_like(fx)
    fy[...] = jnp.zeros_like(fy)
    a[:, 0:rows_all, :] = force_ref[steps - 1, :, 0:rows_all, :]

    col_valid = jnp.where(lanes8 < LANES // 2, jnp.where(has_right, 1.0, 0.0), jnp.where(has_left, 1.0, 0.0))
    col_mask = jnp.where((lanes8 < halo) | (lanes8 >= end), col_valid, 0.0)
    sublane = lax.broadcasted_iota(jnp.int32, (8, LANES), 0)
    top_mask = jnp.where(sublane == (halo - 1) // blocks, jnp.where(has_top, 1.0, 0.0), 1.0)
    bottom_mask = jnp.where(sublane == (halo + height) // blocks, jnp.where(has_bottom, 1.0, 0.0), 1.0)
    every = range(planes)

    def step(index, carry):
        after = jnp.where(index == steps - 1, steps, steps - 2 - index)
        for q in range(2):
            for c in every:
                a[c, rows_all + 8 * q : rows_all + 8 * q + 8, :] = up(a[c, 8 * q : 8 * q + 8, :])

        def chunk(number, inner_carry):
            start = pl.multiple_of(number * (8 * CHUNK), 8 * CHUNK)

            def at(q):
                return pl.ds(start + 8 * q, 8)

            near = [[a[c, at(q), :] for c in every] for q in range(CHUNK + 2)]
            new_y = [[fy[c, at(q), :] for c in every] for q in range(2)]
            total, new_x = [], []
            for q in range(CHUNK):
                new_y.append(
                    [
                        keep_y[c, at(q), :] * fy[c, at(q + 2), :] + gain_y[c, at(q), :] * (near[q + 2][c] - near[q][c])
                        for c in every
                    ]
                )
                ahead = shift_from(near[q], 2, lanes8)
                new_x.append(
                    [keep_x[c, at(q), :] * fx[c, at(q), :] + gain_x[c, at(q), :] * (ahead[c] - near[q][c]) for c in every]
                )
                total.append([near[q][c] + (new_y[q + 2][c] - new_y[q][c]) for c in every])
            behind = [shift_from(new_x[q], -2, lanes8) for q in range(CHUNK)]
            for q in range(CHUNK):
                for c in every:
                    value = total[q][c] + (new_x[q][c] - behind[q][c])
                    if c == inner:
                        value = value * col_mask
                    total[q][c] = value + force_ref[after, c, at(q), :]
            for q in range(CHUNK):
                for c in every:
                    fx[c, at(q), :] = new_x[q][c]
                    fy[c, at(q + 2), :] = new_y[q + 2][c]
                    a[c, at(q), :] = total[q][c]
            return inner_carry

        fy[:, 0:16, :] = jnp.zeros((planes, 16, LANES), jnp.float32)
        lax.fori_loop(0, blocks // CHUNK, chunk, 0)
        for q in range(2):
            for c in every:
                rows = slice(8 * q, 8 * q + 8)
                past = down(fy[c, rows_all + 8 * q : rows_all + 8 * q + 8, :])
                a[c, rows, :] = a[c, rows, :] - (past * col_mask if c == inner else past)
        for row, mask in ((halo - 1, top_mask), (halo + height, bottom_mask)):
            rows = slice(row % blocks * 8, row % blocks * 8 + 8)
            for c in every:
                a[c, rows, :] = a[c, rows, :] * mask
        return carry

    lax.fori_loop(0, steps, step, 0)

    for r in range(0, height, 8):
        s, q = divmod(halo + r, blocks)
        for c in range(inner):
            cols = slice(c * LANES, (c + 1) * LANES)
            value = a[c, pl.ds(8 * q + s, 8, stride=8), :]
            grad_ref[r : r + 8, cols] = jnp.where(keep_ref[r : r + 8, cols] > 0.0, value, 0.0)
    length = 2.0 * width
    kind = lax.broadcasted_iota(jnp.int32, (8, width), 0)
    column = lax.broadcasted_iota(jnp.int32, (8, width), 1)
    steps_off = jnp.where(kind == 0, column, width - 1 - column).astype(jnp.float32)
    weights = jnp.where(kind < 2, jnp.exp(-steps_off / length), 0.0)
    sums = lax.dot_general(
        weights, grad_ref[...], (((1,), (1,)), ((), ())), precision=lax.Precision.HIGHEST,
        preferred_element_type=jnp.float32,
    )
    for i in range(sums_ref.shape[0]):
        sums_ref[i] = sums


def smooth(grad_ref, out_ref):
    width = grad_ref.shape[1]
    length = 2.0 * width
    row = lax.broadcasted_iota(jnp.int32, (width, width), 0)
    column = lax.broadcasted_iota(jnp.int32, (width, width), 1)
    kernel = jnp.exp(-jnp.abs(row - column).astype(jnp.float32) / length)
    out_ref[...] = jnp.dot(
        grad_ref[...], kernel, precision=lax.Precision.HIGHEST, preferred_element_type=jnp.float32
    )


def finish(own_ref, sums_ref, out_ref):
    width = own_ref.shape[1]
    length = 2.0 * width
    count = sums_ref.shape[0]
    me = lax.axis_index("lon")
    row = lax.broadcasted_iota(jnp.int32, (count, width), 0)
    column = lax.broadcasted_iota(jnp.int32, (count, width), 1)
    strip, kind = row >> 3, row & 7
    left = (kind == 0) & (strip > me)
    right = (kind == 1) & (strip < me)
    away = jnp.where(left, (strip - me) * width - column, (me - strip - 1) * width + column + 1)
    weights = jnp.where(left | right, jnp.exp(-jnp.maximum(away, 0).astype(jnp.float32) / length), 0.0)
    out_ref[...] = own_ref[...] + lax.dot_general(
        sums_ref[...], weights, (((0,), (0,)), ((), ())), precision=lax.Precision.HIGHEST,
        preferred_element_type=jnp.float32,
    )


def f32(*shape):
    return jax.ShapeDtypeStruct(shape, jnp.float32)


def spaced(rows):
    return 8 * (rows // 8 | 1)


def vmem(count):
    return [pl.BlockSpec(memory_space=pltpu.VMEM)] * count


def local(depth, surface, friction, wet, coastal_tiles, gauge_route, gauge_cell, gauge_times, gauge_resid):
    height, width = depth.shape
    owned = gauge_route.shape[0]
    blocks = gauge_resid.shape[1]
    steps = blocks * STEPS_BLOCK
    halo = 2 * steps
    assert halo == SEG and height == LANES
    tiles = lax.axis_size(GRID_AXES)
    lons = lax.axis_size("lon")
    row_tiles = lax.axis_size(ROW_AXES)
    parcel_rows = gauge_rows(owned)[0] + 16
    params = pltpu.CompilerParams(vmem_limit_bytes=VMEM_LIMIT)

    keep = (1.0 - friction) * wet.astype(jnp.float32)
    gain = ((courant * 0.5) ** 2 * jnp.maximum(depth + surface, depth_floor)) * keep
    samples, coast_count = gauge_resid.shape[2], coastal_tiles.shape[0]
    assert coast_count <= owned

    assert samples >= 3

    def put(array, group, row):
        groups, rows, lanes = array.shape
        return jnp.pad(array, ((group, blocks + 1 - group - groups), (row, samples - row - rows), (0, owned - lanes)))

    gauges = (
        put(jnp.transpose(gauge_times, (1, 2, 0)), 0, 0)
        + put(gauge_route.reshape(1, 1, owned), blocks, 0)
        + put(gauge_cell.reshape(1, 1, owned), blocks, 1)
        + put(coastal_tiles.reshape(1, 1, coast_count), blocks, 2)
    )
    residuals = jnp.transpose(gauge_resid, (1, 2, 0))
    parcel, south, north, east, west = pl.pallas_call(
        functools.partial(prepare, halo, blocks, samples, coast_count),
        out_shape=(
            f32(tiles, parcel_rows, LANES), f32(2, halo, width), f32(2, halo, width),
            f32(height // 2, LANES), f32(height // 2, LANES),
        ),
        in_specs=vmem(4),
        out_specs=tuple(vmem(5)),
        scratch_shapes=[pltpu.VMEM((24, LANES), jnp.float32)],
        compiler_params=params,
        name="prepare",
    )(keep, gain, gauges, residuals)

    def exchange(array, axes):
        return lax.all_to_all(array, axes, split_axis=0, concat_axis=0, tiled=True)

    parcel = exchange(parcel, GRID_AXES)
    down = [(i, i + 1) for i in range(row_tiles - 1)]
    up = [(i + 1, i) for i in range(row_tiles - 1)]
    top = lax.ppermute(south, ROW_AXES, down)
    bottom = lax.ppermute(north, ROW_AXES, up)
    left = lax.ppermute(east, "lon", [(i, i + 1) for i in range(lons - 1)])
    right = lax.ppermute(west, "lon", [(i + 1, i) for i in range(lons - 1)])

    planes = width // LANES + 1
    rows_all = height + 2 * halo
    wide = max(2 * LANES, owned)
    pushes = pl.pallas_call(
        functools.partial(force, steps, halo, height, width),
        out_shape=f32(steps + 1, planes, spaced(rows_all), LANES),
        in_specs=vmem(1),
        out_specs=vmem(1)[0],
        scratch_shapes=[
            pltpu.VMEM((steps, wide), jnp.float32),
            pltpu.VMEM((rows_all, wide), jnp.bfloat16),
            pltpu.VMEM((2 * wide, planes * LANES), jnp.bfloat16),
        ],
        compiler_params=params,
        cost_estimate=pl.CostEstimate(
            flops=4 * steps * rows_all * wide * planes * LANES, bytes_accessed=4 * steps * planes * rows_all * LANES,
            transcendentals=0,
        ),
        name="force",
    )(parcel)

    plane = pltpu.VMEM((planes, spaced(rows_all), LANES), jnp.float32)
    longer = pltpu.VMEM((planes, spaced(rows_all + 16), LANES), jnp.float32)
    grad, sums = pl.pallas_call(
        functools.partial(sweep, steps),
        out_shape=(f32(height, width), f32(lons, 8, height)),
        in_specs=vmem(8),
        out_specs=tuple(vmem(2)),
        scratch_shapes=[longer, plane, longer] + [plane] * 5,
        compiler_params=params,
        name="sweep",
    )(keep, gain, top, bottom, left, right, parcel, pushes)

    sums = exchange(sums, "lon")
    own = pl.pallas_call(
        smooth, out_shape=f32(height, width), in_specs=vmem(1), out_specs=vmem(1)[0], compiler_params=params,
        cost_estimate=pl.CostEstimate(
            flops=6 * 2 * height * width * width, bytes_accessed=2 * 4 * height * width, transcendentals=width * width
        ),
        name="smooth",
    )(grad)
    return pl.pallas_call(
        finish, out_shape=f32(height, width), in_specs=vmem(2), out_specs=vmem(1)[0], compiler_params=params, name="finish",
    )(own, sums.reshape(lons * 8, height))


def solution(mesh):
    in_specs = (
        P(("lat", "gau"), "lon"),
        P(("scen", "lat", "gau"), "lon"),
        P(("lat", "gau"), "lon"),
        P(("lat", "gau"), "lon"),
        P(),
        P(("scen", "lon", "lat", "gau"), None),
        P(("scen", "lon", "lat", "gau")),
        P(("scen", "lon", "lat", "gau"), None, None),
        P(("scen", "lon", "lat", "gau"), None, None),
    )
    out_specs = P(("scen", "lat", "gau"), "lon")
    return jax.shard_map(local, mesh=mesh, in_specs=in_specs, out_specs=out_specs, check_vma=False)
```

```python
import functools
import math

import jax
import jax.numpy as jnp
from jax import lax
from jax.experimental import pallas as pl
from jax.experimental.pallas import tpu as pltpu
from jax.sharding import PartitionSpec as P

STEPS_BLOCK = 8
LANES = 128
SEG = 32
LEVELS = 4
CHUNK = 4

courant = 0.45
depth_floor = 0.1

GRID_AXES = ("lon", "lat", "gau")
ROW_AXES = ("lat", "gau")
VMEM_LIMIT = 16 * 1024 * 1024


def roll_lanes(x, shift):
    shift = shift % LANES
    return x if shift == 0 else pltpu.roll(x, shift, 1)


def lane_iota(rows):
    return lax.broadcasted_iota(jnp.int32, (rows, LANES), 1)


def pack_lanes(pieces):
    rows = pieces[0][0].shape[0]
    segment = lane_iota(rows) // SEG
    packed = jnp.zeros((rows, LANES), jnp.float32)
    for place, (array, first) in enumerate(pieces):
        packed = jnp.where(segment == place, roll_lanes(array, place * SEG - first), packed)
    return packed


def gauge_rows(owned):
    if 3 * owned <= LANES:
        return STEPS_BLOCK, owned
    assert owned <= LANES
    return 3 * STEPS_BLOCK, 0


def my_place():
    row = lax.axis_index("lat") * lax.axis_size("gau") + lax.axis_index("gau")
    return row, lax.axis_index("lon"), lax.axis_size("lat") * lax.axis_size("gau"), lax.axis_size("lon")


def prepare(
    halo, blocks, samples, coast_count, keep_ref, gain_ref, gauge_ref, resid_ref,
    parcel_ref, south_ref, north_ref, east_ref, west_ref, block_ref,
):
    height, width = keep_ref.shape
    my_row, my_lon, row_tiles, lons = my_place()
    keep, gain = keep_ref[...], gain_ref[...]
    half = height // 2
    first, last = slice(0, LANES), slice(width - LANES, width)
    end = LANES - halo

    owned = gauge_ref.shape[2]
    assert blocks == 2
    route, cell, coast = (gauge_ref[blocks, i : i + 1, :] for i in range(3))
    target = jnp.zeros_like(route)
    for entry in range(coast_count):
        target = jnp.where(route == entry, jnp.broadcast_to(coast[:, entry : entry + 1], route.shape), target)
    row_bits, width_bits = int(math.log2(row_tiles)), int(math.log2(width))
    assert row_tiles == 1 << row_bits and width == 1 << width_bits
    grid_row = (target & (row_tiles - 1)) * height + (cell >> width_bits)
    grid_col = (target >> row_bits) * width + (cell & (width - 1))
    block_ref[...] = jnp.zeros_like(block_ref)
    levels = lax.broadcasted_iota(jnp.int32, (STEPS_BLOCK, owned), 0)
    for block in range(blocks):
        series = jnp.zeros((STEPS_BLOCK, owned), jnp.float32)
        for sample in range(samples):
            times = gauge_ref[block, sample : sample + 1, :]
            resid = resid_ref[block, sample : sample + 1, :]
            series = series + jnp.where(times == levels, resid, 0.0)
        block_ref[block * STEPS_BLOCK : (block + 1) * STEPS_BLOCK, :owned] = series
    at = blocks * STEPS_BLOCK
    block_ref[at : at + 1, :owned] = grid_row.astype(jnp.float32)
    block_ref[at + 1 : at + 2, :owned] = grid_col.astype(jnp.float32)
    size, apart = gauge_rows(owned)
    gauges = block_ref[...]
    if size == STEPS_BLOCK:
        gauges = sum(
            roll_lanes(gauges[i * STEPS_BLOCK : (i + 1) * STEPS_BLOCK], i * apart) for i in range(3)
        )
    tiles = parcel_ref.shape[0]

    def put(tile, carry):
        parcel_ref[tile, 0:size, :] = gauges
        return carry

    lax.fori_loop(0, tiles, put, 0, unroll=tiles <= 16)

    for d_row in (-1, 1):
        top = 0 if d_row < 0 else height - halo
        for d_lon in (-1, 1):
            cols, start = (first, 0) if d_lon < 0 else (last, end)
            to_row, to_lon = my_row + d_row, my_lon + d_lon
            there = (to_row >= 0) & (to_row < row_tiles) & (to_lon >= 0) & (to_lon < lons)

            @pl.when(there)
            def _():
                for kind, source in enumerate((keep, gain)):
                    corner = pack_lanes([(source[top + 8 * i : top + 8 * i + 8, cols], start) for i in range(4)])
                    parcel_ref[to_lon * row_tiles + to_row, size + 8 * kind : size + 8 * kind + 8, :] = corner

    south_ref[0], south_ref[1] = keep[height - halo :], gain[height - halo :]
    north_ref[0], north_ref[1] = keep[:halo], gain[:halo]
    for goal, cols, start in ((east_ref, last, end), (west_ref, first, 0)):
        goal[...] = pack_lanes(
            [(keep[:half, cols], start), (gain[:half, cols], start), (keep[half:, cols], start), (gain[half:, cols], start)]
        )


def natural_rows(shape, axis, blocks):
    place = lax.broadcasted_iota(jnp.int32, shape, axis)
    return (place & 7) * blocks + (place >> 3)


def thirds(value):
    high = value.astype(jnp.bfloat16)
    rest = value - high.astype(jnp.float32)
    middle = rest.astype(jnp.bfloat16)
    return high, middle, (rest - middle.astype(jnp.float32)).astype(jnp.bfloat16)


def pick_rows(onehot, value):
    return sum(jnp.dot(onehot, part, preferred_element_type=jnp.float32) for part in thirds(value))


def shift_from(planes, shift, lanes):
    count = len(planes)
    rolled = [roll_lanes(plane, -shift) for plane in planes]
    if shift > 0:
        return [jnp.where(lanes >= LANES - shift, rolled[(c + 1) % count], rolled[c]) for c in range(count)]
    return [jnp.where(lanes < -shift, rolled[(c - 1) % count], rolled[c]) for c in range(count)]


def force(steps, halo, height, width, parcel_ref, force_ref, series_ref, rows_hot, cols_hot):
    planes, rows_all = force_ref.shape[1], height + 2 * halo
    my_row, my_lon, row_tiles, lons = my_place()
    wide = rows_hot.shape[1]
    tiles, parcel_rows = parcel_ref.shape[:2]
    size = parcel_rows - 16
    apart = wide // tiles if size == STEPS_BLOCK else 0
    owned = apart if apart else LANES
    group = wide // owned
    groups = tiles // group
    per_plane = LANES // owned
    blocks = rows_all // 8
    row_shift = (halo - my_row * height).astype(jnp.float32)
    col_shift = (-my_lon * width).astype(jnp.float32)
    at = natural_rows((rows_all, LANES), 0, blocks).astype(jnp.float32)

    def gather_gauges(index):
        lanes = lane_iota(STEPS_BLOCK)
        for part in range(wide // LANES):
            cols = slice(part * LANES, (part + 1) * LANES)
            fields = []
            for field in range(3):
                total = jnp.zeros((STEPS_BLOCK, LANES), jnp.float32)
                rows = slice(0, 8) if apart else slice(8 * field, 8 * field + 8)
                for i in range(per_plane):
                    source = index * group + part * per_plane + i
                    block = roll_lanes(parcel_ref[source, rows, :], i * owned - field * apart)
                    total = jnp.where((lanes >= i * owned) & (lanes < (i + 1) * owned), block, total)
                fields.append(total)
            series_ref[0:8, cols] = fields[0]
            series_ref[8:16, cols] = fields[1]
            row = fields[2][0:1] + row_shift
            col = fields[2][1:2] + col_shift
            col = jnp.where((col >= -halo) & (col < 0), col + float(planes * LANES), jnp.where(col < width + halo, col, -1.0))
            rows_hot[:, cols] = (at == row).astype(jnp.float32).astype(jnp.bfloat16)
            by_gauge = jnp.transpose(jnp.broadcast_to(col, (LANES, LANES)))
            for c in range(planes):
                spot = (lane_iota(LANES) + c * LANES).astype(jnp.float32)
                hot = (by_gauge == spot).astype(jnp.float32).astype(jnp.bfloat16)
                cols_hot[part * LANES : (part + 1) * LANES, c * LANES : (c + 1) * LANES] = hot
                cols_hot[wide + part * LANES : wide + (part + 1) * LANES, c * LANES : (c + 1) * LANES] = hot

    def levels_of(start, add):
        hot = rows_hot[...]
        both = []
        for level in range(LEVELS):
            value = series_ref[pl.ds(start + level, 1), :]
            high = value.astype(jnp.bfloat16)
            low = (value - high.astype(jnp.float32)).astype(jnp.bfloat16)
            both.append(jnp.concatenate([hot * high, hot * low], axis=1))
        both = jnp.concatenate(both, axis=0)
        for first in range(0, planes, 2):
            count = min(2, planes - first)
            total = jnp.dot(
                both, cols_hot[:, first * LANES : (first + count) * LANES], preferred_element_type=jnp.float32
            )
            for level in range(LEVELS):
                for c in range(count):
                    part = total[level * rows_all : (level + 1) * rows_all, c * LANES : (c + 1) * LANES]
                    goal = (start + level, first + c, slice(0, rows_all))
                    force_ref[goal] = force_ref[goal] + part if add else part

    def levels(add):
        def one(index, carry):
            levels_of(index * LEVELS, add)
            return carry

        lax.fori_loop(0, steps // LEVELS, one, 0)

    force_ref[steps] = jnp.zeros_like(force_ref[steps])
    gather_gauges(0)
    levels(False)
    if groups > 1:

        def more(index, carry):
            gather_gauges(index)
            levels(True)
            return carry

        lax.fori_loop(1, groups, more, 0)


def sweep(
    steps, keep_ref, gain_ref, top_ref, bottom_ref, left_ref, right_ref, parcel_ref, force_ref,
    grad_ref, sums_ref,
    a, fx, fy, keep_x, gain_x, keep_y, gain_y, plain, wet,
):
    height, width = keep_ref.shape
    halo = 2 * steps
    inner = width // LANES
    planes = inner + 1
    rows_all = height + 2 * halo
    blocks = rows_all // 8
    my_row, my_lon, row_tiles, lons = my_place()
    end = LANES - halo
    size = parcel_ref.shape[1] - 16
    has_top, has_bottom = my_row > 0, my_row < row_tiles - 1
    has_left, has_right = my_lon > 0, my_lon < lons - 1
    above, below = jnp.maximum(my_row - 1, 0), jnp.minimum(my_row + 1, row_tiles - 1)
    left, right = jnp.maximum(my_lon - 1, 0), jnp.minimum(my_lon + 1, lons - 1)
    lanes8 = lane_iota(8)

    def known(condition, value):
        return jnp.where(jnp.where(condition, 1, 0) == 1, value, 0.0)

    def up(value):
        return pltpu.roll(value, 7, 0)

    def down(value):
        return pltpu.roll(value, 1, 0)

    square = (rows_all, rows_all)
    spread = natural_rows(square, 0, blocks) == lax.broadcasted_iota(jnp.int32, square, 1)
    spread = spread.astype(jnp.float32).astype(jnp.bfloat16)
    every = range(planes)

    half = height // 2
    for kind, (source, by_x, by_y) in enumerate(((keep_ref, keep_x, keep_y), (gain_ref, gain_x, gain_y))):
        for c in range(inner):
            cols = slice(c * LANES, (c + 1) * LANES)
            plain[c, halo : halo + height, :] = source[:, cols]
            plain[c, 0:halo, :] = top_ref[kind, :, cols]
            plain[c, halo + height : rows_all, :] = bottom_ref[kind, :, cols]
        segment = lane_iota(half) // SEG
        for part in range(2):
            piece = 2 * part + kind
            by_left = roll_lanes(left_ref[...], end - piece * SEG)
            by_right = roll_lanes(right_ref[...], -piece * SEG)
            both = jnp.where(segment == 0, by_right, jnp.where(segment == LANES // SEG - 1, by_left, 0.0))
            plain[inner, halo + part * half : halo + (part + 1) * half, :] = both
        segment = lane_iota(8) // SEG
        for has_row, row, at in ((has_top, above, 0), (has_bottom, below, halo + height)):
            by_left = known(has_row & has_left, parcel_ref[left * row_tiles + row, size + 8 * kind : size + 8 * kind + 8, :])
            by_right = known(has_row & has_right, parcel_ref[right * row_tiles + row, size + 8 * kind : size + 8 * kind + 8, :])
            for i in range(4):
                both = jnp.where(
                    segment == 0, roll_lanes(by_right, -i * SEG),
                    jnp.where(segment == LANES // SEG - 1, roll_lanes(by_left, end - i * SEG), 0.0),
                )
                plain[inner, at + 8 * i : at + 8 * i + 8, :] = both
        placed = [pick_rows(spread, plain[c, 0:rows_all, :]) for c in every]
        for q in range(blocks):
            values = [placed[c][8 * q : 8 * q + 8] for c in every]
            shifted = shift_from(values, 1, lanes8)
            to = (q - 1) % blocks * 8
            for c in every:
                by_x[c, 8 * q : 8 * q + 8, :] = shifted[c]
                by_y[c, to : to + 8, :] = up(values[c]) if q == 0 else values[c]
        if kind == 0:
            for c in range(inner):
                wet[c, 0:rows_all, :] = placed[c]

    fx[...] = jnp.zeros_like(fx)
    fy[...] = jnp.zeros_like(fy)
    a[:, 0:rows_all, :] = force_ref[steps - 1, :, 0:rows_all, :]

    col_valid = jnp.where(lanes8 < LANES // 2, jnp.where(has_right, 1.0, 0.0), jnp.where(has_left, 1.0, 0.0))
    col_mask = jnp.where((lanes8 < halo) | (lanes8 >= end), col_valid, 0.0)
    sublane = lax.broadcasted_iota(jnp.int32, (8, LANES), 0)
    top_mask = jnp.where(sublane == (halo - 1) // blocks, jnp.where(has_top, 1.0, 0.0), 1.0)
    bottom_mask = jnp.where(sublane == (halo + height) // blocks, jnp.where(has_bottom, 1.0, 0.0), 1.0)

    def step(index, carry):
        after = jnp.where(index == steps - 1, steps, steps - 2 - index)
        for q in range(2):
            for c in every:
                a[c, rows_all + 8 * q : rows_all + 8 * q + 8, :] = up(a[c, 8 * q : 8 * q + 8, :])

        def chunk(number, inner_carry):
            start = pl.multiple_of(number * (8 * CHUNK), 8 * CHUNK)

            def at(q):
                return pl.ds(start + 8 * q, 8)

            near = [[a[c, at(q), :] for c in every] for q in range(CHUNK + 2)]
            new_y = [[fy[c, at(q), :] for c in every] for q in range(2)]
            total, new_x = [], []
            for q in range(CHUNK):
                new_y.append(
                    [
                        keep_y[c, at(q), :] * fy[c, at(q + 2), :] + gain_y[c, at(q), :] * (near[q + 2][c] - near[q][c])
                        for c in every
                    ]
                )
                ahead = shift_from(near[q], 2, lanes8)
                new_x.append(
                    [keep_x[c, at(q), :] * fx[c, at(q), :] + gain_x[c, at(q), :] * (ahead[c] - near[q][c]) for c in every]
                )
                total.append([near[q][c] + (new_y[q + 2][c] - new_y[q][c]) for c in every])
            behind = [shift_from(new_x[q], -2, lanes8) for q in range(CHUNK)]
            for q in range(CHUNK):
                for c in every:
                    value = total[q][c] + (new_x[q][c] - behind[q][c])
                    if c == inner:
                        value = value * col_mask
                    total[q][c] = value + force_ref[after, c, at(q), :]
            for q in range(CHUNK):
                for c in every:
                    fx[c, at(q), :] = new_x[q][c]
                    fy[c, at(q + 2), :] = new_y[q + 2][c]
                    a[c, at(q), :] = total[q][c]
            return inner_carry

        fy[:, 0:16, :] = jnp.zeros((planes, 16, LANES), jnp.float32)
        lax.fori_loop(0, blocks // CHUNK, chunk, 0)
        for q in range(2):
            for c in every:
                rows = slice(8 * q, 8 * q + 8)
                past = down(fy[c, rows_all + 8 * q : rows_all + 8 * q + 8, :])
                a[c, rows, :] = a[c, rows, :] - (past * col_mask if c == inner else past)
        for row, mask in ((halo - 1, top_mask), (halo + height, bottom_mask)):
            rows = slice(row % blocks * 8, row % blocks * 8 + 8)
            for c in every:
                a[c, rows, :] = a[c, rows, :] * mask
        return carry

    lax.fori_loop(0, steps, step, 0)

    grad = jnp.concatenate(
        [jnp.where(wet[c, 0:rows_all, :] > 0.0, a[c, 0:rows_all, :], 0.0) for c in range(inner)], axis=1
    )
    grad_ref[...] = grad
    length = 2.0 * width
    kind = lax.broadcasted_iota(jnp.int32, (8, width), 0)
    column = lax.broadcasted_iota(jnp.int32, (8, width), 1)
    steps_off = jnp.where(kind == 0, column, width - 1 - column).astype(jnp.float32)
    weights = jnp.where(kind < 2, jnp.exp(-steps_off / length), 0.0)
    sums = lax.dot_general(
        weights, grad, (((1,), (1,)), ((), ())), precision=lax.Precision.HIGHEST, preferred_element_type=jnp.float32
    )
    tall = (rows_all, height)
    gather = natural_rows(tall, 0, blocks) == lax.broadcasted_iota(jnp.int32, tall, 1) + halo
    sums = jnp.dot(
        sums, gather.astype(jnp.float32), precision=lax.Precision.HIGHEST, preferred_element_type=jnp.float32
    )
    for i in range(sums_ref.shape[0]):
        sums_ref[i] = sums


def smooth(halo, grad_ref, out_ref):
    width, (height, rows_all) = grad_ref.shape[1], (out_ref.shape[0], grad_ref.shape[0])
    wide = (height, rows_all)
    gather = natural_rows(wide, 1, rows_all // 8) == lax.broadcasted_iota(jnp.int32, wide, 0) + halo
    grad = pick_rows(gather.astype(jnp.float32).astype(jnp.bfloat16), grad_ref[...])
    length = 2.0 * width
    row = lax.broadcasted_iota(jnp.int32, (width, width), 0)
    column = lax.broadcasted_iota(jnp.int32, (width, width), 1)
    kernel = jnp.exp(-jnp.abs(row - column).astype(jnp.float32) / length)
    out_ref[...] = jnp.dot(
        grad, kernel, precision=lax.Precision.HIGHEST, preferred_element_type=jnp.float32
    )


def finish(own_ref, sums_ref, out_ref):
    width = own_ref.shape[1]
    length = 2.0 * width
    count = sums_ref.shape[0]
    me = lax.axis_index("lon")
    row = lax.broadcasted_iota(jnp.int32, (count, width), 0)
    column = lax.broadcasted_iota(jnp.int32, (count, width), 1)
    strip, kind = row >> 3, row & 7
    left = (kind == 0) & (strip > me)
    right = (kind == 1) & (strip < me)
    away = jnp.where(left, (strip - me) * width - column, (me - strip - 1) * width + column + 1)
    weights = jnp.where(left | right, jnp.exp(-jnp.maximum(away, 0).astype(jnp.float32) / length), 0.0)
    out_ref[...] = own_ref[...] + lax.dot_general(
        sums_ref[...], weights, (((0,), (0,)), ((), ())), precision=lax.Precision.HIGHEST,
        preferred_element_type=jnp.float32,
    )


def f32(*shape):
    return jax.ShapeDtypeStruct(shape, jnp.float32)


def spaced(rows):
    return 8 * (rows // 8 | 1)


def vmem(count):
    return [pl.BlockSpec(memory_space=pltpu.VMEM)] * count


def local(depth, surface, friction, wet, coastal_tiles, gauge_route, gauge_cell, gauge_times, gauge_resid):
    height, width = depth.shape
    owned = gauge_route.shape[0]
    blocks = gauge_resid.shape[1]
    steps = blocks * STEPS_BLOCK
    halo = 2 * steps
    assert halo == SEG and height == LANES
    tiles = lax.axis_size(GRID_AXES)
    lons = lax.axis_size("lon")
    row_tiles = lax.axis_size(ROW_AXES)
    parcel_rows = gauge_rows(owned)[0] + 16
    params = pltpu.CompilerParams(vmem_limit_bytes=VMEM_LIMIT)

    keep = (1.0 - friction) * wet.astype(jnp.float32)
    gain = ((courant * 0.5) ** 2 * jnp.maximum(depth + surface, depth_floor)) * keep
    samples, coast_count = gauge_resid.shape[2], coastal_tiles.shape[0]
    assert coast_count <= owned

    assert samples >= 3

    def put(array, group, row):
        groups, rows, lanes = array.shape
        return jnp.pad(array, ((group, blocks + 1 - group - groups), (row, samples - row - rows), (0, owned - lanes)))

    gauges = (
        put(jnp.transpose(gauge_times, (1, 2, 0)), 0, 0)
        + put(gauge_route.reshape(1, 1, owned), blocks, 0)
        + put(gauge_cell.reshape(1, 1, owned), blocks, 1)
        + put(coastal_tiles.reshape(1, 1, coast_count), blocks, 2)
    )
    residuals = jnp.transpose(gauge_resid, (1, 2, 0))
    parcel, south, north, east, west = pl.pallas_call(
        functools.partial(prepare, halo, blocks, samples, coast_count),
        out_shape=(
            f32(tiles, parcel_rows, LANES), f32(2, halo, width), f32(2, halo, width),
            f32(height // 2, LANES), f32(height // 2, LANES),
        ),
        in_specs=vmem(4),
        out_specs=tuple(vmem(5)),
        scratch_shapes=[pltpu.VMEM((24, LANES), jnp.float32)],
        compiler_params=params,
        name="prepare",
    )(keep, gain, gauges, residuals)

    def exchange(array, axes):
        return lax.all_to_all(array, axes, split_axis=0, concat_axis=0, tiled=True)

    parcel = exchange(parcel, GRID_AXES)
    down = [(i, i + 1) for i in range(row_tiles - 1)]
    up = [(i + 1, i) for i in range(row_tiles - 1)]
    top = lax.ppermute(south, ROW_AXES, down)
    bottom = lax.ppermute(north, ROW_AXES, up)
    left = lax.ppermute(east, "lon", [(i, i + 1) for i in range(lons - 1)])
    right = lax.ppermute(west, "lon", [(i + 1, i) for i in range(lons - 1)])

    planes = width // LANES + 1
    rows_all = height + 2 * halo
    wide = max(2 * LANES, owned)
    pushes = pl.pallas_call(
        functools.partial(force, steps, halo, height, width),
        out_shape=f32(steps + 1, planes, spaced(rows_all), LANES),
        in_specs=vmem(1),
        out_specs=vmem(1)[0],
        scratch_shapes=[
            pltpu.VMEM((steps, wide), jnp.float32),
            pltpu.VMEM((rows_all, wide), jnp.bfloat16),
            pltpu.VMEM((2 * wide, planes * LANES), jnp.bfloat16),
        ],
        compiler_params=params,
        cost_estimate=pl.CostEstimate(
            flops=4 * steps * rows_all * wide * planes * LANES, bytes_accessed=4 * steps * planes * rows_all * LANES,
            transcendentals=0,
        ),
        name="force",
    )(parcel)

    plane = pltpu.VMEM((planes, spaced(rows_all), LANES), jnp.float32)
    longer = pltpu.VMEM((planes, spaced(rows_all + 16), LANES), jnp.float32)
    grad, sums = pl.pallas_call(
        functools.partial(sweep, steps),
        out_shape=(f32(rows_all, width), f32(lons, 8, height)),
        in_specs=vmem(8),
        out_specs=tuple(vmem(2)),
        scratch_shapes=[longer, plane, longer] + [plane] * 6,
        compiler_params=params,
        name="sweep",
    )(keep, gain, top, bottom, left, right, parcel, pushes)

    sums = exchange(sums, "lon")
    own = pl.pallas_call(
        functools.partial(smooth, halo), out_shape=f32(height, width), in_specs=vmem(1), out_specs=vmem(1)[0], compiler_params=params,
        cost_estimate=pl.CostEstimate(
            flops=6 * 2 * height * width * width, bytes_accessed=2 * 4 * height * width, transcendentals=width * width
        ),
        name="smooth",
    )(grad)
    return pl.pallas_call(
        finish, out_shape=f32(height, width), in_specs=vmem(2), out_specs=vmem(1)[0], compiler_params=params, name="finish",
    )(own, sums.reshape(lons * 8, height))


def solution(mesh):
    in_specs = (
        P(("lat", "gau"), "lon"),
        P(("scen", "lat", "gau"), "lon"),
        P(("lat", "gau"), "lon"),
        P(("lat", "gau"), "lon"),
        P(),
        P(("scen", "lon", "lat", "gau"), None),
        P(("scen", "lon", "lat", "gau")),
        P(("scen", "lon", "lat", "gau"), None, None),
        P(("scen", "lon", "lat", "gau"), None, None),
    )
    out_specs = P(("scen", "lat", "gau"), "lon")
    return jax.shard_map(local, mesh=mesh, in_specs=in_specs, out_specs=out_specs, check_vma=False)
```

```python
import functools
import math

import jax
import jax.numpy as jnp
from jax import lax
from jax.experimental import pallas as pl
from jax.experimental.pallas import tpu as pltpu
from jax.sharding import PartitionSpec as P

STEPS_BLOCK = 8
LANES = 128
SEG = 32
LEVELS = 4

courant = 0.45
depth_floor = 0.1

GRID_AXES = ("lon", "lat", "gau")
ROW_AXES = ("lat", "gau")
VMEM_LIMIT = 16 * 1024 * 1024


def roll_lanes(x, shift):
    shift = shift % LANES
    return x if shift == 0 else pltpu.roll(x, shift, 1)


def lane_iota(rows):
    return lax.broadcasted_iota(jnp.int32, (rows, LANES), 1)


def pack_lanes(pieces):
    rows = pieces[0][0].shape[0]
    segment = lane_iota(rows) // SEG
    packed = jnp.zeros((rows, LANES), jnp.float32)
    for place, (array, first) in enumerate(pieces):
        packed = jnp.where(segment == place, roll_lanes(array, place * SEG - first), packed)
    return packed


def gauge_rows(owned):
    if 3 * owned <= LANES:
        return STEPS_BLOCK, owned
    assert owned <= LANES
    return 3 * STEPS_BLOCK, 0


def my_place():
    row = lax.axis_index("lat") * lax.axis_size("gau") + lax.axis_index("gau")
    return row, lax.axis_index("lon"), lax.axis_size("lat") * lax.axis_size("gau"), lax.axis_size("lon")


def prepare(
    halo, blocks, samples, coast_count, keep_ref, gain_ref, gauge_ref, resid_ref,
    parcel_ref, south_ref, north_ref, east_ref, west_ref, block_ref,
):
    height, width = keep_ref.shape
    my_row, my_lon, row_tiles, lons = my_place()
    keep, gain = keep_ref[...], gain_ref[...]
    half = height // 2
    first, last = slice(0, LANES), slice(width - LANES, width)
    end = LANES - halo

    owned = gauge_ref.shape[2]
    assert blocks == 2
    route, cell, coast = (gauge_ref[blocks, i : i + 1, :] for i in range(3))
    target = jnp.zeros_like(route)
    for entry in range(coast_count):
        target = jnp.where(route == entry, jnp.broadcast_to(coast[:, entry : entry + 1], route.shape), target)
    row_bits, width_bits = int(math.log2(row_tiles)), int(math.log2(width))
    assert row_tiles == 1 << row_bits and width == 1 << width_bits
    grid_row = (target & (row_tiles - 1)) * height + (cell >> width_bits)
    grid_col = (target >> row_bits) * width + (cell & (width - 1))
    block_ref[...] = jnp.zeros_like(block_ref)
    levels = lax.broadcasted_iota(jnp.int32, (STEPS_BLOCK, owned), 0)
    for block in range(blocks):
        series = jnp.zeros((STEPS_BLOCK, owned), jnp.float32)
        for sample in range(samples):
            times = gauge_ref[block, sample : sample + 1, :]
            resid = resid_ref[block, sample : sample + 1, :]
            series = series + jnp.where(times == levels, resid, 0.0)
        block_ref[block * STEPS_BLOCK : (block + 1) * STEPS_BLOCK, :owned] = series
    at = blocks * STEPS_BLOCK
    block_ref[at : at + 1, :owned] = grid_row.astype(jnp.float32)
    block_ref[at + 1 : at + 2, :owned] = grid_col.astype(jnp.float32)
    size, apart = gauge_rows(owned)
    gauges = block_ref[...]
    if size == STEPS_BLOCK:
        gauges = sum(
            roll_lanes(gauges[i * STEPS_BLOCK : (i + 1) * STEPS_BLOCK], i * apart) for i in range(3)
        )
    tiles = parcel_ref.shape[0]

    def put(tile, carry):
        parcel_ref[tile, 0:size, :] = gauges
        return carry

    lax.fori_loop(0, tiles, put, 0, unroll=tiles <= 16)

    for d_row in (-1, 1):
        top = 0 if d_row < 0 else height - halo
        for d_lon in (-1, 1):
            cols, start = (first, 0) if d_lon < 0 else (last, end)
            to_row, to_lon = my_row + d_row, my_lon + d_lon
            there = (to_row >= 0) & (to_row < row_tiles) & (to_lon >= 0) & (to_lon < lons)

            @pl.when(there)
            def _():
                for kind, source in enumerate((keep, gain)):
                    corner = pack_lanes([(source[top + 8 * i : top + 8 * i + 8, cols], start) for i in range(4)])
                    parcel_ref[to_lon * row_tiles + to_row, size + 8 * kind : size + 8 * kind + 8, :] = corner

    south_ref[0], south_ref[1] = keep[height - halo :], gain[height - halo :]
    north_ref[0], north_ref[1] = keep[:halo], gain[:halo]
    for goal, cols, start in ((east_ref, last, end), (west_ref, first, 0)):
        goal[...] = pack_lanes(
            [(keep[:half, cols], start), (gain[:half, cols], start), (keep[half:, cols], start), (gain[half:, cols], start)]
        )


def shift_from(planes, shift, lanes):
    count = len(planes)
    rolled = [roll_lanes(plane, -shift) for plane in planes]
    if shift > 0:
        return [jnp.where(lanes >= LANES - shift, rolled[(c + 1) % count], rolled[c]) for c in range(count)]
    return [jnp.where(lanes < -shift, rolled[(c - 1) % count], rolled[c]) for c in range(count)]


def force(steps, halo, height, width, parcel_ref, force_ref, series_ref, rows_hot, cols_hot):
    planes, rows_all = force_ref.shape[1], height + 2 * halo
    my_row, my_lon, row_tiles, lons = my_place()
    wide = rows_hot.shape[1]
    tiles, parcel_rows = parcel_ref.shape[:2]
    size = parcel_rows - 16
    apart = wide // tiles if size == STEPS_BLOCK else 0
    owned = apart if apart else LANES
    group = wide // owned
    groups = tiles // group
    per_plane = LANES // owned
    blocks = rows_all // 8
    row_shift = (halo - my_row * height).astype(jnp.float32)
    col_shift = (-my_lon * width).astype(jnp.float32)
    place = lax.broadcasted_iota(jnp.int32, (rows_all, LANES), 0)
    at = ((place & 7) * blocks + (place >> 3)).astype(jnp.float32)

    def gather_gauges(index):
        lanes = lane_iota(STEPS_BLOCK)
        for part in range(wide // LANES):
            cols = slice(part * LANES, (part + 1) * LANES)
            fields = []
            for field in range(3):
                total = jnp.zeros((STEPS_BLOCK, LANES), jnp.float32)
                rows = slice(0, 8) if apart else slice(8 * field, 8 * field + 8)
                for i in range(per_plane):
                    source = index * group + part * per_plane + i
                    block = roll_lanes(parcel_ref[source, rows, :], i * owned - field * apart)
                    total = jnp.where((lanes >= i * owned) & (lanes < (i + 1) * owned), block, total)
                fields.append(total)
            series_ref[0:8, cols] = fields[0]
            series_ref[8:16, cols] = fields[1]
            row = fields[2][0:1] + row_shift
            col = fields[2][1:2] + col_shift
            col = jnp.where((col >= -halo) & (col < 0), col + float(planes * LANES), jnp.where(col < width + halo, col, -1.0))
            rows_hot[:, cols] = (at == row).astype(jnp.float32).astype(jnp.bfloat16)
            by_gauge = jnp.transpose(jnp.broadcast_to(col, (LANES, LANES)))
            for c in range(planes):
                spot = (lane_iota(LANES) + c * LANES).astype(jnp.float32)
                hot = (by_gauge == spot).astype(jnp.float32).astype(jnp.bfloat16)
                cols_hot[part * LANES : (part + 1) * LANES, c * LANES : (c + 1) * LANES] = hot
                cols_hot[wide + part * LANES : wide + (part + 1) * LANES, c * LANES : (c + 1) * LANES] = hot

    def levels_of(start, add):
        hot = rows_hot[...]
        both = []
        for level in range(LEVELS):
            value = series_ref[pl.ds(start + level, 1), :]
            high = value.astype(jnp.bfloat16)
            low = (value - high.astype(jnp.float32)).astype(jnp.bfloat16)
            both.append(jnp.concatenate([hot * high, hot * low], axis=1))
        both = jnp.concatenate(both, axis=0)
        for first in range(0, planes, 2):
            count = min(2, planes - first)
            total = jnp.dot(
                both, cols_hot[:, first * LANES : (first + count) * LANES], preferred_element_type=jnp.float32
            )
            for level in range(LEVELS):
                for c in range(count):
                    part = total[level * rows_all : (level + 1) * rows_all, c * LANES : (c + 1) * LANES]
                    goal = (start + level, first + c, slice(0, rows_all))
                    force_ref[goal] = force_ref[goal] + part if add else part

    def levels(add):
        def one(index, carry):
            levels_of(index * LEVELS, add)
            return carry

        lax.fori_loop(0, steps // LEVELS, one, 0)

    force_ref[steps] = jnp.zeros_like(force_ref[steps])
    gather_gauges(0)
    levels(False)
    if groups > 1:

        def more(index, carry):
            gather_gauges(index)
            levels(True)
            return carry

        lax.fori_loop(1, groups, more, 0)


def sweep(
    steps, keep_ref, gain_ref, top_ref, bottom_ref, left_ref, right_ref, parcel_ref, force_ref,
    grad_ref, sums_ref,
    a, fx, fy, keep_x, gain_x, keep_y, gain_y, plain, pushes, arrived,
):
    height, width = keep_ref.shape
    halo = 2 * steps
    inner = width // LANES
    planes = inner + 1
    rows_all = height + 2 * halo
    blocks = rows_all // 8
    my_row, my_lon, row_tiles, lons = my_place()
    end = LANES - halo
    size = parcel_ref.shape[1] - 16
    has_top, has_bottom = my_row > 0, my_row < row_tiles - 1
    has_left, has_right = my_lon > 0, my_lon < lons - 1
    above, below = jnp.maximum(my_row - 1, 0), jnp.minimum(my_row + 1, row_tiles - 1)
    left, right = jnp.maximum(my_lon - 1, 0), jnp.minimum(my_lon + 1, lons - 1)
    lanes8 = lane_iota(8)

    def known(condition, value):
        return jnp.where(jnp.where(condition, 1, 0) == 1, value, 0.0)

    def up(value):
        return pltpu.roll(value, 7, 0)

    def down(value):
        return pltpu.roll(value, 1, 0)

    half = height // 2
    for kind, (source, by_x, by_y) in enumerate(((keep_ref, keep_x, keep_y), (gain_ref, gain_x, gain_y))):
        for c in range(inner):
            cols = slice(c * LANES, (c + 1) * LANES)
            plain[c, halo : halo + height, :] = source[:, cols]
            plain[c, 0:halo, :] = top_ref[kind, :, cols]
            plain[c, halo + height : rows_all, :] = bottom_ref[kind, :, cols]
        segment = lane_iota(half) // SEG
        for part in range(2):
            piece = 2 * part + kind
            by_left = roll_lanes(left_ref[...], end - piece * SEG)
            by_right = roll_lanes(right_ref[...], -piece * SEG)
            both = jnp.where(segment == 0, by_right, jnp.where(segment == LANES // SEG - 1, by_left, 0.0))
            plain[inner, halo + part * half : halo + (part + 1) * half, :] = both
        segment = lane_iota(8) // SEG
        for has_row, row, at in ((has_top, above, 0), (has_bottom, below, halo + height)):
            by_left = known(has_row & has_left, parcel_ref[left * row_tiles + row, size + 8 * kind : size + 8 * kind + 8, :])
            by_right = known(has_row & has_right, parcel_ref[right * row_tiles + row, size + 8 * kind : size + 8 * kind + 8, :])
            for i in range(4):
                both = jnp.where(
                    segment == 0, roll_lanes(by_right, -i * SEG),
                    jnp.where(segment == LANES // SEG - 1, roll_lanes(by_left, end - i * SEG), 0.0),
                )
                plain[inner, at + 8 * i : at + 8 * i + 8, :] = both
        for q in range(blocks):
            values = [plain[c, pl.ds(q, 8, stride=blocks), :] for c in range(planes)]
            shifted = shift_from(values, 1, lanes8)
            to = (q - 1) % blocks * 8
            for c in range(planes):
                by_x[c, 8 * q : 8 * q + 8, :] = shifted[c]
                by_y[c, to : to + 8, :] = up(values[c]) if q == 0 else values[c]

    col_valid = jnp.where(lanes8 < LANES // 2, jnp.where(has_right, 1.0, 0.0), jnp.where(has_left, 1.0, 0.0))
    col_mask = jnp.where((lanes8 < halo) | (lanes8 >= end), col_valid, 0.0)
    sublane = lax.broadcasted_iota(jnp.int32, (8, LANES), 0)
    row_mask = {}
    for row, there in ((halo - 1, has_top), (halo + height, has_bottom)):
        row_mask[row % blocks] = jnp.where(sublane == row // blocks, jnp.where(there, 1.0, 0.0), 1.0)
    every = range(planes)

    def level_of(order):
        return jnp.where(order < steps, steps - 1 - order, steps)

    def fetch(order, odd):
        return pltpu.make_async_copy(force_ref.at[level_of(order)], pushes.at[odd], arrived.at[odd])

    fetch(1, 1).start()
    fetch(2, 0).start()
    fx[...] = jnp.zeros_like(fx)
    fy[...] = jnp.zeros_like(fy)
    a[:, 0:rows_all, :] = force_ref[steps - 1, :, 0:rows_all, :]

    def step(odd):
        near, ahead, new_y, total, behind = {}, {}, {}, {}, {}

        def rows(q):
            return slice(8 * q, 8 * q + 8)

        def first(q):
            near[q] = [a[c, rows(q % blocks), :] for c in every]
            if q < blocks:
                ahead[q] = shift_from(near[q], 2, lanes8)
            else:
                near[q] = [up(value) for value in near[q]]

        def second_y(q):
            new_y[q] = [
                keep_y[c, rows(q), :] * fy[c, rows(q), :] + gain_y[c, rows(q), :] * (near[q + 2][c] - near[q][c])
                for c in every
            ]
            for c in every:
                fy[c, rows(q), :] = new_y[q][c]

        def second_x(q):
            new_x = [
                keep_x[c, rows(q), :] * fx[c, rows(q), :] + gain_x[c, rows(q), :] * (ahead[q][c] - near[q][c])
                for c in every
            ]
            before = new_y[q - 2] if q >= 2 else [down(fy[c, rows(q - 2 + blocks), :]) for c in every]
            total[q] = [near[q][c] + (new_y[q][c] - before[c]) + new_x[c] for c in every]
            behind[q] = shift_from(new_x, -2, lanes8)
            for c in every:
                fx[c, rows(q), :] = new_x[c]

        def third(q):
            for c in every:
                value = total[q][c] - behind[q][c]
                if c == inner:
                    value = value * col_mask
                if q in row_mask:
                    value = value * row_mask[q]
                a[c, rows(q), :] = value + pushes[odd, c, rows(q), :]

        for q in range(4):
            first(q)
        second_y(0)
        second_y(1)
        for q in range(2, blocks):
            first(q + 2)
            second_y(q)
            second_x(q)
            if q > 2:
                third(q - 1)
        for q in range(2):
            first(q)
            new_y[q] = [fy[c, rows(q), :] for c in every]
            second_x(q)
            third(q - 1 if q else blocks - 1)
        third(1)

    def pair(index, carry):
        for odd in (1, 0):
            order = 2 * index + 2 - odd
            fetch(order, odd).wait()
            step(odd)

            @pl.when(index < steps // 2 - 1)
            def _():
                fetch(order + 2, odd).start()

        return carry

    lax.fori_loop(0, steps // 2, pair, 0)

    for r in range(0, height, 8):
        s, q = divmod(halo + r, blocks)
        for c in range(inner):
            cols = slice(c * LANES, (c + 1) * LANES)
            value = a[c, pl.ds(8 * q + s, 8, stride=8), :]
            grad_ref[r : r + 8, cols] = jnp.where(keep_ref[r : r + 8, cols] > 0.0, value, 0.0)
    length = 2.0 * width
    kind = lax.broadcasted_iota(jnp.int32, (8, width), 0)
    column = lax.broadcasted_iota(jnp.int32, (8, width), 1)
    steps_off = jnp.where(kind == 0, column, width - 1 - column).astype(jnp.float32)
    weights = jnp.where(kind < 2, jnp.exp(-steps_off / length), 0.0)
    sums = lax.dot_general(
        weights, grad_ref[...], (((1,), (1,)), ((), ())), precision=lax.Precision.HIGHEST,
        preferred_element_type=jnp.float32,
    )
    for i in range(sums_ref.shape[0]):
        sums_ref[i] = sums


def smooth(grad_ref, out_ref):
    width = grad_ref.shape[1]
    length = 2.0 * width
    row = lax.broadcasted_iota(jnp.int32, (width, width), 0)
    column = lax.broadcasted_iota(jnp.int32, (width, width), 1)
    kernel = jnp.exp(-jnp.abs(row - column).astype(jnp.float32) / length)
    out_ref[...] = jnp.dot(
        grad_ref[...], kernel, precision=lax.Precision.HIGHEST, preferred_element_type=jnp.float32
    )


def finish(own_ref, sums_ref, out_ref):
    width = own_ref.shape[1]
    length = 2.0 * width
    count = sums_ref.shape[0]
    me = lax.axis_index("lon")
    row = lax.broadcasted_iota(jnp.int32, (count, width), 0)
    column = lax.broadcasted_iota(jnp.int32, (count, width), 1)
    strip, kind = row >> 3, row & 7
    left = (kind == 0) & (strip > me)
    right = (kind == 1) & (strip < me)
    away = jnp.where(left, (strip - me) * width - column, (me - strip - 1) * width + column + 1)
    weights = jnp.where(left | right, jnp.exp(-jnp.maximum(away, 0).astype(jnp.float32) / length), 0.0)
    out_ref[...] = own_ref[...] + lax.dot_general(
        sums_ref[...], weights, (((0,), (0,)), ((), ())), precision=lax.Precision.HIGHEST,
        preferred_element_type=jnp.float32,
    )


def f32(*shape):
    return jax.ShapeDtypeStruct(shape, jnp.float32)


def spaced(rows):
    return 8 * (rows // 8 | 1)


def vmem(count):
    return [pl.BlockSpec(memory_space=pltpu.VMEM)] * count


def local(depth, surface, friction, wet, coastal_tiles, gauge_route, gauge_cell, gauge_times, gauge_resid):
    height, width = depth.shape
    owned = gauge_route.shape[0]
    blocks = gauge_resid.shape[1]
    steps = blocks * STEPS_BLOCK
    halo = 2 * steps
    assert halo == SEG and height == LANES
    tiles = lax.axis_size(GRID_AXES)
    lons = lax.axis_size("lon")
    row_tiles = lax.axis_size(ROW_AXES)
    parcel_rows = gauge_rows(owned)[0] + 16
    params = pltpu.CompilerParams(vmem_limit_bytes=VMEM_LIMIT)

    keep = (1.0 - friction) * wet.astype(jnp.float32)
    gain = ((courant * 0.5) ** 2 * jnp.maximum(depth + surface, depth_floor)) * keep
    samples, coast_count = gauge_resid.shape[2], coastal_tiles.shape[0]
    assert coast_count <= owned

    assert samples >= 3

    def put(array, group, row):
        groups, rows, lanes = array.shape
        return jnp.pad(array, ((group, blocks + 1 - group - groups), (row, samples - row - rows), (0, owned - lanes)))

    gauges = (
        put(jnp.transpose(gauge_times, (1, 2, 0)), 0, 0)
        + put(gauge_route.reshape(1, 1, owned), blocks, 0)
        + put(gauge_cell.reshape(1, 1, owned), blocks, 1)
        + put(coastal_tiles.reshape(1, 1, coast_count), blocks, 2)
    )
    residuals = jnp.transpose(gauge_resid, (1, 2, 0))
    parcel, south, north, east, west = pl.pallas_call(
        functools.partial(prepare, halo, blocks, samples, coast_count),
        out_shape=(
            f32(tiles, parcel_rows, LANES), f32(2, halo, width), f32(2, halo, width),
            f32(height // 2, LANES), f32(height // 2, LANES),
        ),
        in_specs=vmem(4),
        out_specs=tuple(vmem(5)),
        scratch_shapes=[pltpu.VMEM((24, LANES), jnp.float32)],
        compiler_params=params,
        name="prepare",
    )(keep, gain, gauges, residuals)

    def exchange(array, axes):
        return lax.all_to_all(array, axes, split_axis=0, concat_axis=0, tiled=True)

    parcel = exchange(parcel, GRID_AXES)
    down = [(i, i + 1) for i in range(row_tiles - 1)]
    up = [(i + 1, i) for i in range(row_tiles - 1)]
    top = lax.ppermute(south, ROW_AXES, down)
    bottom = lax.ppermute(north, ROW_AXES, up)
    left = lax.ppermute(east, "lon", [(i, i + 1) for i in range(lons - 1)])
    right = lax.ppermute(west, "lon", [(i + 1, i) for i in range(lons - 1)])

    planes = width // LANES + 1
    rows_all = height + 2 * halo
    wide = max(2 * LANES, owned)
    pushes = pl.pallas_call(
        functools.partial(force, steps, halo, height, width),
        out_shape=f32(steps + 1, planes, spaced(rows_all), LANES),
        in_specs=vmem(1),
        out_specs=vmem(1)[0],
        scratch_shapes=[
            pltpu.VMEM((steps, wide), jnp.float32),
            pltpu.VMEM((rows_all, wide), jnp.bfloat16),
            pltpu.VMEM((2 * wide, planes * LANES), jnp.bfloat16),
        ],
        compiler_params=params,
        cost_estimate=pl.CostEstimate(
            flops=4 * steps * rows_all * wide * planes * LANES, bytes_accessed=4 * steps * planes * rows_all * LANES,
            transcendentals=0,
        ),
        name="force",
    )(parcel)

    plane = pltpu.VMEM((planes, spaced(rows_all), LANES), jnp.float32)
    grad, sums = pl.pallas_call(
        functools.partial(sweep, steps),
        out_shape=(f32(height, width), f32(lons, 8, height)),
        in_specs=vmem(8),
        out_specs=tuple(vmem(2)),
        scratch_shapes=[plane] * 8 + [
            pltpu.VMEM((2, planes, spaced(rows_all), LANES), jnp.float32), pltpu.SemaphoreType.DMA((2,)),
        ],
        compiler_params=params,
        name="sweep",
    )(keep, gain, top, bottom, left, right, parcel, pushes)

    sums = exchange(sums, "lon")
    own = pl.pallas_call(
        smooth, out_shape=f32(height, width), in_specs=vmem(1), out_specs=vmem(1)[0], compiler_params=params,
        cost_estimate=pl.CostEstimate(
            flops=6 * 2 * height * width * width, bytes_accessed=2 * 4 * height * width, transcendentals=width * width
        ),
        name="smooth",
    )(grad)
    return pl.pallas_call(
        finish, out_shape=f32(height, width), in_specs=vmem(2), out_specs=vmem(1)[0], compiler_params=params, name="finish",
    )(own, sums.reshape(lons * 8, height))


def solution(mesh):
    in_specs = (
        P(("lat", "gau"), "lon"),
        P(("scen", "lat", "gau"), "lon"),
        P(("lat", "gau"), "lon"),
        P(("lat", "gau"), "lon"),
        P(),
        P(("scen", "lon", "lat", "gau"), None),
        P(("scen", "lon", "lat", "gau")),
        P(("scen", "lon", "lat", "gau"), None, None),
        P(("scen", "lon", "lat", "gau"), None, None),
    )
    out_specs = P(("scen", "lat", "gau"), "lon")
    return jax.shard_map(local, mesh=mesh, in_specs=in_specs, out_specs=out_specs, check_vma=False)
```

```python
import functools
import math

import jax
import jax.numpy as jnp
from jax import lax
from jax.experimental import pallas as pl
from jax.experimental.pallas import tpu as pltpu
from jax.sharding import PartitionSpec as P

STEPS_BLOCK = 8
LANES = 128
SEG = 32
LEVELS = 4

courant = 0.45
depth_floor = 0.1

GRID_AXES = ("lon", "lat", "gau")
ROW_AXES = ("lat", "gau")
VMEM_LIMIT = 16 * 1024 * 1024


def roll_lanes(x, shift):
    shift = shift % LANES
    return x if shift == 0 else pltpu.roll(x, shift, 1)


def lane_iota(rows):
    return lax.broadcasted_iota(jnp.int32, (rows, LANES), 1)


def pack_lanes(pieces):
    rows = pieces[0][0].shape[0]
    segment = lane_iota(rows) // SEG
    packed = jnp.zeros((rows, LANES), jnp.float32)
    for place, (array, first) in enumerate(pieces):
        packed = jnp.where(segment == place, roll_lanes(array, place * SEG - first), packed)
    return packed


def gauge_rows(owned):
    if 3 * owned <= LANES:
        return STEPS_BLOCK, owned
    assert owned <= LANES
    return 3 * STEPS_BLOCK, 0


def my_place():
    row = lax.axis_index("lat") * lax.axis_size("gau") + lax.axis_index("gau")
    return row, lax.axis_index("lon"), lax.axis_size("lat") * lax.axis_size("gau"), lax.axis_size("lon")


def prepare(
    halo, blocks, samples, coast_count, keep_ref, gain_ref, gauge_ref, resid_ref,
    parcel_ref, south_ref, north_ref, east_ref, west_ref, block_ref,
):
    height, width = keep_ref.shape
    my_row, my_lon, row_tiles, lons = my_place()
    keep, gain = keep_ref[...], gain_ref[...]
    half = height // 2
    first, last = slice(0, LANES), slice(width - LANES, width)
    end = LANES - halo

    owned = gauge_ref.shape[2]
    assert blocks == 2
    route, cell, coast = (gauge_ref[blocks, i : i + 1, :] for i in range(3))
    target = jnp.zeros_like(route)
    for entry in range(coast_count):
        target = jnp.where(route == entry, jnp.broadcast_to(coast[:, entry : entry + 1], route.shape), target)
    row_bits, width_bits = int(math.log2(row_tiles)), int(math.log2(width))
    assert row_tiles == 1 << row_bits and width == 1 << width_bits
    grid_row = (target & (row_tiles - 1)) * height + (cell >> width_bits)
    grid_col = (target >> row_bits) * width + (cell & (width - 1))
    block_ref[...] = jnp.zeros_like(block_ref)
    levels = lax.broadcasted_iota(jnp.int32, (STEPS_BLOCK, owned), 0)
    for block in range(blocks):
        series = jnp.zeros((STEPS_BLOCK, owned), jnp.float32)
        for sample in range(samples):
            times = gauge_ref[block, sample : sample + 1, :]
            resid = resid_ref[block, sample : sample + 1, :]
            series = series + jnp.where(times == levels, resid, 0.0)
        block_ref[block * STEPS_BLOCK : (block + 1) * STEPS_BLOCK, :owned] = series
    at = blocks * STEPS_BLOCK
    block_ref[at : at + 1, :owned] = grid_row.astype(jnp.float32)
    block_ref[at + 1 : at + 2, :owned] = grid_col.astype(jnp.float32)
    size, apart = gauge_rows(owned)
    gauges = block_ref[...]
    if size == STEPS_BLOCK:
        gauges = sum(
            roll_lanes(gauges[i * STEPS_BLOCK : (i + 1) * STEPS_BLOCK], i * apart) for i in range(3)
        )
    tiles = parcel_ref.shape[0]

    def put(tile, carry):
        parcel_ref[tile, 0:size, :] = gauges
        return carry

    lax.fori_loop(0, tiles, put, 0, unroll=tiles <= 16)

    for d_row in (-1, 1):
        top = 0 if d_row < 0 else height - halo
        for d_lon in (-1, 1):
            cols, start = (first, 0) if d_lon < 0 else (last, end)
            to_row, to_lon = my_row + d_row, my_lon + d_lon
            there = (to_row >= 0) & (to_row < row_tiles) & (to_lon >= 0) & (to_lon < lons)

            @pl.when(there)
            def _():
                for kind, source in enumerate((keep, gain)):
                    corner = pack_lanes([(source[top + 8 * i : top + 8 * i + 8, cols], start) for i in range(4)])
                    parcel_ref[to_lon * row_tiles + to_row, size + 8 * kind : size + 8 * kind + 8, :] = corner

    south_ref[0], south_ref[1] = keep[height - halo :], gain[height - halo :]
    north_ref[0], north_ref[1] = keep[:halo], gain[:halo]
    for goal, cols, start in ((east_ref, last, end), (west_ref, first, 0)):
        goal[...] = pack_lanes(
            [(keep[:half, cols], start), (gain[:half, cols], start), (keep[half:, cols], start), (gain[half:, cols], start)]
        )


def from_rolled(rolled, shift, lanes):
    count = len(rolled)
    if shift > 0:
        return [jnp.where(lanes >= LANES - shift, rolled[(c + 1) % count], rolled[c]) for c in range(count)]
    return [jnp.where(lanes < -shift, rolled[(c - 1) % count], rolled[c]) for c in range(count)]


def shift_from(planes, shift, lanes):
    return from_rolled([roll_lanes(plane, -shift) for plane in planes], shift, lanes)


def force(steps, halo, height, width, parcel_ref, force_ref, series_ref, rows_hot, cols_hot):
    planes, rows_all = force_ref.shape[1], height + 2 * halo
    my_row, my_lon, row_tiles, lons = my_place()
    wide = rows_hot.shape[1]
    tiles, parcel_rows = parcel_ref.shape[:2]
    size = parcel_rows - 16
    apart = wide // tiles if size == STEPS_BLOCK else 0
    owned = apart if apart else LANES
    group = wide // owned
    groups = tiles // group
    per_plane = LANES // owned
    blocks = rows_all // 8
    row_shift = (halo - my_row * height).astype(jnp.float32)
    col_shift = (-my_lon * width).astype(jnp.float32)
    place = lax.broadcasted_iota(jnp.int32, (rows_all, LANES), 0)
    at = ((place & 7) * blocks + (place >> 3)).astype(jnp.float32)

    def gather_gauges(index):
        lanes = lane_iota(STEPS_BLOCK)
        for part in range(wide // LANES):
            cols = slice(part * LANES, (part + 1) * LANES)
            fields = []
            for field in range(3):
                total = jnp.zeros((STEPS_BLOCK, LANES), jnp.float32)
                rows = slice(0, 8) if apart else slice(8 * field, 8 * field + 8)
                for i in range(per_plane):
                    source = index * group + part * per_plane + i
                    block = roll_lanes(parcel_ref[source, rows, :], i * owned - field * apart)
                    total = jnp.where((lanes >= i * owned) & (lanes < (i + 1) * owned), block, total)
                fields.append(total)
            series_ref[0:8, cols] = fields[0]
            series_ref[8:16, cols] = fields[1]
            row = fields[2][0:1] + row_shift
            col = fields[2][1:2] + col_shift
            col = jnp.where((col >= -halo) & (col < 0), col + float(planes * LANES), jnp.where(col < width + halo, col, -1.0))
            rows_hot[:, cols] = (at == row).astype(jnp.float32).astype(jnp.bfloat16)
            by_gauge = jnp.transpose(jnp.broadcast_to(col, (LANES, LANES)))
            for c in range(planes):
                spot = (lane_iota(LANES) + c * LANES).astype(jnp.float32)
                hot = (by_gauge == spot).astype(jnp.float32).astype(jnp.bfloat16)
                cols_hot[part * LANES : (part + 1) * LANES, c * LANES : (c + 1) * LANES] = hot
                cols_hot[wide + part * LANES : wide + (part + 1) * LANES, c * LANES : (c + 1) * LANES] = hot

    def levels_of(start, add):
        hot = rows_hot[...]
        both = []
        for level in range(LEVELS):
            value = series_ref[pl.ds(start + level, 1), :]
            high = value.astype(jnp.bfloat16)
            low = (value - high.astype(jnp.float32)).astype(jnp.bfloat16)
            both.append(jnp.concatenate([hot * high, hot * low], axis=1))
        both = jnp.concatenate(both, axis=0)
        for first in range(0, planes, 2):
            count = min(2, planes - first)
            total = jnp.dot(
                both, cols_hot[:, first * LANES : (first + count) * LANES], preferred_element_type=jnp.float32
            )
            for level in range(LEVELS):
                for c in range(count):
                    part = total[level * rows_all : (level + 1) * rows_all, c * LANES : (c + 1) * LANES]
                    goal = (start + level, first + c, slice(0, rows_all))
                    force_ref[goal] = force_ref[goal] + part if add else part

    def levels(add):
        def one(index, carry):
            levels_of(index * LEVELS, add)
            return carry

        lax.fori_loop(0, steps // LEVELS, one, 0)

    force_ref[steps] = jnp.zeros_like(force_ref[steps])
    gather_gauges(0)
    levels(False)
    if groups > 1:

        def more(index, carry):
            gather_gauges(index)
            levels(True)
            return carry

        lax.fori_loop(1, groups, more, 0)


def sweep(
    steps, keep_ref, gain_ref, top_ref, bottom_ref, left_ref, right_ref, parcel_ref, force_ref,
    grad_ref, sums_ref,
    a, fx, fy, keep_x, gain_x, keep_y, gain_y, plain,
):
    height, width = keep_ref.shape
    halo = 2 * steps
    inner = width // LANES
    planes = inner + 1
    rows_all = height + 2 * halo
    blocks = rows_all // 8
    my_row, my_lon, row_tiles, lons = my_place()
    end = LANES - halo
    size = parcel_ref.shape[1] - 16
    has_top, has_bottom = my_row > 0, my_row < row_tiles - 1
    has_left, has_right = my_lon > 0, my_lon < lons - 1
    above, below = jnp.maximum(my_row - 1, 0), jnp.minimum(my_row + 1, row_tiles - 1)
    left, right = jnp.maximum(my_lon - 1, 0), jnp.minimum(my_lon + 1, lons - 1)
    lanes8 = lane_iota(8)

    def known(condition, value):
        return jnp.where(jnp.where(condition, 1, 0) == 1, value, 0.0)

    def up(value):
        return pltpu.roll(value, 7, 0)

    def down(value):
        return pltpu.roll(value, 1, 0)

    half = height // 2
    for kind, (source, by_x, by_y) in enumerate(((keep_ref, keep_x, keep_y), (gain_ref, gain_x, gain_y))):
        for c in range(inner):
            cols = slice(c * LANES, (c + 1) * LANES)
            plain[c, halo : halo + height, :] = source[:, cols]
            plain[c, 0:halo, :] = top_ref[kind, :, cols]
            plain[c, halo + height : rows_all, :] = bottom_ref[kind, :, cols]
        segment = lane_iota(half) // SEG
        for part in range(2):
            piece = 2 * part + kind
            by_left = roll_lanes(left_ref[...], end - piece * SEG)
            by_right = roll_lanes(right_ref[...], -piece * SEG)
            both = jnp.where(segment == 0, by_right, jnp.where(segment == LANES // SEG - 1, by_left, 0.0))
            plain[inner, halo + part * half : halo + (part + 1) * half, :] = both
        segment = lane_iota(8) // SEG
        for has_row, row, at in ((has_top, above, 0), (has_bottom, below, halo + height)):
            by_left = known(has_row & has_left, parcel_ref[left * row_tiles + row, size + 8 * kind : size + 8 * kind + 8, :])
            by_right = known(has_row & has_right, parcel_ref[right * row_tiles + row, size + 8 * kind : size + 8 * kind + 8, :])
            for i in range(4):
                both = jnp.where(
                    segment == 0, roll_lanes(by_right, -i * SEG),
                    jnp.where(segment == LANES // SEG - 1, roll_lanes(by_left, end - i * SEG), 0.0),
                )
                plain[inner, at + 8 * i : at + 8 * i + 8, :] = both
        for q in range(blocks):
            values = [plain[c, pl.ds(q, 8, stride=blocks), :] for c in range(planes)]
            shifted = shift_from(values, 1, lanes8)
            to = (q - 1) % blocks * 8
            for c in range(planes):
                by_x[c, 8 * q : 8 * q + 8, :] = shifted[c]
                by_y[c, to : to + 8, :] = up(values[c]) if q == 0 else values[c]

    col_valid = jnp.where(lanes8 < LANES // 2, jnp.where(has_right, 1.0, 0.0), jnp.where(has_left, 1.0, 0.0))
    col_mask = jnp.where((lanes8 < halo) | (lanes8 >= end), col_valid, 0.0)
    sublane = lax.broadcasted_iota(jnp.int32, (8, LANES), 0)
    row_mask = {}
    for row, there in ((halo - 1, has_top), (halo + height, has_bottom)):
        row_mask[row % blocks] = jnp.where(sublane == row // blocks, jnp.where(there, 1.0, 0.0), 1.0)
    every = range(planes)

    fx[...] = jnp.zeros_like(fx)
    fy[...] = jnp.zeros_like(fy)
    a[:, 0:rows_all, :] = force_ref[steps - 1, :, 0:rows_all, :]

    def step(index, carry):
        level = jnp.where(index < steps - 1, steps - 2 - index, steps)
        near, ahead, new_y, total, behind, push = {}, {}, {}, {}, {}, {}

        def rows(q):
            return slice(8 * q, 8 * q + 8)

        def first(q):
            near[q] = [a[c, rows(q % blocks), :] for c in every]
            if q < blocks:
                ahead[q] = [roll_lanes(value, -2) for value in near[q]]
                push[q] = [force_ref[level, c, rows(q), :] for c in every]
            else:
                near[q] = [up(value) for value in near[q]]

        def second_y(q):
            new_y[q] = [
                keep_y[c, rows(q), :] * fy[c, rows(q), :] + gain_y[c, rows(q), :] * (near[q + 2][c] - near[q][c])
                for c in every
            ]
            for c in every:
                fy[c, rows(q), :] = new_y[q][c]

        def second_x(q):
            far = from_rolled(ahead[q], 2, lanes8)
            new_x = [
                keep_x[c, rows(q), :] * fx[c, rows(q), :] + gain_x[c, rows(q), :] * (far[c] - near[q][c]) for c in every
            ]
            behind[q] = [roll_lanes(value, 2) for value in new_x]
            before = new_y[q - 2] if q >= 2 else [down(fy[c, rows(q - 2 + blocks), :]) for c in every]
            total[q] = [(near[q][c] + push[q][c]) + (new_y[q][c] - before[c]) + new_x[c] for c in every]
            for c in every:
                fx[c, rows(q), :] = new_x[c]

        def third(q):
            far = from_rolled(behind[q], -2, lanes8)
            for c in every:
                value = total[q][c] - far[c]
                if c == inner:
                    value = value * col_mask
                if q in row_mask:
                    value = value * row_mask[q]
                a[c, rows(q), :] = value

        for q in range(4):
            first(q)
        second_y(0)
        second_y(1)
        for q in range(2, blocks):
            first(q + 2)
            second_y(q)
            second_x(q)
            if q > 2:
                third(q - 1)
        for q in range(2):
            first(q)
            new_y[q] = [fy[c, rows(q), :] for c in every]
        for q in range(2):
            second_x(q)
            third(q - 1 if q else blocks - 1)
        third(1)
        return carry

    lax.fori_loop(0, steps, step, 0)

    for r in range(0, height, 8):
        s, q = divmod(halo + r, blocks)
        for c in range(inner):
            cols = slice(c * LANES, (c + 1) * LANES)
            value = a[c, pl.ds(8 * q + s, 8, stride=8), :]
            grad_ref[r : r + 8, cols] = jnp.where(keep_ref[r : r + 8, cols] > 0.0, value, 0.0)
    length = 2.0 * width
    kind = lax.broadcasted_iota(jnp.int32, (8, width), 0)
    column = lax.broadcasted_iota(jnp.int32, (8, width), 1)
    steps_off = jnp.where(kind == 0, column, width - 1 - column).astype(jnp.float32)
    weights = jnp.where(kind < 2, jnp.exp(-steps_off / length), 0.0)
    sums = lax.dot_general(
        weights, grad_ref[...], (((1,), (1,)), ((), ())), precision=lax.Precision.HIGHEST,
        preferred_element_type=jnp.float32,
    )
    for i in range(sums_ref.shape[0]):
        sums_ref[i] = sums


def smooth(grad_ref, out_ref):
    width = grad_ref.shape[1]
    length = 2.0 * width
    row = lax.broadcasted_iota(jnp.int32, (width, width), 0)
    column = lax.broadcasted_iota(jnp.int32, (width, width), 1)
    kernel = jnp.exp(-jnp.abs(row - column).astype(jnp.float32) / length)
    out_ref[...] = jnp.dot(
        grad_ref[...], kernel, precision=lax.Precision.HIGHEST, preferred_element_type=jnp.float32
    )


def finish(own_ref, sums_ref, out_ref):
    width = own_ref.shape[1]
    length = 2.0 * width
    count = sums_ref.shape[0]
    me = lax.axis_index("lon")
    row = lax.broadcasted_iota(jnp.int32, (count, width), 0)
    column = lax.broadcasted_iota(jnp.int32, (count, width), 1)
    strip, kind = row >> 3, row & 7
    left = (kind == 0) & (strip > me)
    right = (kind == 1) & (strip < me)
    away = jnp.where(left, (strip - me) * width - column, (me - strip - 1) * width + column + 1)
    weights = jnp.where(left | right, jnp.exp(-jnp.maximum(away, 0).astype(jnp.float32) / length), 0.0)
    out_ref[...] = own_ref[...] + lax.dot_general(
        sums_ref[...], weights, (((0,), (0,)), ((), ())), precision=lax.Precision.HIGHEST,
        preferred_element_type=jnp.float32,
    )


def f32(*shape):
    return jax.ShapeDtypeStruct(shape, jnp.float32)


def spaced(rows):
    return 8 * (rows // 8 | 1)


def vmem(count):
    return [pl.BlockSpec(memory_space=pltpu.VMEM)] * count


def local(depth, surface, friction, wet, coastal_tiles, gauge_route, gauge_cell, gauge_times, gauge_resid):
    height, width = depth.shape
    owned = gauge_route.shape[0]
    blocks = gauge_resid.shape[1]
    steps = blocks * STEPS_BLOCK
    halo = 2 * steps
    assert halo == SEG and height == LANES
    tiles = lax.axis_size(GRID_AXES)
    lons = lax.axis_size("lon")
    row_tiles = lax.axis_size(ROW_AXES)
    parcel_rows = gauge_rows(owned)[0] + 16
    params = pltpu.CompilerParams(vmem_limit_bytes=VMEM_LIMIT)

    keep = (1.0 - friction) * wet.astype(jnp.float32)
    gain = ((courant * 0.5) ** 2 * jnp.maximum(depth + surface, depth_floor)) * keep
    samples, coast_count = gauge_resid.shape[2], coastal_tiles.shape[0]
    assert coast_count <= owned

    assert samples >= 3

    def put(array, group, row):
        groups, rows, lanes = array.shape
        return jnp.pad(array, ((group, blocks + 1 - group - groups), (row, samples - row - rows), (0, owned - lanes)))

    gauges = (
        put(jnp.transpose(gauge_times, (1, 2, 0)), 0, 0)
        + put(gauge_route.reshape(1, 1, owned), blocks, 0)
        + put(gauge_cell.reshape(1, 1, owned), blocks, 1)
        + put(coastal_tiles.reshape(1, 1, coast_count), blocks, 2)
    )
    residuals = jnp.transpose(gauge_resid, (1, 2, 0))
    parcel, south, north, east, west = pl.pallas_call(
        functools.partial(prepare, halo, blocks, samples, coast_count),
        out_shape=(
            f32(tiles, parcel_rows, LANES), f32(2, halo, width), f32(2, halo, width),
            f32(height // 2, LANES), f32(height // 2, LANES),
        ),
        in_specs=vmem(4),
        out_specs=tuple(vmem(5)),
        scratch_shapes=[pltpu.VMEM((24, LANES), jnp.float32)],
        compiler_params=params,
        name="prepare",
    )(keep, gain, gauges, residuals)

    def exchange(array, axes):
        return lax.all_to_all(array, axes, split_axis=0, concat_axis=0, tiled=True)

    parcel = exchange(parcel, GRID_AXES)
    down = [(i, i + 1) for i in range(row_tiles - 1)]
    up = [(i + 1, i) for i in range(row_tiles - 1)]
    top = lax.ppermute(south, ROW_AXES, down)
    bottom = lax.ppermute(north, ROW_AXES, up)
    left = lax.ppermute(east, "lon", [(i, i + 1) for i in range(lons - 1)])
    right = lax.ppermute(west, "lon", [(i + 1, i) for i in range(lons - 1)])

    planes = width // LANES + 1
    rows_all = height + 2 * halo
    wide = max(2 * LANES, owned)
    pushes = pl.pallas_call(
        functools.partial(force, steps, halo, height, width),
        out_shape=f32(steps + 1, planes, spaced(rows_all), LANES),
        in_specs=vmem(1),
        out_specs=vmem(1)[0],
        scratch_shapes=[
            pltpu.VMEM((steps, wide), jnp.float32),
            pltpu.VMEM((rows_all, wide), jnp.bfloat16),
            pltpu.VMEM((2 * wide, planes * LANES), jnp.bfloat16),
        ],
        compiler_params=params,
        cost_estimate=pl.CostEstimate(
            flops=4 * steps * rows_all * wide * planes * LANES, bytes_accessed=4 * steps * planes * rows_all * LANES,
            transcendentals=0,
        ),
        name="force",
    )(parcel)

    plane = pltpu.VMEM((planes, spaced(rows_all), LANES), jnp.float32)
    grad, sums = pl.pallas_call(
        functools.partial(sweep, steps),
        out_shape=(f32(height, width), f32(lons, 8, height)),
        in_specs=vmem(8),
        out_specs=tuple(vmem(2)),
        scratch_shapes=[plane] * 8,
        compiler_params=params,
        name="sweep",
    )(keep, gain, top, bottom, left, right, parcel, pushes)

    sums = exchange(sums, "lon")
    own = pl.pallas_call(
        smooth, out_shape=f32(height, width), in_specs=vmem(1), out_specs=vmem(1)[0], compiler_params=params,
        cost_estimate=pl.CostEstimate(
            flops=6 * 2 * height * width * width, bytes_accessed=2 * 4 * height * width, transcendentals=width * width
        ),
        name="smooth",
    )(grad)
    return pl.pallas_call(
        finish, out_shape=f32(height, width), in_specs=vmem(2), out_specs=vmem(1)[0], compiler_params=params, name="finish",
    )(own, sums.reshape(lons * 8, height))


def solution(mesh):
    in_specs = (
        P(("lat", "gau"), "lon"),
        P(("scen", "lat", "gau"), "lon"),
        P(("lat", "gau"), "lon"),
        P(("lat", "gau"), "lon"),
        P(),
        P(("scen", "lon", "lat", "gau"), None),
        P(("scen", "lon", "lat", "gau")),
        P(("scen", "lon", "lat", "gau"), None, None),
        P(("scen", "lon", "lat", "gau"), None, None),
    )
    out_specs = P(("scen", "lat", "gau"), "lon")
    return jax.shard_map(local, mesh=mesh, in_specs=in_specs, out_specs=out_specs, check_vma=False)
```

```python
import functools
import math

import jax
import jax.numpy as jnp
from jax import lax
from jax.experimental import pallas as pl
from jax.experimental.pallas import tpu as pltpu
from jax.sharding import PartitionSpec as P

STEPS_BLOCK = 8
LANES = 128
SEG = 32
LEVELS = 4

courant = 0.45
depth_floor = 0.1

GRID_AXES = ("lon", "lat", "gau")
ROW_AXES = ("lat", "gau")
VMEM_LIMIT = 16 * 1024 * 1024


def roll_lanes(x, shift):
    shift = shift % LANES
    return x if shift == 0 else pltpu.roll(x, shift, 1)


def lane_iota(rows):
    return lax.broadcasted_iota(jnp.int32, (rows, LANES), 1)


def pack_lanes(pieces):
    rows = pieces[0][0].shape[0]
    segment = lane_iota(rows) // SEG
    packed = jnp.zeros((rows, LANES), jnp.float32)
    for place, (array, first) in enumerate(pieces):
        packed = jnp.where(segment == place, roll_lanes(array, place * SEG - first), packed)
    return packed


def gauge_rows(owned):
    if 3 * owned <= LANES:
        return STEPS_BLOCK, owned
    assert owned <= LANES
    return 3 * STEPS_BLOCK, 0


def my_place():
    row = lax.axis_index("lat") * lax.axis_size("gau") + lax.axis_index("gau")
    return row, lax.axis_index("lon"), lax.axis_size("lat") * lax.axis_size("gau"), lax.axis_size("lon")


def prepare(
    halo, blocks, samples, coast_count, keep_ref, gain_ref, gauge_ref, resid_ref,
    parcel_ref, south_ref, north_ref, strips_ref, block_ref,
):
    height, width = keep_ref.shape
    my_row, my_lon, row_tiles, lons = my_place()
    keep, gain = keep_ref[...], gain_ref[...]
    half = height // 2
    first, last = slice(0, LANES), slice(width - LANES, width)
    end = LANES - halo

    owned = gauge_ref.shape[2]
    assert blocks == 2
    route, cell, coast = (gauge_ref[blocks, i : i + 1, :] for i in range(3))
    target = jnp.zeros_like(route)
    for entry in range(coast_count):
        target = jnp.where(route == entry, jnp.broadcast_to(coast[:, entry : entry + 1], route.shape), target)
    row_bits, width_bits = int(math.log2(row_tiles)), int(math.log2(width))
    assert row_tiles == 1 << row_bits and width == 1 << width_bits
    grid_row = (target & (row_tiles - 1)) * height + (cell >> width_bits)
    grid_col = (target >> row_bits) * width + (cell & (width - 1))
    block_ref[...] = jnp.zeros_like(block_ref)
    levels = lax.broadcasted_iota(jnp.int32, (STEPS_BLOCK, owned), 0)
    for block in range(blocks):
        series = jnp.zeros((STEPS_BLOCK, owned), jnp.float32)
        for sample in range(samples):
            times = gauge_ref[block, sample : sample + 1, :]
            resid = resid_ref[block, sample : sample + 1, :]
            series = series + jnp.where(times == levels, resid, 0.0)
        block_ref[block * STEPS_BLOCK : (block + 1) * STEPS_BLOCK, :owned] = series
    at = blocks * STEPS_BLOCK
    block_ref[at : at + 1, :owned] = grid_row.astype(jnp.float32)
    block_ref[at + 1 : at + 2, :owned] = grid_col.astype(jnp.float32)
    size, apart = gauge_rows(owned)
    gauges = block_ref[...]
    if size == STEPS_BLOCK:
        gauges = sum(
            roll_lanes(gauges[i * STEPS_BLOCK : (i + 1) * STEPS_BLOCK], i * apart) for i in range(3)
        )
    tiles = parcel_ref.shape[0]

    def put(tile, carry):
        parcel_ref[tile, 0:size, :] = gauges
        return carry

    lax.fori_loop(0, tiles, put, 0, unroll=tiles <= 16)

    for d_row in (-1, 1):
        top = 0 if d_row < 0 else height - halo
        for d_lon in (-1, 1):
            cols, start = (first, 0) if d_lon < 0 else (last, end)
            to_row, to_lon = my_row + d_row, my_lon + d_lon
            there = (to_row >= 0) & (to_row < row_tiles) & (to_lon >= 0) & (to_lon < lons)

            @pl.when(there)
            def _():
                for kind, source in enumerate((keep, gain)):
                    corner = pack_lanes([(source[top + 8 * i : top + 8 * i + 8, cols], start) for i in range(4)])
                    parcel_ref[to_lon * row_tiles + to_row, size + 8 * kind : size + 8 * kind + 8, :] = corner

    south_ref[0], south_ref[1] = keep[height - halo :], gain[height - halo :]
    north_ref[0], north_ref[1] = keep[:halo], gain[:halo]
    for d_lon, cols, start in ((1, last, end), (-1, first, 0)):
        there = (my_lon + d_lon >= 0) & (my_lon + d_lon < lons)

        @pl.when(there)
        def _():
            strips_ref[my_lon + d_lon] = pack_lanes(
                [(keep[:half, cols], start), (gain[:half, cols], start), (keep[half:, cols], start), (gain[half:, cols], start)]
            )


def from_rolled(rolled, shift, lanes):
    count = len(rolled)
    if shift > 0:
        return [jnp.where(lanes >= LANES - shift, rolled[(c + 1) % count], rolled[c]) for c in range(count)]
    return [jnp.where(lanes < -shift, rolled[(c - 1) % count], rolled[c]) for c in range(count)]


def shift_from(planes, shift, lanes):
    return from_rolled([roll_lanes(plane, -shift) for plane in planes], shift, lanes)


def force(steps, halo, height, width, parcel_ref, force_ref, series_ref, rows_hot, cols_hot):
    planes, rows_all = force_ref.shape[1], height + 2 * halo
    my_row, my_lon, row_tiles, lons = my_place()
    wide = rows_hot.shape[1]
    tiles, parcel_rows = parcel_ref.shape[:2]
    size = parcel_rows - 16
    apart = wide // tiles if size == STEPS_BLOCK else 0
    owned = apart if apart else LANES
    group = wide // owned
    groups = tiles // group
    per_plane = LANES // owned
    blocks = rows_all // 8
    row_shift = (halo - my_row * height).astype(jnp.float32)
    col_shift = (-my_lon * width).astype(jnp.float32)
    place = lax.broadcasted_iota(jnp.int32, (rows_all, LANES), 0)
    at = ((place & 7) * blocks + (place >> 3)).astype(jnp.float32)

    def gather_gauges(index):
        lanes = lane_iota(STEPS_BLOCK)
        for part in range(wide // LANES):
            cols = slice(part * LANES, (part + 1) * LANES)
            fields = []
            for field in range(3):
                total = jnp.zeros((STEPS_BLOCK, LANES), jnp.float32)
                rows = slice(0, 8) if apart else slice(8 * field, 8 * field + 8)
                for i in range(per_plane):
                    source = index * group + part * per_plane + i
                    block = roll_lanes(parcel_ref[source, rows, :], i * owned - field * apart)
                    total = jnp.where((lanes >= i * owned) & (lanes < (i + 1) * owned), block, total)
                fields.append(total)
            series_ref[0:8, cols] = fields[0]
            series_ref[8:16, cols] = fields[1]
            row = fields[2][0:1] + row_shift
            col = fields[2][1:2] + col_shift
            col = jnp.where((col >= -halo) & (col < 0), col + float(planes * LANES), jnp.where(col < width + halo, col, -1.0))
            rows_hot[:, cols] = (at == row).astype(jnp.float32).astype(jnp.bfloat16)
            by_gauge = jnp.transpose(jnp.broadcast_to(col, (LANES, LANES)))
            for c in range(planes):
                spot = (lane_iota(LANES) + c * LANES).astype(jnp.float32)
                hot = (by_gauge == spot).astype(jnp.float32).astype(jnp.bfloat16)
                cols_hot[part * LANES : (part + 1) * LANES, c * LANES : (c + 1) * LANES] = hot
                cols_hot[wide + part * LANES : wide + (part + 1) * LANES, c * LANES : (c + 1) * LANES] = hot

    def levels_of(start, add):
        hot = rows_hot[...]
        both = []
        for level in range(LEVELS):
            value = series_ref[pl.ds(start + level, 1), :]
            high = value.astype(jnp.bfloat16)
            low = (value - high.astype(jnp.float32)).astype(jnp.bfloat16)
            both.append(jnp.concatenate([hot * high, hot * low], axis=1))
        both = jnp.concatenate(both, axis=0)
        for first in range(0, planes, 2):
            count = min(2, planes - first)
            total = jnp.dot(
                both, cols_hot[:, first * LANES : (first + count) * LANES], preferred_element_type=jnp.float32
            )
            for level in range(LEVELS):
                for c in range(count):
                    part = total[level * rows_all : (level + 1) * rows_all, c * LANES : (c + 1) * LANES]
                    goal = (start + level, first + c, slice(0, rows_all))
                    force_ref[goal] = force_ref[goal] + part if add else part

    def levels(add):
        def one(index, carry):
            levels_of(index * LEVELS, add)
            return carry

        lax.fori_loop(0, steps // LEVELS, one, 0)

    force_ref[steps] = jnp.zeros_like(force_ref[steps])
    gather_gauges(0)
    levels(False)
    if groups > 1:

        def more(index, carry):
            gather_gauges(index)
            levels(True)
            return carry

        lax.fori_loop(1, groups, more, 0)


def sweep(
    steps, keep_ref, gain_ref, top_ref, bottom_ref, strips_ref, parcel_ref, force_ref,
    grad_ref, sums_ref,
    a, fx, fy, keep_x, gain_x, keep_y, gain_y, plain,
):
    height, width = keep_ref.shape
    halo = 2 * steps
    inner = width // LANES
    planes = inner + 1
    rows_all = height + 2 * halo
    blocks = rows_all // 8
    my_row, my_lon, row_tiles, lons = my_place()
    end = LANES - halo
    size = parcel_ref.shape[1] - 16
    has_top, has_bottom = my_row > 0, my_row < row_tiles - 1
    has_left, has_right = my_lon > 0, my_lon < lons - 1
    above, below = jnp.maximum(my_row - 1, 0), jnp.minimum(my_row + 1, row_tiles - 1)
    left, right = jnp.maximum(my_lon - 1, 0), jnp.minimum(my_lon + 1, lons - 1)
    lanes8 = lane_iota(8)

    def known(condition, value):
        return jnp.where(jnp.where(condition, 1, 0) == 1, value, 0.0)

    def up(value):
        return pltpu.roll(value, 7, 0)

    def down(value):
        return pltpu.roll(value, 1, 0)

    half = height // 2
    for kind, (source, by_x, by_y) in enumerate(((keep_ref, keep_x, keep_y), (gain_ref, gain_x, gain_y))):
        for c in range(inner):
            cols = slice(c * LANES, (c + 1) * LANES)
            plain[c, halo : halo + height, :] = source[:, cols]
            plain[c, 0:halo, :] = top_ref[kind, :, cols]
            plain[c, halo + height : rows_all, :] = bottom_ref[kind, :, cols]
        segment = lane_iota(half) // SEG
        for part in range(2):
            piece = 2 * part + kind
            by_left = known(has_left, roll_lanes(strips_ref[left], end - piece * SEG))
            by_right = known(has_right, roll_lanes(strips_ref[right], -piece * SEG))
            both = jnp.where(segment == 0, by_right, jnp.where(segment == LANES // SEG - 1, by_left, 0.0))
            plain[inner, halo + part * half : halo + (part + 1) * half, :] = both
        segment = lane_iota(8) // SEG
        for has_row, row, at in ((has_top, above, 0), (has_bottom, below, halo + height)):
            by_left = known(has_row & has_left, parcel_ref[left * row_tiles + row, size + 8 * kind : size + 8 * kind + 8, :])
            by_right = known(has_row & has_right, parcel_ref[right * row_tiles + row, size + 8 * kind : size + 8 * kind + 8, :])
            for i in range(4):
                both = jnp.where(
                    segment == 0, roll_lanes(by_right, -i * SEG),
                    jnp.where(segment == LANES // SEG - 1, roll_lanes(by_left, end - i * SEG), 0.0),
                )
                plain[inner, at + 8 * i : at + 8 * i + 8, :] = both
        for q in range(blocks):
            values = [plain[c, pl.ds(q, 8, stride=blocks), :] for c in range(planes)]
            shifted = shift_from(values, 1, lanes8)
            to = (q - 1) % blocks * 8
            for c in range(planes):
                by_x[c, 8 * q : 8 * q + 8, :] = shifted[c]
                by_y[c, to : to + 8, :] = up(values[c]) if q == 0 else values[c]

    col_valid = jnp.where(lanes8 < LANES // 2, jnp.where(has_right, 1.0, 0.0), jnp.where(has_left, 1.0, 0.0))
    col_mask = jnp.where((lanes8 < halo) | (lanes8 >= end), col_valid, 0.0)
    sublane = lax.broadcasted_iota(jnp.int32, (8, LANES), 0)
    row_mask = {}
    for row, there in ((halo - 1, has_top), (halo + height, has_bottom)):
        row_mask[row % blocks] = jnp.where(sublane == row // blocks, jnp.where(there, 1.0, 0.0), 1.0)
    every = range(planes)

    fx[...] = jnp.zeros_like(fx)
    fy[...] = jnp.zeros_like(fy)
    a[:, 0:rows_all, :] = force_ref[steps - 1, :, 0:rows_all, :]

    def step(index, carry):
        level = jnp.where(index < steps - 1, steps - 2 - index, steps)
        near, ahead, new_y, total, behind = {}, {}, {}, {}, {}

        def rows(q):
            return slice(8 * q, 8 * q + 8)

        def first(q):
            near[q] = [a[c, rows(q % blocks), :] for c in every]
            if q < blocks:
                ahead[q] = [roll_lanes(value, -2) for value in near[q]]
            else:
                near[q] = [up(value) for value in near[q]]

        def second_y(q):
            new_y[q] = [
                keep_y[c, rows(q), :] * fy[c, rows(q), :] + gain_y[c, rows(q), :] * (near[q + 2][c] - near[q][c])
                for c in every
            ]
            for c in every:
                fy[c, rows(q), :] = new_y[q][c]

        def second_x(q):
            far = from_rolled(ahead[q], 2, lanes8)
            new_x = [
                keep_x[c, rows(q), :] * fx[c, rows(q), :] + gain_x[c, rows(q), :] * (far[c] - near[q][c]) for c in every
            ]
            behind[q] = [roll_lanes(value, 2) for value in new_x]
            before = new_y[q - 2] if q >= 2 else [down(fy[c, rows(q - 2 + blocks), :]) for c in every]
            push = [force_ref[level, c, rows(q), :] for c in every]
            total[q] = [(near[q][c] + push[c]) + (new_y[q][c] - before[c]) + new_x[c] for c in every]
            for c in every:
                fx[c, rows(q), :] = new_x[c]

        def third(q):
            far = from_rolled(behind[q], -2, lanes8)
            for c in every:
                value = total[q][c] - far[c]
                if c == inner:
                    value = value * col_mask
                if q in row_mask:
                    value = value * row_mask[q]
                a[c, rows(q), :] = value

        tasks = []
        for odd in range(2):
            tasks += [(odd, True, False)] + [(q, True, True) for q in range(odd + 2, blocks, 2)] + [(odd, False, True)]

        def begin(task):
            q, with_y, with_x = task
            if with_y and not with_x:
                first(q)
                first(q + 2)
            elif with_y:
                first(q + 2)
            else:
                first(q)
                new_y[q] = [fy[c, rows(q), :] for c in every]

        waiting = None
        begin(tasks[0])
        for task, following in zip(tasks, tasks[1:] + [None]):
            q, with_y, with_x = task
            if following is not None:
                begin(following)
            if with_y:
                second_y(q)
            if with_x:
                second_x(q)
            if waiting is not None:
                third(waiting)
            waiting = q if with_x else None
        third(waiting)
        return carry

    lax.fori_loop(0, steps, step, 0)

    for r in range(0, height, 8):
        s, q = divmod(halo + r, blocks)
        for c in range(inner):
            cols = slice(c * LANES, (c + 1) * LANES)
            value = a[c, pl.ds(8 * q + s, 8, stride=8), :]
            grad_ref[r : r + 8, cols] = jnp.where(keep_ref[r : r + 8, cols] > 0.0, value, 0.0)
    length = 2.0 * width
    kind = lax.broadcasted_iota(jnp.int32, (8, width), 0)
    column = lax.broadcasted_iota(jnp.int32, (8, width), 1)
    steps_off = jnp.where(kind == 0, column, width - 1 - column).astype(jnp.float32)
    weights = jnp.where(kind < 2, jnp.exp(-steps_off / length), 0.0)
    sums = lax.dot_general(
        weights, grad_ref[...], (((1,), (1,)), ((), ())), precision=lax.Precision.HIGHEST,
        preferred_element_type=jnp.float32,
    )
    for i in range(sums_ref.shape[0]):
        sums_ref[i] = sums


def smooth(grad_ref, out_ref):
    width = grad_ref.shape[1]
    length = 2.0 * width
    row = lax.broadcasted_iota(jnp.int32, (width, width), 0)
    column = lax.broadcasted_iota(jnp.int32, (width, width), 1)
    kernel = jnp.exp(-jnp.abs(row - column).astype(jnp.float32) / length)
    out_ref[...] = jnp.dot(
        grad_ref[...], kernel, precision=lax.Precision.HIGHEST, preferred_element_type=jnp.float32
    )


def finish(own_ref, sums_ref, out_ref):
    width = own_ref.shape[1]
    length = 2.0 * width
    count = sums_ref.shape[0]
    me = lax.axis_index("lon")
    row = lax.broadcasted_iota(jnp.int32, (count, width), 0)
    column = lax.broadcasted_iota(jnp.int32, (count, width), 1)
    strip, kind = row >> 3, row & 7
    left = (kind == 0) & (strip > me)
    right = (kind == 1) & (strip < me)
    away = jnp.where(left, (strip - me) * width - column, (me - strip - 1) * width + column + 1)
    weights = jnp.where(left | right, jnp.exp(-jnp.maximum(away, 0).astype(jnp.float32) / length), 0.0)
    out_ref[...] = own_ref[...] + lax.dot_general(
        sums_ref[...], weights, (((0,), (0,)), ((), ())), precision=lax.Precision.HIGHEST,
        preferred_element_type=jnp.float32,
    )


def f32(*shape):
    return jax.ShapeDtypeStruct(shape, jnp.float32)


def spaced(rows):
    return 8 * (rows // 8 | 1)


def vmem(count):
    return [pl.BlockSpec(memory_space=pltpu.VMEM)] * count


def local(depth, surface, friction, wet, coastal_tiles, gauge_route, gauge_cell, gauge_times, gauge_resid):
    height, width = depth.shape
    owned = gauge_route.shape[0]
    blocks = gauge_resid.shape[1]
    steps = blocks * STEPS_BLOCK
    halo = 2 * steps
    assert halo == SEG and height == LANES
    tiles = lax.axis_size(GRID_AXES)
    lons = lax.axis_size("lon")
    row_tiles = lax.axis_size(ROW_AXES)
    parcel_rows = gauge_rows(owned)[0] + 16
    params = pltpu.CompilerParams(vmem_limit_bytes=VMEM_LIMIT)

    keep = (1.0 - friction) * wet.astype(jnp.float32)
    gain = ((courant * 0.5) ** 2 * jnp.maximum(depth + surface, depth_floor)) * keep
    samples, coast_count = gauge_resid.shape[2], coastal_tiles.shape[0]
    assert coast_count <= owned

    assert samples >= 3

    def put(array, group, row):
        groups, rows, lanes = array.shape
        return jnp.pad(array, ((group, blocks + 1 - group - groups), (row, samples - row - rows), (0, owned - lanes)))

    gauges = (
        put(jnp.transpose(gauge_times, (1, 2, 0)), 0, 0)
        + put(gauge_route.reshape(1, 1, owned), blocks, 0)
        + put(gauge_cell.reshape(1, 1, owned), blocks, 1)
        + put(coastal_tiles.reshape(1, 1, coast_count), blocks, 2)
    )
    residuals = jnp.transpose(gauge_resid, (1, 2, 0))
    parcel, south, north, strips = pl.pallas_call(
        functools.partial(prepare, halo, blocks, samples, coast_count),
        out_shape=(
            f32(tiles, parcel_rows, LANES), f32(2, halo, width), f32(2, halo, width),
            f32(lons, height // 2, LANES),
        ),
        in_specs=vmem(4),
        out_specs=tuple(vmem(4)),
        scratch_shapes=[pltpu.VMEM((24, LANES), jnp.float32)],
        compiler_params=params,
        name="prepare",
    )(keep, gain, gauges, residuals)

    def exchange(array, axes):
        return lax.all_to_all(array, axes, split_axis=0, concat_axis=0, tiled=True)

    parcel = exchange(parcel, GRID_AXES)
    down = [(i, i + 1) for i in range(row_tiles - 1)]
    up = [(i + 1, i) for i in range(row_tiles - 1)]
    top = lax.ppermute(south, ROW_AXES, down)
    bottom = lax.ppermute(north, ROW_AXES, up)
    strips = exchange(strips, "lon")

    planes = width // LANES + 1
    rows_all = height + 2 * halo
    wide = max(2 * LANES, owned)
    pushes = pl.pallas_call(
        functools.partial(force, steps, halo, height, width),
        out_shape=f32(steps + 1, planes, spaced(rows_all), LANES),
        in_specs=vmem(1),
        out_specs=vmem(1)[0],
        scratch_shapes=[
            pltpu.VMEM((steps, wide), jnp.float32),
            pltpu.VMEM((rows_all, wide), jnp.bfloat16),
            pltpu.VMEM((2 * wide, planes * LANES), jnp.bfloat16),
        ],
        compiler_params=params,
        cost_estimate=pl.CostEstimate(
            flops=4 * steps * rows_all * wide * planes * LANES, bytes_accessed=4 * steps * planes * rows_all * LANES,
            transcendentals=0,
        ),
        name="force",
    )(parcel)

    plane = pltpu.VMEM((planes, spaced(rows_all), LANES), jnp.float32)
    grad, sums = pl.pallas_call(
        functools.partial(sweep, steps),
        out_shape=(f32(height, width), f32(lons, 8, height)),
        in_specs=vmem(7),
        out_specs=tuple(vmem(2)),
        scratch_shapes=[plane] * 8,
        compiler_params=params,
        name="sweep",
    )(keep, gain, top, bottom, strips, parcel, pushes)

    sums = exchange(sums, "lon")
    own = pl.pallas_call(
        smooth, out_shape=f32(height, width), in_specs=vmem(1), out_specs=vmem(1)[0], compiler_params=params,
        cost_estimate=pl.CostEstimate(
            flops=6 * 2 * height * width * width, bytes_accessed=2 * 4 * height * width, transcendentals=width * width
        ),
        name="smooth",
    )(grad)
    return pl.pallas_call(
        finish, out_shape=f32(height, width), in_specs=vmem(2), out_specs=vmem(1)[0], compiler_params=params, name="finish",
    )(own, sums.reshape(lons * 8, height))


def solution(mesh):
    in_specs = (
        P(("lat", "gau"), "lon"),
        P(("scen", "lat", "gau"), "lon"),
        P(("lat", "gau"), "lon"),
        P(("lat", "gau"), "lon"),
        P(),
        P(("scen", "lon", "lat", "gau"), None),
        P(("scen", "lon", "lat", "gau")),
        P(("scen", "lon", "lat", "gau"), None, None),
        P(("scen", "lon", "lat", "gau"), None, None),
    )
    out_specs = P(("scen", "lat", "gau"), "lon")
    return jax.shard_map(local, mesh=mesh, in_specs=in_specs, out_specs=out_specs, check_vma=False)
```

```python
import functools
import math

import jax
import jax.numpy as jnp
from jax import lax
from jax.experimental import pallas as pl
from jax.experimental.pallas import tpu as pltpu
from jax.sharding import PartitionSpec as P

STEPS_BLOCK = 8
LANES = 128
SEG = 32
LEVELS = 4

courant = 0.45
depth_floor = 0.1

GRID_AXES = ("lon", "lat", "gau")
ROW_AXES = ("lat", "gau")
VMEM_LIMIT = 16 * 1024 * 1024


def roll_lanes(x, shift):
    shift = shift % LANES
    return x if shift == 0 else pltpu.roll(x, shift, 1)


def lane_iota(rows):
    return lax.broadcasted_iota(jnp.int32, (rows, LANES), 1)


def gauge_rows(owned):
    if 3 * owned <= LANES:
        return STEPS_BLOCK, owned
    assert owned <= LANES
    return 3 * STEPS_BLOCK, 0


def my_place():
    row = lax.axis_index("lat") * lax.axis_size("gau") + lax.axis_index("gau")
    return row, lax.axis_index("lon"), lax.axis_size("lat") * lax.axis_size("gau"), lax.axis_size("lon")


def prepare(
    halo, blocks, samples, coast_count, keep_ref, gain_ref, gauge_ref,
    parcel_ref, south_ref, north_ref, west_ref, block_ref,
):
    height, width = keep_ref.shape
    my_row, my_lon, row_tiles, lons = my_place()
    keep, gain = keep_ref[...], gain_ref[...]
    owned = gauge_ref.shape[2]
    assert blocks == 2
    route, cell, coast = (gauge_ref[2 * blocks, i : i + 1, :].astype(jnp.int32) for i in range(3))
    target = jnp.zeros_like(route)
    for entry in range(coast_count):
        target = jnp.where(route == entry, jnp.broadcast_to(coast[:, entry : entry + 1], route.shape), target)
    row_bits, width_bits = int(math.log2(row_tiles)), int(math.log2(width))
    assert row_tiles == 1 << row_bits and width == 1 << width_bits
    grid_row = (target & (row_tiles - 1)) * height + (cell >> width_bits)
    grid_col = (target >> row_bits) * width + (cell & (width - 1))
    block_ref[...] = jnp.zeros_like(block_ref)
    levels = lax.broadcasted_iota(jnp.int32, (STEPS_BLOCK, owned), 0).astype(jnp.float32)
    for block in range(blocks):
        series = jnp.zeros((STEPS_BLOCK, owned), jnp.float32)
        for sample in range(samples):
            times = gauge_ref[block, sample : sample + 1, :]
            resid = gauge_ref[blocks + block, sample : sample + 1, :]
            series = series + jnp.where(times == levels, resid, 0.0)
        block_ref[block * STEPS_BLOCK : (block + 1) * STEPS_BLOCK, :owned] = series
    at = blocks * STEPS_BLOCK
    block_ref[at : at + 1, :owned] = grid_row.astype(jnp.float32)
    block_ref[at + 1 : at + 2, :owned] = grid_col.astype(jnp.float32)
    size, apart = gauge_rows(owned)
    gauges = block_ref[...]
    if size == STEPS_BLOCK:
        gauges = sum(
            roll_lanes(gauges[i * STEPS_BLOCK : (i + 1) * STEPS_BLOCK], i * apart) for i in range(3)
        )
    tiles = parcel_ref.shape[0]

    def put(tile, carry):
        parcel_ref[tile, 0:size, :] = gauges
        return carry

    lax.fori_loop(0, tiles, put, 0, unroll=tiles <= 16)

    reach = 2 * halo
    lower = lane_iota(height) < reach
    west = jnp.where(lower, keep[:, :LANES], roll_lanes(gain[:, :LANES], reach))
    west_ref[...] = west
    for d_row in (-1, 1):
        top = 0 if d_row < 0 else height - halo
        to_row, to_lon = my_row + d_row, my_lon - 1

        @pl.when((to_row >= 0) & (to_row < row_tiles) & (to_lon >= 0))
        def _():
            parcel_ref[to_lon * row_tiles + to_row, size : size + halo, :] = west[top : top + halo]

    south_ref[0], south_ref[1] = keep[height - halo :], gain[height - halo :]
    north_ref[0], north_ref[1] = keep[:halo], gain[:halo]


def from_rolled(rolled, shift, lanes):
    count = len(rolled)
    if shift > 0:
        return [jnp.where(lanes >= LANES - shift, rolled[(c + 1) % count], rolled[c]) for c in range(count)]
    return [jnp.where(lanes < -shift, rolled[(c - 1) % count], rolled[c]) for c in range(count)]


def shift_from(planes, shift, lanes):
    return from_rolled([roll_lanes(plane, -shift) for plane in planes], shift, lanes)


def force(steps, halo, height, width, parcel_ref, force_ref, series_ref, rows_hot, cols_hot):
    planes, rows_all = force_ref.shape[1], height + 2 * halo
    my_row, my_lon, row_tiles, lons = my_place()
    wide = rows_hot.shape[1]
    tiles, parcel_rows = parcel_ref.shape[:2]
    size = parcel_rows - halo
    apart = wide // tiles if size == STEPS_BLOCK else 0
    owned = apart if apart else LANES
    group = wide // owned
    groups = tiles // group
    per_plane = LANES // owned
    blocks = rows_all // 8
    row_shift = (halo - my_row * height).astype(jnp.float32)
    col_shift = (-my_lon * width).astype(jnp.float32)
    place = lax.broadcasted_iota(jnp.int32, (rows_all, LANES), 0)
    at = ((place & 7) * blocks + (place >> 3)).astype(jnp.float32)

    def gather_gauges(index):
        lanes = lane_iota(STEPS_BLOCK)
        for part in range(wide // LANES):
            cols = slice(part * LANES, (part + 1) * LANES)
            fields = []
            for field in range(3):
                total = jnp.zeros((STEPS_BLOCK, LANES), jnp.float32)
                rows = slice(0, 8) if apart else slice(8 * field, 8 * field + 8)
                for i in range(per_plane):
                    source = index * group + part * per_plane + i
                    block = roll_lanes(parcel_ref[source, rows, :], i * owned - field * apart)
                    total = jnp.where((lanes >= i * owned) & (lanes < (i + 1) * owned), block, total)
                fields.append(total)
            series_ref[0:8, cols] = fields[0]
            series_ref[8:16, cols] = fields[1]
            row = fields[2][0:1] + row_shift
            col = fields[2][1:2] + col_shift
            col = jnp.where(col < width + 2 * halo, col, -1.0)
            rows_hot[:, cols] = (at == row).astype(jnp.float32).astype(jnp.bfloat16)
            by_gauge = jnp.transpose(jnp.broadcast_to(col, (LANES, LANES)))
            for c in range(planes):
                spot = (lane_iota(LANES) + c * LANES).astype(jnp.float32)
                hot = (by_gauge == spot).astype(jnp.float32).astype(jnp.bfloat16)
                cols_hot[part * LANES : (part + 1) * LANES, c * LANES : (c + 1) * LANES] = hot
                cols_hot[wide + part * LANES : wide + (part + 1) * LANES, c * LANES : (c + 1) * LANES] = hot

    def levels_of(start, add):
        hot = rows_hot[...]
        both = []
        for level in range(LEVELS):
            value = series_ref[pl.ds(start + level, 1), :]
            high = value.astype(jnp.bfloat16)
            low = (value - high.astype(jnp.float32)).astype(jnp.bfloat16)
            both.append(jnp.concatenate([hot * high, hot * low], axis=1))
        both = jnp.concatenate(both, axis=0)
        for first in range(0, planes, 2):
            count = min(2, planes - first)
            total = jnp.dot(
                both, cols_hot[:, first * LANES : (first + count) * LANES], preferred_element_type=jnp.float32
            )
            for level in range(LEVELS):
                for c in range(count):
                    part = total[level * rows_all : (level + 1) * rows_all, c * LANES : (c + 1) * LANES]
                    goal = (start + level, first + c, slice(0, rows_all))
                    force_ref[goal] = force_ref[goal] + part if add else part

    def levels(add):
        def one(index, carry):
            levels_of(index * LEVELS, add)
            return carry

        lax.fori_loop(0, steps // LEVELS, one, 0)

    force_ref[steps] = jnp.zeros_like(force_ref[steps])
    gather_gauges(0)
    levels(False)
    if groups > 1:

        def more(index, carry):
            gather_gauges(index)
            levels(True)
            return carry

        lax.fori_loop(1, groups, more, 0)


def sweep(
    steps, keep_ref, gain_ref, top_ref, bottom_ref, right_ref, parcel_ref, force_ref,
    grad_ref, sums_ref,
    a, fx, fy, keep_x, gain_x, keep_y, gain_y, plain,
):
    height, width = keep_ref.shape
    halo = 2 * steps
    inner = width // LANES
    planes = inner + 1
    rows_all = height + 2 * halo
    blocks = rows_all // 8
    my_row, my_lon, row_tiles, lons = my_place()
    reach = 2 * halo
    size = parcel_ref.shape[1] - halo
    has_top, has_bottom = my_row > 0, my_row < row_tiles - 1
    has_right = my_lon < lons - 1
    above, below = jnp.maximum(my_row - 1, 0), jnp.minimum(my_row + 1, row_tiles - 1)
    right = jnp.minimum(my_lon + 1, lons - 1)
    lanes8 = lane_iota(8)

    def known(condition, value):
        return jnp.where(jnp.where(condition, 1, 0) == 1, value, 0.0)

    def up(value):
        return pltpu.roll(value, 7, 0)

    def down(value):
        return pltpu.roll(value, 1, 0)

    for kind, (source, by_x, by_y) in enumerate(((keep_ref, keep_x, keep_y), (gain_ref, gain_x, gain_y))):
        for c in range(inner):
            cols = slice(c * LANES, (c + 1) * LANES)
            plain[c, halo : halo + height, :] = source[:, cols]
            plain[c, 0:halo, :] = top_ref[kind, :, cols]
            plain[c, halo + height : rows_all, :] = bottom_ref[kind, :, cols]
        lower = lane_iota(height) < reach
        plain[inner, halo : halo + height, :] = jnp.where(lower, roll_lanes(right_ref[...], -reach * kind), 0.0)
        lower = lane_iota(halo) < reach
        for has_row, row, at in ((has_top, above, 0), (has_bottom, below, halo + height)):
            corner = roll_lanes(parcel_ref[right * row_tiles + row, size : size + halo, :], -reach * kind)
            plain[inner, at : at + halo, :] = known(has_row & has_right, jnp.where(lower, corner, 0.0))
        for q in range(blocks):
            values = [plain[c, pl.ds(q, 8, stride=blocks), :] for c in range(planes)]
            shifted = shift_from(values, 1, lanes8)
            to = (q - 1) % blocks * 8
            for c in range(planes):
                by_x[c, 8 * q : 8 * q + 8, :] = shifted[c]
                by_y[c, to : to + 8, :] = up(values[c]) if q == 0 else values[c]

    col_mask = jnp.where(lanes8 < reach, jnp.where(has_right, 1.0, 0.0), 0.0)
    sublane = lax.broadcasted_iota(jnp.int32, (8, LANES), 0)
    row_mask = {}
    for row, there in ((halo - 1, has_top), (halo + height, has_bottom)):
        row_mask[row % blocks] = jnp.where(sublane == row // blocks, jnp.where(there, 1.0, 0.0), 1.0)
    every = range(planes)

    fx[...] = jnp.zeros_like(fx)
    fy[...] = jnp.zeros_like(fy)
    a[:, 0:rows_all, :] = force_ref[steps - 1, :, 0:rows_all, :]

    def step(index, carry):
        level = jnp.where(index < steps - 1, steps - 2 - index, steps)
        near, ahead, new_y, total, behind, push = {}, {}, {}, {}, {}, {}

        def rows(q):
            return slice(8 * q, 8 * q + 8)

        def first(q):
            near[q] = [a[c, rows(q % blocks), :] for c in every]
            if q < blocks:
                ahead[q] = [roll_lanes(value, -2) for value in near[q]]
                push[q] = [force_ref[level, c, rows(q), :] for c in every]
            else:
                near[q] = [up(value) for value in near[q]]

        def second_y(q):
            new_y[q] = [
                keep_y[c, rows(q), :] * fy[c, rows(q), :] + gain_y[c, rows(q), :] * (near[q + 2][c] - near[q][c])
                for c in every
            ]
            for c in every:
                fy[c, rows(q), :] = new_y[q][c]

        def second_x(q):
            far = from_rolled(ahead[q], 2, lanes8)
            new_x = [
                keep_x[c, rows(q), :] * fx[c, rows(q), :] + gain_x[c, rows(q), :] * (far[c] - near[q][c]) for c in every
            ]
            behind[q] = [roll_lanes(value, 2) for value in new_x]
            before = new_y[q - 2] if q >= 2 else [down(fy[c, rows(q - 2 + blocks), :]) for c in every]
            total[q] = [(near[q][c] + push[q][c]) + (new_y[q][c] - before[c]) + new_x[c] for c in every]
            for c in every:
                fx[c, rows(q), :] = new_x[c]

        def third(q):
            far = from_rolled(behind[q], -2, lanes8)
            for c in every:
                value = total[q][c] - far[c]
                if c == inner:
                    value = value * col_mask
                if q in row_mask:
                    value = value * row_mask[q]
                a[c, rows(q), :] = value

        for q in range(4):
            first(q)
        second_y(0)
        second_y(1)
        for q in range(2, blocks):
            first(q + 2)
            second_y(q)
            second_x(q)
            if q > 2:
                third(q - 1)
        for q in range(2):
            first(q)
            new_y[q] = [fy[c, rows(q), :] for c in every]
        for q in range(2):
            second_x(q)
            third(q - 1 if q else blocks - 1)
        third(1)
        return carry

    lax.fori_loop(0, steps, step, 0)

    start = jnp.where(my_lon > 0, halo, 0)
    for r in range(0, height, 8):
        s, q = divmod(halo + r, blocks)
        for c in every:
            cols = slice(c * LANES, (c + 1) * LANES)
            value = a[c, pl.ds(8 * q + s, 8, stride=8), :]
            wet = keep_ref[r : r + 8, cols] if c < inner else right_ref[r : r + 8, :]
            if c == 0:
                wet = jnp.where(lanes8 >= start, wet, 0.0)
            if c == inner:
                wet = jnp.where(lanes8 < halo, wet, 0.0)
            grad_ref[r : r + 8, cols] = jnp.where(wet > 0.0, value, 0.0)
    length = 2.0 * width
    shape = (8 + halo, planes * LANES)
    kind, column = lax.broadcasted_iota(jnp.int32, shape, 0), lax.broadcasted_iota(jnp.int32, shape, 1)
    beyond = column - width
    off = jnp.where(kind == 0, column, jnp.where(kind == 1, -1 - beyond, jnp.where(kind == 2, beyond, width - 1 - beyond)))
    mine = ((kind < 2) & (beyond < 0)) | ((kind >= 2) & (kind < 4) & (beyond >= 0))
    weights = jnp.where(mine, jnp.exp(-jnp.maximum(off, 0).astype(jnp.float32) / length), 0.0)
    weights = jnp.where((kind >= 8) & (beyond == kind - 8), 1.0, weights)
    sums = lax.dot_general(
        weights, grad_ref[...], (((1,), (1,)), ((), ())), precision=lax.Precision.HIGHEST,
        preferred_element_type=jnp.float32,
    )
    for i in range(sums_ref.shape[0]):
        sums_ref[i] = sums


def smooth(halo, lons, grad_ref, out_ref, weights_ref):
    width = out_ref.shape[1]
    length = 2.0 * width
    row = lax.broadcasted_iota(jnp.int32, (width, width), 0)
    column = lax.broadcasted_iota(jnp.int32, (width, width), 1)
    kernel = jnp.exp(-jnp.abs(row - column).astype(jnp.float32) / length)
    out_ref[...] = jnp.dot(
        grad_ref[:, :width], kernel, precision=lax.Precision.HIGHEST, preferred_element_type=jnp.float32
    )
    me = lax.axis_index("lon")
    shape = (8 + halo, width)
    kind, column = lax.broadcasted_iota(jnp.int32, shape, 0), lax.broadcasted_iota(jnp.int32, shape, 1)
    for source in range(lons):
        strip = jnp.where(kind < 2, source, source + 1)
        left = ((kind == 0) | (kind == 2)) & (strip > me)
        right = ((kind == 1) | (kind == 3)) & (strip < me)
        near = (kind >= 8) & (source + 1 == me)
        away = jnp.where(left, (strip - me) * width - column, (me - strip - 1) * width + column + 1)
        away = jnp.where(near, jnp.abs(kind - 8 - column), away)
        weights = jnp.where(left | right | near, jnp.exp(-jnp.maximum(away, 0).astype(jnp.float32) / length), 0.0)
        weights_ref[source * shape[0] : (source + 1) * shape[0], :] = weights


def finish(own_ref, weights_ref, sums_ref, out_ref):
    out_ref[...] = own_ref[...] + lax.dot_general(
        sums_ref[...], weights_ref[...], (((0,), (0,)), ((), ())), precision=lax.Precision.HIGHEST,
        preferred_element_type=jnp.float32,
    )


def f32(*shape):
    return jax.ShapeDtypeStruct(shape, jnp.float32)


def spaced(rows):
    return 8 * (rows // 8 | 1)


def vmem(count):
    return [pl.BlockSpec(memory_space=pltpu.VMEM)] * count


def local(depth, surface, friction, wet, coastal_tiles, gauge_route, gauge_cell, gauge_times, gauge_resid):
    height, width = depth.shape
    owned = gauge_route.shape[0]
    blocks = gauge_resid.shape[1]
    steps = blocks * STEPS_BLOCK
    halo = 2 * steps
    assert halo == SEG and height == LANES
    tiles = lax.axis_size(GRID_AXES)
    lons = lax.axis_size("lon")
    row_tiles = lax.axis_size(ROW_AXES)
    parcel_rows = gauge_rows(owned)[0] + halo
    params = pltpu.CompilerParams(vmem_limit_bytes=VMEM_LIMIT)

    keep = (1.0 - friction) * wet.astype(jnp.float32)
    gain = ((courant * 0.5) ** 2 * jnp.maximum(depth + surface, depth_floor)) * keep
    samples, coast_count = gauge_resid.shape[2], coastal_tiles.shape[0]
    assert coast_count <= owned

    assert samples >= 3

    def put(array, group, row):
        groups, rows, lanes = array.shape
        return jnp.pad(array, ((group, 2 * blocks + 1 - group - groups), (row, samples - row - rows), (0, owned - lanes)))

    gauges = (
        put(jnp.transpose(gauge_times, (1, 2, 0)), 0, 0)
        + put(gauge_route.reshape(1, 1, owned), 2 * blocks, 0)
        + put(gauge_cell.reshape(1, 1, owned), 2 * blocks, 1)
        + put(coastal_tiles.reshape(1, 1, coast_count), 2 * blocks, 2)
    ).astype(jnp.float32) + put(jnp.transpose(gauge_resid, (1, 2, 0)), blocks, 0)
    parcel, south, north, west = pl.pallas_call(
        functools.partial(prepare, halo, blocks, samples, coast_count),
        out_shape=(
            f32(tiles, parcel_rows, LANES), f32(2, halo, width), f32(2, halo, width),
            f32(height, LANES),
        ),
        in_specs=vmem(3),
        out_specs=tuple(vmem(4)),
        scratch_shapes=[pltpu.VMEM((24, LANES), jnp.float32)],
        compiler_params=params,
        name="prepare",
    )(keep, gain, gauges)

    def exchange(array, axes):
        return lax.all_to_all(array, axes, split_axis=0, concat_axis=0, tiled=True)

    parcel = exchange(parcel, GRID_AXES)
    down = [(i, i + 1) for i in range(row_tiles - 1)]
    up = [(i + 1, i) for i in range(row_tiles - 1)]
    top = lax.ppermute(south, ROW_AXES, down)
    bottom = lax.ppermute(north, ROW_AXES, up)
    right = lax.ppermute(west, "lon", [(i + 1, i) for i in range(lons - 1)])

    planes = width // LANES + 1
    rows_all = height + 2 * halo
    wide = max(2 * LANES, owned)
    pushes = pl.pallas_call(
        functools.partial(force, steps, halo, height, width),
        out_shape=f32(steps + 1, planes, spaced(rows_all), LANES),
        in_specs=vmem(1),
        out_specs=vmem(1)[0],
        scratch_shapes=[
            pltpu.VMEM((steps, wide), jnp.float32),
            pltpu.VMEM((rows_all, wide), jnp.bfloat16),
            pltpu.VMEM((2 * wide, planes * LANES), jnp.bfloat16),
        ],
        compiler_params=params,
        cost_estimate=pl.CostEstimate(
            flops=4 * steps * rows_all * wide * planes * LANES, bytes_accessed=4 * steps * planes * rows_all * LANES,
            transcendentals=0,
        ),
        name="force",
    )(parcel)

    plane = pltpu.VMEM((planes, spaced(rows_all), LANES), jnp.float32)
    grad, sums = pl.pallas_call(
        functools.partial(sweep, steps),
        out_shape=(f32(height, planes * LANES), f32(lons, 8 + halo, height)),
        in_specs=vmem(7),
        out_specs=tuple(vmem(2)),
        scratch_shapes=[plane] * 8,
        compiler_params=params,
        name="sweep",
    )(keep, gain, top, bottom, right, parcel, pushes)

    sums = exchange(sums, "lon")
    own, weights = pl.pallas_call(
        functools.partial(smooth, halo, lons),
        out_shape=(f32(height, width), f32(lons * (8 + halo), width)),
        in_specs=vmem(1),
        out_specs=tuple(vmem(2)),
        compiler_params=params,
        cost_estimate=pl.CostEstimate(
            flops=6 * 2 * height * width * width, bytes_accessed=2 * 4 * height * width, transcendentals=width * width
        ),
        name="smooth",
    )(grad)
    return pl.pallas_call(
        finish, out_shape=f32(height, width), in_specs=vmem(3), out_specs=vmem(1)[0], compiler_params=params, name="finish",
    )(own, weights, sums.reshape(lons * (8 + halo), height))


def solution(mesh):
    in_specs = (
        P(("lat", "gau"), "lon"),
        P(("scen", "lat", "gau"), "lon"),
        P(("lat", "gau"), "lon"),
        P(("lat", "gau"), "lon"),
        P(),
        P(("scen", "lon", "lat", "gau"), None),
        P(("scen", "lon", "lat", "gau")),
        P(("scen", "lon", "lat", "gau"), None, None),
        P(("scen", "lon", "lat", "gau"), None, None),
    )
    out_specs = P(("scen", "lat", "gau"), "lon")
    return jax.shard_map(local, mesh=mesh, in_specs=in_specs, out_specs=out_specs, check_vma=False)
```

```python
import functools
import math

import jax
import jax.numpy as jnp
from jax import lax
from jax.experimental import pallas as pl
from jax.experimental.pallas import tpu as pltpu
from jax.sharding import PartitionSpec as P

STEPS_BLOCK = 8
LANES = 128
SEG = 32
LEVELS = 4

courant = 0.45
depth_floor = 0.1

GRID_AXES = ("lon", "lat", "gau")
ROW_AXES = ("lat", "gau")
VMEM_LIMIT = 16 * 1024 * 1024


def roll_lanes(x, shift):
    shift = shift % LANES
    return x if shift == 0 else pltpu.roll(x, shift, 1)


def lane_iota(rows):
    return lax.broadcasted_iota(jnp.int32, (rows, LANES), 1)


def gauge_rows(owned):
    if 3 * owned <= LANES:
        return STEPS_BLOCK, owned
    assert owned <= LANES
    return 3 * STEPS_BLOCK, 0


def my_place():
    row = lax.axis_index("lat") * lax.axis_size("gau") + lax.axis_index("gau")
    return row, lax.axis_index("lon"), lax.axis_size("lat") * lax.axis_size("gau"), lax.axis_size("lon")


def give_west(reach, keep_ref, gain_ref, west_ref):
    lower = lane_iota(west_ref.shape[0]) < reach
    west_ref[...] = jnp.where(lower, keep_ref[:, :LANES], roll_lanes(gain_ref[:, :LANES], reach))


def give_rows(halo, keep_ref, gain_ref, right_ref, south_ref, north_ref):
    height, width = keep_ref.shape
    lower = lane_iota(halo) < 2 * halo
    for goal, rows in ((south_ref, slice(height - halo, height)), (north_ref, slice(0, halo))):
        for kind, source in enumerate((keep_ref, gain_ref)):
            goal[kind, :, :width] = source[rows, :]
            goal[kind, :, width:] = jnp.where(lower, roll_lanes(right_ref[rows, :], -2 * halo * kind), 0.0)


def give_gauges(height, width, blocks, samples, coast_count, gauge_ref, after_ref, parcel_ref, block_ref):
    row_tiles = lax.axis_size("lat") * lax.axis_size("gau")
    owned = gauge_ref.shape[2]
    assert blocks == 2
    route, cell, coast = (gauge_ref[2 * blocks, i : i + 1, :].astype(jnp.int32) for i in range(3))
    target = jnp.zeros_like(route)
    for entry in range(coast_count):
        target = jnp.where(route == entry, jnp.broadcast_to(coast[:, entry : entry + 1], route.shape), target)
    row_bits, width_bits = int(math.log2(row_tiles)), int(math.log2(width))
    assert row_tiles == 1 << row_bits and width == 1 << width_bits
    grid_row = (target & (row_tiles - 1)) * height + (cell >> width_bits)
    grid_col = (target >> row_bits) * width + (cell & (width - 1))
    block_ref[...] = jnp.zeros_like(block_ref)
    levels = lax.broadcasted_iota(jnp.int32, (STEPS_BLOCK, owned), 0).astype(jnp.float32)
    for block in range(blocks):
        series = jnp.zeros((STEPS_BLOCK, owned), jnp.float32)
        for sample in range(samples):
            times = gauge_ref[block, sample : sample + 1, :]
            resid = gauge_ref[blocks + block, sample : sample + 1, :]
            series = series + jnp.where(times == levels, resid, 0.0)
        block_ref[block * STEPS_BLOCK : (block + 1) * STEPS_BLOCK, :owned] = series
    at = blocks * STEPS_BLOCK
    block_ref[at : at + 1, :owned] = grid_row.astype(jnp.float32)
    block_ref[at + 1 : at + 2, :owned] = grid_col.astype(jnp.float32)
    size, apart = gauge_rows(owned)
    gauges = block_ref[...]
    if size == STEPS_BLOCK:
        gauges = sum(
            roll_lanes(gauges[i * STEPS_BLOCK : (i + 1) * STEPS_BLOCK], i * apart) for i in range(3)
        )
    tiles = parcel_ref.shape[0]

    def put(tile, carry):
        parcel_ref[tile, 0:size, :] = gauges
        return carry

    lax.fori_loop(0, tiles, put, 0, unroll=tiles <= 16)


def from_rolled(rolled, shift, lanes):
    count = len(rolled)
    if shift > 0:
        return [jnp.where(lanes >= LANES - shift, rolled[(c + 1) % count], rolled[c]) for c in range(count)]
    return [jnp.where(lanes < -shift, rolled[(c - 1) % count], rolled[c]) for c in range(count)]


def shift_from(planes, shift, lanes):
    return from_rolled([roll_lanes(plane, -shift) for plane in planes], shift, lanes)


def force(steps, halo, height, width, parcel_ref, force_ref, series_ref, rows_hot, cols_hot):
    planes, rows_all = force_ref.shape[1], height + 2 * halo
    my_row, my_lon, row_tiles, lons = my_place()
    wide = rows_hot.shape[1]
    tiles, parcel_rows = parcel_ref.shape[:2]
    size = parcel_rows
    apart = wide // tiles if size == STEPS_BLOCK else 0
    owned = apart if apart else LANES
    group = wide // owned
    groups = tiles // group
    per_plane = LANES // owned
    blocks = rows_all // 8
    row_shift = (halo - my_row * height).astype(jnp.float32)
    col_shift = (-my_lon * width).astype(jnp.float32)
    place = lax.broadcasted_iota(jnp.int32, (rows_all, LANES), 0)
    at = ((place & 7) * blocks + (place >> 3)).astype(jnp.float32)

    def gather_gauges(index):
        lanes = lane_iota(STEPS_BLOCK)
        for part in range(wide // LANES):
            cols = slice(part * LANES, (part + 1) * LANES)
            fields = []
            for field in range(3):
                total = jnp.zeros((STEPS_BLOCK, LANES), jnp.float32)
                rows = slice(0, 8) if apart else slice(8 * field, 8 * field + 8)
                for i in range(per_plane):
                    source = index * group + part * per_plane + i
                    block = roll_lanes(parcel_ref[source, rows, :], i * owned - field * apart)
                    total = jnp.where((lanes >= i * owned) & (lanes < (i + 1) * owned), block, total)
                fields.append(total)
            series_ref[0:8, cols] = fields[0]
            series_ref[8:16, cols] = fields[1]
            row = fields[2][0:1] + row_shift
            col = fields[2][1:2] + col_shift
            col = jnp.where(col < width + 2 * halo, col, -1.0)
            rows_hot[:, cols] = (at == row).astype(jnp.float32).astype(jnp.bfloat16)
            by_gauge = jnp.transpose(jnp.broadcast_to(col, (LANES, LANES)))
            for c in range(planes):
                spot = (lane_iota(LANES) + c * LANES).astype(jnp.float32)
                hot = (by_gauge == spot).astype(jnp.float32).astype(jnp.bfloat16)
                cols_hot[part * LANES : (part + 1) * LANES, c * LANES : (c + 1) * LANES] = hot
                cols_hot[wide + part * LANES : wide + (part + 1) * LANES, c * LANES : (c + 1) * LANES] = hot

    def levels_of(start, add):
        hot = rows_hot[...]
        both = []
        for level in range(LEVELS):
            value = series_ref[pl.ds(start + level, 1), :]
            high = value.astype(jnp.bfloat16)
            low = (value - high.astype(jnp.float32)).astype(jnp.bfloat16)
            both.append(jnp.concatenate([hot * high, hot * low], axis=1))
        both = jnp.concatenate(both, axis=0)
        for first in range(0, planes, 2):
            count = min(2, planes - first)
            total = jnp.dot(
                both, cols_hot[:, first * LANES : (first + count) * LANES], preferred_element_type=jnp.float32
            )
            for level in range(LEVELS):
                for c in range(count):
                    part = total[level * rows_all : (level + 1) * rows_all, c * LANES : (c + 1) * LANES]
                    goal = (start + level, first + c, slice(0, rows_all))
                    force_ref[goal] = force_ref[goal] + part if add else part

    def levels(add):
        def one(index, carry):
            levels_of(index * LEVELS, add)
            return carry

        lax.fori_loop(0, steps // LEVELS, one, 0)

    force_ref[steps] = jnp.zeros_like(force_ref[steps])
    gather_gauges(0)
    levels(False)
    if groups > 1:

        def more(index, carry):
            gather_gauges(index)
            levels(True)
            return carry

        lax.fori_loop(1, groups, more, 0)


def sweep(
    steps, keep_ref, gain_ref, top_ref, bottom_ref, right_ref, force_ref,
    grad_ref, sums_ref,
    a, fx, fy, keep_x, gain_x, keep_y, gain_y, plain,
):
    height, width = keep_ref.shape
    halo = 2 * steps
    inner = width // LANES
    planes = inner + 1
    rows_all = height + 2 * halo
    blocks = rows_all // 8
    my_row, my_lon, row_tiles, lons = my_place()
    reach = 2 * halo
    has_top, has_bottom = my_row > 0, my_row < row_tiles - 1
    has_right = my_lon < lons - 1
    lanes8 = lane_iota(8)

    def up(value):
        return pltpu.roll(value, 7, 0)

    def down(value):
        return pltpu.roll(value, 1, 0)

    for kind, (source, by_x, by_y) in enumerate(((keep_ref, keep_x, keep_y), (gain_ref, gain_x, gain_y))):
        for c in range(planes):
            cols = slice(c * LANES, (c + 1) * LANES)
            plain[c, 0:halo, :] = top_ref[kind, :, cols]
            plain[c, halo + height : rows_all, :] = bottom_ref[kind, :, cols]
            if c < inner:
                plain[c, halo : halo + height, :] = source[:, cols]
        lower = lane_iota(height) < reach
        plain[inner, halo : halo + height, :] = jnp.where(lower, roll_lanes(right_ref[...], -reach * kind), 0.0)
        for q in range(blocks):
            values = [plain[c, pl.ds(q, 8, stride=blocks), :] for c in range(planes)]
            shifted = shift_from(values, 1, lanes8)
            to = (q - 1) % blocks * 8
            for c in range(planes):
                by_x[c, 8 * q : 8 * q + 8, :] = shifted[c]
                by_y[c, to : to + 8, :] = up(values[c]) if q == 0 else values[c]

    col_mask = jnp.where(lanes8 < reach, jnp.where(has_right, 1.0, 0.0), 0.0)
    sublane = lax.broadcasted_iota(jnp.int32, (8, LANES), 0)
    row_mask = {}
    for row, there in ((halo - 1, has_top), (halo + height, has_bottom)):
        row_mask[row % blocks] = jnp.where(sublane == row // blocks, jnp.where(there, 1.0, 0.0), 1.0)
    every = range(planes)

    fx[...] = jnp.zeros_like(fx)
    fy[...] = jnp.zeros_like(fy)
    a[:, 0:rows_all, :] = force_ref[steps - 1, :, 0:rows_all, :]

    def step(index, carry):
        level = jnp.where(index < steps - 1, steps - 2 - index, steps)
        near, ahead, new_y, total, behind, push = {}, {}, {}, {}, {}, {}

        def rows(q):
            return slice(8 * q, 8 * q + 8)

        def first(q):
            near[q] = [a[c, rows(q % blocks), :] for c in every]
            if q < blocks:
                ahead[q] = [roll_lanes(value, -2) for value in near[q]]
                push[q] = [force_ref[level, c, rows(q), :] for c in every]
            else:
                near[q] = [up(value) for value in near[q]]

        def second_y(q):
            new_y[q] = [
                keep_y[c, rows(q), :] * fy[c, rows(q), :] + gain_y[c, rows(q), :] * (near[q + 2][c] - near[q][c])
                for c in every
            ]
            for c in every:
                fy[c, rows(q), :] = new_y[q][c]

        def second_x(q):
            far = from_rolled(ahead[q], 2, lanes8)
            new_x = [
                keep_x[c, rows(q), :] * fx[c, rows(q), :] + gain_x[c, rows(q), :] * (far[c] - near[q][c]) for c in every
            ]
            behind[q] = [roll_lanes(value, 2) for value in new_x]
            before = new_y[q - 2] if q >= 2 else [down(fy[c, rows(q - 2 + blocks), :]) for c in every]
            total[q] = [(near[q][c] + push[q][c]) + (new_y[q][c] - before[c]) + new_x[c] for c in every]
            for c in every:
                fx[c, rows(q), :] = new_x[c]

        def third(q):
            far = from_rolled(behind[q], -2, lanes8)
            for c in every:
                value = total[q][c] - far[c]
                if c == inner:
                    value = value * col_mask
                if q in row_mask:
                    value = value * row_mask[q]
                a[c, rows(q), :] = value

        for q in range(4):
            first(q)
        second_y(0)
        second_y(1)
        for q in range(2, blocks):
            first(q + 2)
            second_y(q)
            second_x(q)
            if q > 2:
                third(q - 1)
        for q in range(2):
            first(q)
            new_y[q] = [fy[c, rows(q), :] for c in every]
        for q in range(2):
            second_x(q)
            third(q - 1 if q else blocks - 1)
        third(1)
        return carry

    lax.fori_loop(0, steps, step, 0)

    start = jnp.where(my_lon > 0, halo, 0)
    for r in range(0, height, 8):
        s, q = divmod(halo + r, blocks)
        for c in every:
            cols = slice(c * LANES, (c + 1) * LANES)
            value = a[c, pl.ds(8 * q + s, 8, stride=8), :]
            wet = keep_ref[r : r + 8, cols] if c < inner else right_ref[r : r + 8, :]
            if c == 0:
                wet = jnp.where(lanes8 >= start, wet, 0.0)
            if c == inner:
                wet = jnp.where(lanes8 < halo, wet, 0.0)
            grad_ref[r : r + 8, cols] = jnp.where(wet > 0.0, value, 0.0)
    length = 2.0 * width
    shape = (8 + halo, planes * LANES)
    kind, column = lax.broadcasted_iota(jnp.int32, shape, 0), lax.broadcasted_iota(jnp.int32, shape, 1)
    beyond = column - width
    off = jnp.where(kind == 0, column, jnp.where(kind == 1, -1 - beyond, jnp.where(kind == 2, beyond, width - 1 - beyond)))
    mine = ((kind < 2) & (beyond < 0)) | ((kind >= 2) & (kind < 4) & (beyond >= 0))
    weights = jnp.where(mine, jnp.exp(-jnp.maximum(off, 0).astype(jnp.float32) / length), 0.0)
    weights = jnp.where((kind >= 8) & (beyond == kind - 8), 1.0, weights)
    sums = lax.dot_general(
        weights, grad_ref[...], (((1,), (1,)), ((), ())), precision=lax.Precision.HIGHEST,
        preferred_element_type=jnp.float32,
    )
    for i in range(sums_ref.shape[0]):
        sums_ref[i] = sums


def smooth(halo, lons, grad_ref, out_ref, weights_ref):
    width = out_ref.shape[1]
    length = 2.0 * width
    row = lax.broadcasted_iota(jnp.int32, (width, width), 0)
    column = lax.broadcasted_iota(jnp.int32, (width, width), 1)
    kernel = jnp.exp(-jnp.abs(row - column).astype(jnp.float32) / length)
    out_ref[...] = jnp.dot(
        grad_ref[:, :width], kernel, precision=lax.Precision.HIGHEST, preferred_element_type=jnp.float32
    )
    me = lax.axis_index("lon")
    shape = (8 + halo, width)
    kind, column = lax.broadcasted_iota(jnp.int32, shape, 0), lax.broadcasted_iota(jnp.int32, shape, 1)
    for source in range(lons):
        strip = jnp.where(kind < 2, source, source + 1)
        left = ((kind == 0) | (kind == 2)) & (strip > me)
        right = ((kind == 1) | (kind == 3)) & (strip < me)
        near = (kind >= 8) & (source + 1 == me)
        away = jnp.where(left, (strip - me) * width - column, (me - strip - 1) * width + column + 1)
        away = jnp.where(near, jnp.abs(kind - 8 - column), away)
        weights = jnp.where(left | right | near, jnp.exp(-jnp.maximum(away, 0).astype(jnp.float32) / length), 0.0)
        weights_ref[source * shape[0] : (source + 1) * shape[0], :] = weights


def finish(own_ref, weights_ref, sums_ref, out_ref):
    out_ref[...] = own_ref[...] + lax.dot_general(
        sums_ref[...], weights_ref[...], (((0,), (0,)), ((), ())), precision=lax.Precision.HIGHEST,
        preferred_element_type=jnp.float32,
    )


def f32(*shape):
    return jax.ShapeDtypeStruct(shape, jnp.float32)


def spaced(rows):
    return 8 * (rows // 8 | 1)


def vmem(count):
    return [pl.BlockSpec(memory_space=pltpu.VMEM)] * count


def local(depth, surface, friction, wet, coastal_tiles, gauge_route, gauge_cell, gauge_times, gauge_resid):
    height, width = depth.shape
    owned = gauge_route.shape[0]
    blocks = gauge_resid.shape[1]
    steps = blocks * STEPS_BLOCK
    halo = 2 * steps
    assert halo == SEG and height == LANES
    tiles = lax.axis_size(GRID_AXES)
    lons = lax.axis_size("lon")
    row_tiles = lax.axis_size(ROW_AXES)
    planes = width // LANES + 1
    rows_all = height + 2 * halo
    params = pltpu.CompilerParams(vmem_limit_bytes=VMEM_LIMIT)

    keep = (1.0 - friction) * wet.astype(jnp.float32)
    gain = ((courant * 0.5) ** 2 * jnp.maximum(depth + surface, depth_floor)) * keep
    samples, coast_count = gauge_resid.shape[2], coastal_tiles.shape[0]
    assert coast_count <= owned

    assert samples >= 3

    def put(array, group, row):
        groups, rows, lanes = array.shape
        return jnp.pad(array, ((group, 2 * blocks + 1 - group - groups), (row, samples - row - rows), (0, owned - lanes)))

    gauges = (
        put(jnp.transpose(gauge_times, (1, 2, 0)), 0, 0)
        + put(gauge_route.reshape(1, 1, owned), 2 * blocks, 0)
        + put(gauge_cell.reshape(1, 1, owned), 2 * blocks, 1)
        + put(coastal_tiles.reshape(1, 1, coast_count), 2 * blocks, 2)
    ).astype(jnp.float32) + put(jnp.transpose(gauge_resid, (1, 2, 0)), blocks, 0)
    west = pl.pallas_call(
        functools.partial(give_west, 2 * halo), out_shape=f32(height, LANES), in_specs=vmem(2), out_specs=vmem(1)[0],
        compiler_params=params, name="give_west",
    )(keep, gain)
    right = lax.ppermute(west, "lon", [(i + 1, i) for i in range(lons - 1)])

    parcel = pl.pallas_call(
        functools.partial(give_gauges, height, width, blocks, samples, coast_count),
        out_shape=f32(tiles, gauge_rows(owned)[0], LANES),
        in_specs=vmem(1) + [pl.BlockSpec(memory_space=pl.ANY)],
        out_specs=vmem(1)[0],
        scratch_shapes=[pltpu.VMEM((24, LANES), jnp.float32)],
        compiler_params=params,
        name="give_gauges",
    )(gauges, west)

    def exchange(array, axes):
        return lax.all_to_all(array, axes, split_axis=0, concat_axis=0, tiled=True)

    parcel = exchange(parcel, GRID_AXES)

    south, north = pl.pallas_call(
        functools.partial(give_rows, halo), out_shape=(f32(2, halo, planes * LANES),) * 2, in_specs=vmem(3),
        out_specs=tuple(vmem(2)), compiler_params=params, name="give_rows",
    )(keep, gain, right)
    top = lax.ppermute(south, ROW_AXES, [(i, i + 1) for i in range(row_tiles - 1)])
    bottom = lax.ppermute(north, ROW_AXES, [(i + 1, i) for i in range(row_tiles - 1)])

    wide = max(2 * LANES, owned)
    pushes = pl.pallas_call(
        functools.partial(force, steps, halo, height, width),
        out_shape=f32(steps + 1, planes, spaced(rows_all), LANES),
        in_specs=vmem(1),
        out_specs=vmem(1)[0],
        scratch_shapes=[
            pltpu.VMEM((steps, wide), jnp.float32),
            pltpu.VMEM((rows_all, wide), jnp.bfloat16),
            pltpu.VMEM((2 * wide, planes * LANES), jnp.bfloat16),
        ],
        compiler_params=params,
        cost_estimate=pl.CostEstimate(
            flops=4 * steps * rows_all * wide * planes * LANES, bytes_accessed=4 * steps * planes * rows_all * LANES,
            transcendentals=0,
        ),
        name="force",
    )(parcel)

    plane = pltpu.VMEM((planes, spaced(rows_all), LANES), jnp.float32)
    grad, sums = pl.pallas_call(
        functools.partial(sweep, steps),
        out_shape=(f32(height, planes * LANES), f32(lons, 8 + halo, height)),
        in_specs=vmem(6),
        out_specs=tuple(vmem(2)),
        scratch_shapes=[plane] * 8,
        compiler_params=params,
        name="sweep",
    )(keep, gain, top, bottom, right, pushes)

    sums = exchange(sums, "lon")
    own, weights = pl.pallas_call(
        functools.partial(smooth, halo, lons),
        out_shape=(f32(height, width), f32(lons * (8 + halo), width)),
        in_specs=vmem(1),
        out_specs=tuple(vmem(2)),
        compiler_params=params,
        cost_estimate=pl.CostEstimate(
            flops=6 * 2 * height * width * width, bytes_accessed=2 * 4 * height * width, transcendentals=width * width
        ),
        name="smooth",
    )(grad)
    return pl.pallas_call(
        finish, out_shape=f32(height, width), in_specs=vmem(3), out_specs=vmem(1)[0], compiler_params=params, name="finish",
    )(own, weights, sums.reshape(lons * (8 + halo), height))


def solution(mesh):
    in_specs = (
        P(("lat", "gau"), "lon"),
        P(("scen", "lat", "gau"), "lon"),
        P(("lat", "gau"), "lon"),
        P(("lat", "gau"), "lon"),
        P(),
        P(("scen", "lon", "lat", "gau"), None),
        P(("scen", "lon", "lat", "gau")),
        P(("scen", "lon", "lat", "gau"), None, None),
        P(("scen", "lon", "lat", "gau"), None, None),
    )
    out_specs = P(("scen", "lat", "gau"), "lon")
    return jax.shard_map(local, mesh=mesh, in_specs=in_specs, out_specs=out_specs, check_vma=False)
```

```python
import functools
import math

import jax
import jax.numpy as jnp
from jax import lax
from jax.experimental import pallas as pl
from jax.experimental.pallas import tpu as pltpu
from jax.sharding import PartitionSpec as P

STEPS_BLOCK = 8
LANES = 128
SEG = 32
LEVELS = 4

courant = 0.45
depth_floor = 0.1

GRID_AXES = ("lon", "lat", "gau")
ROW_AXES = ("lat", "gau")
VMEM_LIMIT = 16 * 1024 * 1024


def roll_lanes(x, shift):
    shift = shift % LANES
    return x if shift == 0 else pltpu.roll(x, shift, 1)


def lane_iota(rows):
    return lax.broadcasted_iota(jnp.int32, (rows, LANES), 1)


def gauge_rows(owned):
    if 3 * owned <= LANES:
        return STEPS_BLOCK, owned
    assert owned <= LANES
    return 3 * STEPS_BLOCK, 0


def my_place():
    row = lax.axis_index("lat") * lax.axis_size("gau") + lax.axis_index("gau")
    return row, lax.axis_index("lon"), lax.axis_size("lat") * lax.axis_size("gau"), lax.axis_size("lon")


def give_west(reach, keep_ref, gain_ref, west_ref):
    lower = lane_iota(west_ref.shape[0]) < reach
    west_ref[...] = jnp.where(lower, keep_ref[:, :LANES], roll_lanes(gain_ref[:, :LANES], reach))


def give_rows(halo, keep_ref, gain_ref, right_ref, south_ref, north_ref):
    height, width = keep_ref.shape
    lower = lane_iota(halo) < 2 * halo
    for goal, rows in ((south_ref, slice(height - halo, height)), (north_ref, slice(0, halo))):
        for kind, source in enumerate((keep_ref, gain_ref)):
            goal[kind, :, :width] = source[rows, :]
            goal[kind, :, width:] = jnp.where(lower, roll_lanes(right_ref[rows, :], -2 * halo * kind), 0.0)


def give_gauges(height, width, blocks, samples, coast_count, gauge_ref, after_ref, parcel_ref, block_ref):
    row_tiles = lax.axis_size("lat") * lax.axis_size("gau")
    owned = gauge_ref.shape[2]
    assert blocks == 2
    route, cell, coast = (gauge_ref[2 * blocks, i : i + 1, :].astype(jnp.int32) for i in range(3))
    target = jnp.zeros_like(route)
    for entry in range(coast_count):
        target = jnp.where(route == entry, jnp.broadcast_to(coast[:, entry : entry + 1], route.shape), target)
    row_bits, width_bits = int(math.log2(row_tiles)), int(math.log2(width))
    assert row_tiles == 1 << row_bits and width == 1 << width_bits
    grid_row = (target & (row_tiles - 1)) * height + (cell >> width_bits)
    grid_col = (target >> row_bits) * width + (cell & (width - 1))
    block_ref[...] = jnp.zeros_like(block_ref)
    levels = lax.broadcasted_iota(jnp.int32, (STEPS_BLOCK, owned), 0).astype(jnp.float32)
    for block in range(blocks):
        series = jnp.zeros((STEPS_BLOCK, owned), jnp.float32)
        for sample in range(samples):
            times = gauge_ref[block, sample : sample + 1, :]
            resid = gauge_ref[blocks + block, sample : sample + 1, :]
            series = series + jnp.where(times == levels, resid, 0.0)
        block_ref[block * STEPS_BLOCK : (block + 1) * STEPS_BLOCK, :owned] = series
    at = blocks * STEPS_BLOCK
    block_ref[at : at + 1, :owned] = grid_row.astype(jnp.float32)
    block_ref[at + 1 : at + 2, :owned] = grid_col.astype(jnp.float32)
    size, apart = gauge_rows(owned)
    gauges = block_ref[...]
    if size == STEPS_BLOCK:
        gauges = sum(
            roll_lanes(gauges[i * STEPS_BLOCK : (i + 1) * STEPS_BLOCK], i * apart) for i in range(3)
        )
    tiles = parcel_ref.shape[0]

    def put(tile, carry):
        parcel_ref[tile, 0:size, :] = gauges
        return carry

    lax.fori_loop(0, tiles, put, 0, unroll=tiles <= 16)


def from_rolled(rolled, shift, lanes):
    count = len(rolled)
    if shift > 0:
        return [jnp.where(lanes >= LANES - shift, rolled[(c + 1) % count], rolled[c]) for c in range(count)]
    return [jnp.where(lanes < -shift, rolled[(c - 1) % count], rolled[c]) for c in range(count)]


def shift_from(planes, shift, lanes):
    return from_rolled([roll_lanes(plane, -shift) for plane in planes], shift, lanes)


def force(steps, halo, height, width, parcel_ref, force_ref, series_ref, rows_hot, cols_hot):
    planes, rows_all = force_ref.shape[1], height + 2 * halo
    my_row, my_lon, row_tiles, lons = my_place()
    wide = rows_hot.shape[1]
    tiles, parcel_rows = parcel_ref.shape[:2]
    size = parcel_rows
    apart = wide // tiles if size == STEPS_BLOCK else 0
    owned = apart if apart else LANES
    group = wide // owned
    groups = tiles // group
    per_plane = LANES // owned
    blocks = rows_all // 8
    row_shift = (halo - my_row * height).astype(jnp.float32)
    col_shift = (-my_lon * width).astype(jnp.float32)
    place = lax.broadcasted_iota(jnp.int32, (rows_all, LANES), 0)
    at = ((place & 7) * blocks + (place >> 3)).astype(jnp.float32)

    def gather_gauges(index):
        lanes = lane_iota(STEPS_BLOCK)
        for part in range(wide // LANES):
            cols = slice(part * LANES, (part + 1) * LANES)
            fields = []
            for field in range(3):
                total = jnp.zeros((STEPS_BLOCK, LANES), jnp.float32)
                rows = slice(0, 8) if apart else slice(8 * field, 8 * field + 8)
                for i in range(per_plane):
                    source = index * group + part * per_plane + i
                    block = roll_lanes(parcel_ref[source, rows, :], i * owned - field * apart)
                    total = jnp.where((lanes >= i * owned) & (lanes < (i + 1) * owned), block, total)
                fields.append(total)
            series_ref[0:8, cols] = fields[0]
            series_ref[8:16, cols] = fields[1]
            row = fields[2][0:1] + row_shift
            col = fields[2][1:2] + col_shift
            col = jnp.where(col < width + 2 * halo, col, -1.0)
            rows_hot[:, cols] = (at == row).astype(jnp.float32).astype(jnp.bfloat16)
            by_gauge = jnp.transpose(jnp.broadcast_to(col, (LANES, LANES)))
            for c in range(planes):
                spot = (lane_iota(LANES) + c * LANES).astype(jnp.float32)
                hot = (by_gauge == spot).astype(jnp.float32).astype(jnp.bfloat16)
                cols_hot[part * LANES : (part + 1) * LANES, c * LANES : (c + 1) * LANES] = hot
                cols_hot[wide + part * LANES : wide + (part + 1) * LANES, c * LANES : (c + 1) * LANES] = hot

    def levels_of(start, add):
        hot = rows_hot[...]
        both = []
        for level in range(LEVELS):
            value = series_ref[pl.ds(start + level, 1), :]
            high = value.astype(jnp.bfloat16)
            low = (value - high.astype(jnp.float32)).astype(jnp.bfloat16)
            both.append(jnp.concatenate([hot * high, hot * low], axis=1))
        both = jnp.concatenate(both, axis=0)
        for first in range(0, planes, 2):
            count = min(2, planes - first)
            total = jnp.dot(
                both, cols_hot[:, first * LANES : (first + count) * LANES], preferred_element_type=jnp.float32
            )
            for level in range(LEVELS):
                for c in range(count):
                    part = total[level * rows_all : (level + 1) * rows_all, c * LANES : (c + 1) * LANES]
                    goal = (start + level, first + c, slice(0, rows_all))
                    force_ref[goal] = force_ref[goal] + part if add else part

    def levels(add):
        def one(index, carry):
            levels_of(index * LEVELS, add)
            return carry

        lax.fori_loop(0, steps // LEVELS, one, 0)

    force_ref[steps] = jnp.zeros_like(force_ref[steps])
    gather_gauges(0)
    levels(False)
    if groups > 1:

        def more(index, carry):
            gather_gauges(index)
            levels(True)
            return carry

        lax.fori_loop(1, groups, more, 0)


def sweep(
    steps, keep_ref, gain_ref, top_ref, bottom_ref, right_ref, force_ref,
    grad_ref, sums_ref,
    a, fx, fy, keep_x, gain_x, keep_y, gain_y, plain,
):
    height, width = keep_ref.shape
    halo = 2 * steps
    inner = width // LANES
    planes = inner + 1
    rows_all = height + 2 * halo
    blocks = rows_all // 8
    my_row, my_lon, row_tiles, lons = my_place()
    reach = 2 * halo
    has_top, has_bottom = my_row > 0, my_row < row_tiles - 1
    has_right = my_lon < lons - 1
    lanes8 = lane_iota(8)

    def up(value):
        return pltpu.roll(value, 7, 0)

    def down(value):
        return pltpu.roll(value, 1, 0)

    for kind, (source, by_x, by_y) in enumerate(((keep_ref, keep_x, keep_y), (gain_ref, gain_x, gain_y))):
        for c in range(planes):
            cols = slice(c * LANES, (c + 1) * LANES)
            plain[c, 0:halo, :] = top_ref[kind, :, cols]
            plain[c, halo + height : rows_all, :] = bottom_ref[kind, :, cols]
            if c < inner:
                plain[c, halo : halo + height, :] = source[:, cols]
        lower = lane_iota(height) < reach
        plain[inner, halo : halo + height, :] = jnp.where(lower, roll_lanes(right_ref[...], -reach * kind), 0.0)
        for q in range(blocks):
            values = [plain[c, pl.ds(q, 8, stride=blocks), :] for c in range(planes)]
            shifted = shift_from(values, 1, lanes8)
            to = (q - 1) % blocks * 8
            for c in range(planes):
                by_x[c, 8 * q : 8 * q + 8, :] = shifted[c]
                by_y[c, to : to + 8, :] = up(values[c]) if q == 0 else values[c]

    col_mask = jnp.where(lanes8 < reach, jnp.where(has_right, 1.0, 0.0), 0.0)
    sublane = lax.broadcasted_iota(jnp.int32, (8, LANES), 0)
    row_mask = {}
    for row, there in ((halo - 1, has_top), (halo + height, has_bottom)):
        row_mask[row % blocks] = jnp.where(sublane == row // blocks, jnp.where(there, 1.0, 0.0), 1.0)
    every = range(planes)

    fx[...] = jnp.zeros_like(fx)
    fy[...] = jnp.zeros_like(fy)
    a[:, 0:rows_all, :] = force_ref[steps - 1, :, 0:rows_all, :]

    def step(index, carry):
        level = jnp.where(index < steps - 1, steps - 2 - index, steps)
        near, ahead, new_y, total, behind, push = {}, {}, {}, {}, {}, {}

        def rows(q):
            return slice(8 * q, 8 * q + 8)

        def first(q):
            near[q] = [a[c, rows(q % blocks), :] for c in every]
            if q < blocks:
                ahead[q] = [roll_lanes(value, -2) for value in near[q]]
                push[q] = [force_ref[level, c, rows(q), :] for c in every]
            else:
                near[q] = [up(value) for value in near[q]]

        def second_y(q):
            new_y[q] = [
                keep_y[c, rows(q), :] * fy[c, rows(q), :] + gain_y[c, rows(q), :] * (near[q + 2][c] - near[q][c])
                for c in every
            ]
            for c in every:
                fy[c, rows(q), :] = new_y[q][c]

        def second_x(q):
            far = from_rolled(ahead[q], 2, lanes8)
            new_x = [
                keep_x[c, rows(q), :] * fx[c, rows(q), :] + gain_x[c, rows(q), :] * (far[c] - near[q][c]) for c in every
            ]
            behind[q] = [roll_lanes(value, 2) for value in new_x]
            before = new_y[q - 2] if q >= 2 else [down(fy[c, rows(q - 2 + blocks), :]) for c in every]
            total[q] = [(near[q][c] + push[q][c]) + (new_y[q][c] - before[c]) + new_x[c] for c in every]
            for c in every:
                fx[c, rows(q), :] = new_x[c]

        def third(q):
            far = from_rolled(behind[q], -2, lanes8)
            for c in every:
                value = total[q][c] - far[c]
                if c == inner:
                    value = value * col_mask
                if q in row_mask:
                    value = value * row_mask[q]
                a[c, rows(q), :] = value

        for q in range(4):
            first(q)
        second_y(0)
        second_y(1)
        for q in range(2, blocks):
            first(q + 2)
            second_y(q)
            second_x(q)
            if q > 2:
                third(q - 1)
        for q in range(2):
            first(q)
            new_y[q] = [fy[c, rows(q), :] for c in every]
        for q in range(2):
            second_x(q)
            third(q - 1 if q else blocks - 1)
        third(1)
        return carry

    lax.fori_loop(0, steps, step, 0)

    start = jnp.where(my_lon > 0, halo, 0)
    for r in range(0, height, 8):
        s, q = divmod(halo + r, blocks)
        for c in every:
            cols = slice(c * LANES, (c + 1) * LANES)
            value = a[c, pl.ds(8 * q + s, 8, stride=8), :]
            wet = keep_ref[r : r + 8, cols] if c < inner else right_ref[r : r + 8, :]
            if c == 0:
                wet = jnp.where(lanes8 >= start, wet, 0.0)
            if c == inner:
                wet = jnp.where(lanes8 < halo, wet, 0.0)
            grad_ref[r : r + 8, cols] = jnp.where(wet > 0.0, value, 0.0)
    length = 2.0 * width
    shape = (8 + halo, planes * LANES)
    kind, column = lax.broadcasted_iota(jnp.int32, shape, 0), lax.broadcasted_iota(jnp.int32, shape, 1)
    beyond = column - width
    off = jnp.where(kind == 0, column, jnp.where(kind == 1, -1 - beyond, jnp.where(kind == 2, beyond, width - 1 - beyond)))
    mine = ((kind < 2) & (beyond < 0)) | ((kind >= 2) & (kind < 4) & (beyond >= 0))
    weights = jnp.where(mine, jnp.exp(-jnp.maximum(off, 0).astype(jnp.float32) / length), 0.0)
    weights = jnp.where((kind >= 8) & (beyond == kind - 8), 1.0, weights)
    sums = lax.dot_general(
        weights, grad_ref[...], (((1,), (1,)), ((), ())), precision=lax.Precision.HIGHEST,
        preferred_element_type=jnp.float32,
    )
    for i in range(sums_ref.shape[0]):
        sums_ref[i] = sums


def smooth(halo, lons, grad_ref, out_ref, weights_ref):
    width = out_ref.shape[1]
    length = 2.0 * width
    row = lax.broadcasted_iota(jnp.int32, (width, width), 0)
    column = lax.broadcasted_iota(jnp.int32, (width, width), 1)
    kernel = jnp.exp(-jnp.abs(row - column).astype(jnp.float32) / length)
    out_ref[...] = jnp.dot(
        grad_ref[:, :width], kernel, precision=lax.Precision.HIGHEST, preferred_element_type=jnp.float32
    )
    me = lax.axis_index("lon")
    shape = (8 + halo, width)
    kind, column = lax.broadcasted_iota(jnp.int32, shape, 0), lax.broadcasted_iota(jnp.int32, shape, 1)
    for source in range(lons):
        strip = jnp.where(kind < 2, source, source + 1)
        left = ((kind == 0) | (kind == 2)) & (strip > me)
        right = ((kind == 1) | (kind == 3)) & (strip < me)
        near = (kind >= 8) & (source + 1 == me)
        away = jnp.where(left, (strip - me) * width - column, (me - strip - 1) * width + column + 1)
        away = jnp.where(near, jnp.abs(kind - 8 - column), away)
        weights = jnp.where(left | right | near, jnp.exp(-jnp.maximum(away, 0).astype(jnp.float32) / length), 0.0)
        weights_ref[source * shape[0] : (source + 1) * shape[0], :] = weights


def finish(own_ref, weights_ref, sums_ref, out_ref):
    out_ref[...] = own_ref[...] + lax.dot_general(
        sums_ref[...], weights_ref[...], (((0,), (0,)), ((), ())), precision=lax.Precision.HIGHEST,
        preferred_element_type=jnp.float32,
    )


def f32(*shape):
    return jax.ShapeDtypeStruct(shape, jnp.float32)


def hint(megabytes):
    return pl.CostEstimate(flops=0, bytes_accessed=megabytes * 1000 * 1000, transcendentals=0)


def spaced(rows):
    return 8 * (rows // 8 | 1)


def vmem(count):
    return [pl.BlockSpec(memory_space=pltpu.VMEM)] * count


def local(depth, surface, friction, wet, coastal_tiles, gauge_route, gauge_cell, gauge_times, gauge_resid):
    height, width = depth.shape
    owned = gauge_route.shape[0]
    blocks = gauge_resid.shape[1]
    steps = blocks * STEPS_BLOCK
    halo = 2 * steps
    assert halo == SEG and height == LANES
    tiles = lax.axis_size(GRID_AXES)
    lons = lax.axis_size("lon")
    row_tiles = lax.axis_size(ROW_AXES)
    planes = width // LANES + 1
    rows_all = height + 2 * halo
    params = pltpu.CompilerParams(vmem_limit_bytes=VMEM_LIMIT)

    keep = (1.0 - friction) * wet.astype(jnp.float32)
    gain = ((courant * 0.5) ** 2 * jnp.maximum(depth + surface, depth_floor)) * keep
    samples, coast_count = gauge_resid.shape[2], coastal_tiles.shape[0]
    assert coast_count <= owned

    assert samples >= 3

    def put(array, group, row):
        groups, rows, lanes = array.shape
        return jnp.pad(array, ((group, 2 * blocks + 1 - group - groups), (row, samples - row - rows), (0, owned - lanes)))

    gauges = (
        put(jnp.transpose(gauge_times, (1, 2, 0)), 0, 0)
        + put(gauge_route.reshape(1, 1, owned), 2 * blocks, 0)
        + put(gauge_cell.reshape(1, 1, owned), 2 * blocks, 1)
        + put(coastal_tiles.reshape(1, 1, coast_count), 2 * blocks, 2)
    ).astype(jnp.float32) + put(jnp.transpose(gauge_resid, (1, 2, 0)), blocks, 0)
    west = pl.pallas_call(
        functools.partial(give_west, 2 * halo), out_shape=f32(height, LANES), in_specs=vmem(2), out_specs=vmem(1)[0],
        compiler_params=params, name="give_west",
    )(keep, gain)
    right = lax.ppermute(west, "lon", [(i + 1, i) for i in range(lons - 1)])

    parcel = pl.pallas_call(
        functools.partial(give_gauges, height, width, blocks, samples, coast_count),
        out_shape=f32(tiles, gauge_rows(owned)[0], LANES),
        in_specs=vmem(1) + [pl.BlockSpec(memory_space=pl.ANY)],
        out_specs=vmem(1)[0],
        scratch_shapes=[pltpu.VMEM((24, LANES), jnp.float32)],
        compiler_params=params,
        cost_estimate=hint(10),
        name="give_gauges",
    )(gauges, west)

    def exchange(array, axes):
        return lax.all_to_all(array, axes, split_axis=0, concat_axis=0, tiled=True)

    parcel = exchange(parcel, GRID_AXES)

    south, north = pl.pallas_call(
        functools.partial(give_rows, halo), out_shape=(f32(2, halo, planes * LANES),) * 2, in_specs=vmem(3),
        out_specs=tuple(vmem(2)), compiler_params=params, cost_estimate=hint(40), name="give_rows",
    )(keep, gain, right)
    top = lax.ppermute(south, ROW_AXES, [(i, i + 1) for i in range(row_tiles - 1)])
    bottom = lax.ppermute(north, ROW_AXES, [(i + 1, i) for i in range(row_tiles - 1)])

    wide = max(2 * LANES, owned)
    pushes = pl.pallas_call(
        functools.partial(force, steps, halo, height, width),
        out_shape=f32(steps + 1, planes, spaced(rows_all), LANES),
        in_specs=vmem(1),
        out_specs=vmem(1)[0],
        scratch_shapes=[
            pltpu.VMEM((steps, wide), jnp.float32),
            pltpu.VMEM((rows_all, wide), jnp.bfloat16),
            pltpu.VMEM((2 * wide, planes * LANES), jnp.bfloat16),
        ],
        compiler_params=params,
        cost_estimate=pl.CostEstimate(
            flops=4 * steps * rows_all * wide * planes * LANES, bytes_accessed=4 * steps * planes * rows_all * LANES,
            transcendentals=0,
        ),
        name="force",
    )(parcel)

    plane = pltpu.VMEM((planes, spaced(rows_all), LANES), jnp.float32)
    grad, sums = pl.pallas_call(
        functools.partial(sweep, steps),
        out_shape=(f32(height, planes * LANES), f32(lons, 8 + halo, height)),
        in_specs=vmem(6),
        out_specs=tuple(vmem(2)),
        scratch_shapes=[plane] * 8,
        compiler_params=params,
        name="sweep",
    )(keep, gain, top, bottom, right, pushes)

    sums = exchange(sums, "lon")
    own, weights = pl.pallas_call(
        functools.partial(smooth, halo, lons),
        out_shape=(f32(height, width), f32(lons * (8 + halo), width)),
        in_specs=vmem(1),
        out_specs=tuple(vmem(2)),
        compiler_params=params,
        cost_estimate=pl.CostEstimate(
            flops=6 * 2 * height * width * width, bytes_accessed=2 * 4 * height * width, transcendentals=width * width
        ),
        name="smooth",
    )(grad)
    return pl.pallas_call(
        finish, out_shape=f32(height, width), in_specs=vmem(3), out_specs=vmem(1)[0], compiler_params=params, name="finish",
    )(own, weights, sums.reshape(lons * (8 + halo), height))


def solution(mesh):
    in_specs = (
        P(("lat", "gau"), "lon"),
        P(("scen", "lat", "gau"), "lon"),
        P(("lat", "gau"), "lon"),
        P(("lat", "gau"), "lon"),
        P(),
        P(("scen", "lon", "lat", "gau"), None),
        P(("scen", "lon", "lat", "gau")),
        P(("scen", "lon", "lat", "gau"), None, None),
        P(("scen", "lon", "lat", "gau"), None, None),
    )
    out_specs = P(("scen", "lat", "gau"), "lon")
    return jax.shard_map(local, mesh=mesh, in_specs=in_specs, out_specs=out_specs, check_vma=False)
```

```python
import functools
import math

import jax
import jax.numpy as jnp
from jax import lax
from jax.experimental import pallas as pl
from jax.experimental.pallas import tpu as pltpu
from jax.sharding import PartitionSpec as P

STEPS_BLOCK = 8
LANES = 128
SEG = 32
LEVELS = 4

courant = 0.45
depth_floor = 0.1

GRID_AXES = ("lon", "lat", "gau")
ROW_AXES = ("lat", "gau")
VMEM_LIMIT = 16 * 1024 * 1024


def roll_lanes(x, shift):
    shift = shift % LANES
    return x if shift == 0 else pltpu.roll(x, shift, 1)


def lane_iota(rows):
    return lax.broadcasted_iota(jnp.int32, (rows, LANES), 1)


def gauge_rows(owned):
    if 3 * owned <= LANES:
        return STEPS_BLOCK, owned
    assert owned <= LANES
    return 3 * STEPS_BLOCK, 0


def my_place():
    row = lax.axis_index("lat") * lax.axis_size("gau") + lax.axis_index("gau")
    return row, lax.axis_index("lon"), lax.axis_size("lat") * lax.axis_size("gau"), lax.axis_size("lon")


def give_west(reach, keep_ref, gain_ref, west_ref):
    lower = lane_iota(west_ref.shape[1]) < reach
    west_ref[0] = jnp.where(lower, keep_ref[:, :LANES], roll_lanes(gain_ref[:, :LANES], reach))
    for spare in range(1, west_ref.shape[0]):
        west_ref[spare] = jnp.zeros(west_ref.shape[1:], jnp.float32)


def give_rows(halo, keep_ref, gain_ref, right_ref, south_ref, north_ref):
    height, width = keep_ref.shape
    lower = lane_iota(halo) < 2 * halo
    for goal, rows in ((south_ref, slice(height - halo, height)), (north_ref, slice(0, halo))):
        for kind, source in enumerate((keep_ref, gain_ref)):
            goal[kind, :, :width] = source[rows, :]
            goal[kind, :, width:] = jnp.where(lower, roll_lanes(right_ref[0, rows, :], -2 * halo * kind), 0.0)


def give_gauges(height, width, blocks, samples, coast_count, gauge_ref, after_ref, parcel_ref, block_ref):
    row_tiles = lax.axis_size("lat") * lax.axis_size("gau")
    owned = gauge_ref.shape[2]
    assert blocks == 2
    route, cell, coast = (gauge_ref[2 * blocks, i : i + 1, :].astype(jnp.int32) for i in range(3))
    target = jnp.zeros_like(route)
    for entry in range(coast_count):
        target = jnp.where(route == entry, jnp.broadcast_to(coast[:, entry : entry + 1], route.shape), target)
    row_bits, width_bits = int(math.log2(row_tiles)), int(math.log2(width))
    assert row_tiles == 1 << row_bits and width == 1 << width_bits
    grid_row = (target & (row_tiles - 1)) * height + (cell >> width_bits)
    grid_col = (target >> row_bits) * width + (cell & (width - 1))
    block_ref[...] = jnp.zeros_like(block_ref)
    levels = lax.broadcasted_iota(jnp.int32, (STEPS_BLOCK, owned), 0).astype(jnp.float32)
    for block in range(blocks):
        series = jnp.zeros((STEPS_BLOCK, owned), jnp.float32)
        for sample in range(samples):
            times = gauge_ref[block, sample : sample + 1, :]
            resid = gauge_ref[blocks + block, sample : sample + 1, :]
            series = series + jnp.where(times == levels, resid, 0.0)
        block_ref[block * STEPS_BLOCK : (block + 1) * STEPS_BLOCK, :owned] = series
    at = blocks * STEPS_BLOCK
    block_ref[at : at + 1, :owned] = grid_row.astype(jnp.float32)
    block_ref[at + 1 : at + 2, :owned] = grid_col.astype(jnp.float32)
    size, apart = gauge_rows(owned)
    gauges = block_ref[...]
    if size == STEPS_BLOCK:
        gauges = sum(
            roll_lanes(gauges[i * STEPS_BLOCK : (i + 1) * STEPS_BLOCK], i * apart) for i in range(3)
        )
    tiles = parcel_ref.shape[0]

    def put(tile, carry):
        parcel_ref[tile, 0:size, :] = gauges
        return carry

    lax.fori_loop(0, tiles, put, 0, unroll=tiles <= 16)


def from_rolled(rolled, shift, lanes):
    count = len(rolled)
    if shift > 0:
        return [jnp.where(lanes >= LANES - shift, rolled[(c + 1) % count], rolled[c]) for c in range(count)]
    return [jnp.where(lanes < -shift, rolled[(c - 1) % count], rolled[c]) for c in range(count)]


def shift_from(planes, shift, lanes):
    return from_rolled([roll_lanes(plane, -shift) for plane in planes], shift, lanes)


def force(steps, halo, height, width, parcel_ref, force_ref, series_ref, rows_hot, cols_hot):
    planes, rows_all = force_ref.shape[1], height + 2 * halo
    my_row, my_lon, row_tiles, lons = my_place()
    wide = rows_hot.shape[1]
    tiles, parcel_rows = parcel_ref.shape[:2]
    size = parcel_rows
    apart = wide // tiles if size == STEPS_BLOCK else 0
    owned = apart if apart else LANES
    group = wide // owned
    groups = tiles // group
    per_plane = LANES // owned
    blocks = rows_all // 8
    row_shift = (halo - my_row * height).astype(jnp.float32)
    col_shift = (-my_lon * width).astype(jnp.float32)
    place = lax.broadcasted_iota(jnp.int32, (rows_all, LANES), 0)
    at = ((place & 7) * blocks + (place >> 3)).astype(jnp.float32)

    def gather_gauges(index):
        lanes = lane_iota(STEPS_BLOCK)
        for part in range(wide // LANES):
            cols = slice(part * LANES, (part + 1) * LANES)
            fields = []
            for field in range(3):
                total = jnp.zeros((STEPS_BLOCK, LANES), jnp.float32)
                rows = slice(0, 8) if apart else slice(8 * field, 8 * field + 8)
                for i in range(per_plane):
                    source = index * group + part * per_plane + i
                    block = roll_lanes(parcel_ref[source, rows, :], i * owned - field * apart)
                    total = jnp.where((lanes >= i * owned) & (lanes < (i + 1) * owned), block, total)
                fields.append(total)
            series_ref[0:8, cols] = fields[0]
            series_ref[8:16, cols] = fields[1]
            row = fields[2][0:1] + row_shift
            col = fields[2][1:2] + col_shift
            col = jnp.where(col < width + 2 * halo, col, -1.0)
            rows_hot[:, cols] = (at == row).astype(jnp.float32).astype(jnp.bfloat16)
            by_gauge = jnp.transpose(jnp.broadcast_to(col, (LANES, LANES)))
            for c in range(planes):
                spot = (lane_iota(LANES) + c * LANES).astype(jnp.float32)
                hot = (by_gauge == spot).astype(jnp.float32).astype(jnp.bfloat16)
                cols_hot[part * LANES : (part + 1) * LANES, c * LANES : (c + 1) * LANES] = hot
                cols_hot[wide + part * LANES : wide + (part + 1) * LANES, c * LANES : (c + 1) * LANES] = hot

    def levels_of(start, add):
        hot = rows_hot[...]
        both = []
        for level in range(LEVELS):
            value = series_ref[pl.ds(start + level, 1), :]
            high = value.astype(jnp.bfloat16)
            low = (value - high.astype(jnp.float32)).astype(jnp.bfloat16)
            both.append(jnp.concatenate([hot * high, hot * low], axis=1))
        both = jnp.concatenate(both, axis=0)
        for first in range(0, planes, 2):
            count = min(2, planes - first)
            total = jnp.dot(
                both, cols_hot[:, first * LANES : (first + count) * LANES], preferred_element_type=jnp.float32
            )
            for level in range(LEVELS):
                for c in range(count):
                    part = total[level * rows_all : (level + 1) * rows_all, c * LANES : (c + 1) * LANES]
                    goal = (start + level, first + c, slice(0, rows_all))
                    force_ref[goal] = force_ref[goal] + part if add else part

    def levels(add):
        def one(index, carry):
            levels_of(index * LEVELS, add)
            return carry

        lax.fori_loop(0, steps // LEVELS, one, 0)

    force_ref[steps] = jnp.zeros_like(force_ref[steps])
    gather_gauges(0)
    levels(False)
    if groups > 1:

        def more(index, carry):
            gather_gauges(index)
            levels(True)
            return carry

        lax.fori_loop(1, groups, more, 0)


def sweep(
    steps, keep_ref, gain_ref, top_ref, bottom_ref, right_ref, force_ref,
    grad_ref, sums_ref,
    a, fx, fy, keep_x, gain_x, keep_y, gain_y, plain,
):
    height, width = keep_ref.shape
    halo = 2 * steps
    inner = width // LANES
    planes = inner + 1
    rows_all = height + 2 * halo
    blocks = rows_all // 8
    my_row, my_lon, row_tiles, lons = my_place()
    reach = 2 * halo
    has_top, has_bottom = my_row > 0, my_row < row_tiles - 1
    has_right = my_lon < lons - 1
    lanes8 = lane_iota(8)

    def up(value):
        return pltpu.roll(value, 7, 0)

    def down(value):
        return pltpu.roll(value, 1, 0)

    for kind, (source, by_x, by_y) in enumerate(((keep_ref, keep_x, keep_y), (gain_ref, gain_x, gain_y))):
        for c in range(planes):
            cols = slice(c * LANES, (c + 1) * LANES)
            plain[c, 0:halo, :] = top_ref[kind, :, cols]
            plain[c, halo + height : rows_all, :] = bottom_ref[kind, :, cols]
            if c < inner:
                plain[c, halo : halo + height, :] = source[:, cols]
        lower = lane_iota(height) < reach
        plain[inner, halo : halo + height, :] = jnp.where(lower, roll_lanes(right_ref[0], -reach * kind), 0.0)
        for q in range(blocks):
            values = [plain[c, pl.ds(q, 8, stride=blocks), :] for c in range(planes)]
            shifted = shift_from(values, 1, lanes8)
            to = (q - 1) % blocks * 8
            for c in range(planes):
                by_x[c, 8 * q : 8 * q + 8, :] = shifted[c]
                by_y[c, to : to + 8, :] = up(values[c]) if q == 0 else values[c]

    col_mask = jnp.where(lanes8 < reach, jnp.where(has_right, 1.0, 0.0), 0.0)
    sublane = lax.broadcasted_iota(jnp.int32, (8, LANES), 0)
    row_mask = {}
    for row, there in ((halo - 1, has_top), (halo + height, has_bottom)):
        row_mask[row % blocks] = jnp.where(sublane == row // blocks, jnp.where(there, 1.0, 0.0), 1.0)
    every = range(planes)

    fx[...] = jnp.zeros_like(fx)
    fy[...] = jnp.zeros_like(fy)
    a[:, 0:rows_all, :] = force_ref[steps - 1, :, 0:rows_all, :]

    def step(index, carry):
        level = jnp.where(index < steps - 1, steps - 2 - index, steps)
        near, ahead, new_y, total, behind, push = {}, {}, {}, {}, {}, {}

        def rows(q):
            return slice(8 * q, 8 * q + 8)

        def first(q):
            near[q] = [a[c, rows(q % blocks), :] for c in every]
            if q < blocks:
                ahead[q] = [roll_lanes(value, -2) for value in near[q]]
                push[q] = [force_ref[level, c, rows(q), :] for c in every]
            else:
                near[q] = [up(value) for value in near[q]]

        def second_y(q):
            new_y[q] = [
                keep_y[c, rows(q), :] * fy[c, rows(q), :] + gain_y[c, rows(q), :] * (near[q + 2][c] - near[q][c])
                for c in every
            ]
            for c in every:
                fy[c, rows(q), :] = new_y[q][c]

        def second_x(q):
            far = from_rolled(ahead[q], 2, lanes8)
            new_x = [
                keep_x[c, rows(q), :] * fx[c, rows(q), :] + gain_x[c, rows(q), :] * (far[c] - near[q][c]) for c in every
            ]
            behind[q] = [roll_lanes(value, 2) for value in new_x]
            before = new_y[q - 2] if q >= 2 else [down(fy[c, rows(q - 2 + blocks), :]) for c in every]
            total[q] = [(near[q][c] + push[q][c]) + (new_y[q][c] - before[c]) + new_x[c] for c in every]
            for c in every:
                fx[c, rows(q), :] = new_x[c]

        def third(q):
            far = from_rolled(behind[q], -2, lanes8)
            for c in every:
                value = total[q][c] - far[c]
                if c == inner:
                    value = value * col_mask
                if q in row_mask:
                    value = value * row_mask[q]
                a[c, rows(q), :] = value

        for q in range(4):
            first(q)
        second_y(0)
        second_y(1)
        for q in range(2, blocks):
            first(q + 2)
            second_y(q)
            second_x(q)
            if q > 2:
                third(q - 1)
        for q in range(2):
            first(q)
            new_y[q] = [fy[c, rows(q), :] for c in every]
        for q in range(2):
            second_x(q)
            third(q - 1 if q else blocks - 1)
        third(1)
        return carry

    lax.fori_loop(0, steps, step, 0)

    start = jnp.where(my_lon > 0, halo, 0)
    for r in range(0, height, 8):
        s, q = divmod(halo + r, blocks)
        for c in every:
            cols = slice(c * LANES, (c + 1) * LANES)
            value = a[c, pl.ds(8 * q + s, 8, stride=8), :]
            wet = keep_ref[r : r + 8, cols] if c < inner else right_ref[0, r : r + 8, :]
            if c == 0:
                wet = jnp.where(lanes8 >= start, wet, 0.0)
            if c == inner:
                wet = jnp.where(lanes8 < halo, wet, 0.0)
            grad_ref[r : r + 8, cols] = jnp.where(wet > 0.0, value, 0.0)
    length = 2.0 * width
    shape = (8 + halo, planes * LANES)
    kind, column = lax.broadcasted_iota(jnp.int32, shape, 0), lax.broadcasted_iota(jnp.int32, shape, 1)
    beyond = column - width
    off = jnp.where(kind == 0, column, jnp.where(kind == 1, -1 - beyond, jnp.where(kind == 2, beyond, width - 1 - beyond)))
    mine = ((kind < 2) & (beyond < 0)) | ((kind >= 2) & (kind < 4) & (beyond >= 0))
    weights = jnp.where(mine, jnp.exp(-jnp.maximum(off, 0).astype(jnp.float32) / length), 0.0)
    weights = jnp.where((kind >= 8) & (beyond == kind - 8), 1.0, weights)
    sums = lax.dot_general(
        weights, grad_ref[...], (((1,), (1,)), ((), ())), precision=lax.Precision.HIGHEST,
        preferred_element_type=jnp.float32,
    )
    for i in range(sums_ref.shape[0]):
        sums_ref[i] = sums


def smooth(halo, lons, grad_ref, out_ref, weights_ref):
    width = out_ref.shape[1]
    length = 2.0 * width
    row = lax.broadcasted_iota(jnp.int32, (width, width), 0)
    column = lax.broadcasted_iota(jnp.int32, (width, width), 1)
    kernel = jnp.exp(-jnp.abs(row - column).astype(jnp.float32) / length)
    out_ref[...] = jnp.dot(
        grad_ref[:, :width], kernel, precision=lax.Precision.HIGHEST, preferred_element_type=jnp.float32
    )
    me = lax.axis_index("lon")
    shape = (8 + halo, width)
    kind, column = lax.broadcasted_iota(jnp.int32, shape, 0), lax.broadcasted_iota(jnp.int32, shape, 1)
    for source in range(lons):
        strip = jnp.where(kind < 2, source, source + 1)
        left = ((kind == 0) | (kind == 2)) & (strip > me)
        right = ((kind == 1) | (kind == 3)) & (strip < me)
        near = (kind >= 8) & (source + 1 == me)
        away = jnp.where(left, (strip - me) * width - column, (me - strip - 1) * width + column + 1)
        away = jnp.where(near, jnp.abs(kind - 8 - column), away)
        weights = jnp.where(left | right | near, jnp.exp(-jnp.maximum(away, 0).astype(jnp.float32) / length), 0.0)
        weights_ref[source * shape[0] : (source + 1) * shape[0], :] = weights


def finish(own_ref, weights_ref, sums_ref, out_ref):
    out_ref[...] = own_ref[...] + lax.dot_general(
        sums_ref[...], weights_ref[...], (((0,), (0,)), ((), ())), precision=lax.Precision.HIGHEST,
        preferred_element_type=jnp.float32,
    )


def f32(*shape):
    return jax.ShapeDtypeStruct(shape, jnp.float32)


def hint(megabytes):
    return pl.CostEstimate(flops=0, bytes_accessed=megabytes * 1000 * 1000, transcendentals=0)


def spaced(rows):
    return 8 * (rows // 8 | 1)


def vmem(count):
    return [pl.BlockSpec(memory_space=pltpu.VMEM)] * count


def local(depth, surface, friction, wet, coastal_tiles, gauge_route, gauge_cell, gauge_times, gauge_resid):
    height, width = depth.shape
    owned = gauge_route.shape[0]
    blocks = gauge_resid.shape[1]
    steps = blocks * STEPS_BLOCK
    halo = 2 * steps
    assert halo == SEG and height == LANES
    tiles = lax.axis_size(GRID_AXES)
    lons = lax.axis_size("lon")
    row_tiles = lax.axis_size(ROW_AXES)
    planes = width // LANES + 1
    rows_all = height + 2 * halo
    params = pltpu.CompilerParams(vmem_limit_bytes=VMEM_LIMIT)

    keep = (1.0 - friction) * wet.astype(jnp.float32)
    gain = ((courant * 0.5) ** 2 * jnp.maximum(depth + surface, depth_floor)) * keep
    samples, coast_count = gauge_resid.shape[2], coastal_tiles.shape[0]
    assert coast_count <= owned

    assert samples >= 3

    def put(array, group, row):
        groups, rows, lanes = array.shape
        return jnp.pad(array, ((group, 2 * blocks + 1 - group - groups), (row, samples - row - rows), (0, owned - lanes)))

    gauges = (
        put(jnp.transpose(gauge_times, (1, 2, 0)), 0, 0)
        + put(gauge_route.reshape(1, 1, owned), 2 * blocks, 0)
        + put(gauge_cell.reshape(1, 1, owned), 2 * blocks, 1)
        + put(coastal_tiles.reshape(1, 1, coast_count), 2 * blocks, 2)
    ).astype(jnp.float32) + put(jnp.transpose(gauge_resid, (1, 2, 0)), blocks, 0)
    west = pl.pallas_call(
        functools.partial(give_west, 2 * halo), out_shape=f32(4, height, LANES), in_specs=vmem(2), out_specs=vmem(1)[0],
        compiler_params=params, name="give_west",
    )(keep, gain)
    right = lax.ppermute(west, "lon", [(i + 1, i) for i in range(lons - 1)])

    parcel = pl.pallas_call(
        functools.partial(give_gauges, height, width, blocks, samples, coast_count),
        out_shape=f32(tiles, gauge_rows(owned)[0], LANES),
        in_specs=vmem(1) + [pl.BlockSpec(memory_space=pl.ANY)],
        out_specs=vmem(1)[0],
        scratch_shapes=[pltpu.VMEM((24, LANES), jnp.float32)],
        compiler_params=params,
        cost_estimate=hint(10),
        name="give_gauges",
    )(gauges, west)

    def exchange(array, axes):
        return lax.all_to_all(array, axes, split_axis=0, concat_axis=0, tiled=True)

    parcel = exchange(parcel, GRID_AXES)

    south, north = pl.pallas_call(
        functools.partial(give_rows, halo), out_shape=(f32(2, halo, planes * LANES),) * 2, in_specs=vmem(3),
        out_specs=tuple(vmem(2)), compiler_params=params, cost_estimate=hint(40), name="give_rows",
    )(keep, gain, right)
    top = lax.ppermute(south, ROW_AXES, [(i, i + 1) for i in range(row_tiles - 1)])
    bottom = lax.ppermute(north, ROW_AXES, [(i + 1, i) for i in range(row_tiles - 1)])

    wide = max(2 * LANES, owned)
    pushes = pl.pallas_call(
        functools.partial(force, steps, halo, height, width),
        out_shape=f32(steps + 1, planes, spaced(rows_all), LANES),
        in_specs=vmem(1),
        out_specs=vmem(1)[0],
        scratch_shapes=[
            pltpu.VMEM((steps, wide), jnp.float32),
            pltpu.VMEM((rows_all, wide), jnp.bfloat16),
            pltpu.VMEM((2 * wide, planes * LANES), jnp.bfloat16),
        ],
        compiler_params=params,
        cost_estimate=pl.CostEstimate(
            flops=4 * steps * rows_all * wide * planes * LANES, bytes_accessed=4 * steps * planes * rows_all * LANES,
            transcendentals=0,
        ),
        name="force",
    )(parcel)

    plane = pltpu.VMEM((planes, spaced(rows_all), LANES), jnp.float32)
    grad, sums = pl.pallas_call(
        functools.partial(sweep, steps),
        out_shape=(f32(height, planes * LANES), f32(lons, 8 + halo, height)),
        in_specs=vmem(6),
        out_specs=tuple(vmem(2)),
        scratch_shapes=[plane] * 8,
        compiler_params=params,
        name="sweep",
    )(keep, gain, top, bottom, right, pushes)

    sums = exchange(sums, "lon")
    own, weights = pl.pallas_call(
        functools.partial(smooth, halo, lons),
        out_shape=(f32(height, width), f32(lons * (8 + halo), width)),
        in_specs=vmem(1),
        out_specs=tuple(vmem(2)),
        compiler_params=params,
        cost_estimate=pl.CostEstimate(
            flops=6 * 2 * height * width * width, bytes_accessed=2 * 4 * height * width, transcendentals=width * width
        ),
        name="smooth",
    )(grad)
    return pl.pallas_call(
        finish, out_shape=f32(height, width), in_specs=vmem(3), out_specs=vmem(1)[0], compiler_params=params, name="finish",
    )(own, weights, sums.reshape(lons * (8 + halo), height))


def solution(mesh):
    in_specs = (
        P(("lat", "gau"), "lon"),
        P(("scen", "lat", "gau"), "lon"),
        P(("lat", "gau"), "lon"),
        P(("lat", "gau"), "lon"),
        P(),
        P(("scen", "lon", "lat", "gau"), None),
        P(("scen", "lon", "lat", "gau")),
        P(("scen", "lon", "lat", "gau"), None, None),
        P(("scen", "lon", "lat", "gau"), None, None),
    )
    out_specs = P(("scen", "lat", "gau"), "lon")
    return jax.shard_map(local, mesh=mesh, in_specs=in_specs, out_specs=out_specs, check_vma=False)
```

```python
import functools
import math

import jax
import jax.numpy as jnp
from jax import lax
from jax.experimental import pallas as pl
from jax.experimental.pallas import tpu as pltpu
from jax.sharding import PartitionSpec as P

STEPS_BLOCK = 8
LANES = 128
SEG = 32
LEVELS = 4
BEHIND = 2

courant = 0.45
depth_floor = 0.1

GRID_AXES = ("lon", "lat", "gau")
ROW_AXES = ("lat", "gau")
VMEM_LIMIT = 16 * 1024 * 1024


def roll_lanes(x, shift):
    shift = shift % LANES
    return x if shift == 0 else pltpu.roll(x, shift, 1)


def lane_iota(rows):
    return lax.broadcasted_iota(jnp.int32, (rows, LANES), 1)


def gauge_rows(owned):
    if 3 * owned <= LANES:
        return STEPS_BLOCK, owned
    assert owned <= LANES
    return 3 * STEPS_BLOCK, 0


def my_place():
    row = lax.axis_index("lat") * lax.axis_size("gau") + lax.axis_index("gau")
    return row, lax.axis_index("lon"), lax.axis_size("lat") * lax.axis_size("gau"), lax.axis_size("lon")


def give_west(reach, keep_ref, gain_ref, west_ref):
    lower = lane_iota(west_ref.shape[1]) < reach
    west_ref[0] = jnp.where(lower, keep_ref[:, :LANES], roll_lanes(gain_ref[:, :LANES], reach))
    for spare in range(1, west_ref.shape[0]):
        west_ref[spare] = jnp.zeros(west_ref.shape[1:], jnp.float32)


def give_rows(halo, keep_ref, gain_ref, right_ref, far_ref, near_ref):
    height, width = keep_ref.shape
    lower = lane_iota(halo) < 2 * halo
    odd = my_place()[0] & 1
    for goal, south in ((far_ref, odd), (near_ref, 1 - odd)):
        rows = pl.ds(pl.multiple_of(south * (height - halo), halo), halo)
        for kind, source in enumerate((keep_ref, gain_ref)):
            goal[kind, :, :width] = source[rows, :]
            goal[kind, :, width:] = jnp.where(lower, roll_lanes(right_ref[0, rows, :], -2 * halo * kind), 0.0)


def give_gauges(height, width, blocks, samples, coast_count, gauge_ref, after_ref, parcel_ref, block_ref):
    row_tiles = lax.axis_size("lat") * lax.axis_size("gau")
    owned = gauge_ref.shape[2]
    assert blocks == 2
    route, cell, coast = (gauge_ref[2 * blocks, i : i + 1, :].astype(jnp.int32) for i in range(3))
    target = jnp.zeros_like(route)
    for entry in range(coast_count):
        target = jnp.where(route == entry, jnp.broadcast_to(coast[:, entry : entry + 1], route.shape), target)
    row_bits, width_bits = int(math.log2(row_tiles)), int(math.log2(width))
    assert row_tiles == 1 << row_bits and width == 1 << width_bits
    grid_row = (target & (row_tiles - 1)) * height + (cell >> width_bits)
    grid_col = (target >> row_bits) * width + (cell & (width - 1))
    block_ref[...] = jnp.zeros_like(block_ref)
    levels = lax.broadcasted_iota(jnp.int32, (STEPS_BLOCK, owned), 0).astype(jnp.float32)
    for block in range(blocks):
        series = jnp.zeros((STEPS_BLOCK, owned), jnp.float32)
        for sample in range(samples):
            times = gauge_ref[block, sample : sample + 1, :]
            resid = gauge_ref[blocks + block, sample : sample + 1, :]
            series = series + jnp.where(times == levels, resid, 0.0)
        block_ref[block * STEPS_BLOCK : (block + 1) * STEPS_BLOCK, :owned] = series
    at = blocks * STEPS_BLOCK
    block_ref[at : at + 1, :owned] = grid_row.astype(jnp.float32)
    block_ref[at + 1 : at + 2, :owned] = grid_col.astype(jnp.float32)
    size, apart = gauge_rows(owned)
    gauges = block_ref[...]
    if size == STEPS_BLOCK:
        gauges = sum(
            roll_lanes(gauges[i * STEPS_BLOCK : (i + 1) * STEPS_BLOCK], i * apart) for i in range(3)
        )
    tiles = parcel_ref.shape[0]

    def put(tile, carry):
        parcel_ref[tile, 0:size, :] = gauges
        return carry

    lax.fori_loop(0, tiles, put, 0, unroll=tiles <= 16)


def from_rolled(rolled, shift, lanes):
    count = len(rolled)
    if shift > 0:
        return [jnp.where(lanes >= LANES - shift, rolled[(c + 1) % count], rolled[c]) for c in range(count)]
    return [jnp.where(lanes < -shift, rolled[(c - 1) % count], rolled[c]) for c in range(count)]


def shift_from(planes, shift, lanes):
    return from_rolled([roll_lanes(plane, -shift) for plane in planes], shift, lanes)


def force(steps, halo, height, width, parcel_ref, force_ref, series_ref, rows_hot, cols_hot):
    planes, rows_all = force_ref.shape[1], height + 2 * halo
    my_row, my_lon, row_tiles, lons = my_place()
    wide = rows_hot.shape[1]
    tiles, parcel_rows = parcel_ref.shape[:2]
    size = parcel_rows
    apart = wide // tiles if size == STEPS_BLOCK else 0
    owned = apart if apart else LANES
    group = wide // owned
    groups = tiles // group
    per_plane = LANES // owned
    blocks = rows_all // 8
    row_shift = (halo - my_row * height).astype(jnp.float32)
    col_shift = (-my_lon * width).astype(jnp.float32)
    place = lax.broadcasted_iota(jnp.int32, (rows_all, LANES), 0)
    at = ((place & 7) * blocks + (place >> 3)).astype(jnp.float32)

    def gather_gauges(index):
        lanes = lane_iota(STEPS_BLOCK)
        for part in range(wide // LANES):
            cols = slice(part * LANES, (part + 1) * LANES)
            fields = []
            for field in range(3):
                total = jnp.zeros((STEPS_BLOCK, LANES), jnp.float32)
                rows = slice(0, 8) if apart else slice(8 * field, 8 * field + 8)
                for i in range(per_plane):
                    source = index * group + part * per_plane + i
                    block = roll_lanes(parcel_ref[source, rows, :], i * owned - field * apart)
                    total = jnp.where((lanes >= i * owned) & (lanes < (i + 1) * owned), block, total)
                fields.append(total)
            series_ref[0:8, cols] = fields[0]
            series_ref[8:16, cols] = fields[1]
            row = fields[2][0:1] + row_shift
            col = fields[2][1:2] + col_shift
            col = jnp.where(col < width + 2 * halo, col, -1.0)
            rows_hot[:, cols] = (at == row).astype(jnp.float32).astype(jnp.bfloat16)
            by_gauge = jnp.transpose(jnp.broadcast_to(col, (LANES, LANES)))
            for c in range(planes):
                spot = (lane_iota(LANES) + c * LANES).astype(jnp.float32)
                hot = (by_gauge == spot).astype(jnp.float32).astype(jnp.bfloat16)
                cols_hot[part * LANES : (part + 1) * LANES, c * LANES : (c + 1) * LANES] = hot
                cols_hot[wide + part * LANES : wide + (part + 1) * LANES, c * LANES : (c + 1) * LANES] = hot

    def levels_of(start, add):
        hot = rows_hot[...]
        both = []
        for level in range(LEVELS):
            value = series_ref[pl.ds(start + level, 1), :]
            high = value.astype(jnp.bfloat16)
            low = (value - high.astype(jnp.float32)).astype(jnp.bfloat16)
            both.append(jnp.concatenate([hot * high, hot * low], axis=1))
        both = jnp.concatenate(both, axis=0)
        for first in range(0, planes, 2):
            count = min(2, planes - first)
            total = jnp.dot(
                both, cols_hot[:, first * LANES : (first + count) * LANES], preferred_element_type=jnp.float32
            )
            for level in range(LEVELS):
                for c in range(count):
                    part = total[level * rows_all : (level + 1) * rows_all, c * LANES : (c + 1) * LANES]
                    goal = (start + level, first + c, slice(0, rows_all))
                    force_ref[goal] = force_ref[goal] + part if add else part

    def levels(add):
        def one(index, carry):
            levels_of(index * LEVELS, add)
            return carry

        lax.fori_loop(0, steps // LEVELS, one, 0)

    force_ref[steps] = jnp.zeros_like(force_ref[steps])
    gather_gauges(0)
    levels(False)
    if groups > 1:

        def more(index, carry):
            gather_gauges(index)
            levels(True)
            return carry

        lax.fori_loop(1, groups, more, 0)


def sweep(
    steps, keep_ref, gain_ref, far_ref, near_ref, right_ref, force_ref,
    grad_ref, sums_ref,
    a, fx, fy, keep_x, gain_x, keep_y, gain_y, plain,
):
    height, width = keep_ref.shape
    halo = 2 * steps
    inner = width // LANES
    planes = inner + 1
    rows_all = height + 2 * halo
    blocks = rows_all // 8
    my_row, my_lon, row_tiles, lons = my_place()
    reach = 2 * halo
    has_top, has_bottom = my_row > 0, my_row < row_tiles - 1
    has_right = my_lon < lons - 1
    odd = (jnp.zeros((halo, LANES), jnp.int32) + (my_row & 1)) == 1
    lanes8 = lane_iota(8)

    def up(value):
        return pltpu.roll(value, 7, 0)

    def down(value):
        return pltpu.roll(value, 1, 0)

    for kind, (source, by_x, by_y) in enumerate(((keep_ref, keep_x, keep_y), (gain_ref, gain_x, gain_y))):
        for c in range(planes):
            cols = slice(c * LANES, (c + 1) * LANES)
            far, near = far_ref[kind, :, cols], near_ref[kind, :, cols]
            plain[c, 0:halo, :] = jnp.where(odd, near, far)
            plain[c, halo + height : rows_all, :] = jnp.where(odd, far, near)
            if c < inner:
                plain[c, halo : halo + height, :] = source[:, cols]
        lower = lane_iota(height) < reach
        plain[inner, halo : halo + height, :] = jnp.where(lower, roll_lanes(right_ref[0], -reach * kind), 0.0)
        for q in range(blocks):
            values = [plain[c, pl.ds(q, 8, stride=blocks), :] for c in range(planes)]
            shifted = shift_from(values, 1, lanes8)
            to = (q - 1) % blocks * 8
            for c in range(planes):
                by_x[c, 8 * q : 8 * q + 8, :] = shifted[c]
                by_y[c, to : to + 8, :] = up(values[c]) if q == 0 else values[c]

    col_mask = jnp.where(lanes8 < reach, jnp.where(has_right, 1.0, 0.0), 0.0)
    sublane = lax.broadcasted_iota(jnp.int32, (8, LANES), 0)
    row_mask = {}
    for row, there in ((halo - 1, has_top), (halo + height, has_bottom)):
        row_mask[row % blocks] = jnp.where(sublane == row // blocks, jnp.where(there, 1.0, 0.0), 1.0)
    every = range(planes)

    fx[...] = jnp.zeros_like(fx)
    fy[...] = jnp.zeros_like(fy)
    a[:, 0:rows_all, :] = force_ref[steps - 1, :, 0:rows_all, :]

    def step(index, carry):
        level = jnp.where(index < steps - 1, steps - 2 - index, steps)
        near, ahead, new_y, total, behind = {}, {}, {}, {}, {}

        def rows(q):
            return slice(8 * q, 8 * q + 8)

        def first(q):
            near[q] = [a[c, rows(q % blocks), :] for c in every]
            if q < blocks:
                ahead[q] = [roll_lanes(value, -2) for value in near[q]]
            else:
                near[q] = [up(value) for value in near[q]]

        def second_y(q):
            new_y[q] = [
                keep_y[c, rows(q), :] * fy[c, rows(q), :] + gain_y[c, rows(q), :] * (near[q + 2][c] - near[q][c])
                for c in every
            ]
            for c in every:
                fy[c, rows(q), :] = new_y[q][c]

        def second_x(q):
            far = from_rolled(ahead[q], 2, lanes8)
            new_x = [
                keep_x[c, rows(q), :] * fx[c, rows(q), :] + gain_x[c, rows(q), :] * (far[c] - near[q][c]) for c in every
            ]
            behind[q] = [roll_lanes(value, 2) for value in new_x]
            before = new_y[q - 2] if q >= 2 else [down(fy[c, rows(q - 2 + blocks), :]) for c in every]
            push = [force_ref[level, c, rows(q), :] for c in every]
            total[q] = [(near[q][c] + push[c]) + (new_y[q][c] - before[c]) + new_x[c] for c in every]
            for c in every:
                fx[c, rows(q), :] = new_x[c]

        def third(q):
            far = from_rolled(behind[q], -2, lanes8)
            for c in every:
                value = total[q][c] - far[c]
                if c == inner:
                    value = value * col_mask
                if q in row_mask:
                    value = value * row_mask[q]
                a[c, rows(q), :] = value

        tasks = []
        for odd in range(2):
            tasks += [(odd, True, False)] + [(q, True, True) for q in range(odd + 2, blocks, 2)] + [(odd, False, True)]

        def begin(task):
            q, with_y, with_x = task
            if with_y and not with_x:
                first(q)
                first(q + 2)
            elif with_y:
                first(q + 2)
            else:
                first(q)
                new_y[q] = [fy[c, rows(q), :] for c in every]

        waiting = []
        begin(tasks[0])
        for task, following in zip(tasks, tasks[1:] + [None]):
            q, with_y, with_x = task
            if following is not None:
                begin(following)
            if with_y:
                second_y(q)
            if with_x:
                second_x(q)
                waiting.append(q)
            if len(waiting) > BEHIND:
                third(waiting.pop(0))
        for q in waiting:
            third(q)
        return carry

    lax.fori_loop(0, steps, step, 0)

    start = jnp.where(my_lon > 0, halo, 0)
    for r in range(0, height, 8):
        s, q = divmod(halo + r, blocks)
        for c in every:
            cols = slice(c * LANES, (c + 1) * LANES)
            value = a[c, pl.ds(8 * q + s, 8, stride=8), :]
            wet = keep_ref[r : r + 8, cols] if c < inner else right_ref[0, r : r + 8, :]
            if c == 0:
                wet = jnp.where(lanes8 >= start, wet, 0.0)
            if c == inner:
                wet = jnp.where(lanes8 < halo, wet, 0.0)
            grad_ref[r : r + 8, cols] = jnp.where(wet > 0.0, value, 0.0)
    length = 2.0 * width
    shape = (8 + halo, planes * LANES)
    kind, column = lax.broadcasted_iota(jnp.int32, shape, 0), lax.broadcasted_iota(jnp.int32, shape, 1)
    beyond = column - width
    off = jnp.where(kind == 0, column, jnp.where(kind == 1, -1 - beyond, jnp.where(kind == 2, beyond, width - 1 - beyond)))
    mine = ((kind < 2) & (beyond < 0)) | ((kind >= 2) & (kind < 4) & (beyond >= 0))
    weights = jnp.where(mine, jnp.exp(-jnp.maximum(off, 0).astype(jnp.float32) / length), 0.0)
    weights = jnp.where((kind >= 8) & (beyond == kind - 8), 1.0, weights)
    sums = lax.dot_general(
        weights, grad_ref[...], (((1,), (1,)), ((), ())), precision=lax.Precision.HIGHEST,
        preferred_element_type=jnp.float32,
    )
    for i in range(sums_ref.shape[0]):
        sums_ref[i] = sums


def smooth(halo, lons, grad_ref, out_ref, weights_ref):
    width = out_ref.shape[1]
    length = 2.0 * width
    row = lax.broadcasted_iota(jnp.int32, (width, width), 0)
    column = lax.broadcasted_iota(jnp.int32, (width, width), 1)
    kernel = jnp.exp(-jnp.abs(row - column).astype(jnp.float32) / length)
    out_ref[...] = jnp.dot(
        grad_ref[:, :width], kernel, precision=lax.Precision.HIGHEST, preferred_element_type=jnp.float32
    )
    me = lax.axis_index("lon")
    shape = (8 + halo, width)
    kind, column = lax.broadcasted_iota(jnp.int32, shape, 0), lax.broadcasted_iota(jnp.int32, shape, 1)
    for source in range(lons):
        strip = jnp.where(kind < 2, source, source + 1)
        left = ((kind == 0) | (kind == 2)) & (strip > me)
        right = ((kind == 1) | (kind == 3)) & (strip < me)
        near = (kind >= 8) & (source + 1 == me)
        away = jnp.where(left, (strip - me) * width - column, (me - strip - 1) * width + column + 1)
        away = jnp.where(near, jnp.abs(kind - 8 - column), away)
        weights = jnp.where(left | right | near, jnp.exp(-jnp.maximum(away, 0).astype(jnp.float32) / length), 0.0)
        weights_ref[source * shape[0] : (source + 1) * shape[0], :] = weights


def finish(own_ref, weights_ref, sums_ref, out_ref):
    out_ref[...] = own_ref[...] + lax.dot_general(
        sums_ref[...], weights_ref[...], (((0,), (0,)), ((), ())), precision=lax.Precision.HIGHEST,
        preferred_element_type=jnp.float32,
    )


def f32(*shape):
    return jax.ShapeDtypeStruct(shape, jnp.float32)


def hint(megabytes):
    return pl.CostEstimate(flops=0, bytes_accessed=megabytes * 1000 * 1000, transcendentals=0)


def spaced(rows):
    return 8 * (rows // 8 | 1)


def vmem(count):
    return [pl.BlockSpec(memory_space=pltpu.VMEM)] * count


def local(depth, surface, friction, wet, coastal_tiles, gauge_route, gauge_cell, gauge_times, gauge_resid):
    height, width = depth.shape
    owned = gauge_route.shape[0]
    blocks = gauge_resid.shape[1]
    steps = blocks * STEPS_BLOCK
    halo = 2 * steps
    assert halo == SEG and height == LANES
    tiles = lax.axis_size(GRID_AXES)
    lons = lax.axis_size("lon")
    row_tiles = lax.axis_size(ROW_AXES)
    planes = width // LANES + 1
    rows_all = height + 2 * halo
    params = pltpu.CompilerParams(vmem_limit_bytes=VMEM_LIMIT)

    keep = (1.0 - friction) * wet.astype(jnp.float32)
    gain = ((courant * 0.5) ** 2 * jnp.maximum(depth + surface, depth_floor)) * keep
    samples, coast_count = gauge_resid.shape[2], coastal_tiles.shape[0]
    assert coast_count <= owned

    assert samples >= 3

    def put(array, group, row):
        groups, rows, lanes = array.shape
        return jnp.pad(array, ((group, 2 * blocks + 1 - group - groups), (row, samples - row - rows), (0, owned - lanes)))

    gauges = (
        put(jnp.transpose(gauge_times, (1, 2, 0)), 0, 0)
        + put(gauge_route.reshape(1, 1, owned), 2 * blocks, 0)
        + put(gauge_cell.reshape(1, 1, owned), 2 * blocks, 1)
        + put(coastal_tiles.reshape(1, 1, coast_count), 2 * blocks, 2)
    ).astype(jnp.float32) + put(jnp.transpose(gauge_resid, (1, 2, 0)), blocks, 0)
    west = pl.pallas_call(
        functools.partial(give_west, 2 * halo), out_shape=f32(4, height, LANES), in_specs=vmem(2), out_specs=vmem(1)[0],
        compiler_params=params, name="give_west",
    )(keep, gain)
    right = lax.ppermute(west, "lon", [(i + 1, i) for i in range(lons - 1)])

    parcel = pl.pallas_call(
        functools.partial(give_gauges, height, width, blocks, samples, coast_count),
        out_shape=f32(tiles, gauge_rows(owned)[0], LANES),
        in_specs=vmem(1) + [pl.BlockSpec(memory_space=pl.ANY)],
        out_specs=vmem(1)[0],
        scratch_shapes=[pltpu.VMEM((24, LANES), jnp.float32)],
        compiler_params=params,
        cost_estimate=hint(10),
        name="give_gauges",
    )(gauges, west)

    def exchange(array, axes, groups=None):
        return lax.all_to_all(array, axes, split_axis=0, concat_axis=0, axis_index_groups=groups, tiled=True)

    group = sorted(range(tiles), key=lambda tile: (tile % row_tiles in (0, row_tiles - 1), -(tile // row_tiles)))
    parcel = exchange(parcel, GRID_AXES, [group])

    far, near = pl.pallas_call(
        functools.partial(give_rows, halo), out_shape=(f32(2, halo, planes * LANES),) * 2, in_specs=vmem(3),
        out_specs=tuple(vmem(2)), compiler_params=params, cost_estimate=hint(40), name="give_rows",
    )(keep, gain, right)
    far = lax.ppermute(far, ROW_AXES, [pair for i in range(1, row_tiles - 1, 2) for pair in ((i, i + 1), (i + 1, i))])
    near = lax.ppermute(near, ROW_AXES, [pair for i in range(0, row_tiles, 2) for pair in ((i, i + 1), (i + 1, i))])

    wide = max(2 * LANES, owned)
    pushes = pl.pallas_call(
        functools.partial(force, steps, halo, height, width),
        out_shape=f32(steps + 1, planes, spaced(rows_all), LANES),
        in_specs=vmem(1),
        out_specs=vmem(1)[0],
        scratch_shapes=[
            pltpu.VMEM((steps, wide), jnp.float32),
            pltpu.VMEM((rows_all, wide), jnp.bfloat16),
            pltpu.VMEM((2 * wide, planes * LANES), jnp.bfloat16),
        ],
        compiler_params=params,
        cost_estimate=pl.CostEstimate(
            flops=4 * steps * rows_all * wide * planes * LANES, bytes_accessed=4 * steps * planes * rows_all * LANES,
            transcendentals=0,
        ),
        name="force",
    )(parcel)

    plane = pltpu.VMEM((planes, spaced(rows_all), LANES), jnp.float32)
    grad, sums = pl.pallas_call(
        functools.partial(sweep, steps),
        out_shape=(f32(height, planes * LANES), f32(lons, 8 + halo, height)),
        in_specs=vmem(6),
        out_specs=tuple(vmem(2)),
        scratch_shapes=[plane] * 8,
        compiler_params=params,
        name="sweep",
    )(keep, gain, far, near, right, pushes)

    sums = exchange(sums, "lon")
    own, weights = pl.pallas_call(
        functools.partial(smooth, halo, lons),
        out_shape=(f32(height, width), f32(lons * (8 + halo), width)),
        in_specs=vmem(1),
        out_specs=tuple(vmem(2)),
        compiler_params=params,
        cost_estimate=pl.CostEstimate(
            flops=6 * 2 * height * width * width, bytes_accessed=2 * 4 * height * width, transcendentals=width * width
        ),
        name="smooth",
    )(grad)
    return pl.pallas_call(
        finish, out_shape=f32(height, width), in_specs=vmem(3), out_specs=vmem(1)[0], compiler_params=params, name="finish",
    )(own, weights, sums.reshape(lons * (8 + halo), height))


def solution(mesh):
    in_specs = (
        P(("lat", "gau"), "lon"),
        P(("scen", "lat", "gau"), "lon"),
        P(("lat", "gau"), "lon"),
        P(("lat", "gau"), "lon"),
        P(),
        P(("scen", "lon", "lat", "gau"), None),
        P(("scen", "lon", "lat", "gau")),
        P(("scen", "lon", "lat", "gau"), None, None),
        P(("scen", "lon", "lat", "gau"), None, None),
    )
    out_specs = P(("scen", "lat", "gau"), "lon")
    return jax.shard_map(local, mesh=mesh, in_specs=in_specs, out_specs=out_specs, check_vma=False)
```

```python
import functools
import math

import jax
import jax.numpy as jnp
from jax import lax
from jax.experimental import pallas as pl
from jax.experimental.pallas import tpu as pltpu
from jax.sharding import PartitionSpec as P

STEPS_BLOCK = 8
LANES = 128
SEG = 32
LEVELS = 4

courant = 0.45
depth_floor = 0.1

GRID_AXES = ("lon", "lat", "gau")
ROW_AXES = ("lat", "gau")
VMEM_LIMIT = 16 * 1024 * 1024


def roll_lanes(x, shift):
    shift = shift % LANES
    return x if shift == 0 else pltpu.roll(x, shift, 1)


def lane_iota(rows):
    return lax.broadcasted_iota(jnp.int32, (rows, LANES), 1)


def gauge_rows(owned):
    if 3 * owned <= LANES:
        return STEPS_BLOCK, owned
    assert owned <= LANES
    return 3 * STEPS_BLOCK, 0


def my_place():
    row = lax.axis_index("lat") * lax.axis_size("gau") + lax.axis_index("gau")
    return row, lax.axis_index("lon"), lax.axis_size("lat") * lax.axis_size("gau"), lax.axis_size("lon")


def give_west(reach, keep_ref, gain_ref, west_ref):
    lower = lane_iota(west_ref.shape[1]) < reach
    west_ref[0] = jnp.where(lower, keep_ref[:, :LANES], roll_lanes(gain_ref[:, :LANES], reach))
    for spare in range(1, west_ref.shape[0]):
        west_ref[spare] = jnp.zeros(west_ref.shape[1:], jnp.float32)


def give_rows(halo, keep_ref, gain_ref, right_ref, far_ref, near_ref):
    height, width = keep_ref.shape
    lower = lane_iota(halo) < 2 * halo
    odd = my_place()[0] & 1
    for goal, south in ((far_ref, odd), (near_ref, 1 - odd)):
        rows = pl.ds(pl.multiple_of(south * (height - halo), halo), halo)
        for kind, source in enumerate((keep_ref, gain_ref)):
            goal[kind, :, :width] = source[rows, :]
            goal[kind, :, width:] = jnp.where(lower, roll_lanes(right_ref[0, rows, :], -2 * halo * kind), 0.0)


def give_gauges(height, width, blocks, samples, coast_count, gauge_ref, after_ref, parcel_ref, block_ref):
    row_tiles = lax.axis_size("lat") * lax.axis_size("gau")
    owned = gauge_ref.shape[2]
    assert blocks == 2
    route, cell, coast = (gauge_ref[2 * blocks, i : i + 1, :].astype(jnp.int32) for i in range(3))
    target = jnp.zeros_like(route)
    for entry in range(coast_count):
        target = jnp.where(route == entry, jnp.broadcast_to(coast[:, entry : entry + 1], route.shape), target)
    row_bits, width_bits = int(math.log2(row_tiles)), int(math.log2(width))
    assert row_tiles == 1 << row_bits and width == 1 << width_bits
    grid_row = (target & (row_tiles - 1)) * height + (cell >> width_bits)
    grid_col = (target >> row_bits) * width + (cell & (width - 1))
    block_ref[...] = jnp.zeros_like(block_ref)
    levels = lax.broadcasted_iota(jnp.int32, (STEPS_BLOCK, owned), 0).astype(jnp.float32)
    for block in range(blocks):
        series = jnp.zeros((STEPS_BLOCK, owned), jnp.float32)
        for sample in range(samples):
            times = gauge_ref[block, sample : sample + 1, :]
            resid = gauge_ref[blocks + block, sample : sample + 1, :]
            series = series + jnp.where(times == levels, resid, 0.0)
        block_ref[block * STEPS_BLOCK : (block + 1) * STEPS_BLOCK, :owned] = series
    at = blocks * STEPS_BLOCK
    block_ref[at : at + 1, :owned] = grid_row.astype(jnp.float32)
    block_ref[at + 1 : at + 2, :owned] = grid_col.astype(jnp.float32)
    size, apart = gauge_rows(owned)
    gauges = block_ref[...]
    if size == STEPS_BLOCK:
        gauges = sum(
            roll_lanes(gauges[i * STEPS_BLOCK : (i + 1) * STEPS_BLOCK], i * apart) for i in range(3)
        )
    tiles = parcel_ref.shape[0]

    def put(tile, carry):
        parcel_ref[tile, 0:size, :] = gauges
        return carry

    lax.fori_loop(0, tiles, put, 0, unroll=tiles <= 16)


def from_rolled(rolled, shift, lanes):
    count = len(rolled)
    if shift > 0:
        return [jnp.where(lanes >= LANES - shift, rolled[(c + 1) % count], rolled[c]) for c in range(count)]
    return [jnp.where(lanes < -shift, rolled[(c - 1) % count], rolled[c]) for c in range(count)]


def shift_from(planes, shift, lanes):
    return from_rolled([roll_lanes(plane, -shift) for plane in planes], shift, lanes)


def force(steps, halo, height, width, parcel_ref, force_ref, series_ref, rows_hot, cols_hot):
    planes, rows_all = force_ref.shape[1], height + 2 * halo
    my_row, my_lon, row_tiles, lons = my_place()
    wide = rows_hot.shape[1]
    tiles, parcel_rows = parcel_ref.shape[:2]
    size = parcel_rows
    apart = wide // tiles if size == STEPS_BLOCK else 0
    owned = apart if apart else LANES
    group = wide // owned
    groups = tiles // group
    per_plane = LANES // owned
    blocks = rows_all // 8
    row_shift = (halo - my_row * height).astype(jnp.float32)
    col_shift = (-my_lon * width).astype(jnp.float32)
    place = lax.broadcasted_iota(jnp.int32, (rows_all, LANES), 0)
    at = ((place & 7) * blocks + (place >> 3)).astype(jnp.float32)

    def gather_gauges(index):
        lanes = lane_iota(STEPS_BLOCK)
        for part in range(wide // LANES):
            cols = slice(part * LANES, (part + 1) * LANES)
            fields = []
            for field in range(3):
                total = jnp.zeros((STEPS_BLOCK, LANES), jnp.float32)
                rows = slice(0, 8) if apart else slice(8 * field, 8 * field + 8)
                for i in range(per_plane):
                    source = index * group + part * per_plane + i
                    block = roll_lanes(parcel_ref[source, rows, :], i * owned - field * apart)
                    total = jnp.where((lanes >= i * owned) & (lanes < (i + 1) * owned), block, total)
                fields.append(total)
            series_ref[0:8, cols] = fields[0]
            series_ref[8:16, cols] = fields[1]
            row = fields[2][0:1] + row_shift
            col = fields[2][1:2] + col_shift
            col = jnp.where(col < width + 2 * halo, col, -1.0)
            rows_hot[:, cols] = (at == row).astype(jnp.float32).astype(jnp.bfloat16)
            by_gauge = jnp.transpose(jnp.broadcast_to(col, (LANES, LANES)))
            for c in range(planes):
                spot = (lane_iota(LANES) + c * LANES).astype(jnp.float32)
                hot = (by_gauge == spot).astype(jnp.float32).astype(jnp.bfloat16)
                cols_hot[part * LANES : (part + 1) * LANES, c * LANES : (c + 1) * LANES] = hot
                cols_hot[wide + part * LANES : wide + (part + 1) * LANES, c * LANES : (c + 1) * LANES] = hot

    def levels_of(start, add):
        hot = rows_hot[...]
        both = []
        for level in range(LEVELS):
            value = series_ref[pl.ds(start + level, 1), :]
            high = value.astype(jnp.bfloat16)
            low = (value - high.astype(jnp.float32)).astype(jnp.bfloat16)
            both.append(jnp.concatenate([hot * high, hot * low], axis=1))
        both = jnp.concatenate(both, axis=0)
        for first in range(0, planes, 2):
            count = min(2, planes - first)
            total = jnp.dot(
                both, cols_hot[:, first * LANES : (first + count) * LANES], preferred_element_type=jnp.float32
            )
            for level in range(LEVELS):
                for c in range(count):
                    part = total[level * rows_all : (level + 1) * rows_all, c * LANES : (c + 1) * LANES]
                    goal = (start + level, first + c, slice(0, rows_all))
                    force_ref[goal] = force_ref[goal] + part if add else part

    def levels(add):
        def one(index, carry):
            levels_of(index * LEVELS, add)
            return carry

        lax.fori_loop(0, steps // LEVELS, one, 0)

    force_ref[steps] = jnp.zeros_like(force_ref[steps])
    gather_gauges(0)
    levels(False)
    if groups > 1:

        def more(index, carry):
            gather_gauges(index)
            levels(True)
            return carry

        lax.fori_loop(1, groups, more, 0)


def sweep(
    steps, keep_ref, gain_ref, far_ref, near_ref, right_ref, force_ref,
    grad_ref, sums_ref,
    a, fx, fy, keep_y, gain_y, plain,
):
    height, width = keep_ref.shape
    halo = 2 * steps
    inner = width // LANES
    planes = inner + 1
    rows_all = height + 2 * halo
    blocks = rows_all // 8
    my_row, my_lon, row_tiles, lons = my_place()
    reach = 2 * halo
    has_top, has_bottom = my_row > 0, my_row < row_tiles - 1
    has_right = my_lon < lons - 1
    odd = (jnp.zeros((halo, LANES), jnp.int32) + (my_row & 1)) == 1
    lanes8 = lane_iota(8)

    def up(value):
        return pltpu.roll(value, 7, 0)

    def down(value):
        return pltpu.roll(value, 1, 0)

    for kind, (source, by_y) in enumerate(((keep_ref, keep_y), (gain_ref, gain_y))):
        for c in range(planes):
            cols = slice(c * LANES, (c + 1) * LANES)
            far, near = far_ref[kind, :, cols], near_ref[kind, :, cols]
            plain[c, 0:halo, :] = jnp.where(odd, near, far)
            plain[c, halo + height : rows_all, :] = jnp.where(odd, far, near)
            if c < inner:
                plain[c, halo : halo + height, :] = source[:, cols]
        lower = lane_iota(height) < reach
        plain[inner, halo : halo + height, :] = jnp.where(lower, roll_lanes(right_ref[0], -reach * kind), 0.0)
        for q in range(blocks):
            to = (q - 1) % blocks * 8
            for c in range(planes):
                value = plain[c, pl.ds(q, 8, stride=blocks), :]
                by_y[c, to : to + 8, :] = up(value) if q == 0 else value

    col_mask = jnp.where(lanes8 < reach, jnp.where(has_right, 1.0, 0.0), 0.0)
    sublane = lax.broadcasted_iota(jnp.int32, (8, LANES), 0)
    row_mask = {}
    for row, there in ((halo - 1, has_top), (halo + height, has_bottom)):
        row_mask[row % blocks] = jnp.where(sublane == row // blocks, jnp.where(there, 1.0, 0.0), 1.0)
    every = range(planes)

    fx[...] = jnp.zeros_like(fx)
    fy[...] = jnp.zeros_like(fy)
    a[:, 0:rows_all, :] = force_ref[steps - 1, :, 0:rows_all, :]

    def step(index, carry):
        level = jnp.where(index < steps - 1, steps - 2 - index, steps)
        near, ahead, new_y, beside, total, behind = {}, {}, {}, {}, {}, {}

        def rows(q):
            return slice(8 * q, 8 * q + 8)

        def first(q):
            near[q] = [a[c, rows(q % blocks), :] for c in every]
            if q < blocks:
                ahead[q] = [roll_lanes(value, -2) for value in near[q]]
            else:
                near[q] = [up(value) for value in near[q]]

        def second_y(q):
            keep, gain = ([ref[c, rows(q), :] for c in every] for ref in (keep_y, gain_y))
            new_y[q] = [keep[c] * fy[c, rows(q), :] + gain[c] * (near[q + 2][c] - near[q][c]) for c in every]
            for c in every:
                fy[c, rows(q), :] = new_y[q][c]
            beside[q + 1] = [[roll_lanes(value, -1) for value in part] for part in (keep, gain)]

        def second_x(q):
            keep, gain = (from_rolled(part, 1, lanes8) for part in beside[q])
            far = from_rolled(ahead[q], 2, lanes8)
            new_x = [keep[c] * fx[c, rows(q), :] + gain[c] * (far[c] - near[q][c]) for c in every]
            behind[q] = [roll_lanes(value, 2) for value in new_x]
            before = new_y[q - 2] if q >= 2 else [down(fy[c, rows(q - 2 + blocks), :]) for c in every]
            push = [force_ref[level, c, rows(q), :] for c in every]
            total[q] = [(near[q][c] + push[c]) + (new_y[q][c] - before[c]) + new_x[c] for c in every]
            for c in every:
                fx[c, rows(q), :] = new_x[c]

        def third(q):
            far = from_rolled(behind[q], -2, lanes8)
            for c in every:
                value = total[q][c] - far[c]
                if c == inner:
                    value = value * col_mask
                if q in row_mask:
                    value = value * row_mask[q]
                a[c, rows(q), :] = value

        for q in range(4):
            first(q)
        second_y(0)
        second_y(1)
        for q in range(2, blocks):
            first(q + 2)
            second_y(q)
            second_x(q)
            if q > 2:
                third(q - 1)
        for q in range(2):
            first(q)
            new_y[q] = [fy[c, rows(q), :] for c in every]
            keep, gain = ([ref[c, rows((q - 1) % blocks), :] for c in every] for ref in (keep_y, gain_y))
            if q == 0:
                keep, gain = ([down(value) for value in part] for part in (keep, gain))
            beside[q] = [[roll_lanes(value, -1) for value in part] for part in (keep, gain)]
        for q in range(2):
            second_x(q)
            third(q - 1 if q else blocks - 1)
        third(1)
        return carry

    lax.fori_loop(0, steps, step, 0)

    start = jnp.where(my_lon > 0, halo, 0)
    for r in range(0, height, 8):
        s, q = divmod(halo + r, blocks)
        for c in every:
            cols = slice(c * LANES, (c + 1) * LANES)
            value = a[c, pl.ds(8 * q + s, 8, stride=8), :]
            wet = keep_ref[r : r + 8, cols] if c < inner else right_ref[0, r : r + 8, :]
            if c == 0:
                wet = jnp.where(lanes8 >= start, wet, 0.0)
            if c == inner:
                wet = jnp.where(lanes8 < halo, wet, 0.0)
            grad_ref[r : r + 8, cols] = jnp.where(wet > 0.0, value, 0.0)
    length = 2.0 * width
    shape = (8 + halo, planes * LANES)
    kind, column = lax.broadcasted_iota(jnp.int32, shape, 0), lax.broadcasted_iota(jnp.int32, shape, 1)
    beyond = column - width
    off = jnp.where(kind == 0, column, jnp.where(kind == 1, -1 - beyond, jnp.where(kind == 2, beyond, width - 1 - beyond)))
    mine = ((kind < 2) & (beyond < 0)) | ((kind >= 2) & (kind < 4) & (beyond >= 0))
    weights = jnp.where(mine, jnp.exp(-jnp.maximum(off, 0).astype(jnp.float32) / length), 0.0)
    weights = jnp.where((kind >= 8) & (beyond == kind - 8), 1.0, weights)
    sums = lax.dot_general(
        weights, grad_ref[...], (((1,), (1,)), ((), ())), precision=lax.Precision.HIGHEST,
        preferred_element_type=jnp.float32,
    )
    for i in range(sums_ref.shape[0]):
        sums_ref[i] = sums


def smooth(halo, lons, grad_ref, out_ref, weights_ref):
    width = out_ref.shape[1]
    length = 2.0 * width
    row = lax.broadcasted_iota(jnp.int32, (width, width), 0)
    column = lax.broadcasted_iota(jnp.int32, (width, width), 1)
    kernel = jnp.exp(-jnp.abs(row - column).astype(jnp.float32) / length)
    out_ref[...] = jnp.dot(
        grad_ref[:, :width], kernel, precision=lax.Precision.HIGHEST, preferred_element_type=jnp.float32
    )
    me = lax.axis_index("lon")
    shape = (8 + halo, width)
    kind, column = lax.broadcasted_iota(jnp.int32, shape, 0), lax.broadcasted_iota(jnp.int32, shape, 1)
    for source in range(lons):
        strip = jnp.where(kind < 2, source, source + 1)
        left = ((kind == 0) | (kind == 2)) & (strip > me)
        right = ((kind == 1) | (kind == 3)) & (strip < me)
        near = (kind >= 8) & (source + 1 == me)
        away = jnp.where(left, (strip - me) * width - column, (me - strip - 1) * width + column + 1)
        away = jnp.where(near, jnp.abs(kind - 8 - column), away)
        weights = jnp.where(left | right | near, jnp.exp(-jnp.maximum(away, 0).astype(jnp.float32) / length), 0.0)
        weights_ref[source * shape[0] : (source + 1) * shape[0], :] = weights


def finish(own_ref, weights_ref, sums_ref, out_ref):
    out_ref[...] = own_ref[...] + lax.dot_general(
        sums_ref[...], weights_ref[...], (((0,), (0,)), ((), ())), precision=lax.Precision.HIGHEST,
        preferred_element_type=jnp.float32,
    )


def f32(*shape):
    return jax.ShapeDtypeStruct(shape, jnp.float32)


def hint(megabytes):
    return pl.CostEstimate(flops=0, bytes_accessed=megabytes * 1000 * 1000, transcendentals=0)


def spaced(rows):
    return 8 * (rows // 8 | 1)


def vmem(count):
    return [pl.BlockSpec(memory_space=pltpu.VMEM)] * count


def local(depth, surface, friction, wet, coastal_tiles, gauge_route, gauge_cell, gauge_times, gauge_resid):
    height, width = depth.shape
    owned = gauge_route.shape[0]
    blocks = gauge_resid.shape[1]
    steps = blocks * STEPS_BLOCK
    halo = 2 * steps
    assert halo == SEG and height == LANES
    tiles = lax.axis_size(GRID_AXES)
    lons = lax.axis_size("lon")
    row_tiles = lax.axis_size(ROW_AXES)
    planes = width // LANES + 1
    rows_all = height + 2 * halo
    params = pltpu.CompilerParams(vmem_limit_bytes=VMEM_LIMIT)

    keep = (1.0 - friction) * wet.astype(jnp.float32)
    gain = ((courant * 0.5) ** 2 * jnp.maximum(depth + surface, depth_floor)) * keep
    samples, coast_count = gauge_resid.shape[2], coastal_tiles.shape[0]
    assert coast_count <= owned

    assert samples >= 3

    def put(array, group, row):
        groups, rows, lanes = array.shape
        return jnp.pad(array, ((group, 2 * blocks + 1 - group - groups), (row, samples - row - rows), (0, owned - lanes)))

    gauges = (
        put(jnp.transpose(gauge_times, (1, 2, 0)), 0, 0)
        + put(gauge_route.reshape(1, 1, owned), 2 * blocks, 0)
        + put(gauge_cell.reshape(1, 1, owned), 2 * blocks, 1)
        + put(coastal_tiles.reshape(1, 1, coast_count), 2 * blocks, 2)
    ).astype(jnp.float32) + put(jnp.transpose(gauge_resid, (1, 2, 0)), blocks, 0)
    west = pl.pallas_call(
        functools.partial(give_west, 2 * halo), out_shape=f32(4, height, LANES), in_specs=vmem(2), out_specs=vmem(1)[0],
        compiler_params=params, name="give_west",
    )(keep, gain)
    right = lax.ppermute(west, "lon", [(i + 1, i) for i in range(lons - 1)])

    parcel = pl.pallas_call(
        functools.partial(give_gauges, height, width, blocks, samples, coast_count),
        out_shape=f32(tiles, gauge_rows(owned)[0], LANES),
        in_specs=vmem(1) + [pl.BlockSpec(memory_space=pl.ANY)],
        out_specs=vmem(1)[0],
        scratch_shapes=[pltpu.VMEM((24, LANES), jnp.float32)],
        compiler_params=params,
        cost_estimate=hint(10),
        name="give_gauges",
    )(gauges, west)

    def exchange(array, axes, groups=None):
        return lax.all_to_all(array, axes, split_axis=0, concat_axis=0, axis_index_groups=groups, tiled=True)

    group = sorted(range(tiles), key=lambda tile: (tile % row_tiles in (0, row_tiles - 1), -(tile // row_tiles)))
    parcel = exchange(parcel, GRID_AXES, [group])

    far, near = pl.pallas_call(
        functools.partial(give_rows, halo), out_shape=(f32(2, halo, planes * LANES),) * 2, in_specs=vmem(3),
        out_specs=tuple(vmem(2)), compiler_params=params, cost_estimate=hint(40), name="give_rows",
    )(keep, gain, right)
    far = lax.ppermute(far, ROW_AXES, [pair for i in range(1, row_tiles - 1, 2) for pair in ((i, i + 1), (i + 1, i))])
    near = lax.ppermute(near, ROW_AXES, [pair for i in range(0, row_tiles, 2) for pair in ((i, i + 1), (i + 1, i))])

    wide = max(2 * LANES, owned)
    pushes = pl.pallas_call(
        functools.partial(force, steps, halo, height, width),
        out_shape=f32(steps + 1, planes, spaced(rows_all), LANES),
        in_specs=vmem(1),
        out_specs=vmem(1)[0],
        scratch_shapes=[
            pltpu.VMEM((steps, wide), jnp.float32),
            pltpu.VMEM((rows_all, wide), jnp.bfloat16),
            pltpu.VMEM((2 * wide, planes * LANES), jnp.bfloat16),
        ],
        compiler_params=params,
        cost_estimate=pl.CostEstimate(
            flops=4 * steps * rows_all * wide * planes * LANES, bytes_accessed=4 * steps * planes * rows_all * LANES,
            transcendentals=0,
        ),
        name="force",
    )(parcel)

    plane = pltpu.VMEM((planes, spaced(rows_all), LANES), jnp.float32)
    grad, sums = pl.pallas_call(
        functools.partial(sweep, steps),
        out_shape=(f32(height, planes * LANES), f32(lons, 8 + halo, height)),
        in_specs=vmem(6),
        out_specs=tuple(vmem(2)),
        scratch_shapes=[plane] * 6,
        compiler_params=params,
        name="sweep",
    )(keep, gain, far, near, right, pushes)

    sums = exchange(sums, "lon")
    own, weights = pl.pallas_call(
        functools.partial(smooth, halo, lons),
        out_shape=(f32(height, width), f32(lons * (8 + halo), width)),
        in_specs=vmem(1),
        out_specs=tuple(vmem(2)),
        compiler_params=params,
        cost_estimate=pl.CostEstimate(
            flops=6 * 2 * height * width * width, bytes_accessed=2 * 4 * height * width, transcendentals=width * width
        ),
        name="smooth",
    )(grad)
    return pl.pallas_call(
        finish, out_shape=f32(height, width), in_specs=vmem(3), out_specs=vmem(1)[0], compiler_params=params, name="finish",
    )(own, weights, sums.reshape(lons * (8 + halo), height))


def solution(mesh):
    in_specs = (
        P(("lat", "gau"), "lon"),
        P(("scen", "lat", "gau"), "lon"),
        P(("lat", "gau"), "lon"),
        P(("lat", "gau"), "lon"),
        P(),
        P(("scen", "lon", "lat", "gau"), None),
        P(("scen", "lon", "lat", "gau")),
        P(("scen", "lon", "lat", "gau"), None, None),
        P(("scen", "lon", "lat", "gau"), None, None),
    )
    out_specs = P(("scen", "lat", "gau"), "lon")
    return jax.shard_map(local, mesh=mesh, in_specs=in_specs, out_specs=out_specs, check_vma=False)
```

```python
import functools
import math

import jax
import jax.numpy as jnp
from jax import lax
from jax.experimental import pallas as pl
from jax.experimental.pallas import tpu as pltpu
from jax.sharding import PartitionSpec as P

STEPS_BLOCK = 8
LANES = 128
SEG = 32
LEVELS = 4

courant = 0.45
depth_floor = 0.1

GRID_AXES = ("lon", "lat", "gau")
ROW_AXES = ("lat", "gau")
VMEM_LIMIT = 16 * 1024 * 1024


def roll_lanes(x, shift):
    shift = shift % LANES
    return x if shift == 0 else pltpu.roll(x, shift, 1)


def lane_iota(rows):
    return lax.broadcasted_iota(jnp.int32, (rows, LANES), 1)


def gauge_rows(owned):
    if 3 * owned <= LANES:
        return STEPS_BLOCK, owned
    assert owned <= LANES
    return 3 * STEPS_BLOCK, 0


def my_place():
    row = lax.axis_index("lat") * lax.axis_size("gau") + lax.axis_index("gau")
    return row, lax.axis_index("lon"), lax.axis_size("lat") * lax.axis_size("gau"), lax.axis_size("lon")


def give_west(reach, keep_ref, gain_ref, west_ref):
    lower = lane_iota(west_ref.shape[1]) < reach
    west_ref[0] = jnp.where(lower, keep_ref[:, :LANES], roll_lanes(gain_ref[:, :LANES], reach))
    for spare in range(1, west_ref.shape[0]):
        west_ref[spare] = jnp.zeros(west_ref.shape[1:], jnp.float32)


def give_rows(halo, keep_ref, gain_ref, right_ref, far_ref, near_ref):
    height, width = keep_ref.shape
    lower = lane_iota(halo) < 2 * halo
    odd = my_place()[0] & 1
    for goal, south in ((far_ref, odd), (near_ref, 1 - odd)):
        rows = pl.ds(pl.multiple_of(south * (height - halo), halo), halo)
        for kind, source in enumerate((keep_ref, gain_ref)):
            goal[kind, :, :width] = source[rows, :]
            goal[kind, :, width:] = jnp.where(lower, roll_lanes(right_ref[0, rows, :], -2 * halo * kind), 0.0)


def give_gauges(height, width, blocks, samples, coast_count, gauge_ref, after_ref, parcel_ref, block_ref):
    row_tiles = lax.axis_size("lat") * lax.axis_size("gau")
    owned = gauge_ref.shape[2]
    assert blocks == 2
    route, cell, coast = (gauge_ref[2 * blocks, i : i + 1, :].astype(jnp.int32) for i in range(3))
    target = jnp.zeros_like(route)
    for entry in range(coast_count):
        target = jnp.where(route == entry, jnp.broadcast_to(coast[:, entry : entry + 1], route.shape), target)
    row_bits, width_bits = int(math.log2(row_tiles)), int(math.log2(width))
    assert row_tiles == 1 << row_bits and width == 1 << width_bits
    grid_row = (target & (row_tiles - 1)) * height + (cell >> width_bits)
    grid_col = (target >> row_bits) * width + (cell & (width - 1))
    block_ref[...] = jnp.zeros_like(block_ref)
    levels = lax.broadcasted_iota(jnp.int32, (STEPS_BLOCK, owned), 0).astype(jnp.float32)
    for block in range(blocks):
        series = jnp.zeros((STEPS_BLOCK, owned), jnp.float32)
        for sample in range(samples):
            times = gauge_ref[block, sample : sample + 1, :]
            resid = gauge_ref[blocks + block, sample : sample + 1, :]
            series = series + jnp.where(times == levels, resid, 0.0)
        block_ref[block * STEPS_BLOCK : (block + 1) * STEPS_BLOCK, :owned] = series
    at = blocks * STEPS_BLOCK
    block_ref[at : at + 1, :owned] = grid_row.astype(jnp.float32)
    block_ref[at + 1 : at + 2, :owned] = grid_col.astype(jnp.float32)
    size, apart = gauge_rows(owned)
    gauges = block_ref[...]
    if size == STEPS_BLOCK:
        gauges = sum(
            roll_lanes(gauges[i * STEPS_BLOCK : (i + 1) * STEPS_BLOCK], i * apart) for i in range(3)
        )
    tiles = parcel_ref.shape[0]

    def put(tile, carry):
        parcel_ref[tile, 0:size, :] = gauges
        return carry

    lax.fori_loop(0, tiles, put, 0, unroll=tiles <= 16)


def dealt_column(place, planes):
    return (place & (LANES - 1)) * planes + place // LANES


def force(steps, halo, height, width, parcel_ref, force_ref, series_ref, rows_hot, cols_hot):
    planes, rows_all = force_ref.shape[1], height + 2 * halo
    my_row, my_lon, row_tiles, lons = my_place()
    wide = rows_hot.shape[1]
    tiles, parcel_rows = parcel_ref.shape[:2]
    size = parcel_rows
    apart = wide // tiles if size == STEPS_BLOCK else 0
    owned = apart if apart else LANES
    group = wide // owned
    groups = tiles // group
    per_plane = LANES // owned
    blocks = rows_all // 8
    row_shift = (halo - my_row * height).astype(jnp.float32)
    col_shift = (-my_lon * width).astype(jnp.float32)
    place = lax.broadcasted_iota(jnp.int32, (rows_all, LANES), 0)
    at = ((place & 7) * blocks + (place >> 3)).astype(jnp.float32)

    def gather_gauges(index):
        lanes = lane_iota(STEPS_BLOCK)
        for part in range(wide // LANES):
            cols = slice(part * LANES, (part + 1) * LANES)
            fields = []
            for field in range(3):
                total = jnp.zeros((STEPS_BLOCK, LANES), jnp.float32)
                rows = slice(0, 8) if apart else slice(8 * field, 8 * field + 8)
                for i in range(per_plane):
                    source = index * group + part * per_plane + i
                    block = roll_lanes(parcel_ref[source, rows, :], i * owned - field * apart)
                    total = jnp.where((lanes >= i * owned) & (lanes < (i + 1) * owned), block, total)
                fields.append(total)
            series_ref[0:8, cols] = fields[0]
            series_ref[8:16, cols] = fields[1]
            row = fields[2][0:1] + row_shift
            col = fields[2][1:2] + col_shift
            col = jnp.where(col < width + 2 * halo, col, -1.0)
            rows_hot[:, cols] = (at == row).astype(jnp.float32).astype(jnp.bfloat16)
            by_gauge = jnp.transpose(jnp.broadcast_to(col, (LANES, LANES)))
            for c in range(planes):
                spot = (lane_iota(LANES) * planes + c).astype(jnp.float32)
                hot = (by_gauge == spot).astype(jnp.float32).astype(jnp.bfloat16)
                cols_hot[part * LANES : (part + 1) * LANES, c * LANES : (c + 1) * LANES] = hot
                cols_hot[wide + part * LANES : wide + (part + 1) * LANES, c * LANES : (c + 1) * LANES] = hot

    def levels_of(start, add):
        hot = rows_hot[...]
        both = []
        for level in range(LEVELS):
            value = series_ref[pl.ds(start + level, 1), :]
            high = value.astype(jnp.bfloat16)
            low = (value - high.astype(jnp.float32)).astype(jnp.bfloat16)
            both.append(jnp.concatenate([hot * high, hot * low], axis=1))
        both = jnp.concatenate(both, axis=0)
        for first in range(0, planes, 2):
            count = min(2, planes - first)
            total = jnp.dot(
                both, cols_hot[:, first * LANES : (first + count) * LANES], preferred_element_type=jnp.float32
            )
            for level in range(LEVELS):
                for c in range(count):
                    part = total[level * rows_all : (level + 1) * rows_all, c * LANES : (c + 1) * LANES]
                    goal = (start + level, first + c, slice(0, rows_all))
                    force_ref[goal] = force_ref[goal] + part if add else part

    def levels(add):
        def one(index, carry):
            levels_of(index * LEVELS, add)
            return carry

        lax.fori_loop(0, steps // LEVELS, one, 0)

    force_ref[steps] = jnp.zeros_like(force_ref[steps])
    gather_gauges(0)
    levels(False)
    if groups > 1:

        def more(index, carry):
            gather_gauges(index)
            levels(True)
            return carry

        lax.fori_loop(1, groups, more, 0)


def sweep(
    steps, keep_ref, gain_ref, far_ref, near_ref, right_ref, force_ref,
    grad_ref, sums_ref,
    a, fx, fy, keeps, gains, plain,
):
    height, width = keep_ref.shape
    halo = 2 * steps
    inner = width // LANES
    planes = inner + 1
    rows_all = height + 2 * halo
    blocks = rows_all // 8
    my_row, my_lon, row_tiles, lons = my_place()
    reach = 2 * halo
    has_top, has_bottom = my_row > 0, my_row < row_tiles - 1
    has_right = my_lon < lons - 1
    odd = (jnp.zeros((halo, planes * LANES), jnp.int32) + (my_row & 1)) == 1
    lanes8 = lane_iota(8)

    def up(value):
        return pltpu.roll(value, 7, 0)

    def down(value):
        return pltpu.roll(value, 1, 0)

    every = range(planes)
    columns = planes * LANES

    parts = []
    for kind, source in enumerate((keep_ref, gain_ref)):
        far, near = far_ref[kind], near_ref[kind]
        beside = jnp.where(lane_iota(height) < reach, roll_lanes(right_ref[0], -reach * kind), 0.0)
        whole = jnp.concatenate(
            [
                jnp.where(odd, near, far),
                jnp.concatenate([source[...], beside], axis=1),
                jnp.where(odd, far, near),
            ],
            axis=0,
        )
        high = whole.astype(jnp.bfloat16)
        parts += [high, (whole - high.astype(jnp.float32)).astype(jnp.bfloat16)]
    parts = jnp.concatenate(parts, axis=0)
    shape = (columns, LANES)
    column = lax.broadcasted_iota(jnp.int32, shape, 0)
    for c in every:
        deal = (column == lax.broadcasted_iota(jnp.int32, shape, 1) * planes + c).astype(jnp.float32)
        dealt = jnp.dot(parts, deal.astype(jnp.bfloat16), preferred_element_type=jnp.float32)
        for kind in range(2):
            at = 2 * kind * rows_all
            plain[kind, c, 0:rows_all, :] = dealt[at : at + rows_all] + dealt[at + rows_all : at + 2 * rows_all]
    for kind, goal in enumerate((keeps, gains)):
        for q in range(blocks):
            for c in every:
                value = plain[kind, c, pl.ds(q, 8, stride=blocks), :]
                goal[c, 8 * q : 8 * q + 8, :] = value
                if q == 0:
                    goal[c, 8 * blocks : 8 * blocks + 8, :] = up(value)
                if c == 0:
                    goal[planes, 8 * q : 8 * q + 8, :] = roll_lanes(value, -1)

    def cell_mask(column, there):
        lane, plane = column // planes, column % planes
        return plane, jnp.where(lanes8 == lane, there, 1.0)

    column_mask = dict([cell_mask(width, jnp.where(has_right, 1.0, 0.0)), cell_mask(columns - 1, 0.0)])
    assert len(column_mask) == 2
    sublane = lax.broadcasted_iota(jnp.int32, (8, LANES), 0)
    row_mask = {}
    for row, there in ((halo - 1, has_top), (halo + height, has_bottom)):
        row_mask[row % blocks] = jnp.where(sublane == row // blocks, jnp.where(there, 1.0, 0.0), 1.0)

    fx[...] = jnp.zeros_like(fx)
    fy[...] = jnp.zeros_like(fy)
    a[:, 0:rows_all, :] = force_ref[steps - 1, :, 0:rows_all, :]

    def step(index, carry):
        level = jnp.where(index < steps - 1, steps - 2 - index, steps)
        near, ahead, new_y, beside, total, behind = {}, {}, {}, {}, {}, {}

        def rows(q):
            return slice(8 * q, 8 * q + 8)

        def first(q):
            near[q] = [a[c, rows(q % blocks), :] for c in every]
            if q < blocks:
                ahead[q] = near[q][2:] + [roll_lanes(value, -1) for value in near[q][:2]]
            else:
                near[q] = [up(value) for value in near[q]]

        def coefficients(q):
            return [[ref[c, rows(q), :] for c in range(planes + 1)] for ref in (keeps, gains)]

        def second_y(q):
            beside[q + 1] = keep, gain = coefficients(q + 1)
            new_y[q] = [keep[c] * fy[c, rows(q), :] + gain[c] * (near[q + 2][c] - near[q][c]) for c in every]
            for c in every:
                fy[c, rows(q), :] = new_y[q][c]

        def second_x(q):
            keep, gain = beside[q]
            new_x = [
                keep[c + 1] * fx[c, rows(q), :] + gain[c + 1] * (ahead[q][c] - near[q][c]) for c in every
            ]
            behind[q] = [roll_lanes(value, 1) for value in new_x[-2:]] + new_x[:-2]
            before = new_y[q - 2] if q >= 2 else [down(fy[c, rows(q - 2 + blocks), :]) for c in every]
            push = [force_ref[level, c, rows(q), :] for c in every]
            total[q] = [(near[q][c] + push[c]) + (new_y[q][c] - before[c]) + new_x[c] for c in every]
            for c in every:
                fx[c, rows(q), :] = new_x[c]

        def third(q):
            for c in every:
                value = total[q][c] - behind[q][c]
                if c in column_mask:
                    value = value * column_mask[c]
                if q in row_mask:
                    value = value * row_mask[q]
                a[c, rows(q), :] = value

        for q in range(4):
            first(q)
        second_y(0)
        second_y(1)
        for q in range(2, blocks):
            first(q + 2)
            second_y(q)
            second_x(q)
            if q > 2:
                third(q - 1)
        for q in range(2):
            first(q)
            new_y[q] = [fy[c, rows(q), :] for c in every]
            beside[q] = coefficients(q)
        for q in range(2):
            second_x(q)
            third(q - 1 if q else blocks - 1)
        third(1)
        return carry

    lax.fori_loop(0, steps, step, 0)

    start = jnp.where(my_lon > 0, halo, 0)
    for c in every:
        column = lanes8 * planes + c
        known = (column >= start) & (column < width + halo)
        for r in range(0, height, 8):
            s, q = divmod(halo + r, blocks)
            strided = pl.ds(8 * q + s, 8, stride=8)
            value = jnp.where(known & (keeps[c, strided, :] > 0.0), a[c, strided, :], 0.0)
            grad_ref[r : r + 8, c * LANES : (c + 1) * LANES] = value
    length = 2.0 * width
    shape = (8 + halo, planes * LANES)
    kind = lax.broadcasted_iota(jnp.int32, shape, 0)
    column = dealt_column(lax.broadcasted_iota(jnp.int32, shape, 1), planes)
    beyond = column - width
    off = jnp.where(kind == 0, column, jnp.where(kind == 1, -1 - beyond, jnp.where(kind == 2, beyond, width - 1 - beyond)))
    mine = ((kind < 2) & (beyond < 0)) | ((kind >= 2) & (kind < 4) & (beyond >= 0))
    weights = jnp.where(mine, jnp.exp(-jnp.maximum(off, 0).astype(jnp.float32) / length), 0.0)
    weights = jnp.where((kind >= 8) & (beyond == kind - 8), 1.0, weights)
    sums = lax.dot_general(
        weights, grad_ref[...], (((1,), (1,)), ((), ())), precision=lax.Precision.HIGHEST,
        preferred_element_type=jnp.float32,
    )
    for i in range(sums_ref.shape[0]):
        sums_ref[i] = sums


def smooth(halo, lons, grad_ref, out_ref, weights_ref):
    width = out_ref.shape[1]
    length = 2.0 * width
    planes = grad_ref.shape[1] // LANES
    column = lax.broadcasted_iota(jnp.int32, (LANES, width), 1)
    lane = lax.broadcasted_iota(jnp.int32, (LANES, width), 0)
    sources = [lane * planes + c for c in range(planes)]
    kernel = jnp.concatenate(
        [jnp.where(x < width, jnp.exp(-jnp.abs(x - column).astype(jnp.float32) / length), 0.0) for x in sources], axis=0
    )
    out_ref[...] = jnp.dot(
        grad_ref[...], kernel, precision=lax.Precision.HIGHEST, preferred_element_type=jnp.float32
    )
    me = lax.axis_index("lon")
    shape = (8 + halo, width)
    kind, column = lax.broadcasted_iota(jnp.int32, shape, 0), lax.broadcasted_iota(jnp.int32, shape, 1)
    for source in range(lons):
        strip = jnp.where(kind < 2, source, source + 1)
        left = ((kind == 0) | (kind == 2)) & (strip > me)
        right = ((kind == 1) | (kind == 3)) & (strip < me)
        near = (kind >= 8) & (source + 1 == me)
        away = jnp.where(left, (strip - me) * width - column, (me - strip - 1) * width + column + 1)
        away = jnp.where(near, jnp.abs(kind - 8 - column), away)
        weights = jnp.where(left | right | near, jnp.exp(-jnp.maximum(away, 0).astype(jnp.float32) / length), 0.0)
        weights_ref[source * shape[0] : (source + 1) * shape[0], :] = weights


def finish(own_ref, weights_ref, sums_ref, out_ref):
    out_ref[...] = own_ref[...] + lax.dot_general(
        sums_ref[...], weights_ref[...], (((0,), (0,)), ((), ())), precision=lax.Precision.HIGHEST,
        preferred_element_type=jnp.float32,
    )


def f32(*shape):
    return jax.ShapeDtypeStruct(shape, jnp.float32)


def hint(megabytes):
    return pl.CostEstimate(flops=0, bytes_accessed=megabytes * 1000 * 1000, transcendentals=0)


def spaced(rows):
    return 8 * (rows // 8 | 1)


def vmem(count):
    return [pl.BlockSpec(memory_space=pltpu.VMEM)] * count


def local(depth, surface, friction, wet, coastal_tiles, gauge_route, gauge_cell, gauge_times, gauge_resid):
    height, width = depth.shape
    owned = gauge_route.shape[0]
    blocks = gauge_resid.shape[1]
    steps = blocks * STEPS_BLOCK
    halo = 2 * steps
    assert halo == SEG and height == LANES
    tiles = lax.axis_size(GRID_AXES)
    lons = lax.axis_size("lon")
    row_tiles = lax.axis_size(ROW_AXES)
    planes = width // LANES + 1
    rows_all = height + 2 * halo
    params = pltpu.CompilerParams(vmem_limit_bytes=VMEM_LIMIT)

    keep = (1.0 - friction) * wet.astype(jnp.float32)
    gain = ((courant * 0.5) ** 2 * jnp.maximum(depth + surface, depth_floor)) * keep
    samples, coast_count = gauge_resid.shape[2], coastal_tiles.shape[0]
    assert coast_count <= owned

    assert samples >= 3

    def put(array, group, row):
        groups, rows, lanes = array.shape
        return jnp.pad(array, ((group, 2 * blocks + 1 - group - groups), (row, samples - row - rows), (0, owned - lanes)))

    gauges = (
        put(jnp.transpose(gauge_times, (1, 2, 0)), 0, 0)
        + put(gauge_route.reshape(1, 1, owned), 2 * blocks, 0)
        + put(gauge_cell.reshape(1, 1, owned), 2 * blocks, 1)
        + put(coastal_tiles.reshape(1, 1, coast_count), 2 * blocks, 2)
    ).astype(jnp.float32) + put(jnp.transpose(gauge_resid, (1, 2, 0)), blocks, 0)
    west = pl.pallas_call(
        functools.partial(give_west, 2 * halo), out_shape=f32(4, height, LANES), in_specs=vmem(2), out_specs=vmem(1)[0],
        compiler_params=params, name="give_west",
    )(keep, gain)
    right = lax.ppermute(west, "lon", [(i + 1, i) for i in range(lons - 1)])

    parcel = pl.pallas_call(
        functools.partial(give_gauges, height, width, blocks, samples, coast_count),
        out_shape=f32(tiles, gauge_rows(owned)[0], LANES),
        in_specs=vmem(1) + [pl.BlockSpec(memory_space=pl.ANY)],
        out_specs=vmem(1)[0],
        scratch_shapes=[pltpu.VMEM((24, LANES), jnp.float32)],
        compiler_params=params,
        cost_estimate=hint(10),
        name="give_gauges",
    )(gauges, west)

    def exchange(array, axes, groups=None):
        return lax.all_to_all(array, axes, split_axis=0, concat_axis=0, axis_index_groups=groups, tiled=True)

    group = sorted(range(tiles), key=lambda tile: (tile % row_tiles in (0, row_tiles - 1), -(tile // row_tiles)))
    parcel = exchange(parcel, GRID_AXES, [group])

    far, near = pl.pallas_call(
        functools.partial(give_rows, halo), out_shape=(f32(2, halo, planes * LANES),) * 2, in_specs=vmem(3),
        out_specs=tuple(vmem(2)), compiler_params=params, cost_estimate=hint(40), name="give_rows",
    )(keep, gain, right)
    far = lax.ppermute(far, ROW_AXES, [pair for i in range(1, row_tiles - 1, 2) for pair in ((i, i + 1), (i + 1, i))])
    near = lax.ppermute(near, ROW_AXES, [pair for i in range(0, row_tiles, 2) for pair in ((i, i + 1), (i + 1, i))])

    wide = max(2 * LANES, owned)
    pushes = pl.pallas_call(
        functools.partial(force, steps, halo, height, width),
        out_shape=f32(steps + 1, planes, spaced(rows_all), LANES),
        in_specs=vmem(1),
        out_specs=vmem(1)[0],
        scratch_shapes=[
            pltpu.VMEM((steps, wide), jnp.float32),
            pltpu.VMEM((rows_all, wide), jnp.bfloat16),
            pltpu.VMEM((2 * wide, planes * LANES), jnp.bfloat16),
        ],
        compiler_params=params,
        cost_estimate=pl.CostEstimate(
            flops=4 * steps * rows_all * wide * planes * LANES, bytes_accessed=4 * steps * planes * rows_all * LANES,
            transcendentals=0,
        ),
        name="force",
    )(parcel)

    plane = pltpu.VMEM((planes, spaced(rows_all), LANES), jnp.float32)
    grad, sums = pl.pallas_call(
        functools.partial(sweep, steps),
        out_shape=(f32(height, planes * LANES), f32(lons, 8 + halo, height)),
        in_specs=vmem(6),
        out_specs=tuple(vmem(2)),
        scratch_shapes=[plane] * 3 + [
            pltpu.VMEM((planes + 1, spaced(rows_all + 8), LANES), jnp.float32),
            pltpu.VMEM((planes + 1, spaced(rows_all + 8), LANES), jnp.float32),
            pltpu.VMEM((2, planes, spaced(rows_all), LANES), jnp.float32),
        ],
        compiler_params=params,
        name="sweep",
    )(keep, gain, far, near, right, pushes)

    sums = exchange(sums, "lon")
    own, weights = pl.pallas_call(
        functools.partial(smooth, halo, lons),
        out_shape=(f32(height, width), f32(lons * (8 + halo), width)),
        in_specs=vmem(1),
        out_specs=tuple(vmem(2)),
        compiler_params=params,
        cost_estimate=pl.CostEstimate(
            flops=6 * 2 * height * width * width, bytes_accessed=2 * 4 * height * width, transcendentals=width * width
        ),
        name="smooth",
    )(grad)
    return pl.pallas_call(
        finish, out_shape=f32(height, width), in_specs=vmem(3), out_specs=vmem(1)[0], compiler_params=params, name="finish",
    )(own, weights, sums.reshape(lons * (8 + halo), height))


def solution(mesh):
    in_specs = (
        P(("lat", "gau"), "lon"),
        P(("scen", "lat", "gau"), "lon"),
        P(("lat", "gau"), "lon"),
        P(("lat", "gau"), "lon"),
        P(),
        P(("scen", "lon", "lat", "gau"), None),
        P(("scen", "lon", "lat", "gau")),
        P(("scen", "lon", "lat", "gau"), None, None),
        P(("scen", "lon", "lat", "gau"), None, None),
    )
    out_specs = P(("scen", "lat", "gau"), "lon")
    return jax.shard_map(local, mesh=mesh, in_specs=in_specs, out_specs=out_specs, check_vma=False)
```

```python
import functools
import math

import jax
import jax.numpy as jnp
from jax import lax
from jax.experimental import pallas as pl
from jax.experimental.pallas import tpu as pltpu
from jax.sharding import PartitionSpec as P

STEPS_BLOCK = 8
LANES = 128
SEG = 32
LEVELS = 4

courant = 0.45
depth_floor = 0.1

GRID_AXES = ("lon", "lat", "gau")
ROW_AXES = ("lat", "gau")
VMEM_LIMIT = 16 * 1024 * 1024


def roll_lanes(x, shift):
    shift = shift % LANES
    return x if shift == 0 else pltpu.roll(x, shift, 1)


def lane_iota(rows):
    return lax.broadcasted_iota(jnp.int32, (rows, LANES), 1)


def gauge_rows(owned):
    if 3 * owned <= LANES:
        return STEPS_BLOCK, owned
    assert owned <= LANES
    return 3 * STEPS_BLOCK, 0


def my_place():
    row = lax.axis_index("lat") * lax.axis_size("gau") + lax.axis_index("gau")
    return row, lax.axis_index("lon"), lax.axis_size("lat") * lax.axis_size("gau"), lax.axis_size("lon")


def give_west(reach, keep_ref, gain_ref, west_ref):
    lower = lane_iota(west_ref.shape[1]) < reach
    west_ref[0] = jnp.where(lower, keep_ref[:, :LANES], roll_lanes(gain_ref[:, :LANES], reach))
    for spare in range(1, west_ref.shape[0]):
        west_ref[spare] = jnp.zeros(west_ref.shape[1:], jnp.float32)


def give_rows(halo, keep_ref, gain_ref, right_ref, far_ref, near_ref):
    height, width = keep_ref.shape
    lower = lane_iota(halo) < 2 * halo
    odd = my_place()[0] & 1
    for goal, south in ((far_ref, odd), (near_ref, 1 - odd)):
        rows = pl.ds(pl.multiple_of(south * (height - halo), halo), halo)
        for kind, source in enumerate((keep_ref, gain_ref)):
            goal[kind, :, :width] = source[rows, :]
            goal[kind, :, width:] = jnp.where(lower, roll_lanes(right_ref[0, rows, :], -2 * halo * kind), 0.0)


def give_gauges(height, width, blocks, samples, coast_count, gauge_ref, after_ref, parcel_ref, block_ref):
    row_tiles = lax.axis_size("lat") * lax.axis_size("gau")
    owned = gauge_ref.shape[2]
    assert blocks == 2
    route, cell, coast = (gauge_ref[2 * blocks, i : i + 1, :].astype(jnp.int32) for i in range(3))
    target = jnp.zeros_like(route)
    for entry in range(coast_count):
        target = jnp.where(route == entry, jnp.broadcast_to(coast[:, entry : entry + 1], route.shape), target)
    row_bits, width_bits = int(math.log2(row_tiles)), int(math.log2(width))
    assert row_tiles == 1 << row_bits and width == 1 << width_bits
    grid_row = (target & (row_tiles - 1)) * height + (cell >> width_bits)
    grid_col = (target >> row_bits) * width + (cell & (width - 1))
    block_ref[...] = jnp.zeros_like(block_ref)
    levels = lax.broadcasted_iota(jnp.int32, (STEPS_BLOCK, owned), 0).astype(jnp.float32)
    for block in range(blocks):
        series = jnp.zeros((STEPS_BLOCK, owned), jnp.float32)
        for sample in range(samples):
            times = gauge_ref[block, sample : sample + 1, :]
            resid = gauge_ref[blocks + block, sample : sample + 1, :]
            series = series + jnp.where(times == levels, resid, 0.0)
        block_ref[block * STEPS_BLOCK : (block + 1) * STEPS_BLOCK, :owned] = series
    at = blocks * STEPS_BLOCK
    block_ref[at : at + 1, :owned] = grid_row.astype(jnp.float32)
    block_ref[at + 1 : at + 2, :owned] = grid_col.astype(jnp.float32)
    size, apart = gauge_rows(owned)
    gauges = block_ref[...]
    if size == STEPS_BLOCK:
        gauges = sum(
            roll_lanes(gauges[i * STEPS_BLOCK : (i + 1) * STEPS_BLOCK], i * apart) for i in range(3)
        )
    tiles = parcel_ref.shape[0]

    def put(tile, carry):
        parcel_ref[tile, 0:size, :] = gauges
        return carry

    lax.fori_loop(0, tiles, put, 0, unroll=tiles <= 16)


def dealt_column(place, planes):
    return (place & (LANES - 1)) * planes + place // LANES


def force(steps, halo, height, width, parcel_ref, force_ref, series_ref, rows_hot, cols_hot):
    planes, rows_all = force_ref.shape[1], height + 2 * halo
    my_row, my_lon, row_tiles, lons = my_place()
    wide = rows_hot.shape[1]
    tiles, parcel_rows = parcel_ref.shape[:2]
    size = parcel_rows
    apart = wide // tiles if size == STEPS_BLOCK else 0
    owned = apart if apart else LANES
    group = wide // owned
    groups = tiles // group
    per_plane = LANES // owned
    blocks = rows_all // 8
    row_shift = (halo - my_row * height).astype(jnp.float32)
    col_shift = (-my_lon * width).astype(jnp.float32)
    place = lax.broadcasted_iota(jnp.int32, (rows_all, LANES), 0)
    at = ((place & 7) * blocks + (place >> 3)).astype(jnp.float32)

    def gather_gauges(index):
        lanes = lane_iota(STEPS_BLOCK)
        for part in range(wide // LANES):
            cols = slice(part * LANES, (part + 1) * LANES)
            fields = []
            for field in range(3):
                total = jnp.zeros((STEPS_BLOCK, LANES), jnp.float32)
                rows = slice(0, 8) if apart else slice(8 * field, 8 * field + 8)
                for i in range(per_plane):
                    source = index * group + part * per_plane + i
                    block = roll_lanes(parcel_ref[source, rows, :], i * owned - field * apart)
                    total = jnp.where((lanes >= i * owned) & (lanes < (i + 1) * owned), block, total)
                fields.append(total)
            series_ref[0:8, cols] = fields[0]
            series_ref[8:16, cols] = fields[1]
            row = fields[2][0:1] + row_shift
            col = fields[2][1:2] + col_shift
            col = jnp.where(col < width + 2 * halo, col, -1.0)
            rows_hot[:, cols] = (at == row).astype(jnp.float32).astype(jnp.bfloat16)
            by_gauge = jnp.transpose(jnp.broadcast_to(col, (LANES, LANES)))
            for c in range(planes):
                spot = (lane_iota(LANES) * planes + c).astype(jnp.float32)
                hot = (by_gauge == spot).astype(jnp.float32).astype(jnp.bfloat16)
                cols_hot[part * LANES : (part + 1) * LANES, c * LANES : (c + 1) * LANES] = hot
                cols_hot[wide + part * LANES : wide + (part + 1) * LANES, c * LANES : (c + 1) * LANES] = hot

    def levels_of(start, add):
        hot = rows_hot[...]
        both = []
        for level in range(LEVELS):
            value = series_ref[pl.ds(start + level, 1), :]
            high = value.astype(jnp.bfloat16)
            low = (value - high.astype(jnp.float32)).astype(jnp.bfloat16)
            both.append(jnp.concatenate([hot * high, hot * low], axis=1))
        both = jnp.concatenate(both, axis=0)
        for first in range(0, planes, 2):
            count = min(2, planes - first)
            total = jnp.dot(
                both, cols_hot[:, first * LANES : (first + count) * LANES], preferred_element_type=jnp.float32
            )
            for level in range(LEVELS):
                for c in range(count):
                    part = total[level * rows_all : (level + 1) * rows_all, c * LANES : (c + 1) * LANES]
                    goal = (start + level, first + c, slice(0, rows_all))
                    force_ref[goal] = force_ref[goal] + part if add else part

    def levels(add):
        def one(index, carry):
            levels_of(index * LEVELS, add)
            return carry

        lax.fori_loop(0, steps // LEVELS, one, 0)

    force_ref[steps] = jnp.zeros_like(force_ref[steps])
    gather_gauges(0)
    levels(False)
    if groups > 1:

        def more(index, carry):
            gather_gauges(index)
            levels(True)
            return carry

        lax.fori_loop(1, groups, more, 0)


def sweep(
    steps, keep_ref, gain_ref, far_ref, near_ref, right_ref, force_ref,
    grad_ref, sums_ref,
    a, fx, fy, keeps, gains, plain,
):
    height, width = keep_ref.shape
    halo = 2 * steps
    inner = width // LANES
    planes = inner + 1
    rows_all = height + 2 * halo
    blocks = rows_all // 8
    my_row, my_lon, row_tiles, lons = my_place()
    reach = 2 * halo
    has_top, has_bottom = my_row > 0, my_row < row_tiles - 1
    has_right = my_lon < lons - 1
    odd = (jnp.zeros((halo, planes * LANES), jnp.int32) + (my_row & 1)) == 1
    lanes8 = lane_iota(8)

    def up(value):
        return pltpu.roll(value, 7, 0)

    def down(value):
        return pltpu.roll(value, 1, 0)

    every = range(planes)
    columns = planes * LANES

    parts = []
    for kind, source in enumerate((keep_ref, gain_ref)):
        far, near = far_ref[kind], near_ref[kind]
        beside = jnp.where(lane_iota(height) < reach, roll_lanes(right_ref[0], -reach * kind), 0.0)
        whole = jnp.concatenate(
            [
                jnp.where(odd, near, far),
                jnp.concatenate([source[...], beside], axis=1),
                jnp.where(odd, far, near),
            ],
            axis=0,
        )
        high = whole.astype(jnp.bfloat16)
        parts += [high, (whole - high.astype(jnp.float32)).astype(jnp.bfloat16)]
    parts = jnp.concatenate(parts, axis=0)
    shape = (columns, LANES)
    column = lax.broadcasted_iota(jnp.int32, shape, 0)
    for c in every:
        deal = (column == lax.broadcasted_iota(jnp.int32, shape, 1) * planes + c).astype(jnp.float32)
        dealt = jnp.dot(parts, deal.astype(jnp.bfloat16), preferred_element_type=jnp.float32)
        for kind in range(2):
            at = 2 * kind * rows_all
            plain[kind, c, 0:rows_all, :] = dealt[at : at + rows_all] + dealt[at + rows_all : at + 2 * rows_all]
    for kind, goal in enumerate((keeps, gains)):
        for q in range(blocks):
            for c in every:
                value = plain[kind, c, pl.ds(q, 8, stride=blocks), :]
                goal[c, 8 * q : 8 * q + 8, :] = value
                if q == 0:
                    goal[c, 8 * blocks : 8 * blocks + 8, :] = up(value)
                if c == 0:
                    goal[planes, 8 * q : 8 * q + 8, :] = roll_lanes(value, -1)

    def cell_mask(column, there):
        lane, plane = column // planes, column % planes
        return plane, jnp.where(lanes8 == lane, there, 1.0)

    column_mask = dict([cell_mask(width, jnp.where(has_right, 1.0, 0.0)), cell_mask(columns - 1, 0.0)])
    assert len(column_mask) == 2
    sublane = lax.broadcasted_iota(jnp.int32, (8, LANES), 0)
    row_mask = {}
    for row, there in ((halo - 1, has_top), (halo + height, has_bottom)):
        row_mask[row % blocks] = jnp.where(sublane == row // blocks, jnp.where(there, 1.0, 0.0), 1.0)

    fx[...] = jnp.zeros_like(fx)
    fy[...] = jnp.zeros_like(fy)
    a[:, 0:rows_all, :] = force_ref[steps - 1, :, 0:rows_all, :]

    def step(index, carry):
        level = jnp.where(index < steps - 1, steps - 2 - index, steps)
        near, ahead, new_y, beside, total, behind = {}, {}, {}, {}, {}, {}

        def rows(q):
            return slice(8 * q, 8 * q + 8)

        def first(q):
            near[q] = [a[c, rows(q % blocks), :] for c in every]
            if q < blocks:
                ahead[q] = near[q][2:] + [roll_lanes(value, -1) for value in near[q][:2]]
            else:
                near[q] = [up(value) for value in near[q]]

        def coefficients(q):
            return [[ref[c, rows(q), :] for c in range(planes + 1)] for ref in (keeps, gains)]

        def second_y(q):
            beside[q + 1] = keep, gain = coefficients(q + 1)
            new_y[q] = [keep[c] * fy[c, rows(q), :] + gain[c] * (near[q + 2][c] - near[q][c]) for c in every]
            for c in every:
                fy[c, rows(q), :] = new_y[q][c]

        def second_x(q):
            keep, gain = beside[q]
            new_x = [
                keep[c + 1] * fx[c, rows(q), :] + gain[c + 1] * (ahead[q][c] - near[q][c]) for c in every
            ]
            behind[q] = [roll_lanes(value, 1) for value in new_x[-2:]] + new_x[:-2]
            before = new_y[q - 2] if q >= 2 else [down(fy[c, rows(q - 2 + blocks), :]) for c in every]
            push = [force_ref[level, c, rows(q), :] for c in every]
            total[q] = [(near[q][c] + push[c]) + (new_y[q][c] - before[c]) + new_x[c] for c in every]
            for c in every:
                fx[c, rows(q), :] = new_x[c]

        def third(q):
            for c in every:
                value = total[q][c] - behind[q][c]
                if c in column_mask:
                    value = value * column_mask[c]
                if q in row_mask:
                    value = value * row_mask[q]
                a[c, rows(q), :] = value

        for q in range(4):
            first(q)
        second_y(0)
        second_y(1)
        for q in range(2, blocks):
            first(q + 2)
            second_y(q)
            second_x(q)
            if q > 2:
                third(q - 1)
        for q in range(2):
            first(q)
            new_y[q] = [fy[c, rows(q), :] for c in every]
            beside[q] = coefficients(q)
        for q in range(2):
            second_x(q)
            third(q - 1 if q else blocks - 1)
        third(1)
        return carry

    lax.fori_loop(0, steps, step, 0)

    start = jnp.where(my_lon > 0, halo, 0)
    for c in every:
        column = lanes8 * planes + c
        known = (column >= start) & (column < width + halo)
        for r in range(0, height, 8):
            s, q = divmod(halo + r, blocks)
            strided = pl.ds(8 * q + s, 8, stride=8)
            value = jnp.where(known & (keeps[c, strided, :] > 0.0), a[c, strided, :], 0.0)
            grad_ref[r : r + 8, c * LANES : (c + 1) * LANES] = value
    length = 2.0 * width
    shape = (8 + halo, planes * LANES)
    kind = lax.broadcasted_iota(jnp.int32, shape, 0)
    column = dealt_column(lax.broadcasted_iota(jnp.int32, shape, 1), planes)
    beyond = column - width
    off = jnp.where(kind == 0, column, jnp.where(kind == 1, -1 - beyond, jnp.where(kind == 2, beyond, width - 1 - beyond)))
    mine = ((kind < 2) & (beyond < 0)) | ((kind >= 2) & (kind < 4) & (beyond >= 0))
    weights = jnp.where(mine, jnp.exp(-jnp.maximum(off, 0).astype(jnp.float32) / length), 0.0)
    weights = jnp.where((kind >= 8) & (beyond == kind - 8), 1.0, weights)
    sums = lax.dot_general(
        weights, grad_ref[...], (((1,), (1,)), ((), ())), precision=lax.Precision.HIGHEST,
        preferred_element_type=jnp.float32,
    )
    for i in range(sums_ref.shape[0]):
        sums_ref[i] = sums


def smooth(halo, order, grad_ref, out_ref, weights_ref):
    width = out_ref.shape[1]
    length = 2.0 * width
    planes = grad_ref.shape[1] // LANES
    column = lax.broadcasted_iota(jnp.int32, (LANES, width), 1)
    lane = lax.broadcasted_iota(jnp.int32, (LANES, width), 0)
    sources = [lane * planes + c for c in range(planes)]
    kernel = jnp.concatenate(
        [jnp.where(x < width, jnp.exp(-jnp.abs(x - column).astype(jnp.float32) / length), 0.0) for x in sources], axis=0
    )
    out_ref[...] = jnp.dot(
        grad_ref[...], kernel, precision=lax.Precision.HIGHEST, preferred_element_type=jnp.float32
    )
    me = lax.axis_index("lon")
    shape = (8 + halo, width)
    kind, column = lax.broadcasted_iota(jnp.int32, shape, 0), lax.broadcasted_iota(jnp.int32, shape, 1)
    for place, source in enumerate(order):
        strip = jnp.where(kind < 2, source, source + 1)
        left = ((kind == 0) | (kind == 2)) & (strip > me)
        right = ((kind == 1) | (kind == 3)) & (strip < me)
        near = (kind >= 8) & (source + 1 == me)
        away = jnp.where(left, (strip - me) * width - column, (me - strip - 1) * width + column + 1)
        away = jnp.where(near, jnp.abs(kind - 8 - column), away)
        weights = jnp.where(left | right | near, jnp.exp(-jnp.maximum(away, 0).astype(jnp.float32) / length), 0.0)
        weights_ref[place * shape[0] : (place + 1) * shape[0], :] = weights


def finish(own_ref, weights_ref, sums_ref, out_ref):
    out_ref[...] = own_ref[...] + lax.dot_general(
        sums_ref[...], weights_ref[...], (((0,), (0,)), ((), ())), precision=lax.Precision.HIGHEST,
        preferred_element_type=jnp.float32,
    )


def f32(*shape):
    return jax.ShapeDtypeStruct(shape, jnp.float32)


def hint(megabytes):
    return pl.CostEstimate(flops=0, bytes_accessed=megabytes * 1000 * 1000, transcendentals=0)


def spaced(rows):
    return 8 * (rows // 8 | 1)


def vmem(count):
    return [pl.BlockSpec(memory_space=pltpu.VMEM)] * count


def local(depth, surface, friction, wet, coastal_tiles, gauge_route, gauge_cell, gauge_times, gauge_resid):
    height, width = depth.shape
    owned = gauge_route.shape[0]
    blocks = gauge_resid.shape[1]
    steps = blocks * STEPS_BLOCK
    halo = 2 * steps
    assert halo == SEG and height == LANES
    tiles = lax.axis_size(GRID_AXES)
    lons = lax.axis_size("lon")
    row_tiles = lax.axis_size(ROW_AXES)
    planes = width // LANES + 1
    rows_all = height + 2 * halo
    params = pltpu.CompilerParams(vmem_limit_bytes=VMEM_LIMIT)

    keep = (1.0 - friction) * wet.astype(jnp.float32)
    gain = ((courant * 0.5) ** 2 * jnp.maximum(depth + surface, depth_floor)) * keep
    samples, coast_count = gauge_resid.shape[2], coastal_tiles.shape[0]
    assert coast_count <= owned

    assert samples >= 3

    def put(array, group, row):
        groups, rows, lanes = array.shape
        return jnp.pad(array, ((group, 2 * blocks + 1 - group - groups), (row, samples - row - rows), (0, owned - lanes)))

    gauges = (
        put(jnp.transpose(gauge_times, (1, 2, 0)), 0, 0)
        + put(gauge_route.reshape(1, 1, owned), 2 * blocks, 0)
        + put(gauge_cell.reshape(1, 1, owned), 2 * blocks, 1)
        + put(coastal_tiles.reshape(1, 1, coast_count), 2 * blocks, 2)
    ).astype(jnp.float32) + put(jnp.transpose(gauge_resid, (1, 2, 0)), blocks, 0)
    west = pl.pallas_call(
        functools.partial(give_west, 2 * halo), out_shape=f32(2, height, LANES), in_specs=vmem(2), out_specs=vmem(1)[0],
        compiler_params=params, name="give_west",
    )(keep, gain)
    right = lax.ppermute(west, "lon", [(i + 1, i) for i in range(lons - 1)])

    parcel = pl.pallas_call(
        functools.partial(give_gauges, height, width, blocks, samples, coast_count),
        out_shape=f32(tiles, gauge_rows(owned)[0], LANES),
        in_specs=vmem(1) + [pl.BlockSpec(memory_space=pl.ANY)],
        out_specs=vmem(1)[0],
        scratch_shapes=[pltpu.VMEM((24, LANES), jnp.float32)],
        compiler_params=params,
        cost_estimate=hint(10),
        name="give_gauges",
    )(gauges, west)

    def exchange(array, axes, groups=None):
        return lax.all_to_all(array, axes, split_axis=0, concat_axis=0, axis_index_groups=groups, tiled=True)

    group = sorted(range(tiles), key=lambda tile: (tile % row_tiles in (0, row_tiles - 1), -(tile // row_tiles)))
    parcel = exchange(parcel, GRID_AXES, [group])

    far, near = pl.pallas_call(
        functools.partial(give_rows, halo), out_shape=(f32(2, halo, planes * LANES),) * 2, in_specs=vmem(3),
        out_specs=tuple(vmem(2)), compiler_params=params, cost_estimate=hint(40), name="give_rows",
    )(keep, gain, right)
    far = lax.ppermute(far, ROW_AXES, [pair for i in range(1, row_tiles - 1, 2) for pair in ((i, i + 1), (i + 1, i))])
    near = lax.ppermute(near, ROW_AXES, [pair for i in range(0, row_tiles, 2) for pair in ((i, i + 1), (i + 1, i))])

    wide = max(2 * LANES, owned)
    pushes = pl.pallas_call(
        functools.partial(force, steps, halo, height, width),
        out_shape=f32(steps + 1, planes, spaced(rows_all), LANES),
        in_specs=vmem(1),
        out_specs=vmem(1)[0],
        scratch_shapes=[
            pltpu.VMEM((steps, wide), jnp.float32),
            pltpu.VMEM((rows_all, wide), jnp.bfloat16),
            pltpu.VMEM((2 * wide, planes * LANES), jnp.bfloat16),
        ],
        compiler_params=params,
        cost_estimate=pl.CostEstimate(
            flops=4 * steps * rows_all * wide * planes * LANES, bytes_accessed=4 * steps * planes * rows_all * LANES,
            transcendentals=0,
        ),
        name="force",
    )(parcel)

    plane = pltpu.VMEM((planes, spaced(rows_all), LANES), jnp.float32)
    grad, sums = pl.pallas_call(
        functools.partial(sweep, steps),
        out_shape=(f32(height, planes * LANES), f32(lons, 8 + halo, height)),
        in_specs=vmem(6),
        out_specs=tuple(vmem(2)),
        scratch_shapes=[plane] * 3 + [
            pltpu.VMEM((planes + 1, spaced(rows_all + 8), LANES), jnp.float32),
            pltpu.VMEM((planes + 1, spaced(rows_all + 8), LANES), jnp.float32),
            pltpu.VMEM((2, planes, spaced(rows_all), LANES), jnp.float32),
        ],
        compiler_params=params,
        name="sweep",
    )(keep, gain, far, near, right, pushes)

    order = list(range(lons // 2, lons)) + list(range(lons // 2))[::-1]
    sums = exchange(sums, "lon", [order])
    own, weights = pl.pallas_call(
        functools.partial(smooth, halo, order),
        out_shape=(f32(height, width), f32(lons * (8 + halo), width)),
        in_specs=vmem(1),
        out_specs=tuple(vmem(2)),
        compiler_params=params,
        cost_estimate=pl.CostEstimate(
            flops=6 * 2 * height * width * width, bytes_accessed=2 * 4 * height * width, transcendentals=width * width
        ),
        name="smooth",
    )(grad)
    return pl.pallas_call(
        finish, out_shape=f32(height, width), in_specs=vmem(3), out_specs=vmem(1)[0], compiler_params=params, name="finish",
    )(own, weights, sums.reshape(lons * (8 + halo), height))


def solution(mesh):
    in_specs = (
        P(("lat", "gau"), "lon"),
        P(("scen", "lat", "gau"), "lon"),
        P(("lat", "gau"), "lon"),
        P(("lat", "gau"), "lon"),
        P(),
        P(("scen", "lon", "lat", "gau"), None),
        P(("scen", "lon", "lat", "gau")),
        P(("scen", "lon", "lat", "gau"), None, None),
        P(("scen", "lon", "lat", "gau"), None, None),
    )
    out_specs = P(("scen", "lat", "gau"), "lon")
    return jax.shard_map(local, mesh=mesh, in_specs=in_specs, out_specs=out_specs, check_vma=False)
```

```python
import functools
import math

import jax
import jax.numpy as jnp
from jax import lax
from jax.experimental import pallas as pl
from jax.experimental.pallas import tpu as pltpu
from jax.sharding import PartitionSpec as P

STEPS_BLOCK = 8
LANES = 128
SEG = 32
LEVELS = 4

courant = 0.45
depth_floor = 0.1

GRID_AXES = ("lon", "lat", "gau")
ROW_AXES = ("lat", "gau")
VMEM_LIMIT = 16 * 1024 * 1024


def roll_lanes(x, shift):
    shift = shift % LANES
    return x if shift == 0 else pltpu.roll(x, shift, 1)


def lane_iota(rows):
    return lax.broadcasted_iota(jnp.int32, (rows, LANES), 1)


def gauge_rows(owned):
    if 3 * owned <= LANES:
        return STEPS_BLOCK, owned
    assert owned <= LANES
    return 3 * STEPS_BLOCK, 0


def my_place():
    row = lax.axis_index("lat") * lax.axis_size("gau") + lax.axis_index("gau")
    return row, lax.axis_index("lon"), lax.axis_size("lat") * lax.axis_size("gau"), lax.axis_size("lon")


def give_west(reach, keep_ref, gain_ref, west_ref):
    lower = lane_iota(west_ref.shape[1]) < reach
    west_ref[0] = jnp.where(lower, keep_ref[:, :LANES], roll_lanes(gain_ref[:, :LANES], reach))
    for spare in range(1, west_ref.shape[0]):
        west_ref[spare] = jnp.zeros(west_ref.shape[1:], jnp.float32)


def give_rows(halo, keep_ref, gain_ref, right_ref, far_ref, near_ref):
    height, width = keep_ref.shape
    lower = lane_iota(halo) < 2 * halo
    odd = my_place()[0] & 1
    for goal, south in ((far_ref, odd), (near_ref, 1 - odd)):
        rows = pl.ds(pl.multiple_of(south * (height - halo), halo), halo)
        for kind, source in enumerate((keep_ref, gain_ref)):
            goal[kind, :, :width] = source[rows, :]
            goal[kind, :, width:] = jnp.where(lower, roll_lanes(right_ref[0, rows, :], -2 * halo * kind), 0.0)


def give_gauges(height, width, blocks, samples, coast_count, gauge_ref, after_ref, parcel_ref, block_ref):
    row_tiles = lax.axis_size("lat") * lax.axis_size("gau")
    owned = gauge_ref.shape[2]
    assert blocks == 2
    route, cell, coast = (gauge_ref[2 * blocks, i : i + 1, :].astype(jnp.int32) for i in range(3))
    target = jnp.zeros_like(route)
    for entry in range(coast_count):
        target = jnp.where(route == entry, jnp.broadcast_to(coast[:, entry : entry + 1], route.shape), target)
    row_bits, width_bits = int(math.log2(row_tiles)), int(math.log2(width))
    assert row_tiles == 1 << row_bits and width == 1 << width_bits
    grid_row = (target & (row_tiles - 1)) * height + (cell >> width_bits)
    grid_col = (target >> row_bits) * width + (cell & (width - 1))
    block_ref[...] = jnp.zeros_like(block_ref)
    levels = lax.broadcasted_iota(jnp.int32, (STEPS_BLOCK, owned), 0).astype(jnp.float32)
    for block in range(blocks):
        series = jnp.zeros((STEPS_BLOCK, owned), jnp.float32)
        for sample in range(samples):
            times = gauge_ref[block, sample : sample + 1, :]
            resid = gauge_ref[blocks + block, sample : sample + 1, :]
            series = series + jnp.where(times == levels, resid, 0.0)
        block_ref[block * STEPS_BLOCK : (block + 1) * STEPS_BLOCK, :owned] = series
    at = blocks * STEPS_BLOCK
    block_ref[at : at + 1, :owned] = grid_row.astype(jnp.float32)
    block_ref[at + 1 : at + 2, :owned] = grid_col.astype(jnp.float32)
    size, apart = gauge_rows(owned)
    gauges = block_ref[...]
    if size == STEPS_BLOCK:
        gauges = sum(
            roll_lanes(gauges[i * STEPS_BLOCK : (i + 1) * STEPS_BLOCK], i * apart) for i in range(3)
        )
    tiles = parcel_ref.shape[0]

    def put(tile, carry):
        parcel_ref[tile, 0:size, :] = gauges
        return carry

    lax.fori_loop(0, tiles, put, 0, unroll=tiles <= 16)


def dealt_column(place, planes):
    return (place & (LANES - 1)) * planes + place // LANES


def force(steps, halo, height, width, parcel_ref, force_ref, series_ref, rows_hot, cols_hot):
    planes, rows_all = force_ref.shape[1], height + 2 * halo
    my_row, my_lon, row_tiles, lons = my_place()
    wide = rows_hot.shape[1]
    tiles, parcel_rows = parcel_ref.shape[:2]
    size = parcel_rows
    apart = wide // tiles if size == STEPS_BLOCK else 0
    owned = apart if apart else LANES
    group = wide // owned
    groups = tiles // group
    per_plane = LANES // owned
    blocks = rows_all // 8
    row_shift = (halo - my_row * height).astype(jnp.float32)
    col_shift = (-my_lon * width).astype(jnp.float32)
    place = lax.broadcasted_iota(jnp.int32, (rows_all, LANES), 0)
    at = ((place & 7) * blocks + (place >> 3)).astype(jnp.float32)

    def gather_gauges(index):
        lanes = lane_iota(STEPS_BLOCK)
        for part in range(wide // LANES):
            cols = slice(part * LANES, (part + 1) * LANES)
            fields = []
            for field in range(3):
                total = jnp.zeros((STEPS_BLOCK, LANES), jnp.float32)
                rows = slice(0, 8) if apart else slice(8 * field, 8 * field + 8)
                for i in range(per_plane):
                    source = index * group + part * per_plane + i
                    block = roll_lanes(parcel_ref[source, rows, :], i * owned - field * apart)
                    total = jnp.where((lanes >= i * owned) & (lanes < (i + 1) * owned), block, total)
                fields.append(total)
            series_ref[0:8, cols] = fields[0]
            series_ref[8:16, cols] = fields[1]
            row = fields[2][0:1] + row_shift
            col = fields[2][1:2] + col_shift
            col = jnp.where(col < width + 2 * halo, col, -1.0)
            rows_hot[:, cols] = (at == row).astype(jnp.float32).astype(jnp.bfloat16)
            by_gauge = jnp.transpose(jnp.broadcast_to(col, (LANES, LANES)))
            for c in range(planes):
                spot = (lane_iota(LANES) * planes + c).astype(jnp.float32)
                hot = (by_gauge == spot).astype(jnp.float32).astype(jnp.bfloat16)
                cols_hot[part * LANES : (part + 1) * LANES, c * LANES : (c + 1) * LANES] = hot
                cols_hot[wide + part * LANES : wide + (part + 1) * LANES, c * LANES : (c + 1) * LANES] = hot

    def levels_of(start, add):
        hot = rows_hot[...]
        both = []
        for level in range(LEVELS):
            value = series_ref[pl.ds(start + level, 1), :]
            high = value.astype(jnp.bfloat16)
            low = (value - high.astype(jnp.float32)).astype(jnp.bfloat16)
            both.append(jnp.concatenate([hot * high, hot * low], axis=1))
        both = jnp.concatenate(both, axis=0)
        for first in range(0, planes, 2):
            count = min(2, planes - first)
            total = jnp.dot(
                both, cols_hot[:, first * LANES : (first + count) * LANES], preferred_element_type=jnp.float32
            )
            for level in range(LEVELS):
                for c in range(count):
                    part = total[level * rows_all : (level + 1) * rows_all, c * LANES : (c + 1) * LANES]
                    goal = (start + level, first + c, slice(0, rows_all))
                    force_ref[goal] = force_ref[goal] + part if add else part

    def levels(add):
        def one(index, carry):
            levels_of(index * LEVELS, add)
            return carry

        lax.fori_loop(0, steps // LEVELS, one, 0)

    force_ref[steps] = jnp.zeros_like(force_ref[steps])
    gather_gauges(0)
    levels(False)
    if groups > 1:

        def more(index, carry):
            gather_gauges(index)
            levels(True)
            return carry

        lax.fori_loop(1, groups, more, 0)


def sweep(
    steps, keep_ref, gain_ref, far_ref, near_ref, right_ref, force_ref,
    grad_ref, sums_ref,
    a, fx, fy, keeps, gains, plain,
):
    height, width = keep_ref.shape
    halo = 2 * steps
    inner = width // LANES
    planes = inner + 1
    rows_all = height + 2 * halo
    blocks = rows_all // 8
    my_row, my_lon, row_tiles, lons = my_place()
    reach = 2 * halo
    has_top, has_bottom = my_row > 0, my_row < row_tiles - 1
    has_right = my_lon < lons - 1
    odd = (jnp.zeros((halo, planes * LANES), jnp.int32) + (my_row & 1)) == 1
    lanes8 = lane_iota(8)

    def up(value):
        return pltpu.roll(value, 7, 0)

    def down(value):
        return pltpu.roll(value, 1, 0)

    every = range(planes)
    columns = planes * LANES

    parts = []
    for kind, source in enumerate((keep_ref, gain_ref)):
        far, near = far_ref[kind], near_ref[kind]
        beside = jnp.where(lane_iota(height) < reach, roll_lanes(right_ref[0], -reach * kind), 0.0)
        whole = jnp.concatenate(
            [
                jnp.where(odd, near, far),
                jnp.concatenate([source[...], beside], axis=1),
                jnp.where(odd, far, near),
            ],
            axis=0,
        )
        high = whole.astype(jnp.bfloat16)
        parts += [high, (whole - high.astype(jnp.float32)).astype(jnp.bfloat16)]
    parts = jnp.concatenate(parts, axis=0)
    shape = (columns, LANES)
    ahead = lax.broadcasted_iota(jnp.int32, shape, 0) - lax.broadcasted_iota(jnp.int32, shape, 1) * planes
    for first in range(0, planes, 2):
        pair = range(first, min(first + 2, planes))
        deal = jnp.concatenate([(ahead == c).astype(jnp.float32).astype(jnp.bfloat16) for c in pair], axis=1)
        dealt = jnp.dot(parts, deal, preferred_element_type=jnp.float32)
        for i, c in enumerate(pair):
            piece = dealt[:, i * LANES : (i + 1) * LANES]
            for kind in range(2):
                at = 2 * kind * rows_all
                plain[kind, c, 0:rows_all, :] = piece[at : at + rows_all] + piece[at + rows_all : at + 2 * rows_all]
    for kind, goal in enumerate((keeps, gains)):
        for q in range(blocks):
            for c in every:
                value = plain[kind, c, pl.ds(q, 8, stride=blocks), :]
                goal[c, 8 * q : 8 * q + 8, :] = value
                if q == 0:
                    goal[c, 8 * blocks : 8 * blocks + 8, :] = up(value)
                if c == 0:
                    goal[planes, 8 * q : 8 * q + 8, :] = roll_lanes(value, -1)

    def cell_mask(column, there):
        lane, plane = column // planes, column % planes
        return plane, jnp.where(lanes8 == lane, there, 1.0)

    column_mask = dict([cell_mask(width, jnp.where(has_right, 1.0, 0.0)), cell_mask(columns - 1, 0.0)])
    assert len(column_mask) == 2
    sublane = lax.broadcasted_iota(jnp.int32, (8, LANES), 0)
    row_mask = {}
    for row, there in ((halo - 1, has_top), (halo + height, has_bottom)):
        row_mask[row % blocks] = jnp.where(sublane == row // blocks, jnp.where(there, 1.0, 0.0), 1.0)

    fx[...] = jnp.zeros_like(fx)
    fy[...] = jnp.zeros_like(fy)
    a[:, 0:rows_all, :] = force_ref[steps - 1, :, 0:rows_all, :]

    def step(index, carry):
        level = jnp.where(index < steps - 1, steps - 2 - index, steps)
        near, ahead, new_y, beside, total, behind = {}, {}, {}, {}, {}, {}

        def rows(q):
            return slice(8 * q, 8 * q + 8)

        def first(q):
            near[q] = [a[c, rows(q % blocks), :] for c in every]
            if q < blocks:
                ahead[q] = near[q][2:] + [roll_lanes(value, -1) for value in near[q][:2]]
            else:
                near[q] = [up(value) for value in near[q]]

        def coefficients(q):
            return [[ref[c, rows(q), :] for c in range(planes + 1)] for ref in (keeps, gains)]

        def second_y(q):
            beside[q + 1] = keep, gain = coefficients(q + 1)
            new_y[q] = [keep[c] * fy[c, rows(q), :] + gain[c] * (near[q + 2][c] - near[q][c]) for c in every]
            for c in every:
                fy[c, rows(q), :] = new_y[q][c]

        def second_x(q):
            keep, gain = beside[q]
            new_x = [
                keep[c + 1] * fx[c, rows(q), :] + gain[c + 1] * (ahead[q][c] - near[q][c]) for c in every
            ]
            behind[q] = [roll_lanes(value, 1) for value in new_x[-2:]] + new_x[:-2]
            before = new_y[q - 2] if q >= 2 else [down(fy[c, rows(q - 2 + blocks), :]) for c in every]
            push = [force_ref[level, c, rows(q), :] for c in every]
            total[q] = [(near[q][c] + push[c]) + (new_y[q][c] - before[c]) + new_x[c] for c in every]
            for c in every:
                fx[c, rows(q), :] = new_x[c]

        def third(q):
            for c in every:
                value = total[q][c] - behind[q][c]
                if c in column_mask:
                    value = value * column_mask[c]
                if q in row_mask:
                    value = value * row_mask[q]
                a[c, rows(q), :] = value

        for q in range(4):
            first(q)
        second_y(0)
        second_y(1)
        for q in range(2, blocks):
            first(q + 2)
            second_y(q)
            second_x(q)
            if q > 2:
                third(q - 1)
        for q in range(2):
            first(q)
            new_y[q] = [fy[c, rows(q), :] for c in every]
            beside[q] = coefficients(q)
        for q in range(2):
            second_x(q)
            third(q - 1 if q else blocks - 1)
        third(1)
        return carry

    lax.fori_loop(0, steps, step, 0)

    start = jnp.where(my_lon > 0, halo, 0)
    for c in every:
        column = lanes8 * planes + c
        known = (column >= start) & (column < width + halo)
        for r in range(0, height, 8):
            s, q = divmod(halo + r, blocks)
            strided = pl.ds(8 * q + s, 8, stride=8)
            value = jnp.where(known & (keeps[c, strided, :] > 0.0), a[c, strided, :], 0.0)
            grad_ref[r : r + 8, c * LANES : (c + 1) * LANES] = value
    length = 2.0 * width
    shape = (8 + halo, planes * LANES)
    kind = lax.broadcasted_iota(jnp.int32, shape, 0)
    column = dealt_column(lax.broadcasted_iota(jnp.int32, shape, 1), planes)
    beyond = column - width
    off = jnp.where(kind == 0, column, jnp.where(kind == 1, -1 - beyond, jnp.where(kind == 2, beyond, width - 1 - beyond)))
    mine = ((kind < 2) & (beyond < 0)) | ((kind >= 2) & (kind < 4) & (beyond >= 0))
    weights = jnp.where(mine, jnp.exp(-jnp.maximum(off, 0).astype(jnp.float32) / length), 0.0)
    weights = jnp.where((kind >= 8) & (beyond == kind - 8), 1.0, weights)
    sums = lax.dot_general(
        weights, grad_ref[...], (((1,), (1,)), ((), ())), precision=lax.Precision.HIGHEST,
        preferred_element_type=jnp.float32,
    )
    for i in range(sums_ref.shape[0]):
        sums_ref[i] = sums


def smooth(halo, order, grad_ref, out_ref, weights_ref):
    width = out_ref.shape[1]
    length = 2.0 * width
    planes = grad_ref.shape[1] // LANES
    column = lax.broadcasted_iota(jnp.int32, (LANES, width), 1)
    lane = lax.broadcasted_iota(jnp.int32, (LANES, width), 0)
    sources = [lane * planes + c for c in range(planes)]
    kernel = jnp.concatenate(
        [jnp.where(x < width, jnp.exp(-jnp.abs(x - column).astype(jnp.float32) / length), 0.0) for x in sources], axis=0
    )
    out_ref[...] = jnp.dot(
        grad_ref[...], kernel, precision=lax.Precision.HIGHEST, preferred_element_type=jnp.float32
    )
    me = lax.axis_index("lon")
    shape = (8 + halo, width)
    kind, column = lax.broadcasted_iota(jnp.int32, shape, 0), lax.broadcasted_iota(jnp.int32, shape, 1)
    for place, source in enumerate(order):
        strip = jnp.where(kind < 2, source, source + 1)
        left = ((kind == 0) | (kind == 2)) & (strip > me)
        right = ((kind == 1) | (kind == 3)) & (strip < me)
        near = (kind >= 8) & (source + 1 == me)
        away = jnp.where(left, (strip - me) * width - column, (me - strip - 1) * width + column + 1)
        away = jnp.where(near, jnp.abs(kind - 8 - column), away)
        weights = jnp.where(left | right | near, jnp.exp(-jnp.maximum(away, 0).astype(jnp.float32) / length), 0.0)
        weights_ref[place * shape[0] : (place + 1) * shape[0], :] = weights


def finish(own_ref, weights_ref, sums_ref, out_ref):
    out_ref[...] = own_ref[...] + lax.dot_general(
        sums_ref[...], weights_ref[...], (((0,), (0,)), ((), ())), precision=lax.Precision.HIGHEST,
        preferred_element_type=jnp.float32,
    )


def f32(*shape):
    return jax.ShapeDtypeStruct(shape, jnp.float32)


def hint(megabytes):
    return pl.CostEstimate(flops=0, bytes_accessed=megabytes * 1000 * 1000, transcendentals=0)


def spaced(rows):
    return 8 * (rows // 8 | 1)


def vmem(count):
    return [pl.BlockSpec(memory_space=pltpu.VMEM)] * count


def local(depth, surface, friction, wet, coastal_tiles, gauge_route, gauge_cell, gauge_times, gauge_resid):
    height, width = depth.shape
    owned = gauge_route.shape[0]
    blocks = gauge_resid.shape[1]
    steps = blocks * STEPS_BLOCK
    halo = 2 * steps
    assert halo == SEG and height == LANES
    tiles = lax.axis_size(GRID_AXES)
    lons = lax.axis_size("lon")
    row_tiles = lax.axis_size(ROW_AXES)
    planes = width // LANES + 1
    rows_all = height + 2 * halo
    params = pltpu.CompilerParams(vmem_limit_bytes=VMEM_LIMIT)

    keep = (1.0 - friction) * wet.astype(jnp.float32)
    gain = ((courant * 0.5) ** 2 * jnp.maximum(depth + surface, depth_floor)) * keep
    samples, coast_count = gauge_resid.shape[2], coastal_tiles.shape[0]
    assert coast_count <= owned

    assert samples >= 3

    def put(array, group, row):
        groups, rows, lanes = array.shape
        return jnp.pad(array, ((group, 2 * blocks + 1 - group - groups), (row, samples - row - rows), (0, owned - lanes)))

    gauges = (
        put(jnp.transpose(gauge_times, (1, 2, 0)), 0, 0)
        + put(gauge_route.reshape(1, 1, owned), 2 * blocks, 0)
        + put(gauge_cell.reshape(1, 1, owned), 2 * blocks, 1)
        + put(coastal_tiles.reshape(1, 1, coast_count), 2 * blocks, 2)
    ).astype(jnp.float32) + put(jnp.transpose(gauge_resid, (1, 2, 0)), blocks, 0)
    west = pl.pallas_call(
        functools.partial(give_west, 2 * halo), out_shape=f32(2, height, LANES), in_specs=vmem(2), out_specs=vmem(1)[0],
        compiler_params=params, name="give_west",
    )(keep, gain)
    right = lax.ppermute(west, "lon", [(i + 1, i) for i in range(lons - 1)])

    parcel = pl.pallas_call(
        functools.partial(give_gauges, height, width, blocks, samples, coast_count),
        out_shape=f32(tiles, gauge_rows(owned)[0], LANES),
        in_specs=vmem(1) + [pl.BlockSpec(memory_space=pl.ANY)],
        out_specs=vmem(1)[0],
        scratch_shapes=[pltpu.VMEM((24, LANES), jnp.float32)],
        compiler_params=params,
        cost_estimate=hint(10),
        name="give_gauges",
    )(gauges, west)

    def exchange(array, axes, groups=None):
        return lax.all_to_all(array, axes, split_axis=0, concat_axis=0, axis_index_groups=groups, tiled=True)

    order = list(range(lons // 2, lons)) + list(range(lons // 2))[::-1]
    group = sorted(range(tiles), key=lambda tile: (tile % row_tiles in (0, row_tiles - 1), order.index(tile // row_tiles)))
    parcel = exchange(parcel, GRID_AXES, [group])

    far, near = pl.pallas_call(
        functools.partial(give_rows, halo), out_shape=(f32(2, halo, planes * LANES),) * 2, in_specs=vmem(3),
        out_specs=tuple(vmem(2)), compiler_params=params, cost_estimate=hint(40), name="give_rows",
    )(keep, gain, right)
    far = lax.ppermute(far, ROW_AXES, [pair for i in range(1, row_tiles - 1, 2) for pair in ((i, i + 1), (i + 1, i))])
    near = lax.ppermute(near, ROW_AXES, [pair for i in range(0, row_tiles, 2) for pair in ((i, i + 1), (i + 1, i))])

    wide = max(2 * LANES, owned)
    pushes = pl.pallas_call(
        functools.partial(force, steps, halo, height, width),
        out_shape=f32(steps + 1, planes, spaced(rows_all), LANES),
        in_specs=vmem(1),
        out_specs=vmem(1)[0],
        scratch_shapes=[
            pltpu.VMEM((steps, wide), jnp.float32),
            pltpu.VMEM((rows_all, wide), jnp.bfloat16),
            pltpu.VMEM((2 * wide, planes * LANES), jnp.bfloat16),
        ],
        compiler_params=params,
        cost_estimate=pl.CostEstimate(
            flops=4 * steps * rows_all * wide * planes * LANES, bytes_accessed=4 * steps * planes * rows_all * LANES,
            transcendentals=0,
        ),
        name="force",
    )(parcel)

    plane = pltpu.VMEM((planes, spaced(rows_all), LANES), jnp.float32)
    grad, sums = pl.pallas_call(
        functools.partial(sweep, steps),
        out_shape=(f32(height, planes * LANES), f32(lons, 8 + halo, height)),
        in_specs=vmem(6),
        out_specs=tuple(vmem(2)),
        scratch_shapes=[plane] * 3 + [
            pltpu.VMEM((planes + 1, spaced(rows_all + 8), LANES), jnp.float32),
            pltpu.VMEM((planes + 1, spaced(rows_all + 8), LANES), jnp.float32),
            pltpu.VMEM((2, planes, spaced(rows_all), LANES), jnp.float32),
        ],
        compiler_params=params,
        name="sweep",
    )(keep, gain, far, near, right, pushes)

    sums = exchange(sums, "lon", [order])
    own, weights = pl.pallas_call(
        functools.partial(smooth, halo, order),
        out_shape=(f32(height, width), f32(lons * (8 + halo), width)),
        in_specs=vmem(1),
        out_specs=tuple(vmem(2)),
        compiler_params=params,
        cost_estimate=pl.CostEstimate(
            flops=6 * 2 * height * width * width, bytes_accessed=2 * 4 * height * width, transcendentals=width * width
        ),
        name="smooth",
    )(grad)
    return pl.pallas_call(
        finish, out_shape=f32(height, width), in_specs=vmem(3), out_specs=vmem(1)[0], compiler_params=params, name="finish",
    )(own, weights, sums.reshape(lons * (8 + halo), height))


def solution(mesh):
    in_specs = (
        P(("lat", "gau"), "lon"),
        P(("scen", "lat", "gau"), "lon"),
        P(("lat", "gau"), "lon"),
        P(("lat", "gau"), "lon"),
        P(),
        P(("scen", "lon", "lat", "gau"), None),
        P(("scen", "lon", "lat", "gau")),
        P(("scen", "lon", "lat", "gau"), None, None),
        P(("scen", "lon", "lat", "gau"), None, None),
    )
    out_specs = P(("scen", "lat", "gau"), "lon")
    return jax.shard_map(local, mesh=mesh, in_specs=in_specs, out_specs=out_specs, check_vma=False)
```

```python
import functools
import math

import jax
import jax.numpy as jnp
from jax import lax
from jax.experimental import pallas as pl
from jax.experimental.pallas import tpu as pltpu
from jax.sharding import PartitionSpec as P

STEPS_BLOCK = 8
LANES = 128
SEG = 32
LEVELS = 16

courant = 0.45
depth_floor = 0.1

GRID_AXES = ("lon", "lat", "gau")
ROW_AXES = ("lat", "gau")
VMEM_LIMIT = 16 * 1024 * 1024


def roll_lanes(x, shift):
    shift = shift % LANES
    return x if shift == 0 else pltpu.roll(x, shift, 1)


def lane_iota(rows):
    return lax.broadcasted_iota(jnp.int32, (rows, LANES), 1)


def gauge_rows(owned):
    if 3 * owned <= LANES:
        return STEPS_BLOCK, owned
    assert owned <= LANES
    return 3 * STEPS_BLOCK, 0


def my_place():
    row = lax.axis_index("lat") * lax.axis_size("gau") + lax.axis_index("gau")
    return row, lax.axis_index("lon"), lax.axis_size("lat") * lax.axis_size("gau"), lax.axis_size("lon")


def give_west(reach, keep_ref, gain_ref, west_ref):
    height = keep_ref.shape[0]
    lower = lane_iota(height) < reach
    west_ref[:height] = jnp.where(lower, keep_ref[:, :LANES], roll_lanes(gain_ref[:, :LANES], reach))
    west_ref[height:] = jnp.zeros((west_ref.shape[0] - height, LANES), jnp.float32)


def give_rows(halo, keep_ref, gain_ref, right_ref, far_ref, near_ref):
    height, width = keep_ref.shape
    lower = lane_iota(halo) < 2 * halo
    odd = my_place()[0] & 1
    for goal, south in ((far_ref, odd), (near_ref, 1 - odd)):
        rows = pl.ds(pl.multiple_of(south * (height - halo), halo), halo)
        for kind, source in enumerate((keep_ref, gain_ref)):
            goal[kind, :, :width] = source[rows, :]
            goal[kind, :, width:] = jnp.where(lower, roll_lanes(right_ref[rows, :], -2 * halo * kind), 0.0)


def give_gauges(height, width, blocks, samples, coast_count, gauge_ref, after_ref, parcel_ref, block_ref):
    row_tiles = lax.axis_size("lat") * lax.axis_size("gau")
    owned = gauge_ref.shape[2]
    assert blocks == 2
    route, cell, coast = (gauge_ref[2 * blocks, i : i + 1, :].astype(jnp.int32) for i in range(3))
    target = jnp.zeros_like(route)
    for entry in range(coast_count):
        target = jnp.where(route == entry, jnp.broadcast_to(coast[:, entry : entry + 1], route.shape), target)
    row_bits, width_bits = int(math.log2(row_tiles)), int(math.log2(width))
    assert row_tiles == 1 << row_bits and width == 1 << width_bits
    grid_row = (target & (row_tiles - 1)) * height + (cell >> width_bits)
    grid_col = (target >> row_bits) * width + (cell & (width - 1))
    block_ref[...] = jnp.zeros_like(block_ref)
    levels = lax.broadcasted_iota(jnp.int32, (STEPS_BLOCK, owned), 0).astype(jnp.float32)
    for block in range(blocks):
        series = jnp.zeros((STEPS_BLOCK, owned), jnp.float32)
        for sample in range(samples):
            times = gauge_ref[block, sample : sample + 1, :]
            resid = gauge_ref[blocks + block, sample : sample + 1, :]
            series = series + jnp.where(times == levels, resid, 0.0)
        block_ref[block * STEPS_BLOCK : (block + 1) * STEPS_BLOCK, :owned] = series
    at = blocks * STEPS_BLOCK
    block_ref[at : at + 1, :owned] = grid_row.astype(jnp.float32)
    block_ref[at + 1 : at + 2, :owned] = grid_col.astype(jnp.float32)
    size, apart = gauge_rows(owned)
    gauges = block_ref[...]
    if size == STEPS_BLOCK:
        gauges = sum(
            roll_lanes(gauges[i * STEPS_BLOCK : (i + 1) * STEPS_BLOCK], i * apart) for i in range(3)
        )
    tiles = parcel_ref.shape[0]

    def put(tile, carry):
        parcel_ref[tile, 0:size, :] = gauges
        return carry

    lax.fori_loop(0, tiles, put, 0, unroll=tiles <= 16)


def halves(value):
    high = value.astype(jnp.bfloat16)
    return high, (value - high.astype(jnp.float32)).astype(jnp.bfloat16)


def dealt_column(place, planes):
    return (place & (LANES - 1)) * planes + place // LANES


def force(steps, halo, height, width, parcel_ref, force_ref, series_ref, rows_hot, cols_hot):
    planes, rows_all = force_ref.shape[1], height + 2 * halo
    my_row, my_lon, row_tiles, lons = my_place()
    wide = rows_hot.shape[1]
    tiles, parcel_rows = parcel_ref.shape[:2]
    size = parcel_rows
    apart = wide // tiles if size == STEPS_BLOCK else 0
    owned = apart if apart else LANES
    group = wide // owned
    groups = tiles // group
    per_plane = LANES // owned
    blocks = rows_all // 8
    row_shift = (halo - my_row * height).astype(jnp.float32)
    col_shift = (-my_lon * width).astype(jnp.float32)
    place = lax.broadcasted_iota(jnp.int32, (rows_all, LANES), 0)
    at = ((place & 7) * blocks + (place >> 3)).astype(jnp.float32)

    def gather_gauges(index):
        lanes = lane_iota(STEPS_BLOCK)
        for part in range(wide // LANES):
            cols = slice(part * LANES, (part + 1) * LANES)
            fields = []
            for field in range(3):
                total = jnp.zeros((STEPS_BLOCK, LANES), jnp.float32)
                rows = slice(0, 8) if apart else slice(8 * field, 8 * field + 8)
                for i in range(per_plane):
                    source = index * group + part * per_plane + i
                    block = roll_lanes(parcel_ref[source, rows, :], i * owned - field * apart)
                    total = jnp.where((lanes >= i * owned) & (lanes < (i + 1) * owned), block, total)
                fields.append(total)
            series_ref[0:8, cols] = fields[0]
            series_ref[8:16, cols] = fields[1]
            row = fields[2][0:1] + row_shift
            col = fields[2][1:2] + col_shift
            col = jnp.where(col < width + 2 * halo, col, -1.0)
            rows_hot[:, cols] = (at == row).astype(jnp.float32).astype(jnp.bfloat16)
            by_gauge = jnp.transpose(jnp.broadcast_to(col, (LANES, LANES)))
            for c in range(planes):
                spot = (lane_iota(LANES) * planes + c).astype(jnp.float32)
                hot = (by_gauge == spot).astype(jnp.float32).astype(jnp.bfloat16)
                cols_hot[part * LANES : (part + 1) * LANES, c * LANES : (c + 1) * LANES] = hot
                cols_hot[wide + part * LANES : wide + (part + 1) * LANES, c * LANES : (c + 1) * LANES] = hot

    def levels_of(start, add):
        hot = rows_hot[...]
        both = []
        for level in range(LEVELS):
            value = series_ref[pl.ds(start + level, 1), :]
            high, low = halves(value)
            both.append(jnp.concatenate([hot * high, hot * low], axis=1))
        both = jnp.concatenate(both, axis=0)
        for first in range(0, planes, 2):
            count = min(2, planes - first)
            total = jnp.dot(
                both, cols_hot[:, first * LANES : (first + count) * LANES], preferred_element_type=jnp.float32
            )
            for level in range(LEVELS):
                for c in range(count):
                    part = total[level * rows_all : (level + 1) * rows_all, c * LANES : (c + 1) * LANES]
                    goal = (start + level, first + c, slice(0, rows_all))
                    force_ref[goal] = force_ref[goal] + part if add else part

    def levels(add):
        def one(index, carry):
            levels_of(index * LEVELS, add)
            return carry

        lax.fori_loop(0, steps // LEVELS, one, 0)

    force_ref[steps] = jnp.zeros_like(force_ref[steps])
    gather_gauges(0)
    levels(False)
    if groups > 1:

        def more(index, carry):
            gather_gauges(index)
            levels(True)
            return carry

        lax.fori_loop(1, groups, more, 0)


def sweep(
    steps, keep_ref, gain_ref, far_ref, near_ref, right_ref, force_ref,
    grad_ref, sums_ref,
    a, fx, fy, keeps, gains, plain,
):
    height, width = keep_ref.shape
    halo = 2 * steps
    inner = width // LANES
    planes = inner + 1
    rows_all = height + 2 * halo
    blocks = rows_all // 8
    my_row, my_lon, row_tiles, lons = my_place()
    reach = 2 * halo
    has_top, has_bottom = my_row > 0, my_row < row_tiles - 1
    has_right = my_lon < lons - 1
    odd = (jnp.zeros((halo, planes * LANES), jnp.int32) + (my_row & 1)) == 1
    lanes8 = lane_iota(8)

    def up(value):
        return pltpu.roll(value, 7, 0)

    def down(value):
        return pltpu.roll(value, 1, 0)

    every = range(planes)
    columns = planes * LANES

    parts = []
    for kind, source in enumerate((keep_ref, gain_ref)):
        far, near = far_ref[kind], near_ref[kind]
        beside = jnp.where(lane_iota(height) < reach, roll_lanes(right_ref[:height], -reach * kind), 0.0)
        whole = jnp.concatenate(
            [
                jnp.where(odd, near, far),
                jnp.concatenate([source[...], beside], axis=1),
                jnp.where(odd, far, near),
            ],
            axis=0,
        )
        parts += halves(whole)
    parts = jnp.concatenate(parts, axis=0)
    shape = (columns, LANES)
    ahead = lax.broadcasted_iota(jnp.int32, shape, 0) - lax.broadcasted_iota(jnp.int32, shape, 1) * planes
    for first in range(0, planes, 2):
        pair = range(first, min(first + 2, planes))
        deal = jnp.concatenate([(ahead == c).astype(jnp.float32).astype(jnp.bfloat16) for c in pair], axis=1)
        dealt = jnp.dot(parts, deal, preferred_element_type=jnp.float32)
        for i, c in enumerate(pair):
            piece = dealt[:, i * LANES : (i + 1) * LANES]
            for kind in range(2):
                at = 2 * kind * rows_all
                plain[kind, c, 0:rows_all, :] = piece[at : at + rows_all] + piece[at + rows_all : at + 2 * rows_all]
    for kind, goal in enumerate((keeps, gains)):
        for q in range(blocks):
            for c in every:
                value = plain[kind, c, pl.ds(q, 8, stride=blocks), :]
                goal[c, 8 * q : 8 * q + 8, :] = value
                if q == 0:
                    goal[c, 8 * blocks : 8 * blocks + 8, :] = up(value)
                if c == 0:
                    goal[planes, 8 * q : 8 * q + 8, :] = roll_lanes(value, -1)

    def cell_mask(column, there):
        lane, plane = column // planes, column % planes
        return plane, jnp.where(lanes8 == lane, there, 1.0)

    column_mask = dict([cell_mask(width, jnp.where(has_right, 1.0, 0.0)), cell_mask(columns - 1, 0.0)])
    assert len(column_mask) == 2
    sublane = lax.broadcasted_iota(jnp.int32, (8, LANES), 0)
    row_mask = {}
    for row, there in ((halo - 1, has_top), (halo + height, has_bottom)):
        row_mask[row % blocks] = jnp.where(sublane == row // blocks, jnp.where(there, 1.0, 0.0), 1.0)

    fx[...] = jnp.zeros_like(fx)
    fy[...] = jnp.zeros_like(fy)
    a[:, 0:rows_all, :] = force_ref[steps - 1, :, 0:rows_all, :]

    def step(index, carry):
        level = jnp.where(index < steps - 1, steps - 2 - index, steps)
        near, ahead, new_y, beside, total, behind = {}, {}, {}, {}, {}, {}

        def rows(q):
            return slice(8 * q, 8 * q + 8)

        def first(q):
            near[q] = [a[c, rows(q % blocks), :] for c in every]
            if q < blocks:
                ahead[q] = near[q][2:] + [roll_lanes(value, -1) for value in near[q][:2]]
            else:
                near[q] = [up(value) for value in near[q]]

        def coefficients(q):
            return [[ref[c, rows(q), :] for c in range(planes + 1)] for ref in (keeps, gains)]

        def second_y(q):
            beside[q + 1] = keep, gain = coefficients(q + 1)
            new_y[q] = [keep[c] * fy[c, rows(q), :] + gain[c] * (near[q + 2][c] - near[q][c]) for c in every]
            for c in every:
                fy[c, rows(q), :] = new_y[q][c]

        def second_x(q):
            keep, gain = beside[q]
            new_x = [
                keep[c + 1] * fx[c, rows(q), :] + gain[c + 1] * (ahead[q][c] - near[q][c]) for c in every
            ]
            behind[q] = [roll_lanes(value, 1) for value in new_x[-2:]] + new_x[:-2]
            before = new_y[q - 2] if q >= 2 else [down(fy[c, rows(q - 2 + blocks), :]) for c in every]
            push = [force_ref[level, c, rows(q), :] for c in every]
            total[q] = [(near[q][c] + push[c]) + (new_y[q][c] - before[c]) + new_x[c] for c in every]
            for c in every:
                fx[c, rows(q), :] = new_x[c]

        def third(q):
            for c in every:
                value = total[q][c] - behind[q][c]
                if c in column_mask:
                    value = value * column_mask[c]
                if q in row_mask:
                    value = value * row_mask[q]
                a[c, rows(q), :] = value

        for q in range(4):
            first(q)
        second_y(0)
        second_y(1)
        for q in range(2, blocks):
            first(q + 2)
            second_y(q)
            second_x(q)
            if q > 2:
                third(q - 1)
        for q in range(2):
            first(q)
            new_y[q] = [fy[c, rows(q), :] for c in every]
            beside[q] = coefficients(q)
        for q in range(2):
            second_x(q)
            third(q - 1 if q else blocks - 1)
        third(1)
        return carry

    lax.fori_loop(0, steps, step, 0)

    start = jnp.where(my_lon > 0, halo, 0)
    for c in every:
        column = lanes8 * planes + c
        known = (column >= start) & (column < width + halo)
        for r in range(0, height, 8):
            s, q = divmod(halo + r, blocks)
            strided = pl.ds(8 * q + s, 8, stride=8)
            value = jnp.where(known & (keeps[c, strided, :] > 0.0), a[c, strided, :], 0.0)
            grad_ref[r : r + 8, c * LANES : (c + 1) * LANES] = value
    length = 2.0 * width
    shape = (8 + halo, planes * LANES)
    kind = lax.broadcasted_iota(jnp.int32, shape, 0)
    column = dealt_column(lax.broadcasted_iota(jnp.int32, shape, 1), planes)
    beyond = column - width
    off = jnp.where(kind == 0, column, jnp.where(kind == 1, -1 - beyond, jnp.where(kind == 2, beyond, width - 1 - beyond)))
    mine = ((kind < 2) & (beyond < 0)) | ((kind >= 2) & (kind < 4) & (beyond >= 0))
    weights = jnp.where(mine, jnp.exp(-jnp.maximum(off, 0).astype(jnp.float32) / length), 0.0)
    weights = jnp.where((kind >= 8) & (beyond == kind - 8), 1.0, weights)
    sums = lax.dot_general(
        weights, grad_ref[...], (((1,), (1,)), ((), ())), precision=lax.Precision.HIGHEST,
        preferred_element_type=jnp.float32,
    )
    for i in range(sums_ref.shape[0]):
        sums_ref[i] = sums


def smooth(halo, order, grad_ref, out_ref, weights_ref, exact_ref):
    width = out_ref.shape[1]
    length = 2.0 * width
    planes = grad_ref.shape[1] // LANES
    column = lax.broadcasted_iota(jnp.int32, (LANES, width), 1)
    lane = lax.broadcasted_iota(jnp.int32, (LANES, width), 0)
    sources = [lane * planes + c for c in range(planes)]
    kernel = jnp.concatenate(
        [jnp.where(x < width, jnp.exp(-jnp.abs(x - column).astype(jnp.float32) / length), 0.0) for x in sources], axis=0
    )
    out_ref[...] = jnp.dot(
        grad_ref[...], kernel, precision=lax.Precision.HIGHEST, preferred_element_type=jnp.float32
    )
    me = lax.axis_index("lon")
    shape = (8 + halo, width)
    kind, column = lax.broadcasted_iota(jnp.int32, shape, 0), lax.broadcasted_iota(jnp.int32, shape, 1)
    for place, source in enumerate(order):
        strip = jnp.where(kind < 2, source, source + 1)
        left = ((kind == 0) | (kind == 2)) & (strip > me)
        right = ((kind == 1) | (kind == 3)) & (strip < me)
        near = (kind >= 8) & (source + 1 == me)
        away = jnp.where(left, (strip - me) * width - column, (me - strip - 1) * width + column + 1)
        away = jnp.where(near, jnp.abs(kind - 8 - column), away)
        weights = jnp.where(left | right | near, jnp.exp(-jnp.maximum(away, 0).astype(jnp.float32) / length), 0.0)
        exact_ref[place * shape[0] : (place + 1) * shape[0], :] = weights
    high, low = halves(exact_ref[...])
    count = high.shape[0]
    for place, part in enumerate((high, high, low)):
        weights_ref[place * count : (place + 1) * count, :] = part


def finish(own_ref, weights_ref, sums_ref, out_ref):
    high, low = halves(sums_ref[...])
    out_ref[...] = own_ref[...] + lax.dot_general(
        jnp.concatenate([high, low, high], axis=0), weights_ref[...], (((0,), (0,)), ((), ())),
        preferred_element_type=jnp.float32,
    )


def f32(*shape):
    return jax.ShapeDtypeStruct(shape, jnp.float32)


def hint(megabytes):
    return pl.CostEstimate(flops=0, bytes_accessed=megabytes * 1000 * 1000, transcendentals=0)


def spaced(rows):
    return 8 * (rows // 8 | 1)


def vmem(count):
    return [pl.BlockSpec(memory_space=pltpu.VMEM)] * count


def local(depth, surface, friction, wet, coastal_tiles, gauge_route, gauge_cell, gauge_times, gauge_resid):
    height, width = depth.shape
    owned = gauge_route.shape[0]
    blocks = gauge_resid.shape[1]
    steps = blocks * STEPS_BLOCK
    halo = 2 * steps
    assert halo == SEG and height == LANES
    tiles = lax.axis_size(GRID_AXES)
    lons = lax.axis_size("lon")
    row_tiles = lax.axis_size(ROW_AXES)
    planes = width // LANES + 1
    rows_all = height + 2 * halo
    params = pltpu.CompilerParams(vmem_limit_bytes=VMEM_LIMIT)

    keep = (1.0 - friction) * wet.astype(jnp.float32)
    gain = ((courant * 0.5) ** 2 * jnp.maximum(depth + surface, depth_floor)) * keep
    samples, coast_count = gauge_resid.shape[2], coastal_tiles.shape[0]
    assert coast_count <= owned

    assert samples >= 3

    def put(array, group, row):
        groups, rows, lanes = array.shape
        return jnp.pad(array, ((group, 2 * blocks + 1 - group - groups), (row, samples - row - rows), (0, owned - lanes)))

    gauges = (
        put(jnp.transpose(gauge_times, (1, 2, 0)), 0, 0)
        + put(gauge_route.reshape(1, 1, owned), 2 * blocks, 0)
        + put(gauge_cell.reshape(1, 1, owned), 2 * blocks, 1)
        + put(coastal_tiles.reshape(1, 1, coast_count), 2 * blocks, 2)
    ).astype(jnp.float32) + put(jnp.transpose(gauge_resid, (1, 2, 0)), blocks, 0)
    west = pl.pallas_call(
        functools.partial(give_west, 2 * halo), out_shape=f32(height + 16, LANES), in_specs=vmem(2), out_specs=vmem(1)[0],
        compiler_params=params, name="give_west",
    )(keep, gain)
    right = lax.ppermute(west, "lon", [(i + 1, i) for i in range(lons - 1)])

    parcel = pl.pallas_call(
        functools.partial(give_gauges, height, width, blocks, samples, coast_count),
        out_shape=f32(tiles, gauge_rows(owned)[0], LANES),
        in_specs=vmem(1) + [pl.BlockSpec(memory_space=pl.ANY)],
        out_specs=vmem(1)[0],
        scratch_shapes=[pltpu.VMEM((24, LANES), jnp.float32)],
        compiler_params=params,
        cost_estimate=hint(10),
        name="give_gauges",
    )(gauges, west)

    def exchange(array, axes, groups=None):
        return lax.all_to_all(array, axes, split_axis=0, concat_axis=0, axis_index_groups=groups, tiled=True)

    order = list(range(lons // 2, lons)) + list(range(lons // 2))[::-1]
    group = sorted(range(tiles), key=lambda tile: (tile % row_tiles in (0, row_tiles - 1), order.index(tile // row_tiles)))
    parcel = exchange(parcel, GRID_AXES, [group])

    far, near = pl.pallas_call(
        functools.partial(give_rows, halo), out_shape=(f32(2, halo, planes * LANES),) * 2, in_specs=vmem(3),
        out_specs=tuple(vmem(2)), compiler_params=params, cost_estimate=hint(40), name="give_rows",
    )(keep, gain, right)
    far = lax.ppermute(far, ROW_AXES, [pair for i in range(1, row_tiles - 1, 2) for pair in ((i, i + 1), (i + 1, i))])
    near = lax.ppermute(near, ROW_AXES, [pair for i in range(0, row_tiles, 2) for pair in ((i, i + 1), (i + 1, i))])

    wide = max(2 * LANES, owned)
    pushes = pl.pallas_call(
        functools.partial(force, steps, halo, height, width),
        out_shape=f32(steps + 1, planes, spaced(rows_all), LANES),
        in_specs=vmem(1),
        out_specs=vmem(1)[0],
        scratch_shapes=[
            pltpu.VMEM((steps, wide), jnp.float32),
            pltpu.VMEM((rows_all, wide), jnp.bfloat16),
            pltpu.VMEM((2 * wide, planes * LANES), jnp.bfloat16),
        ],
        compiler_params=params,
        cost_estimate=pl.CostEstimate(
            flops=4 * steps * rows_all * wide * planes * LANES, bytes_accessed=4 * steps * planes * rows_all * LANES,
            transcendentals=0,
        ),
        name="force",
    )(parcel)

    plane = pltpu.VMEM((planes, spaced(rows_all), LANES), jnp.float32)
    grad, sums = pl.pallas_call(
        functools.partial(sweep, steps),
        out_shape=(f32(height, planes * LANES), f32(lons, 8 + halo, height)),
        in_specs=vmem(6),
        out_specs=tuple(vmem(2)),
        scratch_shapes=[plane] * 3 + [
            pltpu.VMEM((planes + 1, spaced(rows_all + 8), LANES), jnp.float32),
            pltpu.VMEM((planes + 1, spaced(rows_all + 8), LANES), jnp.float32),
            pltpu.VMEM((2, planes, spaced(rows_all), LANES), jnp.float32),
        ],
        compiler_params=params,
        name="sweep",
    )(keep, gain, far, near, right, pushes)

    sums = exchange(sums, "lon", [order])
    own, weights = pl.pallas_call(
        functools.partial(smooth, halo, order),
        out_shape=(f32(height, width), jax.ShapeDtypeStruct((3 * lons * (8 + halo), width), jnp.bfloat16)),
        in_specs=vmem(1),
        out_specs=tuple(vmem(2)),
        scratch_shapes=[pltpu.VMEM((lons * (8 + halo), width), jnp.float32)],
        compiler_params=params,
        cost_estimate=pl.CostEstimate(
            flops=6 * 2 * height * width * width, bytes_accessed=2 * 4 * height * width, transcendentals=width * width
        ),
        name="smooth",
    )(grad)
    return pl.pallas_call(
        finish, out_shape=f32(height, width), in_specs=vmem(3), out_specs=vmem(1)[0], compiler_params=params, name="finish",
    )(own, weights, sums.reshape(lons * (8 + halo), height))


def solution(mesh):
    in_specs = (
        P(("lat", "gau"), "lon"),
        P(("scen", "lat", "gau"), "lon"),
        P(("lat", "gau"), "lon"),
        P(("lat", "gau"), "lon"),
        P(),
        P(("scen", "lon", "lat", "gau"), None),
        P(("scen", "lon", "lat", "gau")),
        P(("scen", "lon", "lat", "gau"), None, None),
        P(("scen", "lon", "lat", "gau"), None, None),
    )
    out_specs = P(("scen", "lat", "gau"), "lon")
    return jax.shard_map(local, mesh=mesh, in_specs=in_specs, out_specs=out_specs, check_vma=False)
```

```python
import functools
import math

import jax
import jax.numpy as jnp
from jax import lax
from jax.experimental import pallas as pl
from jax.experimental.pallas import tpu as pltpu
from jax.sharding import PartitionSpec as P

STEPS_BLOCK = 8
LANES = 128
SEG = 32
LEVELS = 16

courant = 0.45
depth_floor = 0.1

GRID_AXES = ("lon", "lat", "gau")
ROW_AXES = ("lat", "gau")
VMEM_LIMIT = 16 * 1024 * 1024


def roll_lanes(x, shift):
    shift = shift % LANES
    return x if shift == 0 else pltpu.roll(x, shift, 1)


def lane_iota(rows):
    return lax.broadcasted_iota(jnp.int32, (rows, LANES), 1)


def gauge_rows(owned):
    if 3 * owned <= LANES:
        return STEPS_BLOCK, owned
    assert owned <= LANES
    return 3 * STEPS_BLOCK, 0


def my_place():
    row = lax.axis_index("lat") * lax.axis_size("gau") + lax.axis_index("gau")
    return row, lax.axis_index("lon"), lax.axis_size("lat") * lax.axis_size("gau"), lax.axis_size("lon")


def give_west(reach, keep_ref, gain_ref, west_ref):
    height = keep_ref.shape[0]
    lower = lane_iota(height) < reach
    west_ref[:height] = jnp.where(lower, keep_ref[:, :LANES], roll_lanes(gain_ref[:, :LANES], reach))
    west_ref[height:] = jnp.zeros((west_ref.shape[0] - height, LANES), jnp.float32)


def give_rows(halo, keep_ref, gain_ref, right_ref, far_ref, near_ref):
    height, width = keep_ref.shape
    lower = lane_iota(halo) < 2 * halo
    odd = my_place()[0] & 1
    for goal, south in ((far_ref, odd), (near_ref, 1 - odd)):
        rows = pl.ds(pl.multiple_of(south * (height - halo), halo), halo)
        for kind, source in enumerate((keep_ref, gain_ref)):
            goal[kind, :, :width] = source[rows, :]
            goal[kind, :, width:] = jnp.where(lower, roll_lanes(right_ref[rows, :], -2 * halo * kind), 0.0)


def give_gauges(height, width, blocks, samples, coast_count, gauge_ref, after_ref, parcel_ref, block_ref):
    row_tiles = lax.axis_size("lat") * lax.axis_size("gau")
    owned = gauge_ref.shape[2]
    assert blocks == 2
    route, cell, coast = (gauge_ref[2 * blocks, i : i + 1, :].astype(jnp.int32) for i in range(3))
    target = jnp.zeros_like(route)
    for entry in range(coast_count):
        target = jnp.where(route == entry, jnp.broadcast_to(coast[:, entry : entry + 1], route.shape), target)
    row_bits, width_bits = int(math.log2(row_tiles)), int(math.log2(width))
    assert row_tiles == 1 << row_bits and width == 1 << width_bits
    grid_row = (target & (row_tiles - 1)) * height + (cell >> width_bits)
    grid_col = (target >> row_bits) * width + (cell & (width - 1))
    block_ref[...] = jnp.zeros_like(block_ref)
    levels = lax.broadcasted_iota(jnp.int32, (STEPS_BLOCK, owned), 0).astype(jnp.float32)
    for block in range(blocks):
        series = jnp.zeros((STEPS_BLOCK, owned), jnp.float32)
        for sample in range(samples):
            times = gauge_ref[block, sample : sample + 1, :]
            resid = gauge_ref[blocks + block, sample : sample + 1, :]
            series = series + jnp.where(times == levels, resid, 0.0)
        block_ref[block * STEPS_BLOCK : (block + 1) * STEPS_BLOCK, :owned] = series
    at = blocks * STEPS_BLOCK
    block_ref[at : at + 1, :owned] = grid_row.astype(jnp.float32)
    block_ref[at + 1 : at + 2, :owned] = grid_col.astype(jnp.float32)
    size, apart = gauge_rows(owned)
    gauges = block_ref[...]
    if size == STEPS_BLOCK:
        gauges = sum(
            roll_lanes(gauges[i * STEPS_BLOCK : (i + 1) * STEPS_BLOCK], i * apart) for i in range(3)
        )
    tiles = parcel_ref.shape[0]

    def put(tile, carry):
        parcel_ref[tile, 0:size, :] = gauges
        return carry

    lax.fori_loop(0, tiles, put, 0, unroll=tiles <= 16)


def halves(value):
    high = value.astype(jnp.bfloat16)
    return high, (value - high.astype(jnp.float32)).astype(jnp.bfloat16)


def dealt_column(place, planes):
    return (place & (LANES - 1)) * planes + place // LANES


def force(steps, halo, height, width, parcel_ref, force_ref, series_ref, rows_hot, cols_hot):
    planes, rows_all = force_ref.shape[1], height + 2 * halo
    my_row, my_lon, row_tiles, lons = my_place()
    wide = rows_hot.shape[1]
    tiles, parcel_rows = parcel_ref.shape[:2]
    size = parcel_rows
    apart = wide // tiles if size == STEPS_BLOCK else 0
    owned = apart if apart else LANES
    group = wide // owned
    groups = tiles // group
    per_plane = LANES // owned
    blocks = rows_all // 8
    row_shift = (halo - my_row * height).astype(jnp.float32)
    col_shift = (-my_lon * width).astype(jnp.float32)
    place = lax.broadcasted_iota(jnp.int32, (rows_all, LANES), 0)
    at = ((place & 7) * blocks + (place >> 3)).astype(jnp.float32)

    def gather_gauges(index):
        lanes = lane_iota(STEPS_BLOCK)
        for part in range(wide // LANES):
            cols = slice(part * LANES, (part + 1) * LANES)
            fields = []
            for field in range(3):
                total = jnp.zeros((STEPS_BLOCK, LANES), jnp.float32)
                rows = slice(0, 8) if apart else slice(8 * field, 8 * field + 8)
                for i in range(per_plane):
                    source = index * group + part * per_plane + i
                    block = roll_lanes(parcel_ref[source, rows, :], i * owned - field * apart)
                    total = jnp.where((lanes >= i * owned) & (lanes < (i + 1) * owned), block, total)
                fields.append(total)
            series_ref[0:8, cols] = fields[0]
            series_ref[8:16, cols] = fields[1]
            row = fields[2][0:1] + row_shift
            col = fields[2][1:2] + col_shift
            col = jnp.where(col < width + 2 * halo, col, -1.0)
            rows_hot[:, cols] = (at == row).astype(jnp.float32).astype(jnp.bfloat16)
            by_gauge = jnp.transpose(jnp.broadcast_to(col, (LANES, LANES)))
            for c in range(planes):
                spot = (lane_iota(LANES) * planes + c).astype(jnp.float32)
                hot = (by_gauge == spot).astype(jnp.float32).astype(jnp.bfloat16)
                cols_hot[part * LANES : (part + 1) * LANES, c * LANES : (c + 1) * LANES] = hot
                cols_hot[wide + part * LANES : wide + (part + 1) * LANES, c * LANES : (c + 1) * LANES] = hot

    def levels_of(start, add):
        hot = rows_hot[...]
        both = []
        for level in range(LEVELS):
            value = series_ref[pl.ds(start + level, 1), :]
            high, low = halves(value)
            both.append(jnp.concatenate([hot * high, hot * low], axis=1))
        both = jnp.concatenate(both, axis=0)
        for first in range(0, planes, 2):
            count = min(2, planes - first)
            total = jnp.dot(
                both, cols_hot[:, first * LANES : (first + count) * LANES], preferred_element_type=jnp.float32
            )
            for level in range(LEVELS):
                for c in range(count):
                    part = total[level * rows_all : (level + 1) * rows_all, c * LANES : (c + 1) * LANES]
                    goal = (start + level, first + c, slice(0, rows_all))
                    force_ref[goal] = force_ref[goal] + part if add else part

    def levels(add):
        def one(index, carry):
            levels_of(index * LEVELS, add)
            return carry

        lax.fori_loop(0, steps // LEVELS, one, 0)

    force_ref[steps] = jnp.zeros_like(force_ref[steps])
    gather_gauges(0)
    levels(False)
    if groups > 1:

        def more(index, carry):
            gather_gauges(index)
            levels(True)
            return carry

        lax.fori_loop(1, groups, more, 0)


def sweep(
    steps, keep_ref, gain_ref, far_ref, near_ref, right_ref, force_ref,
    grad_ref, sums_ref,
    a, fx, fy, keeps, gains, plain,
):
    height, width = keep_ref.shape
    halo = 2 * steps
    inner = width // LANES
    planes = inner + 1
    rows_all = height + 2 * halo
    blocks = rows_all // 8
    my_row, my_lon, row_tiles, lons = my_place()
    reach = 2 * halo
    has_top, has_bottom = my_row > 0, my_row < row_tiles - 1
    has_right = my_lon < lons - 1
    odd = (jnp.zeros((halo, planes * LANES), jnp.int32) + (my_row & 1)) == 1
    lanes8 = lane_iota(8)

    def up(value):
        return pltpu.roll(value, 7, 0)

    def down(value):
        return pltpu.roll(value, 1, 0)

    every = range(planes)
    columns = planes * LANES

    parts = []
    for kind, source in enumerate((keep_ref, gain_ref)):
        far, near = far_ref[kind], near_ref[kind]
        beside = jnp.where(lane_iota(height) < reach, roll_lanes(right_ref[:height], -reach * kind), 0.0)
        whole = jnp.concatenate(
            [
                jnp.where(odd, near, far),
                jnp.concatenate([source[...], beside], axis=1),
                jnp.where(odd, far, near),
            ],
            axis=0,
        )
        parts += halves(whole)
    parts = jnp.concatenate(parts, axis=0)
    shape = (columns, LANES)
    ahead = lax.broadcasted_iota(jnp.int32, shape, 0) - lax.broadcasted_iota(jnp.int32, shape, 1) * planes
    for first in range(0, planes, 2):
        pair = range(first, min(first + 2, planes))
        deal = jnp.concatenate([(ahead == c).astype(jnp.float32).astype(jnp.bfloat16) for c in pair], axis=1)
        dealt = jnp.dot(parts, deal, preferred_element_type=jnp.float32)
        for i, c in enumerate(pair):
            piece = dealt[:, i * LANES : (i + 1) * LANES]
            for kind in range(2):
                at = 2 * kind * rows_all
                plain[kind, c, 0:rows_all, :] = piece[at : at + rows_all] + piece[at + rows_all : at + 2 * rows_all]
    for kind, goal in enumerate((keeps, gains)):
        for q in range(blocks):
            for c in every:
                value = plain[kind, c, pl.ds(q, 8, stride=blocks), :]
                goal[c, 8 * q : 8 * q + 8, :] = value
                if q == 0:
                    goal[c, 8 * blocks : 8 * blocks + 8, :] = up(value)
                if c == 0:
                    goal[planes, 8 * q : 8 * q + 8, :] = roll_lanes(value, -1)

    def cell_mask(column, there):
        lane, plane = column // planes, column % planes
        return plane, jnp.where(lanes8 == lane, there, 1.0)

    column_mask = dict([cell_mask(width, jnp.where(has_right, 1.0, 0.0)), cell_mask(columns - 1, 0.0)])
    assert len(column_mask) == 2
    sublane = lax.broadcasted_iota(jnp.int32, (8, LANES), 0)
    row_mask = {}
    for row, there in ((halo - 1, has_top), (halo + height, has_bottom)):
        row_mask[row % blocks] = jnp.where(sublane == row // blocks, jnp.where(there, 1.0, 0.0), 1.0)

    fx[...] = jnp.zeros_like(fx)
    fy[...] = jnp.zeros_like(fy)
    a[:, 0:rows_all, :] = force_ref[steps - 1, :, 0:rows_all, :]

    def step(index, carry):
        level = jnp.where(index < steps - 1, steps - 2 - index, steps)
        near, ahead, new_y, beside, total, behind = {}, {}, {}, {}, {}, {}

        def rows(q):
            return slice(8 * q, 8 * q + 8)

        def first(q):
            near[q] = [a[c, rows(q % blocks), :] for c in every]
            if q < blocks:
                ahead[q] = near[q][2:] + [roll_lanes(value, -1) for value in near[q][:2]]
            else:
                near[q] = [up(value) for value in near[q]]

        def coefficients(q):
            return [[ref[c, rows(q), :] for c in range(planes + 1)] for ref in (keeps, gains)]

        def second_y(q):
            beside[q + 1] = keep, gain = coefficients(q + 1)
            new_y[q] = [keep[c] * fy[c, rows(q), :] + gain[c] * (near[q + 2][c] - near[q][c]) for c in every]
            for c in every:
                fy[c, rows(q), :] = new_y[q][c]

        def second_x(q):
            keep, gain = beside[q]
            new_x = [
                keep[c + 1] * fx[c, rows(q), :] + gain[c + 1] * (ahead[q][c] - near[q][c]) for c in every
            ]
            behind[q] = [roll_lanes(value, 1) for value in new_x[-2:]] + new_x[:-2]
            before = new_y[q - 2] if q >= 2 else [down(fy[c, rows(q - 2 + blocks), :]) for c in every]
            push = [force_ref[level, c, rows(q), :] for c in every]
            total[q] = [(near[q][c] + push[c]) + (new_y[q][c] - before[c]) + new_x[c] for c in every]
            for c in every:
                fx[c, rows(q), :] = new_x[c]

        def third(q):
            for c in every:
                value = total[q][c] - behind[q][c]
                if c in column_mask:
                    value = value * column_mask[c]
                if q in row_mask:
                    value = value * row_mask[q]
                a[c, rows(q), :] = value

        for q in range(4):
            first(q)
        second_y(0)
        second_y(1)
        for q in range(2, blocks):
            first(q + 2)
            second_y(q)
            second_x(q)
            if q > 2:
                third(q - 1)
        for q in range(2):
            first(q)
            new_y[q] = [fy[c, rows(q), :] for c in every]
            beside[q] = coefficients(q)
        for q in range(2):
            second_x(q)
            third(q - 1 if q else blocks - 1)
        third(1)
        return carry

    lax.fori_loop(0, steps, step, 0)

    start = jnp.where(my_lon > 0, halo, 0)
    for c in every:
        column = lanes8 * planes + c
        known = (column >= start) & (column < width + halo)
        for r in range(0, height, 8):
            s, q = divmod(halo + r, blocks)
            strided = pl.ds(8 * q + s, 8, stride=8)
            value = jnp.where(known & (keeps[c, strided, :] > 0.0), a[c, strided, :], 0.0)
            grad_ref[r : r + 8, c * LANES : (c + 1) * LANES] = value
    length = 2.0 * width
    shape = (8 + halo, planes * LANES)
    kind = lax.broadcasted_iota(jnp.int32, shape, 0)
    column = dealt_column(lax.broadcasted_iota(jnp.int32, shape, 1), planes)
    beyond = column - width
    off = jnp.where(kind == 0, column, jnp.where(kind == 1, -1 - beyond, jnp.where(kind == 2, beyond, width - 1 - beyond)))
    mine = ((kind < 2) & (beyond < 0)) | ((kind >= 2) & (kind < 4) & (beyond >= 0))
    weights = jnp.where(mine, jnp.exp(-jnp.maximum(off, 0).astype(jnp.float32) / length), 0.0)
    weights = jnp.where((kind >= 8) & (beyond == kind - 8), 1.0, weights)
    sums = lax.dot_general(
        weights, grad_ref[...], (((1,), (1,)), ((), ())), precision=lax.Precision.HIGHEST,
        preferred_element_type=jnp.float32,
    )
    for i in range(sums_ref.shape[0]):
        sums_ref[i] = sums


def smooth(halo, order, grad_ref, out_ref, weights_ref, exact_ref):
    width = out_ref.shape[1]
    length = 2.0 * width
    planes = grad_ref.shape[1] // LANES
    column = lax.broadcasted_iota(jnp.int32, (LANES, width), 1)
    lane = lax.broadcasted_iota(jnp.int32, (LANES, width), 0)
    sources = [lane * planes + c for c in range(planes)]
    kernel = jnp.concatenate(
        [jnp.where(x < width, jnp.exp(-jnp.abs(x - column).astype(jnp.float32) / length), 0.0) for x in sources], axis=0
    )
    out_ref[...] = jnp.dot(
        grad_ref[...], kernel, precision=lax.Precision.HIGHEST, preferred_element_type=jnp.float32
    )
    me = lax.axis_index("lon")
    shape = (8 + halo, width)
    kind, column = lax.broadcasted_iota(jnp.int32, shape, 0), lax.broadcasted_iota(jnp.int32, shape, 1)
    for place, source in enumerate(order):
        strip = jnp.where(kind < 2, source, source + 1)
        left = ((kind == 0) | (kind == 2)) & (strip > me)
        right = ((kind == 1) | (kind == 3)) & (strip < me)
        near = (kind >= 8) & (source + 1 == me)
        away = jnp.where(left, (strip - me) * width - column, (me - strip - 1) * width + column + 1)
        away = jnp.where(near, jnp.abs(kind - 8 - column), away)
        weights = jnp.where(left | right | near, jnp.exp(-jnp.maximum(away, 0).astype(jnp.float32) / length), 0.0)
        exact_ref[place * shape[0] : (place + 1) * shape[0], :] = weights
    high, low = halves(exact_ref[...])
    count = high.shape[0]
    for place, part in enumerate((high, high, low)):
        weights_ref[place * count : (place + 1) * count, :] = part


def finish(own_ref, weights_ref, sums_ref, out_ref):
    high, low = halves(sums_ref[...])
    out_ref[...] = own_ref[...] + lax.dot_general(
        jnp.concatenate([high, low, high], axis=0), weights_ref[...], (((0,), (0,)), ((), ())),
        preferred_element_type=jnp.float32,
    )


def f32(*shape):
    return jax.ShapeDtypeStruct(shape, jnp.float32)


def hint(megabytes):
    return pl.CostEstimate(flops=0, bytes_accessed=megabytes * 1000 * 1000, transcendentals=0)


def spaced(rows):
    return 8 * (rows // 8 | 1)


def vmem(count):
    return [pl.BlockSpec(memory_space=pltpu.VMEM)] * count


def local(depth, surface, friction, wet, coastal_tiles, gauge_route, gauge_cell, gauge_times, gauge_resid):
    height, width = depth.shape
    owned = gauge_route.shape[0]
    blocks = gauge_resid.shape[1]
    steps = blocks * STEPS_BLOCK
    halo = 2 * steps
    assert halo == SEG and height == LANES
    tiles = lax.axis_size(GRID_AXES)
    lons = lax.axis_size("lon")
    row_tiles = lax.axis_size(ROW_AXES)
    planes = width // LANES + 1
    rows_all = height + 2 * halo
    params = pltpu.CompilerParams(vmem_limit_bytes=VMEM_LIMIT)

    keep = (1.0 - friction) * wet.astype(jnp.float32)
    gain = ((courant * 0.5) ** 2 * jnp.maximum(depth + surface, depth_floor)) * keep
    samples, coast_count = gauge_resid.shape[2], coastal_tiles.shape[0]
    assert coast_count <= owned

    assert samples >= 3

    def put(array, group, row):
        groups, rows, lanes = array.shape
        return jnp.pad(array, ((group, 2 * blocks + 1 - group - groups), (row, samples - row - rows), (0, owned - lanes)))

    gauges = (
        put(jnp.transpose(gauge_times, (1, 2, 0)), 0, 0)
        + put(gauge_route.reshape(1, 1, owned), 2 * blocks, 0)
        + put(gauge_cell.reshape(1, 1, owned), 2 * blocks, 1)
        + put(coastal_tiles.reshape(1, 1, coast_count), 2 * blocks, 2)
    ).astype(jnp.float32) + put(jnp.transpose(gauge_resid, (1, 2, 0)), blocks, 0)
    west = pl.pallas_call(
        functools.partial(give_west, 2 * halo), out_shape=f32(2 * height, LANES), in_specs=vmem(2), out_specs=vmem(1)[0],
        compiler_params=params, name="give_west",
    )(keep, gain)
    right = lax.ppermute(west, "lon", [(i + 1, i) for i in range(lons - 1)])

    parcel = pl.pallas_call(
        functools.partial(give_gauges, height, width, blocks, samples, coast_count),
        out_shape=f32(tiles, gauge_rows(owned)[0], LANES),
        in_specs=vmem(1) + [pl.BlockSpec(memory_space=pl.ANY)],
        out_specs=vmem(1)[0],
        scratch_shapes=[pltpu.VMEM((24, LANES), jnp.float32)],
        compiler_params=params,
        cost_estimate=hint(10),
        name="give_gauges",
    )(gauges, west)

    def exchange(array, axes, groups=None):
        return lax.all_to_all(array, axes, split_axis=0, concat_axis=0, axis_index_groups=groups, tiled=True)

    order = list(range(lons // 2, lons)) + list(range(lons // 2))[::-1]
    group = sorted(range(tiles), key=lambda tile: (tile % row_tiles in (0, row_tiles - 1), (tile // row_tiles - 1) % lons))
    parcel = exchange(parcel, GRID_AXES, [group])

    far, near = pl.pallas_call(
        functools.partial(give_rows, halo), out_shape=(f32(2, halo, planes * LANES),) * 2, in_specs=vmem(3),
        out_specs=tuple(vmem(2)), compiler_params=params, cost_estimate=hint(40), name="give_rows",
    )(keep, gain, right)
    far = lax.ppermute(far, ROW_AXES, [pair for i in range(1, row_tiles - 1, 2) for pair in ((i, i + 1), (i + 1, i))])
    near = lax.ppermute(near, ROW_AXES, [pair for i in range(0, row_tiles, 2) for pair in ((i, i + 1), (i + 1, i))])

    wide = max(2 * LANES, owned)
    pushes = pl.pallas_call(
        functools.partial(force, steps, halo, height, width),
        out_shape=f32(steps + 1, planes, spaced(rows_all), LANES),
        in_specs=vmem(1),
        out_specs=vmem(1)[0],
        scratch_shapes=[
            pltpu.VMEM((steps, wide), jnp.float32),
            pltpu.VMEM((rows_all, wide), jnp.bfloat16),
            pltpu.VMEM((2 * wide, planes * LANES), jnp.bfloat16),
        ],
        compiler_params=params,
        cost_estimate=pl.CostEstimate(
            flops=4 * steps * rows_all * wide * planes * LANES, bytes_accessed=4 * steps * planes * rows_all * LANES,
            transcendentals=0,
        ),
        name="force",
    )(parcel)

    plane = pltpu.VMEM((planes, spaced(rows_all), LANES), jnp.float32)
    grad, sums = pl.pallas_call(
        functools.partial(sweep, steps),
        out_shape=(f32(height, planes * LANES), f32(lons, 8 + halo, height)),
        in_specs=vmem(6),
        out_specs=tuple(vmem(2)),
        scratch_shapes=[plane] * 3 + [
            pltpu.VMEM((planes + 1, spaced(rows_all + 8), LANES), jnp.float32),
            pltpu.VMEM((planes + 1, spaced(rows_all + 8), LANES), jnp.float32),
            pltpu.VMEM((2, planes, spaced(rows_all), LANES), jnp.float32),
        ],
        compiler_params=params,
        name="sweep",
    )(keep, gain, far, near, right, pushes)

    sums = exchange(sums, "lon", [order])
    own, weights = pl.pallas_call(
        functools.partial(smooth, halo, order),
        out_shape=(f32(height, width), jax.ShapeDtypeStruct((3 * lons * (8 + halo), width), jnp.bfloat16)),
        in_specs=vmem(1),
        out_specs=tuple(vmem(2)),
        scratch_shapes=[pltpu.VMEM((lons * (8 + halo), width), jnp.float32)],
        compiler_params=params,
        cost_estimate=pl.CostEstimate(
            flops=6 * 2 * height * width * width, bytes_accessed=2 * 4 * height * width, transcendentals=width * width
        ),
        name="smooth",
    )(grad)
    return pl.pallas_call(
        finish, out_shape=f32(height, width), in_specs=vmem(3), out_specs=vmem(1)[0], compiler_params=params, name="finish",
    )(own, weights, sums.reshape(lons * (8 + halo), height))


def solution(mesh):
    in_specs = (
        P(("lat", "gau"), "lon"),
        P(("scen", "lat", "gau"), "lon"),
        P(("lat", "gau"), "lon"),
        P(("lat", "gau"), "lon"),
        P(),
        P(("scen", "lon", "lat", "gau"), None),
        P(("scen", "lon", "lat", "gau")),
        P(("scen", "lon", "lat", "gau"), None, None),
        P(("scen", "lon", "lat", "gau"), None, None),
    )
    out_specs = P(("scen", "lat", "gau"), "lon")
    return jax.shard_map(local, mesh=mesh, in_specs=in_specs, out_specs=out_specs, check_vma=False)
```

```python
import functools
import math

import jax
import jax.numpy as jnp
from jax import lax
from jax.experimental import pallas as pl
from jax.experimental.pallas import tpu as pltpu
from jax.sharding import PartitionSpec as P

STEPS_BLOCK = 8
LANES = 128
SEG = 32
LEVELS = 16

courant = 0.45
depth_floor = 0.1

GRID_AXES = ("lon", "lat", "gau")
ROW_AXES = ("lat", "gau")
VMEM_LIMIT = 16 * 1024 * 1024


def roll_lanes(x, shift):
    shift = shift % LANES
    return x if shift == 0 else pltpu.roll(x, shift, 1)


def lane_iota(rows):
    return lax.broadcasted_iota(jnp.int32, (rows, LANES), 1)


def gauge_rows(owned):
    if 3 * owned <= LANES:
        return STEPS_BLOCK, owned
    assert owned <= LANES
    return 3 * STEPS_BLOCK, 0


def my_place():
    row = lax.axis_index("lat") * lax.axis_size("gau") + lax.axis_index("gau")
    return row, lax.axis_index("lon"), lax.axis_size("lat") * lax.axis_size("gau"), lax.axis_size("lon")


def give_east(reach, keep_ref, gain_ref, east_ref):
    height, width = keep_ref.shape
    last = slice(width - LANES, width)
    upper = lane_iota(height) >= LANES - reach
    east_ref[:height] = jnp.where(upper, keep_ref[:, last], roll_lanes(gain_ref[:, last], reach))
    east_ref[height:] = jnp.zeros((east_ref.shape[0] - height, LANES), jnp.float32)


def give_rows(halo, keep_ref, gain_ref, left_ref, far_ref, near_ref):
    height, width = keep_ref.shape
    upper = lane_iota(halo) >= LANES - 2 * halo
    odd = my_place()[0] & 1
    for goal, south in ((far_ref, odd), (near_ref, 1 - odd)):
        rows = pl.ds(pl.multiple_of(south * (height - halo), halo), halo)
        for kind, source in enumerate((keep_ref, gain_ref)):
            goal[kind, :, :width] = source[rows, :]
            goal[kind, :, width:] = jnp.where(upper, roll_lanes(left_ref[rows, :], 2 * halo * kind), 0.0)


def give_gauges(height, width, blocks, samples, coast_count, gauge_ref, after_ref, parcel_ref, block_ref):
    row_tiles = lax.axis_size("lat") * lax.axis_size("gau")
    owned = gauge_ref.shape[2]
    assert blocks == 2
    route, cell, coast = (gauge_ref[2 * blocks, i : i + 1, :].astype(jnp.int32) for i in range(3))
    target = jnp.zeros_like(route)
    for entry in range(coast_count):
        target = jnp.where(route == entry, jnp.broadcast_to(coast[:, entry : entry + 1], route.shape), target)
    row_bits, width_bits = int(math.log2(row_tiles)), int(math.log2(width))
    assert row_tiles == 1 << row_bits and width == 1 << width_bits
    grid_row = (target & (row_tiles - 1)) * height + (cell >> width_bits)
    grid_col = (target >> row_bits) * width + (cell & (width - 1))
    block_ref[...] = jnp.zeros_like(block_ref)
    levels = lax.broadcasted_iota(jnp.int32, (STEPS_BLOCK, owned), 0).astype(jnp.float32)
    for block in range(blocks):
        series = jnp.zeros((STEPS_BLOCK, owned), jnp.float32)
        for sample in range(samples):
            times = gauge_ref[block, sample : sample + 1, :]
            resid = gauge_ref[blocks + block, sample : sample + 1, :]
            series = series + jnp.where(times == levels, resid, 0.0)
        block_ref[block * STEPS_BLOCK : (block + 1) * STEPS_BLOCK, :owned] = series
    at = blocks * STEPS_BLOCK
    block_ref[at : at + 1, :owned] = grid_row.astype(jnp.float32)
    block_ref[at + 1 : at + 2, :owned] = grid_col.astype(jnp.float32)
    size, apart = gauge_rows(owned)
    gauges = block_ref[...]
    if size == STEPS_BLOCK:
        gauges = sum(
            roll_lanes(gauges[i * STEPS_BLOCK : (i + 1) * STEPS_BLOCK], i * apart) for i in range(3)
        )
    tiles = parcel_ref.shape[0]

    def put(tile, carry):
        parcel_ref[tile, 0:size, :] = gauges
        return carry

    lax.fori_loop(0, tiles, put, 0, unroll=tiles <= 16)


def halves(value):
    high = value.astype(jnp.bfloat16)
    return high, (value - high.astype(jnp.float32)).astype(jnp.bfloat16)


def dealt_column(place, planes):
    return (place & (LANES - 1)) * planes + place // LANES


def force(steps, halo, height, width, parcel_ref, force_ref, series_ref, rows_hot, cols_hot):
    planes, rows_all = force_ref.shape[1], height + 2 * halo
    my_row, my_lon, row_tiles, lons = my_place()
    wide = rows_hot.shape[1]
    tiles, parcel_rows = parcel_ref.shape[:2]
    size = parcel_rows
    apart = wide // tiles if size == STEPS_BLOCK else 0
    owned = apart if apart else LANES
    group = wide // owned
    groups = tiles // group
    per_plane = LANES // owned
    blocks = rows_all // 8
    row_shift = (halo - my_row * height).astype(jnp.float32)
    col_shift = (-my_lon * width).astype(jnp.float32)
    place = lax.broadcasted_iota(jnp.int32, (rows_all, LANES), 0)
    at = ((place & 7) * blocks + (place >> 3)).astype(jnp.float32)

    def gather_gauges(index):
        lanes = lane_iota(STEPS_BLOCK)
        for part in range(wide // LANES):
            cols = slice(part * LANES, (part + 1) * LANES)
            fields = []
            for field in range(3):
                total = jnp.zeros((STEPS_BLOCK, LANES), jnp.float32)
                rows = slice(0, 8) if apart else slice(8 * field, 8 * field + 8)
                for i in range(per_plane):
                    source = index * group + part * per_plane + i
                    block = roll_lanes(parcel_ref[source, rows, :], i * owned - field * apart)
                    total = jnp.where((lanes >= i * owned) & (lanes < (i + 1) * owned), block, total)
                fields.append(total)
            series_ref[0:8, cols] = fields[0]
            series_ref[8:16, cols] = fields[1]
            row = fields[2][0:1] + row_shift
            col = fields[2][1:2] + col_shift
            inside = jnp.where(col < width, col, -1.0)
            col = jnp.where(col >= 0, inside, jnp.where(col >= -2 * halo, col + float(planes * LANES), -1.0))
            rows_hot[:, cols] = (at == row).astype(jnp.float32).astype(jnp.bfloat16)
            by_gauge = jnp.transpose(jnp.broadcast_to(col, (LANES, LANES)))
            for c in range(planes):
                spot = (lane_iota(LANES) * planes + c).astype(jnp.float32)
                hot = (by_gauge == spot).astype(jnp.float32).astype(jnp.bfloat16)
                cols_hot[part * LANES : (part + 1) * LANES, c * LANES : (c + 1) * LANES] = hot
                cols_hot[wide + part * LANES : wide + (part + 1) * LANES, c * LANES : (c + 1) * LANES] = hot

    def levels_of(start, add):
        hot = rows_hot[...]
        both = []
        for level in range(LEVELS):
            value = series_ref[pl.ds(start + level, 1), :]
            high, low = halves(value)
            both.append(jnp.concatenate([hot * high, hot * low], axis=1))
        both = jnp.concatenate(both, axis=0)
        for first in range(0, planes, 2):
            count = min(2, planes - first)
            total = jnp.dot(
                both, cols_hot[:, first * LANES : (first + count) * LANES], preferred_element_type=jnp.float32
            )
            for level in range(LEVELS):
                for c in range(count):
                    part = total[level * rows_all : (level + 1) * rows_all, c * LANES : (c + 1) * LANES]
                    goal = (start + level, first + c, slice(0, rows_all))
                    force_ref[goal] = force_ref[goal] + part if add else part

    def levels(add):
        def one(index, carry):
            levels_of(index * LEVELS, add)
            return carry

        lax.fori_loop(0, steps // LEVELS, one, 0)

    force_ref[steps] = jnp.zeros_like(force_ref[steps])
    gather_gauges(0)
    levels(False)
    if groups > 1:

        def more(index, carry):
            gather_gauges(index)
            levels(True)
            return carry

        lax.fori_loop(1, groups, more, 0)


def sweep(
    steps, keep_ref, gain_ref, far_ref, near_ref, left_ref, force_ref,
    grad_ref, sums_ref,
    a, fx, fy, keeps, gains, plain,
):
    height, width = keep_ref.shape
    halo = 2 * steps
    inner = width // LANES
    planes = inner + 1
    rows_all = height + 2 * halo
    blocks = rows_all // 8
    my_row, my_lon, row_tiles, lons = my_place()
    reach = 2 * halo
    has_top, has_bottom = my_row > 0, my_row < row_tiles - 1
    has_left = my_lon > 0
    odd = (jnp.zeros((halo, planes * LANES), jnp.int32) + (my_row & 1)) == 1
    lanes8 = lane_iota(8)

    def up(value):
        return pltpu.roll(value, 7, 0)

    def down(value):
        return pltpu.roll(value, 1, 0)

    every = range(planes)
    columns = planes * LANES

    parts = []
    for kind, source in enumerate((keep_ref, gain_ref)):
        far, near = far_ref[kind], near_ref[kind]
        beside = jnp.where(lane_iota(height) >= LANES - reach, roll_lanes(left_ref[:height], reach * kind), 0.0)
        whole = jnp.concatenate(
            [
                jnp.where(odd, near, far),
                jnp.concatenate([source[...], beside], axis=1),
                jnp.where(odd, far, near),
            ],
            axis=0,
        )
        parts += halves(whole)
    parts = jnp.concatenate(parts, axis=0)
    shape = (columns, LANES)
    ahead = lax.broadcasted_iota(jnp.int32, shape, 0) - lax.broadcasted_iota(jnp.int32, shape, 1) * planes
    for first in range(0, planes, 2):
        pair = range(first, min(first + 2, planes))
        deal = jnp.concatenate([(ahead == c).astype(jnp.float32).astype(jnp.bfloat16) for c in pair], axis=1)
        dealt = jnp.dot(parts, deal, preferred_element_type=jnp.float32)
        for i, c in enumerate(pair):
            piece = dealt[:, i * LANES : (i + 1) * LANES]
            for kind in range(2):
                at = 2 * kind * rows_all
                plain[kind, c, 0:rows_all, :] = piece[at : at + rows_all] + piece[at + rows_all : at + 2 * rows_all]
    for kind, goal in enumerate((keeps, gains)):
        for q in range(blocks):
            for c in every:
                value = plain[kind, c, pl.ds(q, 8, stride=blocks), :]
                goal[c, 8 * q : 8 * q + 8, :] = value
                if q == 0:
                    goal[c, 8 * blocks : 8 * blocks + 8, :] = up(value)
                if c == 0:
                    goal[planes, 8 * q : 8 * q + 8, :] = roll_lanes(value, -1)

    def cell_mask(column, there):
        lane, plane = column // planes, column % planes
        return plane, jnp.where(lanes8 == lane, there, 1.0)

    column_mask = dict([cell_mask(width, 0.0), cell_mask(columns - 1, jnp.where(has_left, 1.0, 0.0))])
    assert len(column_mask) == 2
    sublane = lax.broadcasted_iota(jnp.int32, (8, LANES), 0)
    row_mask = {}
    for row, there in ((halo - 1, has_top), (halo + height, has_bottom)):
        row_mask[row % blocks] = jnp.where(sublane == row // blocks, jnp.where(there, 1.0, 0.0), 1.0)

    fx[...] = jnp.zeros_like(fx)
    fy[...] = jnp.zeros_like(fy)
    a[:, 0:rows_all, :] = force_ref[steps - 1, :, 0:rows_all, :]

    def step(index, carry):
        level = jnp.where(index < steps - 1, steps - 2 - index, steps)
        near, ahead, new_y, beside, total, behind = {}, {}, {}, {}, {}, {}

        def rows(q):
            return slice(8 * q, 8 * q + 8)

        def first(q):
            near[q] = [a[c, rows(q % blocks), :] for c in every]
            if q < blocks:
                ahead[q] = near[q][2:] + [roll_lanes(value, -1) for value in near[q][:2]]
            else:
                near[q] = [up(value) for value in near[q]]

        def coefficients(q):
            return [[ref[c, rows(q), :] for c in range(planes + 1)] for ref in (keeps, gains)]

        def second_y(q):
            beside[q + 1] = keep, gain = coefficients(q + 1)
            new_y[q] = [keep[c] * fy[c, rows(q), :] + gain[c] * (near[q + 2][c] - near[q][c]) for c in every]
            for c in every:
                fy[c, rows(q), :] = new_y[q][c]

        def second_x(q):
            keep, gain = beside[q]
            new_x = [
                keep[c + 1] * fx[c, rows(q), :] + gain[c + 1] * (ahead[q][c] - near[q][c]) for c in every
            ]
            behind[q] = [roll_lanes(value, 1) for value in new_x[-2:]] + new_x[:-2]
            before = new_y[q - 2] if q >= 2 else [down(fy[c, rows(q - 2 + blocks), :]) for c in every]
            push = [force_ref[level, c, rows(q), :] for c in every]
            total[q] = [(near[q][c] + push[c]) + (new_y[q][c] - before[c]) + new_x[c] for c in every]
            for c in every:
                fx[c, rows(q), :] = new_x[c]

        def third(q):
            for c in every:
                value = total[q][c] - behind[q][c]
                if c in column_mask:
                    value = value * column_mask[c]
                if q in row_mask:
                    value = value * row_mask[q]
                a[c, rows(q), :] = value

        for q in range(4):
            first(q)
        second_y(0)
        second_y(1)
        for q in range(2, blocks):
            first(q + 2)
            second_y(q)
            second_x(q)
            if q > 2:
                third(q - 1)
        for q in range(2):
            first(q)
            new_y[q] = [fy[c, rows(q), :] for c in every]
            beside[q] = coefficients(q)
        for q in range(2):
            second_x(q)
            third(q - 1 if q else blocks - 1)
        third(1)
        return carry

    lax.fori_loop(0, steps, step, 0)

    stop = jnp.where(my_lon < lons - 1, width - halo, width)
    for c in every:
        column = lanes8 * planes + c
        known = (column < stop) | (column >= columns - halo)
        for r in range(0, height, 8):
            s, q = divmod(halo + r, blocks)
            strided = pl.ds(8 * q + s, 8, stride=8)
            value = jnp.where(known & (keeps[c, strided, :] > 0.0), a[c, strided, :], 0.0)
            grad_ref[r : r + 8, c * LANES : (c + 1) * LANES] = value
    length = 2.0 * width
    shape = (8 + halo, planes * LANES)
    kind = lax.broadcasted_iota(jnp.int32, shape, 0)
    column = dealt_column(lax.broadcasted_iota(jnp.int32, shape, 1), planes)
    own, back = column < width, columns - 1 - column
    off = jnp.where(kind == 0, column, jnp.where(kind == 1, width - 1 - column, jnp.where(kind == 2, width - 1 - back, back)))
    mine = ((kind < 2) & own) | ((kind >= 2) & (kind < 4) & ~own)
    weights = jnp.where(mine, jnp.exp(-jnp.maximum(off, 0).astype(jnp.float32) / length), 0.0)
    weights = jnp.where((kind >= 8) & (column == columns - halo - 8 + kind), 1.0, weights)
    sums = lax.dot_general(
        weights, grad_ref[...], (((1,), (1,)), ((), ())), precision=lax.Precision.HIGHEST,
        preferred_element_type=jnp.float32,
    )
    for i in range(sums_ref.shape[0]):
        sums_ref[i] = sums


def smooth(halo, order, grad_ref, out_ref, weights_ref, exact_ref):
    width = out_ref.shape[1]
    length = 2.0 * width
    planes = grad_ref.shape[1] // LANES
    column = lax.broadcasted_iota(jnp.int32, (LANES, width), 1)
    lane = lax.broadcasted_iota(jnp.int32, (LANES, width), 0)
    sources = [lane * planes + c for c in range(planes)]
    kernel = jnp.concatenate(
        [jnp.where(x < width, jnp.exp(-jnp.abs(x - column).astype(jnp.float32) / length), 0.0) for x in sources], axis=0
    )
    out_ref[...] = jnp.dot(
        grad_ref[...], kernel, precision=lax.Precision.HIGHEST, preferred_element_type=jnp.float32
    )
    me = lax.axis_index("lon")
    shape = (8 + halo, width)
    kind, column = lax.broadcasted_iota(jnp.int32, shape, 0), lax.broadcasted_iota(jnp.int32, shape, 1)
    for place, source in enumerate(order):
        strip = jnp.where(kind < 2, source, source - 1)
        left = ((kind == 0) | (kind == 2)) & (strip > me)
        right = ((kind == 1) | (kind == 3)) & (strip < me)
        near = (kind >= 8) & (source - 1 == me)
        away = jnp.where(left, (strip - me) * width - column, (me - strip - 1) * width + column + 1)
        away = jnp.where(near, jnp.abs(width - halo - 8 + kind - column), away)
        weights = jnp.where(left | right | near, jnp.exp(-jnp.maximum(away, 0).astype(jnp.float32) / length), 0.0)
        exact_ref[place * shape[0] : (place + 1) * shape[0], :] = weights
    high, low = halves(exact_ref[...])
    count = high.shape[0]
    for place, part in enumerate((high, high, low)):
        weights_ref[place * count : (place + 1) * count, :] = part


def finish(own_ref, weights_ref, sums_ref, out_ref):
    high, low = halves(sums_ref[...])
    out_ref[...] = own_ref[...] + lax.dot_general(
        jnp.concatenate([high, low, high], axis=0), weights_ref[...], (((0,), (0,)), ((), ())),
        preferred_element_type=jnp.float32,
    )


def f32(*shape):
    return jax.ShapeDtypeStruct(shape, jnp.float32)


def hint(megabytes):
    return pl.CostEstimate(flops=0, bytes_accessed=megabytes * 1000 * 1000, transcendentals=0)


def spaced(rows):
    return 8 * (rows // 8 | 1)


def vmem(count):
    return [pl.BlockSpec(memory_space=pltpu.VMEM)] * count


def local(depth, surface, friction, wet, coastal_tiles, gauge_route, gauge_cell, gauge_times, gauge_resid):
    height, width = depth.shape
    owned = gauge_route.shape[0]
    blocks = gauge_resid.shape[1]
    steps = blocks * STEPS_BLOCK
    halo = 2 * steps
    assert halo == SEG and height == LANES
    tiles = lax.axis_size(GRID_AXES)
    lons = lax.axis_size("lon")
    row_tiles = lax.axis_size(ROW_AXES)
    planes = width // LANES + 1
    rows_all = height + 2 * halo
    params = pltpu.CompilerParams(vmem_limit_bytes=VMEM_LIMIT)

    keep = (1.0 - friction) * wet.astype(jnp.float32)
    gain = ((courant * 0.5) ** 2 * jnp.maximum(depth + surface, depth_floor)) * keep
    samples, coast_count = gauge_resid.shape[2], coastal_tiles.shape[0]
    assert coast_count <= owned

    assert samples >= 3

    def put(array, group, row):
        groups, rows, lanes = array.shape
        return jnp.pad(array, ((group, 2 * blocks + 1 - group - groups), (row, samples - row - rows), (0, owned - lanes)))

    gauges = (
        put(jnp.transpose(gauge_times, (1, 2, 0)), 0, 0)
        + put(gauge_route.reshape(1, 1, owned), 2 * blocks, 0)
        + put(gauge_cell.reshape(1, 1, owned), 2 * blocks, 1)
        + put(coastal_tiles.reshape(1, 1, coast_count), 2 * blocks, 2)
    ).astype(jnp.float32) + put(jnp.transpose(gauge_resid, (1, 2, 0)), blocks, 0)
    east = pl.pallas_call(
        functools.partial(give_east, 2 * halo), out_shape=f32(2 * height, LANES), in_specs=vmem(2), out_specs=vmem(1)[0],
        compiler_params=params, name="give_east",
    )(keep, gain)
    left = lax.ppermute(east, "lon", [(i, i + 1) for i in range(lons - 1)])

    parcel = pl.pallas_call(
        functools.partial(give_gauges, height, width, blocks, samples, coast_count),
        out_shape=f32(tiles, gauge_rows(owned)[0], LANES),
        in_specs=vmem(1) + [pl.BlockSpec(memory_space=pl.ANY)],
        out_specs=vmem(1)[0],
        scratch_shapes=[pltpu.VMEM((24, LANES), jnp.float32)],
        compiler_params=params,
        cost_estimate=hint(10),
        name="give_gauges",
    )(gauges, east)

    def exchange(array, axes, groups=None):
        return lax.all_to_all(array, axes, split_axis=0, concat_axis=0, axis_index_groups=groups, tiled=True)

    order = list(range(lons // 2))[::-1] + list(range(lons // 2, lons))
    group = sorted(range(tiles), key=lambda tile: (tile % row_tiles in (0, row_tiles - 1), order.index(tile // row_tiles)))
    parcel = exchange(parcel, GRID_AXES, [group])

    far, near = pl.pallas_call(
        functools.partial(give_rows, halo), out_shape=(f32(2, halo, planes * LANES),) * 2, in_specs=vmem(3),
        out_specs=tuple(vmem(2)), compiler_params=params, cost_estimate=hint(40), name="give_rows",
    )(keep, gain, left)
    far = lax.ppermute(far, ROW_AXES, [pair for i in range(1, row_tiles - 1, 2) for pair in ((i, i + 1), (i + 1, i))])
    near = lax.ppermute(near, ROW_AXES, [pair for i in range(0, row_tiles, 2) for pair in ((i, i + 1), (i + 1, i))])

    wide = max(2 * LANES, owned)
    pushes = pl.pallas_call(
        functools.partial(force, steps, halo, height, width),
        out_shape=f32(steps + 1, planes, spaced(rows_all), LANES),
        in_specs=vmem(1),
        out_specs=vmem(1)[0],
        scratch_shapes=[
            pltpu.VMEM((steps, wide), jnp.float32),
            pltpu.VMEM((rows_all, wide), jnp.bfloat16),
            pltpu.VMEM((2 * wide, planes * LANES), jnp.bfloat16),
        ],
        compiler_params=params,
        cost_estimate=pl.CostEstimate(
            flops=4 * steps * rows_all * wide * planes * LANES, bytes_accessed=4 * steps * planes * rows_all * LANES,
            transcendentals=0,
        ),
        name="force",
    )(parcel)

    plane = pltpu.VMEM((planes, spaced(rows_all), LANES), jnp.float32)
    grad, sums = pl.pallas_call(
        functools.partial(sweep, steps),
        out_shape=(f32(height, planes * LANES), f32(lons, 8 + halo, height)),
        in_specs=vmem(6),
        out_specs=tuple(vmem(2)),
        scratch_shapes=[plane] * 3 + [
            pltpu.VMEM((planes + 1, spaced(rows_all + 8), LANES), jnp.float32),
            pltpu.VMEM((planes + 1, spaced(rows_all + 8), LANES), jnp.float32),
            pltpu.VMEM((2, planes, spaced(rows_all), LANES), jnp.float32),
        ],
        compiler_params=params,
        name="sweep",
    )(keep, gain, far, near, left, pushes)

    order = list(range(1, lons - 1)) + [0, lons - 1]
    sums = exchange(sums, "lon", [order])
    own, weights = pl.pallas_call(
        functools.partial(smooth, halo, order),
        out_shape=(f32(height, width), jax.ShapeDtypeStruct((3 * lons * (8 + halo), width), jnp.bfloat16)),
        in_specs=vmem(1),
        out_specs=tuple(vmem(2)),
        scratch_shapes=[pltpu.VMEM((lons * (8 + halo), width), jnp.float32)],
        compiler_params=params,
        cost_estimate=pl.CostEstimate(
            flops=6 * 2 * height * width * width, bytes_accessed=2 * 4 * height * width, transcendentals=width * width
        ),
        name="smooth",
    )(grad)
    return pl.pallas_call(
        finish, out_shape=f32(height, width), in_specs=vmem(3), out_specs=vmem(1)[0], compiler_params=params, name="finish",
    )(own, weights, sums.reshape(lons * (8 + halo), height))


def solution(mesh):
    in_specs = (
        P(("lat", "gau"), "lon"),
        P(("scen", "lat", "gau"), "lon"),
        P(("lat", "gau"), "lon"),
        P(("lat", "gau"), "lon"),
        P(),
        P(("scen", "lon", "lat", "gau"), None),
        P(("scen", "lon", "lat", "gau")),
        P(("scen", "lon", "lat", "gau"), None, None),
        P(("scen", "lon", "lat", "gau"), None, None),
    )
    out_specs = P(("scen", "lat", "gau"), "lon")
    return jax.shard_map(local, mesh=mesh, in_specs=in_specs, out_specs=out_specs, check_vma=False)
```

```python
import functools
import math

import jax
import jax.numpy as jnp
from jax import lax
from jax.experimental import pallas as pl
from jax.experimental.pallas import tpu as pltpu
from jax.sharding import PartitionSpec as P

STEPS_BLOCK = 8
LANES = 128
SEG = 32
LEVELS = 16

courant = 0.45
depth_floor = 0.1

GRID_AXES = ("lon", "lat", "gau")
ROW_AXES = ("lat", "gau")
VMEM_LIMIT = 16 * 1024 * 1024


def roll_lanes(x, shift):
    shift = shift % LANES
    return x if shift == 0 else pltpu.roll(x, shift, 1)


def lane_iota(rows):
    return lax.broadcasted_iota(jnp.int32, (rows, LANES), 1)


def gauge_rows(owned):
    if 3 * owned <= LANES:
        return STEPS_BLOCK, owned
    assert owned <= LANES
    return 3 * STEPS_BLOCK, 0


def my_place():
    row = lax.axis_index("lat") * lax.axis_size("gau") + lax.axis_index("gau")
    return row, lax.axis_index("lon"), lax.axis_size("lat") * lax.axis_size("gau"), lax.axis_size("lon")


def give_rows(halo, keep_ref, gain_ref, right_ref, far_ref, near_ref):
    height, width = keep_ref.shape
    lower = lane_iota(halo) < 2 * halo
    odd = my_place()[0] & 1
    for goal, south in ((far_ref, odd), (near_ref, 1 - odd)):
        rows = pl.ds(pl.multiple_of(south * (height - halo), halo), halo)
        for kind, source in enumerate((keep_ref, gain_ref)):
            goal[kind, :, :width] = source[rows, :]
            goal[kind, :, width:] = jnp.where(lower, roll_lanes(right_ref[rows, :], -2 * halo * kind), 0.0)


def prepare(reach, count, *refs):
    given, (keep_ref, gain_ref, west_ref, parcel_ref) = refs[:count], refs[count : count + 4]
    here, (block_ref, arrived) = refs[count + 4 : 2 * count + 4], refs[2 * count + 4 :]
    copies = [pltpu.make_async_copy(given[i], here[i], arrived.at[i]) for i in range(count)]
    for copy in copies:
        copy.start()
    depth_ref, surface_ref, friction_ref, wet_ref, coast_ref, route_ref, cell_ref, times_ref, resid_ref = here
    height, width = depth_ref.shape
    row_tiles = lax.axis_size("lat") * lax.axis_size("gau")
    for copy in copies[4:]:
        copy.wait()
    owned = route_ref.shape[1]
    blocks, samples = times_ref.shape[:2]
    assert blocks == 2
    route, cell, coast = route_ref[...], cell_ref[...], coast_ref[...]
    target = jnp.zeros_like(route)
    for entry in range(coast.shape[1]):
        target = jnp.where(route == entry, jnp.broadcast_to(coast[:, entry : entry + 1], route.shape), target)
    row_bits, width_bits = int(math.log2(row_tiles)), int(math.log2(width))
    assert row_tiles == 1 << row_bits and width == 1 << width_bits
    grid_row = (target & (row_tiles - 1)) * height + (cell >> width_bits)
    grid_col = (target >> row_bits) * width + (cell & (width - 1))
    block_ref[...] = jnp.zeros_like(block_ref)
    levels = lax.broadcasted_iota(jnp.int32, (STEPS_BLOCK, owned), 0)
    for block in range(blocks):
        series = jnp.zeros((STEPS_BLOCK, owned), jnp.float32)
        for sample in range(samples):
            times = times_ref[block, sample : sample + 1, :]
            resid = resid_ref[block, sample : sample + 1, :]
            series = series + jnp.where(times == levels, resid, 0.0)
        block_ref[block * STEPS_BLOCK : (block + 1) * STEPS_BLOCK, :owned] = series
    at = blocks * STEPS_BLOCK
    block_ref[at : at + 1, :owned] = grid_row.astype(jnp.float32)
    block_ref[at + 1 : at + 2, :owned] = grid_col.astype(jnp.float32)
    size, apart = gauge_rows(owned)
    gauges = block_ref[...]
    if size == STEPS_BLOCK:
        gauges = sum(
            roll_lanes(gauges[i * STEPS_BLOCK : (i + 1) * STEPS_BLOCK], i * apart) for i in range(3)
        )
    tiles = parcel_ref.shape[0]

    def put(tile, carry):
        parcel_ref[tile, 0:size, :] = gauges
        return carry

    lax.fori_loop(0, tiles, put, 0, unroll=tiles <= 16)

    for copy in copies[:4]:
        copy.wait()
    keep = (1.0 - friction_ref[...]) * wet_ref[...].astype(jnp.float32)
    gain = ((courant * 0.5) ** 2 * jnp.maximum(depth_ref[...] + surface_ref[...], depth_floor)) * keep
    keep_ref[...], gain_ref[...] = keep, gain
    lower = lane_iota(height) < reach
    west_ref[:height] = jnp.where(lower, keep[:, :LANES], roll_lanes(gain[:, :LANES], reach))
    west_ref[height:] = jnp.zeros((west_ref.shape[0] - height, LANES), jnp.float32)


def halves(value):
    high = value.astype(jnp.bfloat16)
    return high, (value - high.astype(jnp.float32)).astype(jnp.bfloat16)


def dealt_column(place, planes):
    return (place & (LANES - 1)) * planes + place // LANES


def force(steps, halo, height, width, parcel_ref, force_ref, series_ref, rows_hot, cols_hot):
    planes, rows_all = force_ref.shape[1], height + 2 * halo
    my_row, my_lon, row_tiles, lons = my_place()
    wide = rows_hot.shape[1]
    tiles, parcel_rows = parcel_ref.shape[:2]
    size = parcel_rows
    apart = wide // tiles if size == STEPS_BLOCK else 0
    owned = apart if apart else LANES
    group = wide // owned
    groups = tiles // group
    per_plane = LANES // owned
    blocks = rows_all // 8
    row_shift = (halo - my_row * height).astype(jnp.float32)
    col_shift = (-my_lon * width).astype(jnp.float32)
    place = lax.broadcasted_iota(jnp.int32, (rows_all, LANES), 0)
    at = ((place & 7) * blocks + (place >> 3)).astype(jnp.float32)

    def gather_gauges(index):
        lanes = lane_iota(STEPS_BLOCK)
        for part in range(wide // LANES):
            cols = slice(part * LANES, (part + 1) * LANES)
            fields = []
            for field in range(3):
                total = jnp.zeros((STEPS_BLOCK, LANES), jnp.float32)
                rows = slice(0, 8) if apart else slice(8 * field, 8 * field + 8)
                for i in range(per_plane):
                    source = index * group + part * per_plane + i
                    block = roll_lanes(parcel_ref[source, rows, :], i * owned - field * apart)
                    total = jnp.where((lanes >= i * owned) & (lanes < (i + 1) * owned), block, total)
                fields.append(total)
            series_ref[0:8, cols] = fields[0]
            series_ref[8:16, cols] = fields[1]
            row = fields[2][0:1] + row_shift
            col = fields[2][1:2] + col_shift
            col = jnp.where(col < width + 2 * halo, col, -1.0)
            rows_hot[:, cols] = (at == row).astype(jnp.float32).astype(jnp.bfloat16)
            by_gauge = jnp.transpose(jnp.broadcast_to(col, (LANES, LANES)))
            for c in range(planes):
                spot = (lane_iota(LANES) * planes + c).astype(jnp.float32)
                hot = (by_gauge == spot).astype(jnp.float32).astype(jnp.bfloat16)
                cols_hot[part * LANES : (part + 1) * LANES, c * LANES : (c + 1) * LANES] = hot
                cols_hot[wide + part * LANES : wide + (part + 1) * LANES, c * LANES : (c + 1) * LANES] = hot

    def levels_of(start, add):
        hot = rows_hot[...]
        both = []
        for level in range(LEVELS):
            value = series_ref[pl.ds(start + level, 1), :]
            high, low = halves(value)
            both.append(jnp.concatenate([hot * high, hot * low], axis=1))
        both = jnp.concatenate(both, axis=0)
        for first in range(0, planes, 2):
            count = min(2, planes - first)
            total = jnp.dot(
                both, cols_hot[:, first * LANES : (first + count) * LANES], preferred_element_type=jnp.float32
            )
            for level in range(LEVELS):
                for c in range(count):
                    part = total[level * rows_all : (level + 1) * rows_all, c * LANES : (c + 1) * LANES]
                    goal = (start + level, first + c, slice(0, rows_all))
                    force_ref[goal] = force_ref[goal] + part if add else part

    def levels(add):
        def one(index, carry):
            levels_of(index * LEVELS, add)
            return carry

        lax.fori_loop(0, steps // LEVELS, one, 0)

    force_ref[steps] = jnp.zeros_like(force_ref[steps])
    gather_gauges(0)
    levels(False)
    if groups > 1:

        def more(index, carry):
            gather_gauges(index)
            levels(True)
            return carry

        lax.fori_loop(1, groups, more, 0)


def sweep(
    steps, keep_ref, gain_ref, far_ref, near_ref, right_ref, force_ref,
    grad_ref, sums_ref,
    a, fx, fy, keeps, gains, plain,
):
    height, width = keep_ref.shape
    halo = 2 * steps
    inner = width // LANES
    planes = inner + 1
    rows_all = height + 2 * halo
    blocks = rows_all // 8
    my_row, my_lon, row_tiles, lons = my_place()
    reach = 2 * halo
    has_top, has_bottom = my_row > 0, my_row < row_tiles - 1
    has_right = my_lon < lons - 1
    odd = (jnp.zeros((halo, planes * LANES), jnp.int32) + (my_row & 1)) == 1
    lanes8 = lane_iota(8)

    def up(value):
        return pltpu.roll(value, 7, 0)

    def down(value):
        return pltpu.roll(value, 1, 0)

    every = range(planes)
    columns = planes * LANES

    parts = []
    for kind, source in enumerate((keep_ref, gain_ref)):
        far, near = far_ref[kind], near_ref[kind]
        beside = jnp.where(lane_iota(height) < reach, roll_lanes(right_ref[:height], -reach * kind), 0.0)
        whole = jnp.concatenate(
            [
                jnp.where(odd, near, far),
                jnp.concatenate([source[...], beside], axis=1),
                jnp.where(odd, far, near),
            ],
            axis=0,
        )
        parts += halves(whole)
    parts = jnp.concatenate(parts, axis=0)
    shape = (columns, LANES)
    ahead = lax.broadcasted_iota(jnp.int32, shape, 0) - lax.broadcasted_iota(jnp.int32, shape, 1) * planes
    for first in range(0, planes, 2):
        pair = range(first, min(first + 2, planes))
        deal = jnp.concatenate([(ahead == c).astype(jnp.float32).astype(jnp.bfloat16) for c in pair], axis=1)
        dealt = jnp.dot(parts, deal, preferred_element_type=jnp.float32)
        for i, c in enumerate(pair):
            piece = dealt[:, i * LANES : (i + 1) * LANES]
            for kind in range(2):
                at = 2 * kind * rows_all
                plain[kind, c, 0:rows_all, :] = piece[at : at + rows_all] + piece[at + rows_all : at + 2 * rows_all]
    for kind, goal in enumerate((keeps, gains)):
        for q in range(blocks):
            for c in every:
                value = plain[kind, c, pl.ds(q, 8, stride=blocks), :]
                goal[c, 8 * q : 8 * q + 8, :] = value
                if q == 0:
                    goal[c, 8 * blocks : 8 * blocks + 8, :] = up(value)
                if c == 0:
                    goal[planes, 8 * q : 8 * q + 8, :] = roll_lanes(value, -1)

    def cell_mask(column, there):
        lane, plane = column // planes, column % planes
        return plane, jnp.where(lanes8 == lane, there, 1.0)

    column_mask = dict([cell_mask(width, jnp.where(has_right, 1.0, 0.0)), cell_mask(columns - 1, 0.0)])
    assert len(column_mask) == 2
    sublane = lax.broadcasted_iota(jnp.int32, (8, LANES), 0)
    row_mask = {}
    for row, there in ((halo - 1, has_top), (halo + height, has_bottom)):
        row_mask[row % blocks] = jnp.where(sublane == row // blocks, jnp.where(there, 1.0, 0.0), 1.0)

    fx[...] = jnp.zeros_like(fx)
    fy[...] = jnp.zeros_like(fy)
    a[:, 0:rows_all, :] = force_ref[steps - 1, :, 0:rows_all, :]

    def step(index, carry):
        level = jnp.where(index < steps - 1, steps - 2 - index, steps)
        near, ahead, new_y, beside, total, behind = {}, {}, {}, {}, {}, {}

        def rows(q):
            return slice(8 * q, 8 * q + 8)

        def first(q):
            near[q] = [a[c, rows(q % blocks), :] for c in every]
            if q < blocks:
                ahead[q] = near[q][2:] + [roll_lanes(value, -1) for value in near[q][:2]]
            else:
                near[q] = [up(value) for value in near[q]]

        def coefficients(q):
            return [[ref[c, rows(q), :] for c in range(planes + 1)] for ref in (keeps, gains)]

        def second_y(q):
            beside[q + 1] = keep, gain = coefficients(q + 1)
            new_y[q] = [keep[c] * fy[c, rows(q), :] + gain[c] * (near[q + 2][c] - near[q][c]) for c in every]
            for c in every:
                fy[c, rows(q), :] = new_y[q][c]

        def second_x(q):
            keep, gain = beside[q]
            new_x = [
                keep[c + 1] * fx[c, rows(q), :] + gain[c + 1] * (ahead[q][c] - near[q][c]) for c in every
            ]
            behind[q] = [roll_lanes(value, 1) for value in new_x[-2:]] + new_x[:-2]
            before = new_y[q - 2] if q >= 2 else [down(fy[c, rows(q - 2 + blocks), :]) for c in every]
            push = [force_ref[level, c, rows(q), :] for c in every]
            total[q] = [(near[q][c] + push[c]) + (new_y[q][c] - before[c]) + new_x[c] for c in every]
            for c in every:
                fx[c, rows(q), :] = new_x[c]

        def third(q):
            for c in every:
                value = total[q][c] - behind[q][c]
                if c in column_mask:
                    value = value * column_mask[c]
                if q in row_mask:
                    value = value * row_mask[q]
                a[c, rows(q), :] = value

        for q in range(4):
            first(q)
        second_y(0)
        second_y(1)
        for q in range(2, blocks):
            first(q + 2)
            second_y(q)
            second_x(q)
            if q > 2:
                third(q - 1)
        for q in range(2):
            first(q)
            new_y[q] = [fy[c, rows(q), :] for c in every]
            beside[q] = coefficients(q)
        for q in range(2):
            second_x(q)
            third(q - 1 if q else blocks - 1)
        third(1)
        return carry

    lax.fori_loop(0, steps, step, 0)

    start = jnp.where(my_lon > 0, halo, 0)
    for c in every:
        column = lanes8 * planes + c
        known = (column >= start) & (column < width + halo)
        for r in range(0, height, 8):
            s, q = divmod(halo + r, blocks)
            strided = pl.ds(8 * q + s, 8, stride=8)
            value = jnp.where(known & (keeps[c, strided, :] > 0.0), a[c, strided, :], 0.0)
            grad_ref[r : r + 8, c * LANES : (c + 1) * LANES] = value
    length = 2.0 * width
    shape = (8 + halo, planes * LANES)
    kind = lax.broadcasted_iota(jnp.int32, shape, 0)
    column = dealt_column(lax.broadcasted_iota(jnp.int32, shape, 1), planes)
    beyond = column - width
    off = jnp.where(kind == 0, column, jnp.where(kind == 1, -1 - beyond, jnp.where(kind == 2, beyond, width - 1 - beyond)))
    mine = ((kind < 2) & (beyond < 0)) | ((kind >= 2) & (kind < 4) & (beyond >= 0))
    weights = jnp.where(mine, jnp.exp(-jnp.maximum(off, 0).astype(jnp.float32) / length), 0.0)
    weights = jnp.where((kind >= 8) & (beyond == kind - 8), 1.0, weights)
    sums = lax.dot_general(
        weights, grad_ref[...], (((1,), (1,)), ((), ())), precision=lax.Precision.HIGHEST,
        preferred_element_type=jnp.float32,
    )
    for i in range(sums_ref.shape[0]):
        sums_ref[i] = sums


def smooth(halo, order, grad_ref, out_ref, weights_ref, exact_ref):
    width = out_ref.shape[1]
    length = 2.0 * width
    planes = grad_ref.shape[1] // LANES
    column = lax.broadcasted_iota(jnp.int32, (LANES, width), 1)
    lane = lax.broadcasted_iota(jnp.int32, (LANES, width), 0)
    sources = [lane * planes + c for c in range(planes)]
    kernel = jnp.concatenate(
        [jnp.where(x < width, jnp.exp(-jnp.abs(x - column).astype(jnp.float32) / length), 0.0) for x in sources], axis=0
    )
    out_ref[...] = jnp.dot(
        grad_ref[...], kernel, precision=lax.Precision.HIGHEST, preferred_element_type=jnp.float32
    )
    me = lax.axis_index("lon")
    shape = (8 + halo, width)
    kind, column = lax.broadcasted_iota(jnp.int32, shape, 0), lax.broadcasted_iota(jnp.int32, shape, 1)
    for place, source in enumerate(order):
        strip = jnp.where(kind < 2, source, source + 1)
        left = ((kind == 0) | (kind == 2)) & (strip > me)
        right = ((kind == 1) | (kind == 3)) & (strip < me)
        near = (kind >= 8) & (source + 1 == me)
        away = jnp.where(left, (strip - me) * width - column, (me - strip - 1) * width + column + 1)
        away = jnp.where(near, jnp.abs(kind - 8 - column), away)
        weights = jnp.where(left | right | near, jnp.exp(-jnp.maximum(away, 0).astype(jnp.float32) / length), 0.0)
        exact_ref[place * shape[0] : (place + 1) * shape[0], :] = weights
    high, low = halves(exact_ref[...])
    count = high.shape[0]
    for place, part in enumerate((high, high, low)):
        weights_ref[place * count : (place + 1) * count, :] = part


def finish(own_ref, weights_ref, sums_ref, out_ref):
    high, low = halves(sums_ref[...])
    out_ref[...] = own_ref[...] + lax.dot_general(
        jnp.concatenate([high, low, high], axis=0), weights_ref[...], (((0,), (0,)), ((), ())),
        preferred_element_type=jnp.float32,
    )


def f32(*shape):
    return jax.ShapeDtypeStruct(shape, jnp.float32)


def hint(megabytes):
    return pl.CostEstimate(flops=0, bytes_accessed=megabytes * 1000 * 1000, transcendentals=0)


def spaced(rows):
    return 8 * (rows // 8 | 1)


def vmem(count):
    return [pl.BlockSpec(memory_space=pltpu.VMEM)] * count


def local(depth, surface, friction, wet, coastal_tiles, gauge_route, gauge_cell, gauge_times, gauge_resid):
    height, width = depth.shape
    owned = gauge_route.shape[0]
    blocks = gauge_resid.shape[1]
    steps = blocks * STEPS_BLOCK
    halo = 2 * steps
    assert halo == SEG and height == LANES
    tiles = lax.axis_size(GRID_AXES)
    lons = lax.axis_size("lon")
    row_tiles = lax.axis_size(ROW_AXES)
    planes = width // LANES + 1
    rows_all = height + 2 * halo
    params = pltpu.CompilerParams(vmem_limit_bytes=VMEM_LIMIT)

    given = (
        depth, surface, friction, wet, coastal_tiles.reshape(1, -1), gauge_route.reshape(1, owned),
        gauge_cell.reshape(1, owned), jnp.transpose(gauge_times, (1, 2, 0)), jnp.transpose(gauge_resid, (1, 2, 0)),
    )
    keep, gain, west, parcel = pl.pallas_call(
        functools.partial(prepare, 2 * halo, len(given)),
        out_shape=(
            f32(height, width), f32(height, width), f32(2 * height, LANES), f32(tiles, gauge_rows(owned)[0], LANES),
        ),
        in_specs=[pl.BlockSpec(memory_space=pl.ANY)] * len(given),
        out_specs=tuple(vmem(4)),
        scratch_shapes=[pltpu.VMEM(array.shape, array.dtype) for array in given] + [
            pltpu.VMEM((24, LANES), jnp.float32), pltpu.SemaphoreType.DMA((len(given),)),
        ],
        compiler_params=pltpu.CompilerParams(vmem_limit_bytes=62 * 1024 * 1024),
        name="prepare",
    )(*given)
    right = lax.ppermute(west, "lon", [(i + 1, i) for i in range(lons - 1)])

    def exchange(array, axes, groups=None):
        return lax.all_to_all(array, axes, split_axis=0, concat_axis=0, axis_index_groups=groups, tiled=True)

    group = sorted(range(tiles), key=lambda tile: (tile % row_tiles in (0, row_tiles - 1), -(tile // row_tiles)))
    parcel = exchange(parcel, GRID_AXES, [group])

    far, near = pl.pallas_call(
        functools.partial(give_rows, halo), out_shape=(f32(2, halo, planes * LANES),) * 2, in_specs=vmem(3),
        out_specs=tuple(vmem(2)), compiler_params=params, cost_estimate=hint(40), name="give_rows",
    )(keep, gain, right)
    far = lax.ppermute(far, ROW_AXES, [pair for i in range(1, row_tiles - 1, 2) for pair in ((i, i + 1), (i + 1, i))])
    near = lax.ppermute(near, ROW_AXES, [pair for i in range(0, row_tiles, 2) for pair in ((i, i + 1), (i + 1, i))])

    wide = max(2 * LANES, owned)
    pushes = pl.pallas_call(
        functools.partial(force, steps, halo, height, width),
        out_shape=f32(steps + 1, planes, spaced(rows_all), LANES),
        in_specs=vmem(1),
        out_specs=vmem(1)[0],
        scratch_shapes=[
            pltpu.VMEM((steps, wide), jnp.float32),
            pltpu.VMEM((rows_all, wide), jnp.bfloat16),
            pltpu.VMEM((2 * wide, planes * LANES), jnp.bfloat16),
        ],
        compiler_params=params,
        cost_estimate=pl.CostEstimate(
            flops=4 * steps * rows_all * wide * planes * LANES, bytes_accessed=4 * steps * planes * rows_all * LANES,
            transcendentals=0,
        ),
        name="force",
    )(parcel)

    plane = pltpu.VMEM((planes, spaced(rows_all), LANES), jnp.float32)
    grad, sums = pl.pallas_call(
        functools.partial(sweep, steps),
        out_shape=(f32(height, planes * LANES), f32(lons, 8 + halo, height)),
        in_specs=vmem(6),
        out_specs=tuple(vmem(2)),
        scratch_shapes=[plane] * 3 + [
            pltpu.VMEM((planes + 1, spaced(rows_all + 8), LANES), jnp.float32),
            pltpu.VMEM((planes + 1, spaced(rows_all + 8), LANES), jnp.float32),
            pltpu.VMEM((2, planes, spaced(rows_all), LANES), jnp.float32),
        ],
        compiler_params=params,
        name="sweep",
    )(keep, gain, far, near, right, pushes)

    order = list(range(lons // 2, lons)) + list(range(lons // 2))[::-1]
    sums = exchange(sums, "lon", [order])
    own, weights = pl.pallas_call(
        functools.partial(smooth, halo, order),
        out_shape=(f32(height, width), jax.ShapeDtypeStruct((3 * lons * (8 + halo), width), jnp.bfloat16)),
        in_specs=vmem(1),
        out_specs=tuple(vmem(2)),
        scratch_shapes=[pltpu.VMEM((lons * (8 + halo), width), jnp.float32)],
        compiler_params=params,
        cost_estimate=pl.CostEstimate(
            flops=6 * 2 * height * width * width, bytes_accessed=2 * 4 * height * width, transcendentals=width * width
        ),
        name="smooth",
    )(grad)
    return pl.pallas_call(
        finish, out_shape=f32(height, width), in_specs=vmem(3), out_specs=vmem(1)[0], compiler_params=params, name="finish",
    )(own, weights, sums.reshape(lons * (8 + halo), height))


def solution(mesh):
    in_specs = (
        P(("lat", "gau"), "lon"),
        P(("scen", "lat", "gau"), "lon"),
        P(("lat", "gau"), "lon"),
        P(("lat", "gau"), "lon"),
        P(),
        P(("scen", "lon", "lat", "gau"), None),
        P(("scen", "lon", "lat", "gau")),
        P(("scen", "lon", "lat", "gau"), None, None),
        P(("scen", "lon", "lat", "gau"), None, None),
    )
    out_specs = P(("scen", "lat", "gau"), "lon")
    return jax.shard_map(local, mesh=mesh, in_specs=in_specs, out_specs=out_specs, check_vma=False)
```

```python
import functools
import math

import jax
import jax.numpy as jnp
from jax import lax
from jax.experimental import pallas as pl
from jax.experimental.pallas import tpu as pltpu
from jax.sharding import PartitionSpec as P

STEPS_BLOCK = 8
LANES = 128
SEG = 32
LEVELS = 16

courant = 0.45
depth_floor = 0.1

GRID_AXES = ("lon", "lat", "gau")
ROW_AXES = ("lat", "gau")
VMEM_LIMIT = 16 * 1024 * 1024


def roll_lanes(x, shift):
    shift = shift % LANES
    return x if shift == 0 else pltpu.roll(x, shift, 1)


def lane_iota(rows):
    return lax.broadcasted_iota(jnp.int32, (rows, LANES), 1)


def gauge_rows(owned):
    if 3 * owned <= LANES:
        return STEPS_BLOCK, owned
    assert owned <= LANES
    return 3 * STEPS_BLOCK, 0


def my_place():
    row = lax.axis_index("lat") * lax.axis_size("gau") + lax.axis_index("gau")
    return row, lax.axis_index("lon"), lax.axis_size("lat") * lax.axis_size("gau"), lax.axis_size("lon")


def give_west(reach, keep_ref, gain_ref, west_ref):
    height = keep_ref.shape[0]
    lower = lane_iota(height) < reach
    west_ref[:height] = jnp.where(lower, keep_ref[:, :LANES], roll_lanes(gain_ref[:, :LANES], reach))
    west_ref[height:] = jnp.zeros((west_ref.shape[0] - height, LANES), jnp.float32)


def give_rows(halo, keep_ref, gain_ref, right_ref, far_ref, near_ref):
    height, width = keep_ref.shape
    lower = lane_iota(halo) < 2 * halo
    odd = my_place()[0] & 1
    for goal, south in ((far_ref, odd), (near_ref, 1 - odd)):
        rows = pl.ds(pl.multiple_of(south * (height - halo), halo), halo)
        for kind, source in enumerate((keep_ref, gain_ref)):
            goal[kind, :, :width] = source[rows, :]
            goal[kind, :, width:] = jnp.where(lower, roll_lanes(right_ref[rows, :], -2 * halo * kind), 0.0)


def give_gauges(height, width, blocks, samples, coast_count, gauge_ref, after_ref, parcel_ref, block_ref):
    row_tiles = lax.axis_size("lat") * lax.axis_size("gau")
    owned = gauge_ref.shape[2]
    assert blocks == 2
    route, cell, coast = (gauge_ref[2 * blocks, i : i + 1, :].astype(jnp.int32) for i in range(3))
    target = jnp.zeros_like(route)
    for entry in range(coast_count):
        target = jnp.where(route == entry, jnp.broadcast_to(coast[:, entry : entry + 1], route.shape), target)
    row_bits, width_bits = int(math.log2(row_tiles)), int(math.log2(width))
    assert row_tiles == 1 << row_bits and width == 1 << width_bits
    grid_row = (target & (row_tiles - 1)) * height + (cell >> width_bits)
    grid_col = (target >> row_bits) * width + (cell & (width - 1))
    block_ref[...] = jnp.zeros_like(block_ref)
    levels = lax.broadcasted_iota(jnp.int32, (STEPS_BLOCK, owned), 0).astype(jnp.float32)
    for block in range(blocks):
        series = jnp.zeros((STEPS_BLOCK, owned), jnp.float32)
        for sample in range(samples):
            times = gauge_ref[block, sample : sample + 1, :]
            resid = gauge_ref[blocks + block, sample : sample + 1, :]
            series = series + jnp.where(times == levels, resid, 0.0)
        block_ref[block * STEPS_BLOCK : (block + 1) * STEPS_BLOCK, :owned] = series
    at = blocks * STEPS_BLOCK
    block_ref[at : at + 1, :owned] = grid_row.astype(jnp.float32)
    block_ref[at + 1 : at + 2, :owned] = grid_col.astype(jnp.float32)
    size, apart = gauge_rows(owned)
    gauges = block_ref[...]
    if size == STEPS_BLOCK:
        gauges = sum(
            roll_lanes(gauges[i * STEPS_BLOCK : (i + 1) * STEPS_BLOCK], i * apart) for i in range(3)
        )
    tiles = parcel_ref.shape[0]

    def put(tile, carry):
        parcel_ref[tile, 0:size, :] = gauges
        return carry

    lax.fori_loop(0, tiles, put, 0, unroll=tiles <= 16)


def halves(value):
    high = value.astype(jnp.bfloat16)
    return high, (value - high.astype(jnp.float32)).astype(jnp.bfloat16)


def dealt_column(place, planes):
    return (place & (LANES - 1)) * planes + place // LANES


def force(steps, halo, height, width, parcel_ref, force_ref, series_ref, rows_hot, cols_hot):
    planes, rows_all = force_ref.shape[1], height + 2 * halo
    my_row, my_lon, row_tiles, lons = my_place()
    wide = rows_hot.shape[1]
    tiles, parcel_rows = parcel_ref.shape[:2]
    size = parcel_rows
    apart = wide // tiles if size == STEPS_BLOCK else 0
    owned = apart if apart else LANES
    group = wide // owned
    groups = tiles // group
    per_plane = LANES // owned
    blocks = rows_all // 8
    row_shift = (halo - my_row * height).astype(jnp.float32)
    col_shift = (-my_lon * width).astype(jnp.float32)
    place = lax.broadcasted_iota(jnp.int32, (rows_all, LANES), 0)
    at = ((place & 7) * blocks + (place >> 3)).astype(jnp.float32)

    def gather_gauges(index):
        lanes = lane_iota(STEPS_BLOCK)
        for part in range(wide // LANES):
            cols = slice(part * LANES, (part + 1) * LANES)
            fields = []
            for field in range(3):
                total = jnp.zeros((STEPS_BLOCK, LANES), jnp.float32)
                rows = slice(0, 8) if apart else slice(8 * field, 8 * field + 8)
                for i in range(per_plane):
                    source = index * group + part * per_plane + i
                    block = roll_lanes(parcel_ref[source, rows, :], i * owned - field * apart)
                    total = jnp.where((lanes >= i * owned) & (lanes < (i + 1) * owned), block, total)
                fields.append(total)
            series_ref[0:8, cols] = fields[0]
            series_ref[8:16, cols] = fields[1]
            row = fields[2][0:1] + row_shift
            col = fields[2][1:2] + col_shift
            col = jnp.where(col < width + 2 * halo, col, -1.0)
            rows_hot[:, cols] = (at == row).astype(jnp.float32).astype(jnp.bfloat16)
            by_gauge = jnp.transpose(jnp.broadcast_to(col, (LANES, LANES)))
            for c in range(planes):
                spot = (lane_iota(LANES) * planes + c).astype(jnp.float32)
                hot = (by_gauge == spot).astype(jnp.float32).astype(jnp.bfloat16)
                cols_hot[part * LANES : (part + 1) * LANES, c * LANES : (c + 1) * LANES] = hot
                cols_hot[wide + part * LANES : wide + (part + 1) * LANES, c * LANES : (c + 1) * LANES] = hot

    def levels_of(start, add):
        hot = rows_hot[...]
        both = []
        for level in range(LEVELS):
            value = series_ref[pl.ds(start + level, 1), :]
            high, low = halves(value)
            both.append(jnp.concatenate([hot * high, hot * low], axis=1))
        both = jnp.concatenate(both, axis=0)
        for first in range(0, planes, 2):
            count = min(2, planes - first)
            total = jnp.dot(
                both, cols_hot[:, first * LANES : (first + count) * LANES], preferred_element_type=jnp.float32
            )
            for level in range(LEVELS):
                for c in range(count):
                    part = total[level * rows_all : (level + 1) * rows_all, c * LANES : (c + 1) * LANES]
                    goal = (start + level, first + c, slice(0, rows_all))
                    force_ref[goal] = force_ref[goal] + part if add else part

    def levels(add):
        def one(index, carry):
            levels_of(index * LEVELS, add)
            return carry

        lax.fori_loop(0, steps // LEVELS, one, 0)

    force_ref[steps] = jnp.zeros_like(force_ref[steps])
    gather_gauges(0)
    levels(False)
    if groups > 1:

        def more(index, carry):
            gather_gauges(index)
            levels(True)
            return carry

        lax.fori_loop(1, groups, more, 0)


def sweep(
    steps, keep_ref, gain_ref, far_ref, near_ref, right_ref, force_ref,
    grad_ref, sums_ref,
    a, fx, fy, keeps, gains, plain,
):
    height, width = keep_ref.shape
    halo = 2 * steps
    inner = width // LANES
    planes = inner + 1
    rows_all = height + 2 * halo
    blocks = rows_all // 8
    my_row, my_lon, row_tiles, lons = my_place()
    reach = 2 * halo
    has_top, has_bottom = my_row > 0, my_row < row_tiles - 1
    has_right = my_lon < lons - 1
    odd = (jnp.zeros((halo, planes * LANES), jnp.int32) + (my_row & 1)) == 1
    lanes8 = lane_iota(8)

    def up(value):
        return pltpu.roll(value, 7, 0)

    def down(value):
        return pltpu.roll(value, 1, 0)

    every = range(planes)
    columns = planes * LANES

    parts = []
    for kind, source in enumerate((keep_ref, gain_ref)):
        far, near = far_ref[kind], near_ref[kind]
        beside = jnp.where(lane_iota(height) < reach, roll_lanes(right_ref[:height], -reach * kind), 0.0)
        whole = jnp.concatenate(
            [
                jnp.where(odd, near, far),
                jnp.concatenate([source[...], beside], axis=1),
                jnp.where(odd, far, near),
            ],
            axis=0,
        )
        parts += halves(whole)
    parts = jnp.concatenate(parts, axis=0)
    shape = (columns, LANES)
    ahead = lax.broadcasted_iota(jnp.int32, shape, 0) - lax.broadcasted_iota(jnp.int32, shape, 1) * planes
    for first in range(0, planes, 2):
        pair = range(first, min(first + 2, planes))
        deal = jnp.concatenate([(ahead == c).astype(jnp.float32).astype(jnp.bfloat16) for c in pair], axis=1)
        dealt = jnp.dot(parts, deal, preferred_element_type=jnp.float32)
        for i, c in enumerate(pair):
            piece = dealt[:, i * LANES : (i + 1) * LANES]
            for kind in range(2):
                at = 2 * kind * rows_all
                plain[kind, c, 0:rows_all, :] = piece[at : at + rows_all] + piece[at + rows_all : at + 2 * rows_all]
    for kind, goal in enumerate((keeps, gains)):
        for q in range(blocks):
            for c in every:
                value = plain[kind, c, pl.ds(q, 8, stride=blocks), :]
                goal[c, 8 * q : 8 * q + 8, :] = value
                if q == 0:
                    goal[c, 8 * blocks : 8 * blocks + 8, :] = up(value)
                if c == 0:
                    goal[planes, 8 * q : 8 * q + 8, :] = roll_lanes(value, -1)

    def cell_mask(column, there):
        lane, plane = column // planes, column % planes
        return plane, jnp.where(lanes8 == lane, there, 1.0)

    column_mask = dict([cell_mask(width, jnp.where(has_right, 1.0, 0.0)), cell_mask(columns - 1, 0.0)])
    assert len(column_mask) == 2
    sublane = lax.broadcasted_iota(jnp.int32, (8, LANES), 0)
    row_mask = {}
    for row, there in ((halo - 1, has_top), (halo + height, has_bottom)):
        row_mask[row % blocks] = jnp.where(sublane == row // blocks, jnp.where(there, 1.0, 0.0), 1.0)

    fx[...] = jnp.zeros_like(fx)
    fy[...] = jnp.zeros_like(fy)
    a[:, 0:rows_all, :] = force_ref[steps - 1, :, 0:rows_all, :]

    def step(index, carry):
        level = jnp.where(index < steps - 1, steps - 2 - index, steps)
        near, ahead, new_y, beside, total, behind = {}, {}, {}, {}, {}, {}

        def rows(q):
            return slice(8 * q, 8 * q + 8)

        def first(q):
            near[q] = [a[c, rows(q % blocks), :] for c in every]
            if q < blocks:
                ahead[q] = near[q][2:] + [roll_lanes(value, -1) for value in near[q][:2]]
            else:
                near[q] = [up(value) for value in near[q]]

        def coefficients(q):
            return [[ref[c, rows(q), :] for c in range(planes + 1)] for ref in (keeps, gains)]

        def second_y(q):
            beside[q + 1] = keep, gain = coefficients(q + 1)
            new_y[q] = [keep[c] * fy[c, rows(q), :] + gain[c] * (near[q + 2][c] - near[q][c]) for c in every]
            for c in every:
                fy[c, rows(q), :] = new_y[q][c]

        def second_x(q):
            keep, gain = beside[q]
            new_x = [
                keep[c + 1] * fx[c, rows(q), :] + gain[c + 1] * (ahead[q][c] - near[q][c]) for c in every
            ]
            behind[q] = [roll_lanes(value, 1) for value in new_x[-2:]] + new_x[:-2]
            before = new_y[q - 2] if q >= 2 else [down(fy[c, rows(q - 2 + blocks), :]) for c in every]
            push = [force_ref[level, c, rows(q), :] for c in every]
            total[q] = [(near[q][c] + push[c]) + (new_y[q][c] - before[c]) + new_x[c] for c in every]
            for c in every:
                fx[c, rows(q), :] = new_x[c]

        def third(q):
            for c in every:
                value = total[q][c] - behind[q][c]
                if c in column_mask:
                    value = value * column_mask[c]
                if q in row_mask:
                    value = value * row_mask[q]
                a[c, rows(q), :] = value

        for q in range(4):
            first(q)
        second_y(0)
        second_y(1)
        for q in range(2, blocks):
            first(q + 2)
            second_y(q)
            second_x(q)
            if q > 2:
                third(q - 1)
        for q in range(2):
            first(q)
            new_y[q] = [fy[c, rows(q), :] for c in every]
            beside[q] = coefficients(q)
        for q in range(2):
            second_x(q)
            third(q - 1 if q else blocks - 1)
        third(1)
        return carry

    lax.fori_loop(0, steps, step, 0)

    start = jnp.where(my_lon > 0, halo, 0)
    for c in every:
        column = lanes8 * planes + c
        known = (column >= start) & (column < width + halo)
        for r in range(0, height, 8):
            s, q = divmod(halo + r, blocks)
            strided = pl.ds(8 * q + s, 8, stride=8)
            value = jnp.where(known & (keeps[c, strided, :] > 0.0), a[c, strided, :], 0.0)
            grad_ref[r : r + 8, c * LANES : (c + 1) * LANES] = value
    length = 2.0 * width
    shape = (8 + halo, planes * LANES)
    kind = lax.broadcasted_iota(jnp.int32, shape, 0)
    column = dealt_column(lax.broadcasted_iota(jnp.int32, shape, 1), planes)
    beyond = column - width
    off = jnp.where(kind == 0, column, jnp.where(kind == 1, -1 - beyond, jnp.where(kind == 2, beyond, width - 1 - beyond)))
    mine = ((kind < 2) & (beyond < 0)) | ((kind >= 2) & (kind < 4) & (beyond >= 0))
    weights = jnp.where(mine, jnp.exp(-jnp.maximum(off, 0).astype(jnp.float32) / length), 0.0)
    weights = jnp.where((kind >= 8) & (beyond == kind - 8), 1.0, weights)
    sums = lax.dot_general(
        weights, grad_ref[...], (((1,), (1,)), ((), ())), precision=lax.Precision.HIGHEST,
        preferred_element_type=jnp.float32,
    )
    for i in range(sums_ref.shape[0]):
        sums_ref[i] = sums


def smooth(halo, order, grad_ref, out_ref, weights_ref, exact_ref):
    width = out_ref.shape[1]
    length = 2.0 * width
    planes = grad_ref.shape[1] // LANES
    column = lax.broadcasted_iota(jnp.int32, (LANES, width), 1)
    lane = lax.broadcasted_iota(jnp.int32, (LANES, width), 0)
    sources = [lane * planes + c for c in range(planes)]
    kernel = jnp.concatenate(
        [jnp.where(x < width, jnp.exp(-jnp.abs(x - column).astype(jnp.float32) / length), 0.0) for x in sources], axis=0
    )
    out_ref[...] = jnp.dot(
        grad_ref[...], kernel, precision=lax.Precision.HIGHEST, preferred_element_type=jnp.float32
    )
    me = lax.axis_index("lon")
    shape = (8 + halo, width)
    kind, column = lax.broadcasted_iota(jnp.int32, shape, 0), lax.broadcasted_iota(jnp.int32, shape, 1)
    for place, source in enumerate(order):
        strip = jnp.where(kind < 2, source, source + 1)
        left = ((kind == 0) | (kind == 2)) & (strip > me)
        right = ((kind == 1) | (kind == 3)) & (strip < me)
        near = (kind >= 8) & (source + 1 == me)
        away = jnp.where(left, (strip - me) * width - column, (me - strip - 1) * width + column + 1)
        away = jnp.where(near, jnp.abs(kind - 8 - column), away)
        weights = jnp.where(left | right | near, jnp.exp(-jnp.maximum(away, 0).astype(jnp.float32) / length), 0.0)
        exact_ref[place * shape[0] : (place + 1) * shape[0], :] = weights
    high, low = halves(exact_ref[...])
    count = high.shape[0]
    for place, part in enumerate((high, high, low)):
        weights_ref[place * count : (place + 1) * count, :] = part


def finish(own_ref, weights_ref, sums_ref, out_ref):
    high, low = halves(sums_ref[...])
    out_ref[...] = own_ref[...] + lax.dot_general(
        jnp.concatenate([high, low, high], axis=0), weights_ref[...], (((0,), (0,)), ((), ())),
        preferred_element_type=jnp.float32,
    )


def f32(*shape):
    return jax.ShapeDtypeStruct(shape, jnp.float32)


def hint(megabytes):
    return pl.CostEstimate(flops=0, bytes_accessed=megabytes * 1000 * 1000, transcendentals=0)


def spaced(rows):
    return 8 * (rows // 8 | 1)


def vmem(count):
    return [pl.BlockSpec(memory_space=pltpu.VMEM)] * count


def local(depth, surface, friction, wet, coastal_tiles, gauge_route, gauge_cell, gauge_times, gauge_resid):
    height, width = depth.shape
    owned = gauge_route.shape[0]
    blocks = gauge_resid.shape[1]
    steps = blocks * STEPS_BLOCK
    halo = 2 * steps
    assert halo == SEG and height == LANES
    tiles = lax.axis_size(GRID_AXES)
    lons = lax.axis_size("lon")
    row_tiles = lax.axis_size(ROW_AXES)
    planes = width // LANES + 1
    rows_all = height + 2 * halo
    params = pltpu.CompilerParams(vmem_limit_bytes=VMEM_LIMIT)

    keep = (1.0 - friction) * wet.astype(jnp.float32)
    gain = ((courant * 0.5) ** 2 * jnp.maximum(depth + surface, depth_floor)) * keep
    samples, coast_count = gauge_resid.shape[2], coastal_tiles.shape[0]
    assert coast_count <= owned

    assert samples >= 3

    def put(array, group, row):
        groups, rows, lanes = array.shape
        return jnp.pad(array, ((group, 2 * blocks + 1 - group - groups), (row, samples - row - rows), (0, owned - lanes)))

    gauges = (
        put(jnp.transpose(gauge_times, (1, 2, 0)), 0, 0)
        + put(gauge_route.reshape(1, 1, owned), 2 * blocks, 0)
        + put(gauge_cell.reshape(1, 1, owned), 2 * blocks, 1)
        + put(coastal_tiles.reshape(1, 1, coast_count), 2 * blocks, 2)
    ).astype(jnp.float32) + put(jnp.transpose(gauge_resid, (1, 2, 0)), blocks, 0)
    west = pl.pallas_call(
        functools.partial(give_west, 2 * halo), out_shape=f32(2 * height, LANES), in_specs=vmem(2), out_specs=vmem(1)[0],
        compiler_params=params, name="give_west",
    )(keep, gain)
    right = lax.ppermute(west, "lon", [(i + 1, i) for i in range(lons - 1)])

    parcel = pl.pallas_call(
        functools.partial(give_gauges, height, width, blocks, samples, coast_count),
        out_shape=f32(tiles, gauge_rows(owned)[0], LANES),
        in_specs=vmem(1) + [pl.BlockSpec(memory_space=pl.ANY)],
        out_specs=vmem(1)[0],
        scratch_shapes=[pltpu.VMEM((24, LANES), jnp.float32)],
        compiler_params=params,
        cost_estimate=hint(10),
        name="give_gauges",
    )(gauges, west)

    def exchange(array, axes, groups=None):
        return lax.all_to_all(array, axes, split_axis=0, concat_axis=0, axis_index_groups=groups, tiled=True)

    group = sorted(range(tiles), key=lambda tile: (tile % row_tiles in (0, row_tiles - 1), -(tile // row_tiles)))
    parcel = exchange(parcel, GRID_AXES, [group])

    far, near = pl.pallas_call(
        functools.partial(give_rows, halo), out_shape=(f32(2, halo, planes * LANES),) * 2, in_specs=vmem(3),
        out_specs=tuple(vmem(2)), compiler_params=params, cost_estimate=hint(40), name="give_rows",
    )(keep, gain, right)
    far = lax.ppermute(far, ROW_AXES, [pair for i in range(1, row_tiles - 1, 2) for pair in ((i, i + 1), (i + 1, i))])
    near = lax.ppermute(near, ROW_AXES, [pair for i in range(0, row_tiles, 2) for pair in ((i, i + 1), (i + 1, i))])

    wide = max(2 * LANES, owned)
    pushes = pl.pallas_call(
        functools.partial(force, steps, halo, height, width),
        out_shape=f32(steps + 1, planes, spaced(rows_all), LANES),
        in_specs=vmem(1),
        out_specs=vmem(1)[0],
        scratch_shapes=[
            pltpu.VMEM((steps, wide), jnp.float32),
            pltpu.VMEM((rows_all, wide), jnp.bfloat16),
            pltpu.VMEM((2 * wide, planes * LANES), jnp.bfloat16),
        ],
        compiler_params=params,
        cost_estimate=pl.CostEstimate(
            flops=4 * steps * rows_all * wide * planes * LANES, bytes_accessed=4 * steps * planes * rows_all * LANES,
            transcendentals=0,
        ),
        name="force",
    )(parcel)

    plane = pltpu.VMEM((planes, spaced(rows_all), LANES), jnp.float32)
    grad, sums = pl.pallas_call(
        functools.partial(sweep, steps),
        out_shape=(f32(height, planes * LANES), f32(lons, 8 + halo, height)),
        in_specs=vmem(6),
        out_specs=tuple(vmem(2)),
        scratch_shapes=[plane] * 3 + [
            pltpu.VMEM((planes + 1, spaced(rows_all + 8), LANES), jnp.float32),
            pltpu.VMEM((planes + 1, spaced(rows_all + 8), LANES), jnp.float32),
            pltpu.VMEM((2, planes, spaced(rows_all), LANES), jnp.float32),
        ],
        compiler_params=params,
        name="sweep",
    )(keep, gain, far, near, right, pushes)

    order = list(range(lons // 2, lons)) + list(range(lons // 2))[::-1]
    sums = exchange(sums, "lon", [order])
    own, weights = pl.pallas_call(
        functools.partial(smooth, halo, order),
        out_shape=(f32(height, width), jax.ShapeDtypeStruct((3 * lons * (8 + halo), width), jnp.bfloat16)),
        in_specs=vmem(1),
        out_specs=tuple(vmem(2)),
        scratch_shapes=[pltpu.VMEM((lons * (8 + halo), width), jnp.float32)],
        compiler_params=params,
        cost_estimate=pl.CostEstimate(
            flops=6 * 2 * height * width * width, bytes_accessed=2 * 4 * height * width, transcendentals=width * width
        ),
        name="smooth",
    )(grad)
    return pl.pallas_call(
        finish, out_shape=f32(height, width), in_specs=vmem(3), out_specs=vmem(1)[0], compiler_params=params, name="finish",
    )(own, weights, sums.reshape(lons * (8 + halo), height))


def solution(mesh):
    in_specs = (
        P(("lat", "gau"), "lon"),
        P(("scen", "lat", "gau"), "lon"),
        P(("lat", "gau"), "lon"),
        P(("lat", "gau"), "lon"),
        P(),
        P(("scen", "lon", "lat", "gau"), None),
        P(("scen", "lon", "lat", "gau")),
        P(("scen", "lon", "lat", "gau"), None, None),
        P(("scen", "lon", "lat", "gau"), None, None),
    )
    out_specs = P(("scen", "lat", "gau"), "lon")
    return jax.shard_map(local, mesh=mesh, in_specs=in_specs, out_specs=out_specs, check_vma=False)
```

```python
import functools
import math

import jax
import jax.numpy as jnp
from jax import lax
from jax.experimental import pallas as pl
from jax.experimental.pallas import tpu as pltpu
from jax.sharding import PartitionSpec as P

STEPS_BLOCK = 8
LANES = 128
SEG = 32
LEVELS = 16

courant = 0.45
depth_floor = 0.1

GRID_AXES = ("lon", "lat", "gau")
ROW_AXES = ("lat", "gau")
VMEM_LIMIT = 16 * 1024 * 1024


def roll_lanes(x, shift):
    shift = shift % LANES
    return x if shift == 0 else pltpu.roll(x, shift, 1)


def lane_iota(rows):
    return lax.broadcasted_iota(jnp.int32, (rows, LANES), 1)


def gauge_rows(owned):
    if 3 * owned <= LANES:
        return STEPS_BLOCK, owned
    assert owned <= LANES
    return 3 * STEPS_BLOCK, 0


def my_place():
    row = lax.axis_index("lat") * lax.axis_size("gau") + lax.axis_index("gau")
    return row, lax.axis_index("lon"), lax.axis_size("lat") * lax.axis_size("gau"), lax.axis_size("lon")


def give_west(reach, keep_ref, gain_ref, west_ref):
    height = keep_ref.shape[0]
    lower = lane_iota(height) < reach
    west_ref[:height] = jnp.where(lower, keep_ref[:, :LANES], roll_lanes(gain_ref[:, :LANES], reach))
    west_ref[height:] = jnp.zeros((west_ref.shape[0] - height, LANES), jnp.float32)


def give_rows(halo, keep_ref, gain_ref, right_ref, far_ref, near_ref):
    height, width = keep_ref.shape
    lower = lane_iota(halo) < 2 * halo
    odd = my_place()[0] & 1
    for goal, south in ((far_ref, odd), (near_ref, 1 - odd)):
        rows = pl.ds(pl.multiple_of(south * (height - halo), halo), halo)
        for kind, source in enumerate((keep_ref, gain_ref)):
            goal[kind, :, :width] = source[rows, :]
            goal[kind, :, width:] = jnp.where(lower, roll_lanes(right_ref[rows, :], -2 * halo * kind), 0.0)


def give_gauges(height, width, blocks, samples, coast_count, gauge_ref, after_ref, parcel_ref, block_ref):
    row_tiles = lax.axis_size("lat") * lax.axis_size("gau")
    owned = gauge_ref.shape[2]
    assert blocks == 2
    route, cell, coast = (gauge_ref[2 * blocks, i : i + 1, :].astype(jnp.int32) for i in range(3))
    target = jnp.zeros_like(route)
    for entry in range(coast_count):
        target = jnp.where(route == entry, jnp.broadcast_to(coast[:, entry : entry + 1], route.shape), target)
    row_bits, width_bits = int(math.log2(row_tiles)), int(math.log2(width))
    assert row_tiles == 1 << row_bits and width == 1 << width_bits
    grid_row = (target & (row_tiles - 1)) * height + (cell >> width_bits)
    grid_col = (target >> row_bits) * width + (cell & (width - 1))
    block_ref[...] = jnp.zeros_like(block_ref)
    levels = lax.broadcasted_iota(jnp.int32, (STEPS_BLOCK, owned), 0).astype(jnp.float32)
    for block in range(blocks):
        series = jnp.zeros((STEPS_BLOCK, owned), jnp.float32)
        for sample in range(samples):
            times = gauge_ref[block, sample : sample + 1, :]
            resid = gauge_ref[blocks + block, sample : sample + 1, :]
            series = series + jnp.where(times == levels, resid, 0.0)
        block_ref[block * STEPS_BLOCK : (block + 1) * STEPS_BLOCK, :owned] = series
    at = blocks * STEPS_BLOCK
    block_ref[at : at + 1, :owned] = grid_row.astype(jnp.float32)
    block_ref[at + 1 : at + 2, :owned] = grid_col.astype(jnp.float32)
    size, apart = gauge_rows(owned)
    gauges = block_ref[...]
    if size == STEPS_BLOCK:
        gauges = sum(
            roll_lanes(gauges[i * STEPS_BLOCK : (i + 1) * STEPS_BLOCK], i * apart) for i in range(3)
        )
    tiles = parcel_ref.shape[0]

    def put(tile, carry):
        parcel_ref[tile, 0:size, :] = gauges
        return carry

    lax.fori_loop(0, tiles, put, 0, unroll=tiles <= 16)


def halves(value):
    high = value.astype(jnp.bfloat16)
    return high, (value - high.astype(jnp.float32)).astype(jnp.bfloat16)


def dealt_column(place, planes):
    return (place & (LANES - 1)) * planes + place // LANES


def force(steps, halo, height, width, parcel_ref, after_ref, force_ref, series_ref, rows_hot, cols_hot):
    planes, rows_all = force_ref.shape[1], height + 2 * halo
    my_row, my_lon, row_tiles, lons = my_place()
    wide = rows_hot.shape[1]
    tiles, parcel_rows = parcel_ref.shape[:2]
    size = parcel_rows
    apart = wide // tiles if size == STEPS_BLOCK else 0
    owned = apart if apart else LANES
    group = wide // owned
    groups = tiles // group
    per_plane = LANES // owned
    blocks = rows_all // 8
    row_shift = (halo - my_row * height).astype(jnp.float32)
    col_shift = (-my_lon * width).astype(jnp.float32)
    place = lax.broadcasted_iota(jnp.int32, (rows_all, LANES), 0)
    at = ((place & 7) * blocks + (place >> 3)).astype(jnp.float32)

    def gather_gauges(index):
        lanes = lane_iota(STEPS_BLOCK)
        for part in range(wide // LANES):
            cols = slice(part * LANES, (part + 1) * LANES)
            fields = []
            for field in range(3):
                total = jnp.zeros((STEPS_BLOCK, LANES), jnp.float32)
                rows = slice(0, 8) if apart else slice(8 * field, 8 * field + 8)
                for i in range(per_plane):
                    source = index * group + part * per_plane + i
                    block = roll_lanes(parcel_ref[source, rows, :], i * owned - field * apart)
                    total = jnp.where((lanes >= i * owned) & (lanes < (i + 1) * owned), block, total)
                fields.append(total)
            series_ref[0:8, cols] = fields[0]
            series_ref[8:16, cols] = fields[1]
            row = fields[2][0:1] + row_shift
            col = fields[2][1:2] + col_shift
            col = jnp.where(col < width + 2 * halo, col, -1.0)
            rows_hot[:, cols] = (at == row).astype(jnp.float32).astype(jnp.bfloat16)
            by_gauge = jnp.transpose(jnp.broadcast_to(col, (LANES, LANES)))
            for c in range(planes):
                spot = (lane_iota(LANES) * planes + c).astype(jnp.float32)
                hot = (by_gauge == spot).astype(jnp.float32).astype(jnp.bfloat16)
                cols_hot[part * LANES : (part + 1) * LANES, c * LANES : (c + 1) * LANES] = hot
                cols_hot[wide + part * LANES : wide + (part + 1) * LANES, c * LANES : (c + 1) * LANES] = hot

    def levels_of(start, add):
        hot = rows_hot[...]
        both = []
        for level in range(LEVELS):
            value = series_ref[pl.ds(start + level, 1), :]
            high, low = halves(value)
            both.append(jnp.concatenate([hot * high, hot * low], axis=1))
        both = jnp.concatenate(both, axis=0)
        for first in range(0, planes, 2):
            count = min(2, planes - first)
            total = jnp.dot(
                both, cols_hot[:, first * LANES : (first + count) * LANES], preferred_element_type=jnp.float32
            )
            for level in range(LEVELS):
                for c in range(count):
                    part = total[level * rows_all : (level + 1) * rows_all, c * LANES : (c + 1) * LANES]
                    goal = (start + level, first + c, slice(0, rows_all))
                    force_ref[goal] = force_ref[goal] + part if add else part

    def levels(add):
        def one(index, carry):
            levels_of(index * LEVELS, add)
            return carry

        lax.fori_loop(0, steps // LEVELS, one, 0)

    force_ref[steps] = jnp.zeros_like(force_ref[steps])
    gather_gauges(0)
    levels(False)
    if groups > 1:

        def more(index, carry):
            gather_gauges(index)
            levels(True)
            return carry

        lax.fori_loop(1, groups, more, 0)


def deal_own(reach, keep_ref, gain_ref, right_ref, after_ref, deal_ref, own_ref):
    height, width = keep_ref.shape
    planes = own_ref.shape[1]
    columns = planes * LANES
    parts = []
    for kind, source in enumerate((keep_ref, gain_ref)):
        beside = jnp.where(lane_iota(height) < reach, roll_lanes(right_ref[:height], -reach * kind), 0.0)
        parts += halves(jnp.concatenate([source[...], beside], axis=1))
    parts = jnp.concatenate(parts, axis=0)
    shape = (columns, LANES)
    ahead = lax.broadcasted_iota(jnp.int32, shape, 0) - lax.broadcasted_iota(jnp.int32, shape, 1) * planes
    for first in range(0, planes, 2):
        pair = range(first, min(first + 2, planes))
        deal = jnp.concatenate([(ahead == c).astype(jnp.float32).astype(jnp.bfloat16) for c in pair], axis=1)
        deal_ref[:, first * LANES : (first + len(pair)) * LANES] = deal
        dealt = jnp.dot(parts, deal, preferred_element_type=jnp.float32)
        for i, c in enumerate(pair):
            piece = dealt[:, i * LANES : (i + 1) * LANES]
            for kind in range(2):
                at = 2 * kind * height
                own_ref[kind, c] = piece[at : at + height] + piece[at + height : at + 2 * height]


def sweep(
    steps, deal_ref, own_ref, far_ref, near_ref, force_ref,
    grad_ref, sums_ref,
    a, fx, fy, keeps, gains, plain,
):
    planes, height = own_ref.shape[1:3]
    width = (planes - 1) * LANES
    halo = 2 * steps
    rows_all = height + 2 * halo
    blocks = rows_all // 8
    my_row, my_lon, row_tiles, lons = my_place()
    has_top, has_bottom = my_row > 0, my_row < row_tiles - 1
    has_right = my_lon < lons - 1
    odd = (jnp.zeros((halo, planes * LANES), jnp.int32) + (my_row & 1)) == 1
    lanes8 = lane_iota(8)

    def up(value):
        return pltpu.roll(value, 7, 0)

    def down(value):
        return pltpu.roll(value, 1, 0)

    every = range(planes)
    columns = planes * LANES

    parts = []
    for kind in range(2):
        far, near = far_ref[kind], near_ref[kind]
        parts += halves(jnp.concatenate([jnp.where(odd, near, far), jnp.where(odd, far, near)], axis=0))
    parts = jnp.concatenate(parts, axis=0)
    for first in range(0, planes, 2):
        pair = range(first, min(first + 2, planes))
        dealt = jnp.dot(
            parts, deal_ref[:, first * LANES : (first + len(pair)) * LANES], preferred_element_type=jnp.float32
        )
        for i, c in enumerate(pair):
            piece = dealt[:, i * LANES : (i + 1) * LANES]
            for kind in range(2):
                at = 4 * kind * halo
                value = piece[at : at + 2 * halo] + piece[at + 2 * halo : at + 4 * halo]
                plain[kind, c, 0:halo, :] = value[:halo]
                plain[kind, c, halo : halo + height, :] = own_ref[kind, c]
                plain[kind, c, halo + height : rows_all, :] = value[halo:]
    for kind, goal in enumerate((keeps, gains)):
        for q in range(blocks):
            for c in every:
                value = plain[kind, c, pl.ds(q, 8, stride=blocks), :]
                goal[c, 8 * q : 8 * q + 8, :] = value
                if q == 0:
                    goal[c, 8 * blocks : 8 * blocks + 8, :] = up(value)
                if c == 0:
                    goal[planes, 8 * q : 8 * q + 8, :] = roll_lanes(value, -1)

    def cell_mask(column, there):
        lane, plane = column // planes, column % planes
        return plane, jnp.where(lanes8 == lane, there, 1.0)

    column_mask = dict([cell_mask(width, jnp.where(has_right, 1.0, 0.0)), cell_mask(columns - 1, 0.0)])
    assert len(column_mask) == 2
    sublane = lax.broadcasted_iota(jnp.int32, (8, LANES), 0)
    row_mask = {}
    for row, there in ((halo - 1, has_top), (halo + height, has_bottom)):
        row_mask[row % blocks] = jnp.where(sublane == row // blocks, jnp.where(there, 1.0, 0.0), 1.0)

    fx[...] = jnp.zeros_like(fx)
    fy[...] = jnp.zeros_like(fy)
    a[:, 0:rows_all, :] = force_ref[steps - 1, :, 0:rows_all, :]

    def step(index, carry):
        level = jnp.where(index < steps - 1, steps - 2 - index, steps)
        near, ahead, new_y, beside, total, behind = {}, {}, {}, {}, {}, {}

        def rows(q):
            return slice(8 * q, 8 * q + 8)

        def first(q):
            near[q] = [a[c, rows(q % blocks), :] for c in every]
            if q < blocks:
                ahead[q] = near[q][2:] + [roll_lanes(value, -1) for value in near[q][:2]]
            else:
                near[q] = [up(value) for value in near[q]]

        def coefficients(q):
            return [[ref[c, rows(q), :] for c in range(planes + 1)] for ref in (keeps, gains)]

        def second_y(q):
            beside[q + 1] = keep, gain = coefficients(q + 1)
            new_y[q] = [keep[c] * fy[c, rows(q), :] + gain[c] * (near[q + 2][c] - near[q][c]) for c in every]
            for c in every:
                fy[c, rows(q), :] = new_y[q][c]

        def second_x(q):
            keep, gain = beside[q]
            new_x = [
                keep[c + 1] * fx[c, rows(q), :] + gain[c + 1] * (ahead[q][c] - near[q][c]) for c in every
            ]
            behind[q] = [roll_lanes(value, 1) for value in new_x[-2:]] + new_x[:-2]
            before = new_y[q - 2] if q >= 2 else [down(fy[c, rows(q - 2 + blocks), :]) for c in every]
            push = [force_ref[level, c, rows(q), :] for c in every]
            total[q] = [(near[q][c] + push[c]) + (new_y[q][c] - before[c]) + new_x[c] for c in every]
            for c in every:
                fx[c, rows(q), :] = new_x[c]

        def third(q):
            for c in every:
                value = total[q][c] - behind[q][c]
                if c in column_mask:
                    value = value * column_mask[c]
                if q in row_mask:
                    value = value * row_mask[q]
                a[c, rows(q), :] = value

        for q in range(4):
            first(q)
        second_y(0)
        second_y(1)
        for q in range(2, blocks):
            first(q + 2)
            second_y(q)
            second_x(q)
            if q > 2:
                third(q - 1)
        for q in range(2):
            first(q)
            new_y[q] = [fy[c, rows(q), :] for c in every]
            beside[q] = coefficients(q)
        for q in range(2):
            second_x(q)
            third(q - 1 if q else blocks - 1)
        third(1)
        return carry

    lax.fori_loop(0, steps, step, 0)

    start = jnp.where(my_lon > 0, halo, 0)
    for c in every:
        column = lanes8 * planes + c
        known = (column >= start) & (column < width + halo)
        for r in range(0, height, 8):
            s, q = divmod(halo + r, blocks)
            strided = pl.ds(8 * q + s, 8, stride=8)
            value = jnp.where(known & (keeps[c, strided, :] > 0.0), a[c, strided, :], 0.0)
            grad_ref[r : r + 8, c * LANES : (c + 1) * LANES] = value
    length = 2.0 * width
    shape = (8 + halo, planes * LANES)
    kind = lax.broadcasted_iota(jnp.int32, shape, 0)
    column = dealt_column(lax.broadcasted_iota(jnp.int32, shape, 1), planes)
    beyond = column - width
    off = jnp.where(kind == 0, column, jnp.where(kind == 1, -1 - beyond, jnp.where(kind == 2, beyond, width - 1 - beyond)))
    mine = ((kind < 2) & (beyond < 0)) | ((kind >= 2) & (kind < 4) & (beyond >= 0))
    weights = jnp.where(mine, jnp.exp(-jnp.maximum(off, 0).astype(jnp.float32) / length), 0.0)
    weights = jnp.where((kind >= 8) & (beyond == kind - 8), 1.0, weights)
    sums = lax.dot_general(
        weights, grad_ref[...], (((1,), (1,)), ((), ())), precision=lax.Precision.HIGHEST,
        preferred_element_type=jnp.float32,
    )
    for i in range(sums_ref.shape[0]):
        sums_ref[i] = sums


def smooth(halo, order, grad_ref, out_ref, weights_ref, exact_ref):
    width = out_ref.shape[1]
    length = 2.0 * width
    planes = grad_ref.shape[1] // LANES
    column = lax.broadcasted_iota(jnp.int32, (LANES, width), 1)
    lane = lax.broadcasted_iota(jnp.int32, (LANES, width), 0)
    sources = [lane * planes + c for c in range(planes)]
    kernel = jnp.concatenate(
        [jnp.where(x < width, jnp.exp(-jnp.abs(x - column).astype(jnp.float32) / length), 0.0) for x in sources], axis=0
    )
    out_ref[...] = jnp.dot(
        grad_ref[...], kernel, precision=lax.Precision.HIGHEST, preferred_element_type=jnp.float32
    )
    me = lax.axis_index("lon")
    shape = (8 + halo, width)
    kind, column = lax.broadcasted_iota(jnp.int32, shape, 0), lax.broadcasted_iota(jnp.int32, shape, 1)
    for place, source in enumerate(order):
        strip = jnp.where(kind < 2, source, source + 1)
        left = ((kind == 0) | (kind == 2)) & (strip > me)
        right = ((kind == 1) | (kind == 3)) & (strip < me)
        near = (kind >= 8) & (source + 1 == me)
        away = jnp.where(left, (strip - me) * width - column, (me - strip - 1) * width + column + 1)
        away = jnp.where(near, jnp.abs(kind - 8 - column), away)
        weights = jnp.where(left | right | near, jnp.exp(-jnp.maximum(away, 0).astype(jnp.float32) / length), 0.0)
        exact_ref[place * shape[0] : (place + 1) * shape[0], :] = weights
    high, low = halves(exact_ref[...])
    count = high.shape[0]
    for place, part in enumerate((high, high, low)):
        weights_ref[place * count : (place + 1) * count, :] = part


def finish(own_ref, weights_ref, sums_ref, out_ref):
    high, low = halves(sums_ref[...])
    out_ref[...] = own_ref[...] + lax.dot_general(
        jnp.concatenate([high, low, high], axis=0), weights_ref[...], (((0,), (0,)), ((), ())),
        preferred_element_type=jnp.float32,
    )


def f32(*shape):
    return jax.ShapeDtypeStruct(shape, jnp.float32)


def hint(megabytes):
    return pl.CostEstimate(flops=0, bytes_accessed=megabytes * 1000 * 1000, transcendentals=0)


def spaced(rows):
    return 8 * (rows // 8 | 1)


def vmem(count):
    return [pl.BlockSpec(memory_space=pltpu.VMEM)] * count


def local(depth, surface, friction, wet, coastal_tiles, gauge_route, gauge_cell, gauge_times, gauge_resid):
    height, width = depth.shape
    owned = gauge_route.shape[0]
    blocks = gauge_resid.shape[1]
    steps = blocks * STEPS_BLOCK
    halo = 2 * steps
    assert halo == SEG and height == LANES
    tiles = lax.axis_size(GRID_AXES)
    lons = lax.axis_size("lon")
    row_tiles = lax.axis_size(ROW_AXES)
    planes = width // LANES + 1
    rows_all = height + 2 * halo
    params = pltpu.CompilerParams(vmem_limit_bytes=VMEM_LIMIT)

    keep = (1.0 - friction) * wet.astype(jnp.float32)
    gain = ((courant * 0.5) ** 2 * jnp.maximum(depth + surface, depth_floor)) * keep
    samples, coast_count = gauge_resid.shape[2], coastal_tiles.shape[0]
    assert coast_count <= owned

    assert samples >= 3

    def put(array, group, row):
        groups, rows, lanes = array.shape
        return jnp.pad(array, ((group, 2 * blocks + 1 - group - groups), (row, samples - row - rows), (0, owned - lanes)))

    gauges = (
        put(jnp.transpose(gauge_times, (1, 2, 0)), 0, 0)
        + put(gauge_route.reshape(1, 1, owned), 2 * blocks, 0)
        + put(gauge_cell.reshape(1, 1, owned), 2 * blocks, 1)
        + put(coastal_tiles.reshape(1, 1, coast_count), 2 * blocks, 2)
    ).astype(jnp.float32) + put(jnp.transpose(gauge_resid, (1, 2, 0)), blocks, 0)
    west = pl.pallas_call(
        functools.partial(give_west, 2 * halo), out_shape=f32(2 * height, LANES), in_specs=vmem(2), out_specs=vmem(1)[0],
        compiler_params=params, name="give_west",
    )(keep, gain)
    right = lax.ppermute(west, "lon", [(i + 1, i) for i in range(lons - 1)])

    parcel = pl.pallas_call(
        functools.partial(give_gauges, height, width, blocks, samples, coast_count),
        out_shape=f32(tiles, gauge_rows(owned)[0], LANES),
        in_specs=vmem(1) + [pl.BlockSpec(memory_space=pl.ANY)],
        out_specs=vmem(1)[0],
        scratch_shapes=[pltpu.VMEM((24, LANES), jnp.float32)],
        compiler_params=params,
        cost_estimate=hint(10),
        name="give_gauges",
    )(gauges, west)

    def exchange(array, axes, groups=None):
        return lax.all_to_all(array, axes, split_axis=0, concat_axis=0, axis_index_groups=groups, tiled=True)

    group = sorted(range(tiles), key=lambda tile: (tile % row_tiles in (0, row_tiles - 1), -(tile // row_tiles)))
    parcel = exchange(parcel, GRID_AXES, [group])

    to_far, to_near = pl.pallas_call(
        functools.partial(give_rows, halo), out_shape=(f32(2, halo, planes * LANES),) * 2, in_specs=vmem(3),
        out_specs=tuple(vmem(2)), compiler_params=params, cost_estimate=hint(40), name="give_rows",
    )(keep, gain, right)
    far = lax.ppermute(to_far, ROW_AXES, [pair for i in range(1, row_tiles - 1, 2) for pair in ((i, i + 1), (i + 1, i))])
    near = lax.ppermute(to_near, ROW_AXES, [pair for i in range(0, row_tiles, 2) for pair in ((i, i + 1), (i + 1, i))])

    deal, own = pl.pallas_call(
        functools.partial(deal_own, 2 * halo),
        out_shape=(
            jax.ShapeDtypeStruct((planes * LANES, planes * LANES), jnp.bfloat16), f32(2, planes, height, LANES),
        ),
        in_specs=vmem(3) + [pl.BlockSpec(memory_space=pl.ANY)],
        out_specs=tuple(vmem(2)),
        compiler_params=params,
        cost_estimate=hint(4),
        name="deal_own",
    )(keep, gain, right, to_far)

    wide = max(2 * LANES, owned)
    pushes = pl.pallas_call(
        functools.partial(force, steps, halo, height, width),
        out_shape=f32(steps + 1, planes, spaced(rows_all), LANES),
        in_specs=vmem(1) + [pl.BlockSpec(memory_space=pl.ANY)],
        out_specs=vmem(1)[0],
        scratch_shapes=[
            pltpu.VMEM((steps, wide), jnp.float32),
            pltpu.VMEM((rows_all, wide), jnp.bfloat16),
            pltpu.VMEM((2 * wide, planes * LANES), jnp.bfloat16),
        ],
        compiler_params=params,
        cost_estimate=pl.CostEstimate(
            flops=4 * steps * rows_all * wide * planes * LANES, bytes_accessed=4 * steps * planes * rows_all * LANES,
            transcendentals=0,
        ),
        name="force",
    )(parcel, deal)

    plane = pltpu.VMEM((planes, spaced(rows_all), LANES), jnp.float32)
    grad, sums = pl.pallas_call(
        functools.partial(sweep, steps),
        out_shape=(f32(height, planes * LANES), f32(lons, 8 + halo, height)),
        in_specs=vmem(5),
        out_specs=tuple(vmem(2)),
        scratch_shapes=[plane] * 3 + [
            pltpu.VMEM((planes + 1, spaced(rows_all + 8), LANES), jnp.float32),
            pltpu.VMEM((planes + 1, spaced(rows_all + 8), LANES), jnp.float32),
            pltpu.VMEM((2, planes, spaced(rows_all), LANES), jnp.float32),
        ],
        compiler_params=params,
        name="sweep",
    )(deal, own, far, near, pushes)

    order = list(range(lons // 2, lons)) + list(range(lons // 2))[::-1]
    sums = exchange(sums, "lon", [order])
    own, weights = pl.pallas_call(
        functools.partial(smooth, halo, order),
        out_shape=(f32(height, width), jax.ShapeDtypeStruct((3 * lons * (8 + halo), width), jnp.bfloat16)),
        in_specs=vmem(1),
        out_specs=tuple(vmem(2)),
        scratch_shapes=[pltpu.VMEM((lons * (8 + halo), width), jnp.float32)],
        compiler_params=params,
        cost_estimate=pl.CostEstimate(
            flops=6 * 2 * height * width * width, bytes_accessed=2 * 4 * height * width, transcendentals=width * width
        ),
        name="smooth",
    )(grad)
    return pl.pallas_call(
        finish, out_shape=f32(height, width), in_specs=vmem(3), out_specs=vmem(1)[0], compiler_params=params, name="finish",
    )(own, weights, sums.reshape(lons * (8 + halo), height))


def solution(mesh):
    in_specs = (
        P(("lat", "gau"), "lon"),
        P(("scen", "lat", "gau"), "lon"),
        P(("lat", "gau"), "lon"),
        P(("lat", "gau"), "lon"),
        P(),
        P(("scen", "lon", "lat", "gau"), None),
        P(("scen", "lon", "lat", "gau")),
        P(("scen", "lon", "lat", "gau"), None, None),
        P(("scen", "lon", "lat", "gau"), None, None),
    )
    out_specs = P(("scen", "lat", "gau"), "lon")
    return jax.shard_map(local, mesh=mesh, in_specs=in_specs, out_specs=out_specs, check_vma=False)
```

```python
import functools
import math

import jax
import jax.numpy as jnp
from jax import lax
from jax.experimental import pallas as pl
from jax.experimental.pallas import tpu as pltpu
from jax.sharding import PartitionSpec as P

STEPS_BLOCK = 8
LANES = 128
SEG = 32
LEVELS = 16

courant = 0.45
depth_floor = 0.1

GRID_AXES = ("lon", "lat", "gau")
ROW_AXES = ("lat", "gau")
VMEM_LIMIT = 16 * 1024 * 1024


def roll_lanes(x, shift):
    shift = shift % LANES
    return x if shift == 0 else pltpu.roll(x, shift, 1)


def lane_iota(rows):
    return lax.broadcasted_iota(jnp.int32, (rows, LANES), 1)


def gauge_rows(owned):
    if 3 * owned <= LANES:
        return STEPS_BLOCK, owned
    assert owned <= LANES
    return 3 * STEPS_BLOCK, 0


def my_place():
    row = lax.axis_index("lat") * lax.axis_size("gau") + lax.axis_index("gau")
    return row, lax.axis_index("lon"), lax.axis_size("lat") * lax.axis_size("gau"), lax.axis_size("lon")


def give_west(reach, keep_ref, gain_ref, west_ref):
    height = keep_ref.shape[0]
    lower = lane_iota(height) < reach
    west_ref[:height] = jnp.where(lower, keep_ref[:, :LANES], roll_lanes(gain_ref[:, :LANES], reach))
    west_ref[height:] = jnp.zeros((west_ref.shape[0] - height, LANES), jnp.float32)


def give_rows(halo, keep_ref, gain_ref, right_ref, far_ref, near_ref):
    height, width = keep_ref.shape
    lower = lane_iota(halo) < 2 * halo
    odd = my_place()[0] & 1
    for goal, south in ((far_ref, odd), (near_ref, 1 - odd)):
        rows = pl.ds(pl.multiple_of(south * (height - halo), halo), halo)
        for kind, source in enumerate((keep_ref, gain_ref)):
            goal[kind, :, :width] = source[rows, :]
            goal[kind, :, width:] = jnp.where(lower, roll_lanes(right_ref[rows, :], -2 * halo * kind), 0.0)


def give_gauges(height, width, blocks, samples, coast_count, gauge_ref, after_ref, parcel_ref, block_ref):
    row_tiles = lax.axis_size("lat") * lax.axis_size("gau")
    owned = gauge_ref.shape[2]
    assert blocks == 2
    route, cell, coast = (gauge_ref[2 * blocks, i : i + 1, :].astype(jnp.int32) for i in range(3))
    target = jnp.zeros_like(route)
    for entry in range(coast_count):
        target = jnp.where(route == entry, jnp.broadcast_to(coast[:, entry : entry + 1], route.shape), target)
    row_bits, width_bits = int(math.log2(row_tiles)), int(math.log2(width))
    assert row_tiles == 1 << row_bits and width == 1 << width_bits
    grid_row = (target & (row_tiles - 1)) * height + (cell >> width_bits)
    grid_col = (target >> row_bits) * width + (cell & (width - 1))
    block_ref[...] = jnp.zeros_like(block_ref)
    levels = lax.broadcasted_iota(jnp.int32, (STEPS_BLOCK, owned), 0).astype(jnp.float32)
    for block in range(blocks):
        series = jnp.zeros((STEPS_BLOCK, owned), jnp.float32)
        for sample in range(samples):
            times = gauge_ref[block, sample : sample + 1, :]
            resid = gauge_ref[blocks + block, sample : sample + 1, :]
            series = series + jnp.where(times == levels, resid, 0.0)
        block_ref[block * STEPS_BLOCK : (block + 1) * STEPS_BLOCK, :owned] = series
    at = blocks * STEPS_BLOCK
    block_ref[at : at + 1, :owned] = grid_row.astype(jnp.float32)
    block_ref[at + 1 : at + 2, :owned] = grid_col.astype(jnp.float32)
    size, apart = gauge_rows(owned)
    gauges = block_ref[...]
    if size == STEPS_BLOCK:
        gauges = sum(
            roll_lanes(gauges[i * STEPS_BLOCK : (i + 1) * STEPS_BLOCK], i * apart) for i in range(3)
        )
    tiles = parcel_ref.shape[0]

    def put(tile, carry):
        parcel_ref[tile, 0:size, :] = gauges
        return carry

    lax.fori_loop(0, tiles, put, 0, unroll=tiles <= 16)


def halves(value):
    high = value.astype(jnp.bfloat16)
    return high, (value - high.astype(jnp.float32)).astype(jnp.bfloat16)


def dealt_column(place, planes):
    return (place & (LANES - 1)) * planes + place // LANES


def force(steps, halo, height, width, parcel_ref, after_ref, force_ref, series_ref, rows_hot, cols_hot):
    planes, rows_all = force_ref.shape[1], height + 2 * halo
    my_row, my_lon, row_tiles, lons = my_place()
    wide = rows_hot.shape[1]
    tiles, parcel_rows = parcel_ref.shape[:2]
    size = parcel_rows
    apart = wide // tiles if size == STEPS_BLOCK else 0
    owned = apart if apart else LANES
    group = wide // owned
    groups = tiles // group
    per_plane = LANES // owned
    blocks = rows_all // 8
    row_shift = (halo - my_row * height).astype(jnp.float32)
    col_shift = (-my_lon * width).astype(jnp.float32)
    place = lax.broadcasted_iota(jnp.int32, (rows_all, LANES), 0)
    at = ((place & 7) * blocks + (place >> 3)).astype(jnp.float32)

    def gather_gauges(index):
        lanes = lane_iota(STEPS_BLOCK)
        for part in range(wide // LANES):
            cols = slice(part * LANES, (part + 1) * LANES)
            fields = []
            for field in range(3):
                total = jnp.zeros((STEPS_BLOCK, LANES), jnp.float32)
                rows = slice(0, 8) if apart else slice(8 * field, 8 * field + 8)
                for i in range(per_plane):
                    source = index * group + part * per_plane + i
                    block = roll_lanes(parcel_ref[source, rows, :], i * owned - field * apart)
                    total = jnp.where((lanes >= i * owned) & (lanes < (i + 1) * owned), block, total)
                fields.append(total)
            series_ref[0:8, cols] = fields[0]
            series_ref[8:16, cols] = fields[1]
            row = fields[2][0:1] + row_shift
            col = fields[2][1:2] + col_shift
            col = jnp.where(col < width + 2 * halo, col, -1.0)
            rows_hot[:, cols] = (at == row).astype(jnp.float32).astype(jnp.bfloat16)
            by_gauge = jnp.transpose(jnp.broadcast_to(col, (LANES, LANES)))
            for c in range(planes):
                spot = (lane_iota(LANES) * planes + c).astype(jnp.float32)
                hot = (by_gauge == spot).astype(jnp.float32).astype(jnp.bfloat16)
                cols_hot[part * LANES : (part + 1) * LANES, c * LANES : (c + 1) * LANES] = hot
                cols_hot[wide + part * LANES : wide + (part + 1) * LANES, c * LANES : (c + 1) * LANES] = hot

    def levels_of(start, add):
        hot = rows_hot[...]
        both = []
        for level in range(LEVELS):
            value = series_ref[pl.ds(start + level, 1), :]
            high, low = halves(value)
            both.append(jnp.concatenate([hot * high, hot * low], axis=1))
        both = jnp.concatenate(both, axis=0)
        for first in range(0, planes, 2):
            count = min(2, planes - first)
            total = jnp.dot(
                both, cols_hot[:, first * LANES : (first + count) * LANES], preferred_element_type=jnp.float32
            )
            for level in range(LEVELS):
                for c in range(count):
                    part = total[level * rows_all : (level + 1) * rows_all, c * LANES : (c + 1) * LANES]
                    goal = (start + level, first + c, slice(0, rows_all))
                    force_ref[goal] = force_ref[goal] + part if add else part

    def levels(add):
        def one(index, carry):
            levels_of(index * LEVELS, add)
            return carry

        if steps == LEVELS:
            levels_of(0, add)
        else:
            lax.fori_loop(0, steps // LEVELS, one, 0)

    force_ref[steps] = jnp.zeros_like(force_ref[steps])
    gather_gauges(0)
    levels(False)
    if groups > 1:

        def more(index, carry):
            gather_gauges(index)
            levels(True)
            return carry

        lax.fori_loop(1, groups, more, 0)


def deal_own(reach, keep_ref, gain_ref, right_ref, after_ref, deal_ref, own_ref):
    height, width = keep_ref.shape
    planes = own_ref.shape[1]
    columns = planes * LANES
    parts = []
    for kind, source in enumerate((keep_ref, gain_ref)):
        beside = jnp.where(lane_iota(height) < reach, roll_lanes(right_ref[:height], -reach * kind), 0.0)
        parts += halves(jnp.concatenate([source[...], beside], axis=1))
    parts = jnp.concatenate(parts, axis=0)
    shape = (columns, LANES)
    ahead = lax.broadcasted_iota(jnp.int32, shape, 0) - lax.broadcasted_iota(jnp.int32, shape, 1) * planes
    for first in range(0, planes, 2):
        pair = range(first, min(first + 2, planes))
        deal = jnp.concatenate([(ahead == c).astype(jnp.float32).astype(jnp.bfloat16) for c in pair], axis=1)
        deal_ref[:, first * LANES : (first + len(pair)) * LANES] = deal
        dealt = jnp.dot(parts, deal, preferred_element_type=jnp.float32)
        for i, c in enumerate(pair):
            piece = dealt[:, i * LANES : (i + 1) * LANES]
            for kind in range(2):
                at = 2 * kind * height
                own_ref[kind, c] = piece[at : at + height] + piece[at + height : at + 2 * height]


def sweep(
    steps, deal_ref, own_ref, far_ref, near_ref, force_ref,
    grad_ref, sums_ref,
    a, fx, fy, keeps, gains, plain,
):
    planes, height = own_ref.shape[1:3]
    width = (planes - 1) * LANES
    halo = 2 * steps
    rows_all = height + 2 * halo
    blocks = rows_all // 8
    my_row, my_lon, row_tiles, lons = my_place()
    has_top, has_bottom = my_row > 0, my_row < row_tiles - 1
    has_right = my_lon < lons - 1
    odd = (jnp.zeros((halo, planes * LANES), jnp.int32) + (my_row & 1)) == 1
    lanes8 = lane_iota(8)

    def up(value):
        return pltpu.roll(value, 7, 0)

    def down(value):
        return pltpu.roll(value, 1, 0)

    every = range(planes)
    columns = planes * LANES

    parts = []
    for kind in range(2):
        far, near = far_ref[kind], near_ref[kind]
        parts += halves(jnp.concatenate([jnp.where(odd, near, far), jnp.where(odd, far, near)], axis=0))
    parts = jnp.concatenate(parts, axis=0)
    for first in range(0, planes, 2):
        pair = range(first, min(first + 2, planes))
        dealt = jnp.dot(
            parts, deal_ref[:, first * LANES : (first + len(pair)) * LANES], preferred_element_type=jnp.float32
        )
        for i, c in enumerate(pair):
            piece = dealt[:, i * LANES : (i + 1) * LANES]
            for kind in range(2):
                at = 4 * kind * halo
                value = piece[at : at + 2 * halo] + piece[at + 2 * halo : at + 4 * halo]
                plain[kind, c, 0:halo, :] = value[:halo]
                plain[kind, c, halo : halo + height, :] = own_ref[kind, c]
                plain[kind, c, halo + height : rows_all, :] = value[halo:]
    for kind, goal in enumerate((keeps, gains)):
        for q in range(blocks):
            for c in every:
                value = plain[kind, c, pl.ds(q, 8, stride=blocks), :]
                goal[c, 8 * q : 8 * q + 8, :] = value
                if q == 0:
                    goal[c, 8 * blocks : 8 * blocks + 8, :] = up(value)
                if c == 0:
                    goal[planes, 8 * q : 8 * q + 8, :] = roll_lanes(value, -1)

    def cell_mask(column, there):
        lane, plane = column // planes, column % planes
        return plane, jnp.where(lanes8 == lane, there, 1.0)

    column_mask = dict([cell_mask(width, jnp.where(has_right, 1.0, 0.0)), cell_mask(columns - 1, 0.0)])
    assert len(column_mask) == 2
    sublane = lax.broadcasted_iota(jnp.int32, (8, LANES), 0)
    row_mask = {}
    for row, there in ((halo - 1, has_top), (halo + height, has_bottom)):
        row_mask[row % blocks] = jnp.where(sublane == row // blocks, jnp.where(there, 1.0, 0.0), 1.0)

    def step(index, carry, opening=False):
        level = jnp.where(index < steps - 1, steps - 2 - index, steps)
        near, ahead, new_y, beside, total, behind = {}, {}, {}, {}, {}, {}

        def rows(q):
            return slice(8 * q, 8 * q + 8)

        def first(q):
            source = force_ref.at[steps - 1] if opening else a
            near[q] = [source[c, rows(q % blocks), :] for c in every]
            if q < blocks:
                ahead[q] = near[q][2:] + [roll_lanes(value, -1) for value in near[q][:2]]
            else:
                near[q] = [up(value) for value in near[q]]

        def coefficients(q):
            return [[ref[c, rows(q), :] for c in range(planes + 1)] for ref in (keeps, gains)]

        def second_y(q):
            beside[q + 1] = keep, gain = coefficients(q + 1)
            new_y[q] = [gain[c] * (near[q + 2][c] - near[q][c]) for c in every]
            if not opening:
                new_y[q] = [new_y[q][c] + keep[c] * fy[c, rows(q), :] for c in every]
            for c in every:
                fy[c, rows(q), :] = new_y[q][c]

        def second_x(q):
            keep, gain = beside[q]
            new_x = [gain[c + 1] * (ahead[q][c] - near[q][c]) for c in every]
            if not opening:
                new_x = [new_x[c] + keep[c + 1] * fx[c, rows(q), :] for c in every]
            behind[q] = [roll_lanes(value, 1) for value in new_x[-2:]] + new_x[:-2]
            before = new_y[q - 2] if q >= 2 else [down(fy[c, rows(q - 2 + blocks), :]) for c in every]
            push = [force_ref[level, c, rows(q), :] for c in every]
            total[q] = [(near[q][c] + push[c]) + (new_y[q][c] - before[c]) + new_x[c] for c in every]
            for c in every:
                fx[c, rows(q), :] = new_x[c]

        def third(q):
            for c in every:
                value = total[q][c] - behind[q][c]
                if c in column_mask:
                    value = value * column_mask[c]
                if q in row_mask:
                    value = value * row_mask[q]
                a[c, rows(q), :] = value

        for q in range(4):
            first(q)
        second_y(0)
        second_y(1)
        for q in range(2, blocks):
            first(q + 2)
            second_y(q)
            second_x(q)
            if q > 2:
                third(q - 1)
        for q in range(2):
            first(q)
            new_y[q] = [fy[c, rows(q), :] for c in every]
            beside[q] = coefficients(q)
        for q in range(2):
            second_x(q)
            third(q - 1 if q else blocks - 1)
        third(1)
        return carry

    step(0, 0, opening=True)
    lax.fori_loop(1, steps, step, 0)

    start = jnp.where(my_lon > 0, halo, 0)
    for c in every:
        column = lanes8 * planes + c
        known = (column >= start) & (column < width + halo)
        for r in range(0, height, 8):
            s, q = divmod(halo + r, blocks)
            strided = pl.ds(8 * q + s, 8, stride=8)
            value = jnp.where(known & (keeps[c, strided, :] > 0.0), a[c, strided, :], 0.0)
            grad_ref[r : r + 8, c * LANES : (c + 1) * LANES] = value
    length = 2.0 * width
    shape = (8 + halo, planes * LANES)
    kind = lax.broadcasted_iota(jnp.int32, shape, 0)
    column = dealt_column(lax.broadcasted_iota(jnp.int32, shape, 1), planes)
    beyond = column - width
    off = jnp.where(kind == 0, column, jnp.where(kind == 1, -1 - beyond, jnp.where(kind == 2, beyond, width - 1 - beyond)))
    mine = ((kind < 2) & (beyond < 0)) | ((kind >= 2) & (kind < 4) & (beyond >= 0))
    weights = jnp.where(mine, jnp.exp(-jnp.maximum(off, 0).astype(jnp.float32) / length), 0.0)
    weights = jnp.where((kind >= 8) & (beyond == kind - 8), 1.0, weights)
    sums = lax.dot_general(
        weights, grad_ref[...], (((1,), (1,)), ((), ())), precision=lax.Precision.HIGHEST,
        preferred_element_type=jnp.float32,
    )
    for i in range(sums_ref.shape[0]):
        sums_ref[i] = sums


def smooth(halo, order, grad_ref, out_ref, weights_ref, exact_ref):
    width = out_ref.shape[1]
    length = 2.0 * width
    planes = grad_ref.shape[1] // LANES
    column = lax.broadcasted_iota(jnp.int32, (LANES, width), 1)
    lane = lax.broadcasted_iota(jnp.int32, (LANES, width), 0)
    sources = [lane * planes + c for c in range(planes)]
    kernel = jnp.concatenate(
        [jnp.where(x < width, jnp.exp(-jnp.abs(x - column).astype(jnp.float32) / length), 0.0) for x in sources], axis=0
    )
    out_ref[...] = jnp.dot(
        grad_ref[...], kernel, precision=lax.Precision.HIGHEST, preferred_element_type=jnp.float32
    )
    me = lax.axis_index("lon")
    shape = (8 + halo, width)
    kind, column = lax.broadcasted_iota(jnp.int32, shape, 0), lax.broadcasted_iota(jnp.int32, shape, 1)
    for place, source in enumerate(order):
        strip = jnp.where(kind < 2, source, source + 1)
        left = ((kind == 0) | (kind == 2)) & (strip > me)
        right = ((kind == 1) | (kind == 3)) & (strip < me)
        near = (kind >= 8) & (source + 1 == me)
        away = jnp.where(left, (strip - me) * width - column, (me - strip - 1) * width + column + 1)
        away = jnp.where(near, jnp.abs(kind - 8 - column), away)
        weights = jnp.where(left | right | near, jnp.exp(-jnp.maximum(away, 0).astype(jnp.float32) / length), 0.0)
        exact_ref[place * shape[0] : (place + 1) * shape[0], :] = weights
    high, low = halves(exact_ref[...])
    count = high.shape[0]
    for place, part in enumerate((high, high, low)):
        weights_ref[place * count : (place + 1) * count, :] = part


def finish(own_ref, weights_ref, sums_ref, out_ref):
    high, low = halves(sums_ref[...])
    out_ref[...] = own_ref[...] + lax.dot_general(
        jnp.concatenate([high, low, high], axis=0), weights_ref[...], (((0,), (0,)), ((), ())),
        preferred_element_type=jnp.float32,
    )


def f32(*shape):
    return jax.ShapeDtypeStruct(shape, jnp.float32)


def hint(megabytes):
    return pl.CostEstimate(flops=0, bytes_accessed=megabytes * 1000 * 1000, transcendentals=0)


def spaced(rows):
    return 8 * (rows // 8 | 1)


def vmem(count):
    return [pl.BlockSpec(memory_space=pltpu.VMEM)] * count


def local(depth, surface, friction, wet, coastal_tiles, gauge_route, gauge_cell, gauge_times, gauge_resid):
    height, width = depth.shape
    owned = gauge_route.shape[0]
    blocks = gauge_resid.shape[1]
    steps = blocks * STEPS_BLOCK
    halo = 2 * steps
    assert halo == SEG and height == LANES
    tiles = lax.axis_size(GRID_AXES)
    lons = lax.axis_size("lon")
    row_tiles = lax.axis_size(ROW_AXES)
    planes = width // LANES + 1
    rows_all = height + 2 * halo
    params = pltpu.CompilerParams(vmem_limit_bytes=VMEM_LIMIT)

    keep = (1.0 - friction) * wet.astype(jnp.float32)
    gain = ((courant * 0.5) ** 2 * jnp.maximum(depth + surface, depth_floor)) * keep
    samples, coast_count = gauge_resid.shape[2], coastal_tiles.shape[0]
    assert coast_count <= owned

    assert samples >= 3

    def put(array, group, row):
        groups, rows, lanes = array.shape
        return jnp.pad(array, ((group, 2 * blocks + 1 - group - groups), (row, samples - row - rows), (0, owned - lanes)))

    gauges = (
        put(jnp.transpose(gauge_times, (1, 2, 0)), 0, 0)
        + put(gauge_route.reshape(1, 1, owned), 2 * blocks, 0)
        + put(gauge_cell.reshape(1, 1, owned), 2 * blocks, 1)
        + put(coastal_tiles.reshape(1, 1, coast_count), 2 * blocks, 2)
    ).astype(jnp.float32) + put(jnp.transpose(gauge_resid, (1, 2, 0)), blocks, 0)
    west = pl.pallas_call(
        functools.partial(give_west, 2 * halo), out_shape=f32(2 * height, LANES), in_specs=vmem(2), out_specs=vmem(1)[0],
        compiler_params=params, name="give_west",
    )(keep, gain)
    right = lax.ppermute(west, "lon", [(i + 1, i) for i in range(lons - 1)])

    parcel = pl.pallas_call(
        functools.partial(give_gauges, height, width, blocks, samples, coast_count),
        out_shape=f32(tiles, gauge_rows(owned)[0], LANES),
        in_specs=vmem(1) + [pl.BlockSpec(memory_space=pl.ANY)],
        out_specs=vmem(1)[0],
        scratch_shapes=[pltpu.VMEM((24, LANES), jnp.float32)],
        compiler_params=params,
        cost_estimate=hint(10),
        name="give_gauges",
    )(gauges, west)

    def exchange(array, axes, groups=None):
        return lax.all_to_all(array, axes, split_axis=0, concat_axis=0, axis_index_groups=groups, tiled=True)

    group = sorted(range(tiles), key=lambda tile: (tile % row_tiles in (0, row_tiles - 1), -(tile // row_tiles)))
    parcel = exchange(parcel, GRID_AXES, [group])

    to_far, to_near = pl.pallas_call(
        functools.partial(give_rows, halo), out_shape=(f32(2, halo, planes * LANES),) * 2, in_specs=vmem(3),
        out_specs=tuple(vmem(2)), compiler_params=params, cost_estimate=hint(40), name="give_rows",
    )(keep, gain, right)
    far = lax.ppermute(to_far, ROW_AXES, [pair for i in range(1, row_tiles - 1, 2) for pair in ((i, i + 1), (i + 1, i))])
    near = lax.ppermute(to_near, ROW_AXES, [pair for i in range(0, row_tiles, 2) for pair in ((i, i + 1), (i + 1, i))])

    deal, own = pl.pallas_call(
        functools.partial(deal_own, 2 * halo),
        out_shape=(
            jax.ShapeDtypeStruct((planes * LANES, planes * LANES), jnp.bfloat16), f32(2, planes, height, LANES),
        ),
        in_specs=vmem(3) + [pl.BlockSpec(memory_space=pl.ANY)],
        out_specs=tuple(vmem(2)),
        compiler_params=params,
        cost_estimate=hint(4),
        name="deal_own",
    )(keep, gain, right, to_far)

    wide = max(2 * LANES, owned)
    pushes = pl.pallas_call(
        functools.partial(force, steps, halo, height, width),
        out_shape=f32(steps + 1, planes, spaced(rows_all), LANES),
        in_specs=vmem(1) + [pl.BlockSpec(memory_space=pl.ANY)],
        out_specs=vmem(1)[0],
        scratch_shapes=[
            pltpu.VMEM((steps, wide), jnp.float32),
            pltpu.VMEM((rows_all, wide), jnp.bfloat16),
            pltpu.VMEM((2 * wide, planes * LANES), jnp.bfloat16),
        ],
        compiler_params=params,
        cost_estimate=pl.CostEstimate(
            flops=4 * steps * rows_all * wide * planes * LANES, bytes_accessed=4 * steps * planes * rows_all * LANES,
            transcendentals=0,
        ),
        name="force",
    )(parcel, deal)

    plane = pltpu.VMEM((planes, spaced(rows_all), LANES), jnp.float32)
    grad, sums = pl.pallas_call(
        functools.partial(sweep, steps),
        out_shape=(f32(height, planes * LANES), f32(lons, 8 + halo, height)),
        in_specs=vmem(5),
        out_specs=tuple(vmem(2)),
        scratch_shapes=[plane] * 3 + [
            pltpu.VMEM((planes + 1, spaced(rows_all + 8), LANES), jnp.float32),
            pltpu.VMEM((planes + 1, spaced(rows_all + 8), LANES), jnp.float32),
            pltpu.VMEM((2, planes, spaced(rows_all), LANES), jnp.float32),
        ],
        compiler_params=params,
        name="sweep",
    )(deal, own, far, near, pushes)

    order = list(range(lons // 2, lons)) + list(range(lons // 2))[::-1]
    sums = exchange(sums, "lon", [order])
    own, weights = pl.pallas_call(
        functools.partial(smooth, halo, order),
        out_shape=(f32(height, width), jax.ShapeDtypeStruct((3 * lons * (8 + halo), width), jnp.bfloat16)),
        in_specs=vmem(1),
        out_specs=tuple(vmem(2)),
        scratch_shapes=[pltpu.VMEM((lons * (8 + halo), width), jnp.float32)],
        compiler_params=params,
        cost_estimate=pl.CostEstimate(
            flops=6 * 2 * height * width * width, bytes_accessed=2 * 4 * height * width, transcendentals=width * width
        ),
        name="smooth",
    )(grad)
    return pl.pallas_call(
        finish, out_shape=f32(height, width), in_specs=vmem(3), out_specs=vmem(1)[0], compiler_params=params, name="finish",
    )(own, weights, sums.reshape(lons * (8 + halo), height))


def solution(mesh):
    in_specs = (
        P(("lat", "gau"), "lon"),
        P(("scen", "lat", "gau"), "lon"),
        P(("lat", "gau"), "lon"),
        P(("lat", "gau"), "lon"),
        P(),
        P(("scen", "lon", "lat", "gau"), None),
        P(("scen", "lon", "lat", "gau")),
        P(("scen", "lon", "lat", "gau"), None, None),
        P(("scen", "lon", "lat", "gau"), None, None),
    )
    out_specs = P(("scen", "lat", "gau"), "lon")
    return jax.shard_map(local, mesh=mesh, in_specs=in_specs, out_specs=out_specs, check_vma=False)
```

```python
import functools
import math

import jax
import jax.numpy as jnp
from jax import lax
from jax.experimental import pallas as pl
from jax.experimental.pallas import tpu as pltpu
from jax.sharding import PartitionSpec as P

STEPS_BLOCK = 8
LANES = 128
SEG = 32
LEVELS = 16

courant = 0.45
depth_floor = 0.1

GRID_AXES = ("lon", "lat", "gau")
ROW_AXES = ("lat", "gau")
VMEM_LIMIT = 16 * 1024 * 1024


def roll_lanes(x, shift):
    shift = shift % LANES
    return x if shift == 0 else pltpu.roll(x, shift, 1)


def lane_iota(rows):
    return lax.broadcasted_iota(jnp.int32, (rows, LANES), 1)


def gauge_rows(owned):
    if 3 * owned <= LANES:
        return STEPS_BLOCK, owned
    assert owned <= LANES
    return 3 * STEPS_BLOCK, 0


def my_place():
    row = lax.axis_index("lat") * lax.axis_size("gau") + lax.axis_index("gau")
    return row, lax.axis_index("lon"), lax.axis_size("lat") * lax.axis_size("gau"), lax.axis_size("lon")


def give_west(reach, keep_ref, gain_ref, west_ref):
    height = keep_ref.shape[0]
    lower = lane_iota(height) < reach
    west_ref[:height] = jnp.where(lower, keep_ref[:, :LANES], roll_lanes(gain_ref[:, :LANES], reach))
    west_ref[height:] = jnp.zeros((west_ref.shape[0] - height, LANES), jnp.float32)


def give_rows(halo, keep_ref, gain_ref, right_ref, far_ref, near_ref):
    height, width = keep_ref.shape
    lower = lane_iota(halo) < 2 * halo
    odd = my_place()[0] & 1
    for goal, south in ((far_ref, odd), (near_ref, 1 - odd)):
        rows = pl.ds(pl.multiple_of(south * (height - halo), halo), halo)
        for kind, source in enumerate((keep_ref, gain_ref)):
            goal[kind, :, :width] = source[rows, :]
            goal[kind, :, width:] = jnp.where(lower, roll_lanes(right_ref[rows, :], -2 * halo * kind), 0.0)


def give_gauges(height, width, blocks, samples, coast_count, gauge_ref, after_ref, parcel_ref, block_ref):
    row_tiles = lax.axis_size("lat") * lax.axis_size("gau")
    owned = gauge_ref.shape[2]
    assert blocks == 2
    route, cell, coast = (gauge_ref[2 * blocks, i : i + 1, :].astype(jnp.int32) for i in range(3))
    target = jnp.zeros_like(route)
    for entry in range(coast_count):
        target = jnp.where(route == entry, jnp.broadcast_to(coast[:, entry : entry + 1], route.shape), target)
    row_bits, width_bits = int(math.log2(row_tiles)), int(math.log2(width))
    assert row_tiles == 1 << row_bits and width == 1 << width_bits
    grid_row = (target & (row_tiles - 1)) * height + (cell >> width_bits)
    grid_col = (target >> row_bits) * width + (cell & (width - 1))
    block_ref[...] = jnp.zeros_like(block_ref)
    levels = lax.broadcasted_iota(jnp.int32, (STEPS_BLOCK, owned), 0).astype(jnp.float32)
    for block in range(blocks):
        series = jnp.zeros((STEPS_BLOCK, owned), jnp.float32)
        for sample in range(samples):
            times = gauge_ref[block, sample : sample + 1, :]
            resid = gauge_ref[blocks + block, sample : sample + 1, :]
            series = series + jnp.where(times == levels, resid, 0.0)
        block_ref[block * STEPS_BLOCK : (block + 1) * STEPS_BLOCK, :owned] = series
    at = blocks * STEPS_BLOCK
    block_ref[at : at + 1, :owned] = grid_row.astype(jnp.float32)
    block_ref[at + 1 : at + 2, :owned] = grid_col.astype(jnp.float32)
    size, apart = gauge_rows(owned)
    gauges = block_ref[...]
    if size == STEPS_BLOCK:
        gauges = sum(
            roll_lanes(gauges[i * STEPS_BLOCK : (i + 1) * STEPS_BLOCK], i * apart) for i in range(3)
        )
    tiles = parcel_ref.shape[0]

    def put(tile, carry):
        parcel_ref[tile, 0:size, :] = gauges
        return carry

    lax.fori_loop(0, tiles, put, 0, unroll=tiles <= 16)


def halves(value):
    high = value.astype(jnp.bfloat16)
    return high, (value - high.astype(jnp.float32)).astype(jnp.bfloat16)


def dealt_column(place, planes):
    return (place & (LANES - 1)) * planes + place // LANES


def force(steps, halo, height, width, parcel_ref, after_ref, force_ref, series_ref, rows_hot, cols_hot):
    planes, rows_all = force_ref.shape[1], height + 2 * halo
    my_row, my_lon, row_tiles, lons = my_place()
    wide = rows_hot.shape[1]
    tiles, parcel_rows = parcel_ref.shape[:2]
    size = parcel_rows
    apart = wide // tiles if size == STEPS_BLOCK else 0
    owned = apart if apart else LANES
    group = wide // owned
    groups = tiles // group
    per_plane = LANES // owned
    blocks = rows_all // 8
    row_shift = (halo - my_row * height).astype(jnp.float32)
    col_shift = (-my_lon * width).astype(jnp.float32)
    place = lax.broadcasted_iota(jnp.int32, (rows_all, LANES), 0)
    at = ((place & 7) * blocks + (place >> 3)).astype(jnp.float32)

    def gather_gauges(index):
        lanes = lane_iota(STEPS_BLOCK)
        for part in range(wide // LANES):
            cols = slice(part * LANES, (part + 1) * LANES)
            fields = []
            for field in range(3):
                total = jnp.zeros((STEPS_BLOCK, LANES), jnp.float32)
                rows = slice(0, 8) if apart else slice(8 * field, 8 * field + 8)
                for i in range(per_plane):
                    source = index * group + part * per_plane + i
                    block = roll_lanes(parcel_ref[source, rows, :], i * owned - field * apart)
                    total = jnp.where((lanes >= i * owned) & (lanes < (i + 1) * owned), block, total)
                fields.append(total)
            series_ref[0:8, cols] = fields[0]
            series_ref[8:16, cols] = fields[1]
            row = fields[2][0:1] + row_shift
            col = fields[2][1:2] + col_shift
            col = jnp.where(col < width + 2 * halo, col, -1.0)
            rows_hot[:, cols] = (at == row).astype(jnp.float32).astype(jnp.bfloat16)
            by_gauge = jnp.transpose(jnp.broadcast_to(col, (LANES, LANES)))
            for c in range(planes):
                spot = (lane_iota(LANES) * planes + c).astype(jnp.float32)
                hot = (by_gauge == spot).astype(jnp.float32).astype(jnp.bfloat16)
                cols_hot[part * LANES : (part + 1) * LANES, c * LANES : (c + 1) * LANES] = hot
                cols_hot[wide + part * LANES : wide + (part + 1) * LANES, c * LANES : (c + 1) * LANES] = hot

    def levels_of(start, add):
        hot = rows_hot[...]
        both = []
        for level in range(LEVELS):
            value = series_ref[pl.ds(start + level, 1), :]
            high, low = halves(value)
            both.append(jnp.concatenate([hot * high, hot * low], axis=1))
        both = jnp.concatenate(both, axis=0)
        for first in range(0, planes, 2):
            count = min(2, planes - first)
            total = jnp.dot(
                both, cols_hot[:, first * LANES : (first + count) * LANES], preferred_element_type=jnp.float32
            )
            for level in range(LEVELS):
                for c in range(count):
                    part = total[level * rows_all : (level + 1) * rows_all, c * LANES : (c + 1) * LANES]
                    goal = (start + level, first + c, slice(0, rows_all))
                    force_ref[goal] = force_ref[goal] + part if add else part

    def levels(add):
        def one(index, carry):
            levels_of(index * LEVELS, add)
            return carry

        if steps == LEVELS:
            levels_of(0, add)
        else:
            lax.fori_loop(0, steps // LEVELS, one, 0)

    force_ref[steps] = jnp.zeros_like(force_ref[steps])
    gather_gauges(0)
    levels(False)
    if groups > 1:

        def more(index, carry):
            gather_gauges(index)
            levels(True)
            return carry

        lax.fori_loop(1, groups, more, 0)


def deal_own(reach, keep_ref, gain_ref, right_ref, after_ref, deal_ref, own_ref):
    height, width = keep_ref.shape
    planes = own_ref.shape[1]
    columns = planes * LANES
    parts = []
    for kind, source in enumerate((keep_ref, gain_ref)):
        beside = jnp.where(lane_iota(height) < reach, roll_lanes(right_ref[:height], -reach * kind), 0.0)
        parts += halves(jnp.concatenate([source[...], beside], axis=1))
    parts = jnp.concatenate(parts, axis=0)
    shape = (columns, LANES)
    ahead = lax.broadcasted_iota(jnp.int32, shape, 0) - lax.broadcasted_iota(jnp.int32, shape, 1) * planes
    for first in range(0, planes, 2):
        pair = range(first, min(first + 2, planes))
        deal = jnp.concatenate([(ahead == c).astype(jnp.float32).astype(jnp.bfloat16) for c in pair], axis=1)
        deal_ref[:, first * LANES : (first + len(pair)) * LANES] = deal
        dealt = jnp.dot(parts, deal, preferred_element_type=jnp.float32)
        for i, c in enumerate(pair):
            piece = dealt[:, i * LANES : (i + 1) * LANES]
            for kind in range(2):
                at = 2 * kind * height
                own_ref[kind, c] = piece[at : at + height] + piece[at + height : at + 2 * height]


def sweep(
    steps, deal_ref, own_ref, far_ref, near_ref, force_ref,
    grad_ref, sums_ref,
    a, fx, fy, keeps, gains, plain,
):
    planes, height = own_ref.shape[1:3]
    width = (planes - 1) * LANES
    halo = 2 * steps
    rows_all = height + 2 * halo
    blocks = rows_all // 8
    my_row, my_lon, row_tiles, lons = my_place()
    has_top, has_bottom = my_row > 0, my_row < row_tiles - 1
    has_right = my_lon < lons - 1
    odd = (jnp.zeros((halo, planes * LANES), jnp.int32) + (my_row & 1)) == 1
    lanes8 = lane_iota(8)

    def up(value):
        return pltpu.roll(value, 7, 0)

    def down(value):
        return pltpu.roll(value, 1, 0)

    every = range(planes)
    columns = planes * LANES

    parts = []
    for kind in range(2):
        far, near = far_ref[kind], near_ref[kind]
        parts += halves(jnp.concatenate([jnp.where(odd, near, far), jnp.where(odd, far, near)], axis=0))
    parts = jnp.concatenate(parts, axis=0)
    for first in range(0, planes, 2):
        pair = range(first, min(first + 2, planes))
        dealt = jnp.dot(
            parts, deal_ref[:, first * LANES : (first + len(pair)) * LANES], preferred_element_type=jnp.float32
        )
        for i, c in enumerate(pair):
            piece = dealt[:, i * LANES : (i + 1) * LANES]
            for kind in range(2):
                at = 4 * kind * halo
                value = piece[at : at + 2 * halo] + piece[at + 2 * halo : at + 4 * halo]
                plain[kind, c, 0:halo, :] = value[:halo]
                plain[kind, c, halo : halo + height, :] = own_ref[kind, c]
                plain[kind, c, halo + height : rows_all, :] = value[halo:]
    for kind, goal in enumerate((keeps, gains)):
        for q in range(blocks):
            for c in every:
                value = plain[kind, c, pl.ds(q, 8, stride=blocks), :]
                goal[c, 8 * q : 8 * q + 8, :] = value
                if q == 0:
                    goal[c, 8 * blocks : 8 * blocks + 8, :] = up(value)
                if c == 0:
                    goal[planes, 8 * q : 8 * q + 8, :] = roll_lanes(value, -1)

    def cell_mask(column, there):
        lane, plane = column // planes, column % planes
        return plane, jnp.where(lanes8 == lane, there, 1.0)

    column_mask = dict([cell_mask(width, jnp.where(has_right, 1.0, 0.0)), cell_mask(columns - 1, 0.0)])
    assert len(column_mask) == 2
    sublane = lax.broadcasted_iota(jnp.int32, (8, LANES), 0)
    row_mask = {}
    for row, there in ((halo - 1, has_top), (halo + height, has_bottom)):
        row_mask[row % blocks] = jnp.where(sublane == row // blocks, jnp.where(there, 1.0, 0.0), 1.0)

    def step(index, carry, opening=False):
        level = jnp.where(index < steps - 1, steps - 2 - index, steps)
        near, ahead, new_y, beside, total, behind = {}, {}, {}, {}, {}, {}

        def rows(q):
            return slice(8 * q, 8 * q + 8)

        def first(q):
            source = force_ref.at[steps - 1] if opening else a
            near[q] = [source[c, rows(q % blocks), :] for c in every]
            if q < blocks:
                ahead[q] = near[q][2:] + [roll_lanes(value, -1) for value in near[q][:2]]
            else:
                near[q] = [up(value) for value in near[q]]

        def coefficients(q):
            return [[ref[c, rows(q), :] for c in range(planes + 1)] for ref in (keeps, gains)]

        def second_y(q):
            beside[q + 1] = keep, gain = coefficients(q + 1)
            new_y[q] = [gain[c] * (near[q + 2][c] - near[q][c]) for c in every]
            if not opening:
                new_y[q] = [new_y[q][c] + keep[c] * fy[c, rows(q), :] for c in every]
            for c in every:
                fy[c, rows(q), :] = new_y[q][c]

        def second_x(q):
            keep, gain = beside[q]
            new_x = [gain[c + 1] * (ahead[q][c] - near[q][c]) for c in every]
            if not opening:
                new_x = [new_x[c] + keep[c + 1] * fx[c, rows(q), :] for c in every]
            behind[q] = [roll_lanes(value, 1) for value in new_x[-2:]] + new_x[:-2]
            before = new_y[q - 2] if q >= 2 else [down(fy[c, rows(q - 2 + blocks), :]) for c in every]
            push = [force_ref[level, c, rows(q), :] for c in every]
            total[q] = [(near[q][c] + push[c]) + (new_y[q][c] - before[c]) + new_x[c] for c in every]
            for c in every:
                fx[c, rows(q), :] = new_x[c]

        def third(q):
            for c in every:
                value = total[q][c] - behind[q][c]
                if c in column_mask:
                    value = value * column_mask[c]
                if q in row_mask:
                    value = value * row_mask[q]
                a[c, rows(q), :] = value

        for q in range(4):
            first(q)
        second_y(0)
        second_y(1)
        for q in range(2, blocks):
            first(q + 2)
            second_y(q)
            second_x(q)
            if q > 2:
                third(q - 1)
        for q in range(2):
            first(q)
            new_y[q] = [fy[c, rows(q), :] for c in every]
            beside[q] = coefficients(q)
        for q in range(2):
            second_x(q)
            third(q - 1 if q else blocks - 1)
        third(1)
        return carry

    step(0, 0, opening=True)
    lax.fori_loop(1, steps, step, 0)

    start = jnp.where(my_lon > 0, halo, 0)
    for c in every:
        column = lanes8 * planes + c
        known = (column >= start) & (column < width + halo)
        for r in range(0, height, 8):
            s, q = divmod(halo + r, blocks)
            strided = pl.ds(8 * q + s, 8, stride=8)
            value = jnp.where(known & (keeps[c, strided, :] > 0.0), a[c, strided, :], 0.0)
            grad_ref[r : r + 8, c * LANES : (c + 1) * LANES] = value
    length = 2.0 * width
    shape = (8 + halo, planes * LANES)
    kind = lax.broadcasted_iota(jnp.int32, shape, 0)
    column = dealt_column(lax.broadcasted_iota(jnp.int32, shape, 1), planes)
    beyond = column - width
    off = jnp.where(kind == 0, column, jnp.where(kind == 1, -1 - beyond, jnp.where(kind == 2, beyond, width - 1 - beyond)))
    mine = ((kind < 2) & (beyond < 0)) | ((kind >= 2) & (kind < 4) & (beyond >= 0))
    weights = jnp.where(mine, jnp.exp(-jnp.maximum(off, 0).astype(jnp.float32) / length), 0.0)
    weights = jnp.where((kind >= 8) & (beyond == kind - 8), 1.0, weights)
    sums = lax.dot_general(
        weights, grad_ref[...], (((1,), (1,)), ((), ())), precision=lax.Precision.HIGHEST,
        preferred_element_type=jnp.float32,
    )
    for i in range(sums_ref.shape[0]):
        sums_ref[i] = sums


def smooth(halo, order, grad_ref, out_ref, weights_ref, exact_ref):
    width = out_ref.shape[1]
    length = 2.0 * width
    planes = grad_ref.shape[1] // LANES
    column = lax.broadcasted_iota(jnp.int32, (LANES, width), 1)
    lane = lax.broadcasted_iota(jnp.int32, (LANES, width), 0)
    sources = [lane * planes + c for c in range(planes)]
    kernel = jnp.concatenate(
        [jnp.where(x < width, jnp.exp(-jnp.abs(x - column).astype(jnp.float32) / length), 0.0) for x in sources], axis=0
    )
    out_ref[...] = jnp.dot(
        grad_ref[...], kernel, precision=lax.Precision.HIGHEST, preferred_element_type=jnp.float32
    )
    me = lax.axis_index("lon")
    shape = (8 + halo, width)
    kind, column = lax.broadcasted_iota(jnp.int32, shape, 0), lax.broadcasted_iota(jnp.int32, shape, 1)
    for place, source in enumerate(order):
        strip = jnp.where(kind < 2, source, source + 1)
        left = ((kind == 0) | (kind == 2)) & (strip > me)
        right = ((kind == 1) | (kind == 3)) & (strip < me)
        near = (kind >= 8) & (source + 1 == me)
        away = jnp.where(left, (strip - me) * width - column, (me - strip - 1) * width + column + 1)
        away = jnp.where(near, jnp.abs(kind - 8 - column), away)
        weights = jnp.where(left | right | near, jnp.exp(-jnp.maximum(away, 0).astype(jnp.float32) / length), 0.0)
        exact_ref[place * shape[0] : (place + 1) * shape[0], :] = weights
    high, low = halves(exact_ref[...])
    count = high.shape[0]
    for place, part in enumerate((high, high, low)):
        weights_ref[place * count : (place + 1) * count, :] = part


def finish(own_ref, weights_ref, sums_ref, out_ref, here, left):
    high, low = halves(sums_ref[...])
    sums = jnp.concatenate([high, low, high], axis=0)
    half = own_ref.shape[1] // 2
    copies = []
    for i in range(2):
        cols = slice(i * half, (i + 1) * half)
        here[i] = own_ref[:, cols] + lax.dot_general(
            sums, weights_ref[:, cols], (((0,), (0,)), ((), ())), preferred_element_type=jnp.float32
        )
        copies.append(pltpu.make_async_copy(here.at[i], out_ref.at[:, cols], left.at[i]))
        copies[i].start()
    for copy in copies:
        copy.wait()


def f32(*shape):
    return jax.ShapeDtypeStruct(shape, jnp.float32)


def hint(megabytes):
    return pl.CostEstimate(flops=0, bytes_accessed=megabytes * 1000 * 1000, transcendentals=0)


def spaced(rows):
    return 8 * (rows // 8 | 1)


def vmem(count):
    return [pl.BlockSpec(memory_space=pltpu.VMEM)] * count


def local(depth, surface, friction, wet, coastal_tiles, gauge_route, gauge_cell, gauge_times, gauge_resid):
    height, width = depth.shape
    owned = gauge_route.shape[0]
    blocks = gauge_resid.shape[1]
    steps = blocks * STEPS_BLOCK
    halo = 2 * steps
    assert halo == SEG and height == LANES
    tiles = lax.axis_size(GRID_AXES)
    lons = lax.axis_size("lon")
    row_tiles = lax.axis_size(ROW_AXES)
    planes = width // LANES + 1
    rows_all = height + 2 * halo
    params = pltpu.CompilerParams(vmem_limit_bytes=VMEM_LIMIT)

    keep = (1.0 - friction) * wet.astype(jnp.float32)
    gain = ((courant * 0.5) ** 2 * jnp.maximum(depth + surface, depth_floor)) * keep
    samples, coast_count = gauge_resid.shape[2], coastal_tiles.shape[0]
    assert coast_count <= owned

    assert samples >= 3

    def put(array, group, row):
        groups, rows, lanes = array.shape
        return jnp.pad(array, ((group, 2 * blocks + 1 - group - groups), (row, samples - row - rows), (0, owned - lanes)))

    gauges = (
        put(jnp.transpose(gauge_times, (1, 2, 0)), 0, 0)
        + put(gauge_route.reshape(1, 1, owned), 2 * blocks, 0)
        + put(gauge_cell.reshape(1, 1, owned), 2 * blocks, 1)
        + put(coastal_tiles.reshape(1, 1, coast_count), 2 * blocks, 2)
    ).astype(jnp.float32) + put(jnp.transpose(gauge_resid, (1, 2, 0)), blocks, 0)
    west = pl.pallas_call(
        functools.partial(give_west, 2 * halo), out_shape=f32(2 * height, LANES), in_specs=vmem(2), out_specs=vmem(1)[0],
        compiler_params=params, name="give_west",
    )(keep, gain)
    right = lax.ppermute(west, "lon", [(i + 1, i) for i in range(lons - 1)])

    parcel = pl.pallas_call(
        functools.partial(give_gauges, height, width, blocks, samples, coast_count),
        out_shape=f32(tiles, gauge_rows(owned)[0], LANES),
        in_specs=vmem(1) + [pl.BlockSpec(memory_space=pl.ANY)],
        out_specs=vmem(1)[0],
        scratch_shapes=[pltpu.VMEM((24, LANES), jnp.float32)],
        compiler_params=params,
        cost_estimate=hint(10),
        name="give_gauges",
    )(gauges, west)

    def exchange(array, axes, groups=None):
        return lax.all_to_all(array, axes, split_axis=0, concat_axis=0, axis_index_groups=groups, tiled=True)

    ends = (row_tiles - 1, 0)
    rank = [row for row in reversed(range(row_tiles)) if row not in ends] + list(ends)
    group = sorted(range(tiles), key=lambda tile: (rank.index(tile % row_tiles), -(tile // row_tiles)))
    parcel = exchange(parcel, GRID_AXES, [group])

    to_far, to_near = pl.pallas_call(
        functools.partial(give_rows, halo), out_shape=(f32(2, halo, planes * LANES),) * 2, in_specs=vmem(3),
        out_specs=tuple(vmem(2)), compiler_params=params, cost_estimate=hint(40), name="give_rows",
    )(keep, gain, right)
    far = lax.ppermute(to_far, ROW_AXES, [pair for i in range(1, row_tiles - 1, 2) for pair in ((i, i + 1), (i + 1, i))])
    near = lax.ppermute(to_near, ROW_AXES, [pair for i in range(0, row_tiles, 2) for pair in ((i, i + 1), (i + 1, i))])

    deal, own = pl.pallas_call(
        functools.partial(deal_own, 2 * halo),
        out_shape=(
            jax.ShapeDtypeStruct((planes * LANES, planes * LANES), jnp.bfloat16), f32(2, planes, height, LANES),
        ),
        in_specs=vmem(3) + [pl.BlockSpec(memory_space=pl.ANY)],
        out_specs=tuple(vmem(2)),
        compiler_params=params,
        cost_estimate=hint(4),
        name="deal_own",
    )(keep, gain, right, to_far)

    wide = max(2 * LANES, owned)
    pushes = pl.pallas_call(
        functools.partial(force, steps, halo, height, width),
        out_shape=f32(steps + 1, planes, spaced(rows_all), LANES),
        in_specs=vmem(1) + [pl.BlockSpec(memory_space=pl.ANY)],
        out_specs=vmem(1)[0],
        scratch_shapes=[
            pltpu.VMEM((steps, wide), jnp.float32),
            pltpu.VMEM((rows_all, wide), jnp.bfloat16),
            pltpu.VMEM((2 * wide, planes * LANES), jnp.bfloat16),
        ],
        compiler_params=params,
        cost_estimate=pl.CostEstimate(
            flops=4 * steps * rows_all * wide * planes * LANES, bytes_accessed=4 * steps * planes * rows_all * LANES,
            transcendentals=0,
        ),
        name="force",
    )(parcel, deal)

    plane = pltpu.VMEM((planes, spaced(rows_all), LANES), jnp.float32)
    grad, sums = pl.pallas_call(
        functools.partial(sweep, steps),
        out_shape=(f32(height, planes * LANES), f32(lons, 8 + halo, height)),
        in_specs=vmem(5),
        out_specs=tuple(vmem(2)),
        scratch_shapes=[plane] * 3 + [
            pltpu.VMEM((planes + 1, spaced(rows_all + 8), LANES), jnp.float32),
            pltpu.VMEM((planes + 1, spaced(rows_all + 8), LANES), jnp.float32),
            pltpu.VMEM((2, planes, spaced(rows_all), LANES), jnp.float32),
        ],
        compiler_params=params,
        name="sweep",
    )(deal, own, far, near, pushes)

    order = list(range(lons))[::-1]
    sums = exchange(sums, "lon", [order])
    own, weights = pl.pallas_call(
        functools.partial(smooth, halo, order),
        out_shape=(f32(height, width), jax.ShapeDtypeStruct((3 * lons * (8 + halo), width), jnp.bfloat16)),
        in_specs=vmem(1),
        out_specs=tuple(vmem(2)),
        scratch_shapes=[pltpu.VMEM((lons * (8 + halo), width), jnp.float32)],
        compiler_params=params,
        cost_estimate=pl.CostEstimate(
            flops=6 * 2 * height * width * width, bytes_accessed=2 * 4 * height * width, transcendentals=width * width
        ),
        name="smooth",
    )(grad)
    return pl.pallas_call(
        finish,
        out_shape=f32(height, width),
        in_specs=vmem(3),
        out_specs=pl.BlockSpec(memory_space=pl.ANY),
        scratch_shapes=[pltpu.VMEM((2, height, width // 2), jnp.float32), pltpu.SemaphoreType.DMA((2,))],
        compiler_params=params,
        name="finish",
    )(own, weights, sums.reshape(lons * (8 + halo), height))


def solution(mesh):
    in_specs = (
        P(("lat", "gau"), "lon"),
        P(("scen", "lat", "gau"), "lon"),
        P(("lat", "gau"), "lon"),
        P(("lat", "gau"), "lon"),
        P(),
        P(("scen", "lon", "lat", "gau"), None),
        P(("scen", "lon", "lat", "gau")),
        P(("scen", "lon", "lat", "gau"), None, None),
        P(("scen", "lon", "lat", "gau"), None, None),
    )
    out_specs = P(("scen", "lat", "gau"), "lon")
    return jax.shard_map(local, mesh=mesh, in_specs=in_specs, out_specs=out_specs, check_vma=False)
```

```python
import functools
import math

import jax
import jax.numpy as jnp
from jax import lax
from jax.experimental import pallas as pl
from jax.experimental.pallas import tpu as pltpu
from jax.sharding import PartitionSpec as P

STEPS_BLOCK = 8
LANES = 128
SEG = 32
LEVELS = 16

courant = 0.45
depth_floor = 0.1

GRID_AXES = ("lon", "lat", "gau")
ROW_AXES = ("lat", "gau")
VMEM_LIMIT = 16 * 1024 * 1024


def roll_lanes(x, shift):
    shift = shift % LANES
    return x if shift == 0 else pltpu.roll(x, shift, 1)


def lane_iota(rows):
    return lax.broadcasted_iota(jnp.int32, (rows, LANES), 1)


def gauge_rows(owned):
    if 3 * owned <= LANES:
        return STEPS_BLOCK, owned
    assert owned <= LANES
    return 3 * STEPS_BLOCK, 0


def my_place():
    row = lax.axis_index("lat") * lax.axis_size("gau") + lax.axis_index("gau")
    return row, lax.axis_index("lon"), lax.axis_size("lat") * lax.axis_size("gau"), lax.axis_size("lon")


def give_west(reach, keep_ref, gain_ref, west_ref):
    height = keep_ref.shape[0]
    lower = lane_iota(height) < reach
    west_ref[:height] = jnp.where(lower, keep_ref[:, :LANES], roll_lanes(gain_ref[:, :LANES], reach))
    west_ref[height:] = jnp.zeros((west_ref.shape[0] - height, LANES), jnp.float32)


def give_rows(halo, keep_ref, gain_ref, right_ref, far_ref, near_ref):
    height, width = keep_ref.shape
    lower = lane_iota(halo) < 2 * halo
    odd = my_place()[0] & 1
    for goal, south in ((far_ref, odd), (near_ref, 1 - odd)):
        rows = pl.ds(pl.multiple_of(south * (height - halo), halo), halo)
        for kind, source in enumerate((keep_ref, gain_ref)):
            goal[kind, :, :width] = source[rows, :]
            goal[kind, :, width:] = jnp.where(lower, roll_lanes(right_ref[rows, :], -2 * halo * kind), 0.0)


def give_gauges(height, width, blocks, samples, coast_count, gauge_ref, after_ref, parcel_ref, block_ref):
    row_tiles = lax.axis_size("lat") * lax.axis_size("gau")
    owned = gauge_ref.shape[2]
    assert blocks == 2
    route, cell, coast = (gauge_ref[2 * blocks, i : i + 1, :].astype(jnp.int32) for i in range(3))
    target = jnp.zeros_like(route)
    for entry in range(coast_count):
        target = jnp.where(route == entry, jnp.broadcast_to(coast[:, entry : entry + 1], route.shape), target)
    row_bits, width_bits = int(math.log2(row_tiles)), int(math.log2(width))
    assert row_tiles == 1 << row_bits and width == 1 << width_bits
    grid_row = (target & (row_tiles - 1)) * height + (cell >> width_bits)
    grid_col = (target >> row_bits) * width + (cell & (width - 1))
    block_ref[...] = jnp.zeros_like(block_ref)
    levels = lax.broadcasted_iota(jnp.int32, (STEPS_BLOCK, owned), 0).astype(jnp.float32)
    for block in range(blocks):
        series = jnp.zeros((STEPS_BLOCK, owned), jnp.float32)
        for sample in range(samples):
            times = gauge_ref[block, sample : sample + 1, :]
            resid = gauge_ref[blocks + block, sample : sample + 1, :]
            series = series + jnp.where(times == levels, resid, 0.0)
        block_ref[block * STEPS_BLOCK : (block + 1) * STEPS_BLOCK, :owned] = series
    at = blocks * STEPS_BLOCK
    block_ref[at : at + 1, :owned] = grid_row.astype(jnp.float32)
    block_ref[at + 1 : at + 2, :owned] = grid_col.astype(jnp.float32)
    size, apart = gauge_rows(owned)
    gauges = block_ref[...]
    if size == STEPS_BLOCK:
        gauges = sum(
            roll_lanes(gauges[i * STEPS_BLOCK : (i + 1) * STEPS_BLOCK], i * apart) for i in range(3)
        )
    tiles = parcel_ref.shape[0]

    def put(tile, carry):
        parcel_ref[tile, 0:size, :] = gauges
        return carry

    lax.fori_loop(0, tiles, put, 0, unroll=tiles <= 16)


def halves(value):
    high = value.astype(jnp.bfloat16)
    return high, (value - high.astype(jnp.float32)).astype(jnp.bfloat16)


def dealt_column(place, planes):
    return (place & (LANES - 1)) * planes + place // LANES


def force(steps, halo, height, width, parcel_ref, after_ref, force_ref, series_ref, rows_hot, cols_hot):
    planes, rows_all = force_ref.shape[1], height + 2 * halo
    my_row, my_lon, row_tiles, lons = my_place()
    wide = rows_hot.shape[1]
    tiles, parcel_rows = parcel_ref.shape[:2]
    size = parcel_rows
    apart = wide // tiles if size == STEPS_BLOCK else 0
    owned = apart if apart else LANES
    group = wide // owned
    groups = tiles // group
    per_plane = LANES // owned
    blocks = rows_all // 8
    row_shift = (halo - my_row * height).astype(jnp.float32)
    col_shift = (-my_lon * width).astype(jnp.float32)
    place = lax.broadcasted_iota(jnp.int32, (rows_all, LANES), 0)
    at = ((place & 7) * blocks + (place >> 3)).astype(jnp.float32)

    def gather_gauges(index):
        lanes = lane_iota(STEPS_BLOCK)
        for part in range(wide // LANES):
            cols = slice(part * LANES, (part + 1) * LANES)
            fields = []
            for field in range(3):
                total = jnp.zeros((STEPS_BLOCK, LANES), jnp.float32)
                rows = slice(0, 8) if apart else slice(8 * field, 8 * field + 8)
                for i in range(per_plane):
                    source = index * group + part * per_plane + i
                    block = roll_lanes(parcel_ref[source, rows, :], i * owned - field * apart)
                    total = jnp.where((lanes >= i * owned) & (lanes < (i + 1) * owned), block, total)
                fields.append(total)
            series_ref[0:8, cols] = fields[0]
            series_ref[8:16, cols] = fields[1]
            row = fields[2][0:1] + row_shift
            col = fields[2][1:2] + col_shift
            col = jnp.where(col < width + 2 * halo, col, -1.0)
            rows_hot[:, cols] = (at == row).astype(jnp.float32).astype(jnp.bfloat16)
            by_gauge = jnp.transpose(jnp.broadcast_to(col, (LANES, LANES)))
            for c in range(planes):
                spot = (lane_iota(LANES) * planes + c).astype(jnp.float32)
                hot = (by_gauge == spot).astype(jnp.float32).astype(jnp.bfloat16)
                cols_hot[part * LANES : (part + 1) * LANES, c * LANES : (c + 1) * LANES] = hot
                cols_hot[wide + part * LANES : wide + (part + 1) * LANES, c * LANES : (c + 1) * LANES] = hot

    def levels_of(start, add):
        hot = rows_hot[...]
        both = []
        for level in range(LEVELS):
            value = series_ref[pl.ds(start + level, 1), :]
            high, low = halves(value)
            both.append(jnp.concatenate([hot * high, hot * low], axis=1))
        both = jnp.concatenate(both, axis=0)
        for first in range(0, planes, 2):
            count = min(2, planes - first)
            total = jnp.dot(
                both, cols_hot[:, first * LANES : (first + count) * LANES], preferred_element_type=jnp.float32
            )
            for level in range(LEVELS):
                for c in range(count):
                    part = total[level * rows_all : (level + 1) * rows_all, c * LANES : (c + 1) * LANES]
                    goal = (start + level, first + c, slice(0, rows_all))
                    force_ref[goal] = force_ref[goal] + part if add else part

    def levels(add):
        def one(index, carry):
            levels_of(index * LEVELS, add)
            return carry

        if steps == LEVELS:
            levels_of(0, add)
        else:
            lax.fori_loop(0, steps // LEVELS, one, 0)

    force_ref[steps] = jnp.zeros_like(force_ref[steps])
    gather_gauges(0)
    levels(False)
    if groups > 1:

        def more(index, carry):
            gather_gauges(index)
            levels(True)
            return carry

        lax.fori_loop(1, groups, more, 0)


def deal_own(reach, keep_ref, gain_ref, right_ref, after_ref, deal_ref, own_ref):
    height, width = keep_ref.shape
    planes = own_ref.shape[1]
    columns = planes * LANES
    parts = []
    for kind, source in enumerate((keep_ref, gain_ref)):
        beside = jnp.where(lane_iota(height) < reach, roll_lanes(right_ref[:height], -reach * kind), 0.0)
        parts += halves(jnp.concatenate([source[...], beside], axis=1))
    parts = jnp.concatenate(parts, axis=0)
    shape = (columns, LANES)
    ahead = lax.broadcasted_iota(jnp.int32, shape, 0) - lax.broadcasted_iota(jnp.int32, shape, 1) * planes
    for first in range(0, planes, 2):
        pair = range(first, min(first + 2, planes))
        deal = jnp.concatenate([(ahead == c).astype(jnp.float32).astype(jnp.bfloat16) for c in pair], axis=1)
        deal_ref[:, first * LANES : (first + len(pair)) * LANES] = deal
        dealt = jnp.dot(parts, deal, preferred_element_type=jnp.float32)
        for i, c in enumerate(pair):
            piece = dealt[:, i * LANES : (i + 1) * LANES]
            for kind in range(2):
                at = 2 * kind * height
                own_ref[kind, c] = piece[at : at + height] + piece[at + height : at + 2 * height]


def sweep(
    steps, deal_ref, own_ref, far_ref, near_ref, force_ref,
    grad_ref, sums_ref,
    a, fx, fy, keeps, gains, plain,
):
    planes, height = own_ref.shape[1:3]
    width = (planes - 1) * LANES
    halo = 2 * steps
    rows_all = height + 2 * halo
    blocks = rows_all // 8
    my_row, my_lon, row_tiles, lons = my_place()
    has_top, has_bottom = my_row > 0, my_row < row_tiles - 1
    has_right = my_lon < lons - 1
    odd = (jnp.zeros((halo, planes * LANES), jnp.int32) + (my_row & 1)) == 1
    lanes8 = lane_iota(8)

    def up(value):
        return pltpu.roll(value, 7, 0)

    def down(value):
        return pltpu.roll(value, 1, 0)

    every = range(planes)
    columns = planes * LANES

    parts = []
    for kind in range(2):
        far, near = far_ref[kind], near_ref[kind]
        parts += halves(jnp.concatenate([jnp.where(odd, near, far), jnp.where(odd, far, near)], axis=0))
    parts = jnp.concatenate(parts, axis=0)
    for first in range(0, planes, 2):
        pair = range(first, min(first + 2, planes))
        dealt = jnp.dot(
            parts, deal_ref[:, first * LANES : (first + len(pair)) * LANES], preferred_element_type=jnp.float32
        )
        for i, c in enumerate(pair):
            piece = dealt[:, i * LANES : (i + 1) * LANES]
            for kind in range(2):
                at = 4 * kind * halo
                value = piece[at : at + 2 * halo] + piece[at + 2 * halo : at + 4 * halo]
                plain[kind, c, 0:halo, :] = value[:halo]
                plain[kind, c, halo : halo + height, :] = own_ref[kind, c]
                plain[kind, c, halo + height : rows_all, :] = value[halo:]
    for kind, goal in enumerate((keeps, gains)):
        for q in range(blocks):
            for c in every:
                value = plain[kind, c, pl.ds(q, 8, stride=blocks), :]
                goal[c, 8 * q : 8 * q + 8, :] = value
                if q == 0:
                    goal[c, 8 * blocks : 8 * blocks + 8, :] = up(value)
                if c == 0:
                    goal[planes, 8 * q : 8 * q + 8, :] = roll_lanes(value, -1)

    def cell_mask(column, there):
        lane, plane = column // planes, column % planes
        return plane, jnp.where(lanes8 == lane, there, 1.0)

    column_mask = dict([cell_mask(width, jnp.where(has_right, 1.0, 0.0)), cell_mask(columns - 1, 0.0)])
    assert len(column_mask) == 2
    sublane = lax.broadcasted_iota(jnp.int32, (8, LANES), 0)
    row_mask = {}
    for row, there in ((halo - 1, has_top), (halo + height, has_bottom)):
        row_mask[row % blocks] = jnp.where(sublane == row // blocks, jnp.where(there, 1.0, 0.0), 1.0)

    def step(index, carry, opening=False):
        level = jnp.where(index < steps - 1, steps - 2 - index, steps)
        near, ahead, new_y, beside, total, behind = {}, {}, {}, {}, {}, {}

        def rows(q):
            return slice(8 * q, 8 * q + 8)

        def first(q):
            source = force_ref.at[steps - 1] if opening else a
            near[q] = [source[c, rows(q % blocks), :] for c in every]
            if q < blocks:
                ahead[q] = near[q][2:] + [roll_lanes(value, -1) for value in near[q][:2]]
            else:
                near[q] = [up(value) for value in near[q]]

        def coefficients(q):
            return [[ref[c, rows(q), :] for c in range(planes + 1)] for ref in (keeps, gains)]

        def second_y(q):
            beside[q + 1] = keep, gain = coefficients(q + 1)
            new_y[q] = [gain[c] * (near[q + 2][c] - near[q][c]) for c in every]
            if not opening:
                new_y[q] = [new_y[q][c] + keep[c] * fy[c, rows(q), :] for c in every]
            for c in every:
                fy[c, rows(q), :] = new_y[q][c]

        def second_x(q):
            keep, gain = beside[q]
            new_x = [gain[c + 1] * (ahead[q][c] - near[q][c]) for c in every]
            if not opening:
                new_x = [new_x[c] + keep[c + 1] * fx[c, rows(q), :] for c in every]
            behind[q] = [roll_lanes(value, 1) for value in new_x[-2:]] + new_x[:-2]
            before = new_y[q - 2] if q >= 2 else [down(fy[c, rows(q - 2 + blocks), :]) for c in every]
            push = [force_ref[level, c, rows(q), :] for c in every]
            total[q] = [(near[q][c] + push[c]) + (new_y[q][c] - before[c]) + new_x[c] for c in every]
            for c in every:
                fx[c, rows(q), :] = new_x[c]

        def third(q):
            for c in every:
                value = total[q][c] - behind[q][c]
                if c in column_mask:
                    value = value * column_mask[c]
                if q in row_mask:
                    value = value * row_mask[q]
                a[c, rows(q), :] = value

        for q in range(4):
            first(q)
        second_y(0)
        second_y(1)
        for q in range(2, blocks):
            first(q + 2)
            second_y(q)
            second_x(q)
            if q > 2:
                third(q - 1)
        for q in range(2):
            first(q)
            new_y[q] = [fy[c, rows(q), :] for c in every]
            beside[q] = coefficients(q)
        for q in range(2):
            second_x(q)
            third(q - 1 if q else blocks - 1)
        third(1)
        return carry

    step(0, 0, opening=True)
    lax.fori_loop(1, steps, step, 0)

    start = jnp.where(my_lon > 0, halo, 0)
    for c in every:
        column = lanes8 * planes + c
        known = (column >= start) & (column < width + halo)
        for r in range(0, height, 8):
            s, q = divmod(halo + r, blocks)
            strided = pl.ds(8 * q + s, 8, stride=8)
            value = jnp.where(known & (keeps[c, strided, :] > 0.0), a[c, strided, :], 0.0)
            grad_ref[r : r + 8, c * LANES : (c + 1) * LANES] = value
    length = 2.0 * width
    shape = (16 + halo, planes * LANES)
    kind = lax.broadcasted_iota(jnp.int32, shape, 0)
    column = dealt_column(lax.broadcasted_iota(jnp.int32, shape, 1), planes)
    beyond = column - width
    off = jnp.where(kind == 0, column, jnp.where(kind == 1, -1 - beyond, jnp.where(kind == 2, beyond, width - 1 - beyond)))
    mine = ((kind < 2) & (beyond < 0)) | ((kind >= 2) & (kind < 4) & (beyond >= 0))
    weights = jnp.where(mine, jnp.exp(-jnp.maximum(off, 0).astype(jnp.float32) / length), 0.0)
    weights = jnp.where((kind >= 8) & (beyond == kind - 8), 1.0, weights)
    (w_high, w_low), (g_high, g_low) = halves(weights), halves(grad_ref[...])
    sums = lax.dot_general(
        jnp.concatenate([w_high, w_high, w_low], axis=1), jnp.concatenate([g_high, g_low, g_high], axis=1),
        (((1,), (1,)), ((), ())), preferred_element_type=jnp.float32,
    )[: 8 + halo]
    for i in range(sums_ref.shape[0]):
        sums_ref[i] = sums


def smooth(halo, order, grad_ref, out_ref, weights_ref, exact_ref):
    width = out_ref.shape[1]
    length = 2.0 * width
    planes = grad_ref.shape[1] // LANES
    column = lax.broadcasted_iota(jnp.int32, (LANES, width), 1)
    lane = lax.broadcasted_iota(jnp.int32, (LANES, width), 0)
    sources = [lane * planes + c for c in range(planes)]
    kernel = jnp.concatenate(
        [jnp.where(x < width, jnp.exp(-jnp.abs(x - column).astype(jnp.float32) / length), 0.0) for x in sources], axis=0
    )
    out_ref[...] = jnp.dot(
        grad_ref[...], kernel, precision=lax.Precision.HIGHEST, preferred_element_type=jnp.float32
    )
    me = lax.axis_index("lon")
    shape = (8 + halo, width)
    kind, column = lax.broadcasted_iota(jnp.int32, shape, 0), lax.broadcasted_iota(jnp.int32, shape, 1)
    for place, source in enumerate(order):
        strip = jnp.where(kind < 2, source, source + 1)
        left = ((kind == 0) | (kind == 2)) & (strip > me)
        right = ((kind == 1) | (kind == 3)) & (strip < me)
        near = (kind >= 8) & (source + 1 == me)
        away = jnp.where(left, (strip - me) * width - column, (me - strip - 1) * width + column + 1)
        away = jnp.where(near, jnp.abs(kind - 8 - column), away)
        weights = jnp.where(left | right | near, jnp.exp(-jnp.maximum(away, 0).astype(jnp.float32) / length), 0.0)
        exact_ref[place * shape[0] : (place + 1) * shape[0], :] = weights
    high, low = halves(exact_ref[...])
    count = high.shape[0]
    for place, part in enumerate((high, high, low)):
        weights_ref[place * count : (place + 1) * count, :] = part


def finish(own_ref, weights_ref, sums_ref, out_ref):
    high, low = halves(sums_ref[...])
    out_ref[...] = own_ref[...] + lax.dot_general(
        jnp.concatenate([high, low, high], axis=0), weights_ref[...], (((0,), (0,)), ((), ())),
        preferred_element_type=jnp.float32,
    )


def f32(*shape):
    return jax.ShapeDtypeStruct(shape, jnp.float32)


def hint(megabytes):
    return pl.CostEstimate(flops=0, bytes_accessed=megabytes * 1000 * 1000, transcendentals=0)


def spaced(rows):
    return 8 * (rows // 8 | 1)


def vmem(count):
    return [pl.BlockSpec(memory_space=pltpu.VMEM)] * count


def local(depth, surface, friction, wet, coastal_tiles, gauge_route, gauge_cell, gauge_times, gauge_resid):
    height, width = depth.shape
    owned = gauge_route.shape[0]
    blocks = gauge_resid.shape[1]
    steps = blocks * STEPS_BLOCK
    halo = 2 * steps
    assert halo == SEG and height == LANES
    tiles = lax.axis_size(GRID_AXES)
    lons = lax.axis_size("lon")
    row_tiles = lax.axis_size(ROW_AXES)
    planes = width // LANES + 1
    rows_all = height + 2 * halo
    params = pltpu.CompilerParams(vmem_limit_bytes=VMEM_LIMIT)

    keep = (1.0 - friction) * wet.astype(jnp.float32)
    gain = ((courant * 0.5) ** 2 * jnp.maximum(depth + surface, depth_floor)) * keep
    samples, coast_count = gauge_resid.shape[2], coastal_tiles.shape[0]
    assert coast_count <= owned

    assert samples >= 3

    def put(array, group, row):
        groups, rows, lanes = array.shape
        return jnp.pad(array, ((group, 2 * blocks + 1 - group - groups), (row, samples - row - rows), (0, owned - lanes)))

    gauges = (
        put(jnp.transpose(gauge_times, (1, 2, 0)), 0, 0)
        + put(gauge_route.reshape(1, 1, owned), 2 * blocks, 0)
        + put(gauge_cell.reshape(1, 1, owned), 2 * blocks, 1)
        + put(coastal_tiles.reshape(1, 1, coast_count), 2 * blocks, 2)
    ).astype(jnp.float32) + put(jnp.transpose(gauge_resid, (1, 2, 0)), blocks, 0)
    west = pl.pallas_call(
        functools.partial(give_west, 2 * halo), out_shape=f32(2 * height, LANES), in_specs=vmem(2), out_specs=vmem(1)[0],
        compiler_params=params, name="give_west",
    )(keep, gain)
    right = lax.ppermute(west, "lon", [(i + 1, i) for i in range(lons - 1)])

    parcel = pl.pallas_call(
        functools.partial(give_gauges, height, width, blocks, samples, coast_count),
        out_shape=f32(tiles, gauge_rows(owned)[0], LANES),
        in_specs=vmem(1) + [pl.BlockSpec(memory_space=pl.ANY)],
        out_specs=vmem(1)[0],
        scratch_shapes=[pltpu.VMEM((24, LANES), jnp.float32)],
        compiler_params=params,
        cost_estimate=hint(10),
        name="give_gauges",
    )(gauges, west)

    def exchange(array, axes, groups=None):
        return lax.all_to_all(array, axes, split_axis=0, concat_axis=0, axis_index_groups=groups, tiled=True)

    rank = {row_tiles - 1: 1, 0: 2}
    group = sorted(range(tiles), key=lambda tile: (rank.get(tile % row_tiles, 0), -(tile // row_tiles)))
    parcel = exchange(parcel, GRID_AXES, [group])

    to_far, to_near = pl.pallas_call(
        functools.partial(give_rows, halo), out_shape=(f32(2, halo, planes * LANES),) * 2, in_specs=vmem(3),
        out_specs=tuple(vmem(2)), compiler_params=params, cost_estimate=hint(40), name="give_rows",
    )(keep, gain, right)
    far = lax.ppermute(to_far, ROW_AXES, [pair for i in range(1, row_tiles - 1, 2) for pair in ((i, i + 1), (i + 1, i))])
    near = lax.ppermute(to_near, ROW_AXES, [pair for i in range(0, row_tiles, 2) for pair in ((i, i + 1), (i + 1, i))])

    deal, own = pl.pallas_call(
        functools.partial(deal_own, 2 * halo),
        out_shape=(
            jax.ShapeDtypeStruct((planes * LANES, planes * LANES), jnp.bfloat16), f32(2, planes, height, LANES),
        ),
        in_specs=vmem(3) + [pl.BlockSpec(memory_space=pl.ANY)],
        out_specs=tuple(vmem(2)),
        compiler_params=params,
        cost_estimate=hint(4),
        name="deal_own",
    )(keep, gain, right, to_far)

    wide = max(2 * LANES, owned)
    pushes = pl.pallas_call(
        functools.partial(force, steps, halo, height, width),
        out_shape=f32(steps + 1, planes, spaced(rows_all), LANES),
        in_specs=vmem(1) + [pl.BlockSpec(memory_space=pl.ANY)],
        out_specs=vmem(1)[0],
        scratch_shapes=[
            pltpu.VMEM((steps, wide), jnp.float32),
            pltpu.VMEM((rows_all, wide), jnp.bfloat16),
            pltpu.VMEM((2 * wide, planes * LANES), jnp.bfloat16),
        ],
        compiler_params=params,
        cost_estimate=pl.CostEstimate(
            flops=4 * steps * rows_all * wide * planes * LANES, bytes_accessed=4 * steps * planes * rows_all * LANES,
            transcendentals=0,
        ),
        name="force",
    )(parcel, deal)

    plane = pltpu.VMEM((planes, spaced(rows_all), LANES), jnp.float32)
    grad, sums = pl.pallas_call(
        functools.partial(sweep, steps),
        out_shape=(f32(height, planes * LANES), f32(lons, 8 + halo, height)),
        in_specs=vmem(5),
        out_specs=tuple(vmem(2)),
        scratch_shapes=[plane] * 3 + [
            pltpu.VMEM((planes + 1, spaced(rows_all + 8), LANES), jnp.float32),
            pltpu.VMEM((planes + 1, spaced(rows_all + 8), LANES), jnp.float32),
            pltpu.VMEM((2, planes, spaced(rows_all), LANES), jnp.float32),
        ],
        compiler_params=params,
        name="sweep",
    )(deal, own, far, near, pushes)

    order = list(range(lons // 2, lons)) + list(range(lons // 2))[::-1]
    sums = exchange(sums, "lon", [order])
    own, weights = pl.pallas_call(
        functools.partial(smooth, halo, order),
        out_shape=(f32(height, width), jax.ShapeDtypeStruct((3 * lons * (8 + halo), width), jnp.bfloat16)),
        in_specs=vmem(1),
        out_specs=tuple(vmem(2)),
        scratch_shapes=[pltpu.VMEM((lons * (8 + halo), width), jnp.float32)],
        compiler_params=params,
        cost_estimate=pl.CostEstimate(
            flops=6 * 2 * height * width * width, bytes_accessed=2 * 4 * height * width, transcendentals=width * width
        ),
        name="smooth",
    )(grad)
    return pl.pallas_call(
        finish, out_shape=f32(height, width), in_specs=vmem(3), out_specs=vmem(1)[0], compiler_params=params, name="finish",
    )(own, weights, sums.reshape(lons * (8 + halo), height))


def solution(mesh):
    in_specs = (
        P(("lat", "gau"), "lon"),
        P(("scen", "lat", "gau"), "lon"),
        P(("lat", "gau"), "lon"),
        P(("lat", "gau"), "lon"),
        P(),
        P(("scen", "lon", "lat", "gau"), None),
        P(("scen", "lon", "lat", "gau")),
        P(("scen", "lon", "lat", "gau"), None, None),
        P(("scen", "lon", "lat", "gau"), None, None),
    )
    out_specs = P(("scen", "lat", "gau"), "lon")
    return jax.shard_map(local, mesh=mesh, in_specs=in_specs, out_specs=out_specs, check_vma=False)
```

```python
import functools
import math

import jax
import jax.numpy as jnp
from jax import lax
from jax.experimental import pallas as pl
from jax.experimental.pallas import tpu as pltpu
from jax.sharding import PartitionSpec as P

STEPS_BLOCK = 8
LANES = 128
SEG = 32
LEVELS = 16

courant = 0.45
depth_floor = 0.1

GRID_AXES = ("lon", "lat", "gau")
ROW_AXES = ("lat", "gau")
VMEM_LIMIT = 16 * 1024 * 1024


def roll_lanes(x, shift):
    shift = shift % LANES
    return x if shift == 0 else pltpu.roll(x, shift, 1)


def lane_iota(rows):
    return lax.broadcasted_iota(jnp.int32, (rows, LANES), 1)


def gauge_rows(owned):
    if 3 * owned <= LANES:
        return STEPS_BLOCK, owned
    assert owned <= LANES
    return 3 * STEPS_BLOCK, 0


def my_place():
    row = lax.axis_index("lat") * lax.axis_size("gau") + lax.axis_index("gau")
    return row, lax.axis_index("lon"), lax.axis_size("lat") * lax.axis_size("gau"), lax.axis_size("lon")


def give_west(reach, keep_ref, gain_ref, west_ref):
    height = keep_ref.shape[0]
    lower = lane_iota(height) < reach
    west_ref[:height] = jnp.where(lower, keep_ref[:, :LANES], roll_lanes(gain_ref[:, :LANES], reach))
    west_ref[height:] = jnp.zeros((west_ref.shape[0] - height, LANES), jnp.float32)


def give_rows(halo, keep_ref, gain_ref, right_ref, far_ref, near_ref):
    height, width = keep_ref.shape
    lower = lane_iota(halo) < 2 * halo
    odd = my_place()[0] & 1
    for goal, south in ((far_ref, odd), (near_ref, 1 - odd)):
        rows = pl.ds(pl.multiple_of(south * (height - halo), halo), halo)
        for kind, source in enumerate((keep_ref, gain_ref)):
            goal[kind, :, :width] = source[rows, :]
            goal[kind, :, width:] = jnp.where(lower, roll_lanes(right_ref[rows, :], -2 * halo * kind), 0.0)


def give_gauges(height, width, blocks, samples, coast_count, gauge_ref, after_ref, parcel_ref, block_ref):
    row_tiles = lax.axis_size("lat") * lax.axis_size("gau")
    owned = gauge_ref.shape[2]
    assert blocks == 2
    route, cell, coast = (gauge_ref[2 * blocks, i : i + 1, :].astype(jnp.int32) for i in range(3))
    target = jnp.zeros_like(route)
    for entry in range(coast_count):
        target = jnp.where(route == entry, jnp.broadcast_to(coast[:, entry : entry + 1], route.shape), target)
    row_bits, width_bits = int(math.log2(row_tiles)), int(math.log2(width))
    assert row_tiles == 1 << row_bits and width == 1 << width_bits
    grid_row = (target & (row_tiles - 1)) * height + (cell >> width_bits)
    grid_col = (target >> row_bits) * width + (cell & (width - 1))
    block_ref[...] = jnp.zeros_like(block_ref)
    levels = lax.broadcasted_iota(jnp.int32, (STEPS_BLOCK, owned), 0).astype(jnp.float32)
    for block in range(blocks):
        series = jnp.zeros((STEPS_BLOCK, owned), jnp.float32)
        for sample in range(samples):
            times = gauge_ref[block, sample : sample + 1, :]
            resid = gauge_ref[blocks + block, sample : sample + 1, :]
            series = series + jnp.where(times == levels, resid, 0.0)
        block_ref[block * STEPS_BLOCK : (block + 1) * STEPS_BLOCK, :owned] = series
    at = blocks * STEPS_BLOCK
    block_ref[at : at + 1, :owned] = grid_row.astype(jnp.float32)
    block_ref[at + 1 : at + 2, :owned] = grid_col.astype(jnp.float32)
    size, apart = gauge_rows(owned)
    gauges = block_ref[...]
    if size == STEPS_BLOCK:
        gauges = sum(
            roll_lanes(gauges[i * STEPS_BLOCK : (i + 1) * STEPS_BLOCK], i * apart) for i in range(3)
        )
    tiles = parcel_ref.shape[0]

    def put(tile, carry):
        parcel_ref[tile, 0:size, :] = gauges
        return carry

    lax.fori_loop(0, tiles, put, 0, unroll=tiles <= 16)


def halves(value):
    high = value.astype(jnp.bfloat16)
    return high, (value - high.astype(jnp.float32)).astype(jnp.bfloat16)


def dealt_column(place, planes):
    return (place & (LANES - 1)) * planes + place // LANES


def force(steps, halo, height, width, parcel_ref, after_ref, force_ref, series_ref, rows_hot, cols_hot):
    planes, rows_all = force_ref.shape[1], height + 2 * halo
    my_row, my_lon, row_tiles, lons = my_place()
    wide = rows_hot.shape[1]
    tiles, parcel_rows = parcel_ref.shape[:2]
    size = parcel_rows
    apart = wide // tiles if size == STEPS_BLOCK else 0
    owned = apart if apart else LANES
    group = wide // owned
    groups = tiles // group
    per_plane = LANES // owned
    blocks = rows_all // 8
    row_shift = (halo - my_row * height).astype(jnp.float32)
    col_shift = (-my_lon * width).astype(jnp.float32)
    place = lax.broadcasted_iota(jnp.int32, (rows_all, LANES), 0)
    at = ((place & 7) * blocks + (place >> 3)).astype(jnp.float32)

    def gather_gauges(index):
        lanes = lane_iota(STEPS_BLOCK)
        for part in range(wide // LANES):
            cols = slice(part * LANES, (part + 1) * LANES)
            fields = []
            for field in range(3):
                total = jnp.zeros((STEPS_BLOCK, LANES), jnp.float32)
                rows = slice(0, 8) if apart else slice(8 * field, 8 * field + 8)
                for i in range(per_plane):
                    source = index * group + part * per_plane + i
                    block = roll_lanes(parcel_ref[source, rows, :], i * owned - field * apart)
                    total = jnp.where((lanes >= i * owned) & (lanes < (i + 1) * owned), block, total)
                fields.append(total)
            series_ref[0:8, cols] = fields[0]
            series_ref[8:16, cols] = fields[1]
            row = fields[2][0:1] + row_shift
            col = fields[2][1:2] + col_shift
            col = jnp.where(col < width + 2 * halo, col, -1.0)
            rows_hot[:, cols] = (at == row).astype(jnp.float32).astype(jnp.bfloat16)
            by_gauge = jnp.transpose(jnp.broadcast_to(col, (LANES, LANES)))
            for c in range(planes):
                spot = (lane_iota(LANES) * planes + c).astype(jnp.float32)
                hot = (by_gauge == spot).astype(jnp.float32).astype(jnp.bfloat16)
                cols_hot[part * LANES : (part + 1) * LANES, c * LANES : (c + 1) * LANES] = hot
                cols_hot[wide + part * LANES : wide + (part + 1) * LANES, c * LANES : (c + 1) * LANES] = hot

    def levels_of(start, add):
        hot = rows_hot[...]
        both = []
        for level in range(LEVELS):
            value = series_ref[pl.ds(start + level, 1), :]
            high, low = halves(value)
            both.append(jnp.concatenate([hot * high, hot * low], axis=1))
        both = jnp.concatenate(both, axis=0)
        for first in range(0, planes, 2):
            count = min(2, planes - first)
            total = jnp.dot(
                both, cols_hot[:, first * LANES : (first + count) * LANES], preferred_element_type=jnp.float32
            )
            for level in range(LEVELS):
                for c in range(count):
                    part = total[level * rows_all : (level + 1) * rows_all, c * LANES : (c + 1) * LANES]
                    goal = (start + level, first + c, slice(0, rows_all))
                    force_ref[goal] = force_ref[goal] + part if add else part

    def levels(add):
        def one(index, carry):
            levels_of(index * LEVELS, add)
            return carry

        if steps == LEVELS:
            levels_of(0, add)
        else:
            lax.fori_loop(0, steps // LEVELS, one, 0)

    force_ref[steps] = jnp.zeros_like(force_ref[steps])
    gather_gauges(0)
    levels(False)
    if groups > 1:

        def more(index, carry):
            gather_gauges(index)
            levels(True)
            return carry

        lax.fori_loop(1, groups, more, 0)


def deal_own(reach, keep_ref, gain_ref, right_ref, after_ref, deal_ref, own_ref, weights_ref):
    height, width = keep_ref.shape
    planes = own_ref.shape[1]
    columns = planes * LANES
    parts = []
    for kind, source in enumerate((keep_ref, gain_ref)):
        beside = jnp.where(lane_iota(height) < reach, roll_lanes(right_ref[:height], -reach * kind), 0.0)
        parts += halves(jnp.concatenate([source[...], beside], axis=1))
    parts = jnp.concatenate(parts, axis=0)
    shape = (columns, LANES)
    ahead = lax.broadcasted_iota(jnp.int32, shape, 0) - lax.broadcasted_iota(jnp.int32, shape, 1) * planes
    for first in range(0, planes, 2):
        pair = range(first, min(first + 2, planes))
        deal = jnp.concatenate([(ahead == c).astype(jnp.float32).astype(jnp.bfloat16) for c in pair], axis=1)
        deal_ref[:, first * LANES : (first + len(pair)) * LANES] = deal
        dealt = jnp.dot(parts, deal, preferred_element_type=jnp.float32)
        for i, c in enumerate(pair):
            piece = dealt[:, i * LANES : (i + 1) * LANES]
            for kind in range(2):
                at = 2 * kind * height
                own_ref[kind, c] = piece[at : at + height] + piece[at + height : at + 2 * height]

    halo = reach // 2
    length = 2.0 * width
    shape = (16 + halo, planes * LANES)
    kind = lax.broadcasted_iota(jnp.int32, shape, 0)
    column = dealt_column(lax.broadcasted_iota(jnp.int32, shape, 1), planes)
    beyond = column - width
    off = jnp.where(kind == 0, column, jnp.where(kind == 1, -1 - beyond, jnp.where(kind == 2, beyond, width - 1 - beyond)))
    mine = ((kind < 2) & (beyond < 0)) | ((kind >= 2) & (kind < 4) & (beyond >= 0))
    weights = jnp.where(mine, jnp.exp(-jnp.maximum(off, 0).astype(jnp.float32) / length), 0.0)
    weights = jnp.where((kind >= 8) & (beyond == kind - 8), 1.0, weights)
    high, low = halves(weights)
    weights_ref[...] = jnp.concatenate([high, high, low], axis=1)


def sweep(
    steps, deal_ref, own_ref, weights_ref, far_ref, near_ref, force_ref,
    grad_ref, sums_ref,
    a, fx, fy, keeps, gains, plain,
):
    planes, height = own_ref.shape[1:3]
    width = (planes - 1) * LANES
    halo = 2 * steps
    rows_all = height + 2 * halo
    blocks = rows_all // 8
    my_row, my_lon, row_tiles, lons = my_place()
    has_top, has_bottom = my_row > 0, my_row < row_tiles - 1
    has_right = my_lon < lons - 1
    odd = (jnp.zeros((halo, planes * LANES), jnp.int32) + (my_row & 1)) == 1
    lanes8 = lane_iota(8)

    def up(value):
        return pltpu.roll(value, 7, 0)

    def down(value):
        return pltpu.roll(value, 1, 0)

    every = range(planes)
    columns = planes * LANES

    parts = []
    for kind in range(2):
        far, near = far_ref[kind], near_ref[kind]
        parts += halves(jnp.concatenate([jnp.where(odd, near, far), jnp.where(odd, far, near)], axis=0))
    parts = jnp.concatenate(parts, axis=0)
    for first in range(0, planes, 2):
        pair = range(first, min(first + 2, planes))
        dealt = jnp.dot(
            parts, deal_ref[:, first * LANES : (first + len(pair)) * LANES], preferred_element_type=jnp.float32
        )
        for i, c in enumerate(pair):
            piece = dealt[:, i * LANES : (i + 1) * LANES]
            for kind in range(2):
                at = 4 * kind * halo
                value = piece[at : at + 2 * halo] + piece[at + 2 * halo : at + 4 * halo]
                plain[kind, c, 0:halo, :] = value[:halo]
                plain[kind, c, halo : halo + height, :] = own_ref[kind, c]
                plain[kind, c, halo + height : rows_all, :] = value[halo:]
    for kind, goal in enumerate((keeps, gains)):
        for q in range(blocks):
            for c in every:
                value = plain[kind, c, pl.ds(q, 8, stride=blocks), :]
                goal[c, 8 * q : 8 * q + 8, :] = value
                if q == 0:
                    goal[c, 8 * blocks : 8 * blocks + 8, :] = up(value)
                if c == 0:
                    goal[planes, 8 * q : 8 * q + 8, :] = roll_lanes(value, -1)

    def cell_mask(column, there):
        lane, plane = column // planes, column % planes
        return plane, jnp.where(lanes8 == lane, there, 1.0)

    column_mask = dict([cell_mask(width, jnp.where(has_right, 1.0, 0.0)), cell_mask(columns - 1, 0.0)])
    assert len(column_mask) == 2
    sublane = lax.broadcasted_iota(jnp.int32, (8, LANES), 0)
    row_mask = {}
    for row, there in ((halo - 1, has_top), (halo + height, has_bottom)):
        row_mask[row % blocks] = jnp.where(sublane == row // blocks, jnp.where(there, 1.0, 0.0), 1.0)

    def step(index, carry, opening=False):
        level = jnp.where(index < steps - 1, steps - 2 - index, steps)
        near, ahead, new_y, beside, total, behind = {}, {}, {}, {}, {}, {}

        def rows(q):
            return slice(8 * q, 8 * q + 8)

        def first(q):
            source = force_ref.at[steps - 1] if opening else a
            near[q] = [source[c, rows(q % blocks), :] for c in every]
            if q < blocks:
                ahead[q] = near[q][2:] + [roll_lanes(value, -1) for value in near[q][:2]]
            else:
                near[q] = [up(value) for value in near[q]]

        def coefficients(q):
            return [[ref[c, rows(q), :] for c in range(planes + 1)] for ref in (keeps, gains)]

        def second_y(q):
            beside[q + 1] = keep, gain = coefficients(q + 1)
            new_y[q] = [gain[c] * (near[q + 2][c] - near[q][c]) for c in every]
            if not opening:
                new_y[q] = [new_y[q][c] + keep[c] * fy[c, rows(q), :] for c in every]
            for c in every:
                fy[c, rows(q), :] = new_y[q][c]

        def second_x(q):
            keep, gain = beside[q]
            new_x = [gain[c + 1] * (ahead[q][c] - near[q][c]) for c in every]
            if not opening:
                new_x = [new_x[c] + keep[c + 1] * fx[c, rows(q), :] for c in every]
            behind[q] = [roll_lanes(value, 1) for value in new_x[-2:]] + new_x[:-2]
            before = new_y[q - 2] if q >= 2 else [down(fy[c, rows(q - 2 + blocks), :]) for c in every]
            push = [force_ref[level, c, rows(q), :] for c in every]
            total[q] = [(near[q][c] + push[c]) + (new_y[q][c] - before[c]) + new_x[c] for c in every]
            for c in every:
                fx[c, rows(q), :] = new_x[c]

        def third(q):
            for c in every:
                value = total[q][c] - behind[q][c]
                if c in column_mask:
                    value = value * column_mask[c]
                if q in row_mask:
                    value = value * row_mask[q]
                a[c, rows(q), :] = value

        for q in range(4):
            first(q)
        second_y(0)
        second_y(1)
        for q in range(2, blocks):
            first(q + 2)
            second_y(q)
            second_x(q)
            if q > 2:
                third(q - 1)
        for q in range(2):
            first(q)
            new_y[q] = [fy[c, rows(q), :] for c in every]
            beside[q] = coefficients(q)
        for q in range(2):
            second_x(q)
            third(q - 1 if q else blocks - 1)
        third(1)
        return carry

    step(0, 0, opening=True)
    lax.fori_loop(1, steps, step, 0)

    start = jnp.where(my_lon > 0, halo, 0)
    for c in every:
        column = lanes8 * planes + c
        known = (column >= start) & (column < width + halo)
        for r in range(0, height, 8):
            s, q = divmod(halo + r, blocks)
            strided = pl.ds(8 * q + s, 8, stride=8)
            value = jnp.where(known & (keeps[c, strided, :] > 0.0), a[c, strided, :], 0.0)
            grad_ref[r : r + 8, c * LANES : (c + 1) * LANES] = value
    high, low = halves(grad_ref[...])
    sums = lax.dot_general(
        weights_ref[...], jnp.concatenate([high, low, high], axis=1), (((1,), (1,)), ((), ())),
        preferred_element_type=jnp.float32,
    )[: 8 + halo]
    for i in range(sums_ref.shape[0]):
        sums_ref[i] = sums


def smooth(halo, order, grad_ref, out_ref, weights_ref, exact_ref):
    width = out_ref.shape[1]
    length = 2.0 * width
    planes = grad_ref.shape[1] // LANES
    column = lax.broadcasted_iota(jnp.int32, (LANES, width), 1)
    lane = lax.broadcasted_iota(jnp.int32, (LANES, width), 0)
    sources = [lane * planes + c for c in range(planes)]
    kernel = jnp.concatenate(
        [jnp.where(x < width, jnp.exp(-jnp.abs(x - column).astype(jnp.float32) / length), 0.0) for x in sources], axis=0
    )
    out_ref[...] = jnp.dot(
        grad_ref[...], kernel, precision=lax.Precision.HIGHEST, preferred_element_type=jnp.float32
    )
    me = lax.axis_index("lon")
    shape = (8 + halo, width)
    kind, column = lax.broadcasted_iota(jnp.int32, shape, 0), lax.broadcasted_iota(jnp.int32, shape, 1)
    for place, source in enumerate(order):
        strip = jnp.where(kind < 2, source, source + 1)
        left = ((kind == 0) | (kind == 2)) & (strip > me)
        right = ((kind == 1) | (kind == 3)) & (strip < me)
        near = (kind >= 8) & (source + 1 == me)
        away = jnp.where(left, (strip - me) * width - column, (me - strip - 1) * width + column + 1)
        away = jnp.where(near, jnp.abs(kind - 8 - column), away)
        weights = jnp.where(left | right | near, jnp.exp(-jnp.maximum(away, 0).astype(jnp.float32) / length), 0.0)
        exact_ref[place * shape[0] : (place + 1) * shape[0], :] = weights
    high, low = halves(exact_ref[...])
    count = high.shape[0]
    for place, part in enumerate((high, high, low)):
        weights_ref[place * count : (place + 1) * count, :] = part


def finish(own_ref, weights_ref, sums_ref, out_ref):
    high, low = halves(sums_ref[...])
    out_ref[...] = own_ref[...] + lax.dot_general(
        jnp.concatenate([high, low, high], axis=0), weights_ref[...], (((0,), (0,)), ((), ())),
        preferred_element_type=jnp.float32,
    )


def f32(*shape):
    return jax.ShapeDtypeStruct(shape, jnp.float32)


def hint(megabytes):
    return pl.CostEstimate(flops=0, bytes_accessed=megabytes * 1000 * 1000, transcendentals=0)


def spaced(rows):
    return 8 * (rows // 8 | 1)


def vmem(count):
    return [pl.BlockSpec(memory_space=pltpu.VMEM)] * count


def local(depth, surface, friction, wet, coastal_tiles, gauge_route, gauge_cell, gauge_times, gauge_resid):
    height, width = depth.shape
    owned = gauge_route.shape[0]
    blocks = gauge_resid.shape[1]
    steps = blocks * STEPS_BLOCK
    halo = 2 * steps
    assert halo == SEG and height == LANES
    tiles = lax.axis_size(GRID_AXES)
    lons = lax.axis_size("lon")
    row_tiles = lax.axis_size(ROW_AXES)
    planes = width // LANES + 1
    rows_all = height + 2 * halo
    params = pltpu.CompilerParams(vmem_limit_bytes=VMEM_LIMIT)

    keep = (1.0 - friction) * wet.astype(jnp.float32)
    gain = ((courant * 0.5) ** 2 * jnp.maximum(depth + surface, depth_floor)) * keep
    samples, coast_count = gauge_resid.shape[2], coastal_tiles.shape[0]
    assert coast_count <= owned

    assert samples >= 3

    def put(array, group, row):
        groups, rows, lanes = array.shape
        return jnp.pad(array, ((group, 2 * blocks + 1 - group - groups), (row, samples - row - rows), (0, owned - lanes)))

    gauges = (
        put(jnp.transpose(gauge_times, (1, 2, 0)), 0, 0)
        + put(gauge_route.reshape(1, 1, owned), 2 * blocks, 0)
        + put(gauge_cell.reshape(1, 1, owned), 2 * blocks, 1)
        + put(coastal_tiles.reshape(1, 1, coast_count), 2 * blocks, 2)
    ).astype(jnp.float32) + put(jnp.transpose(gauge_resid, (1, 2, 0)), blocks, 0)
    west = pl.pallas_call(
        functools.partial(give_west, 2 * halo), out_shape=f32(2 * height, LANES), in_specs=vmem(2), out_specs=vmem(1)[0],
        compiler_params=params, name="give_west",
    )(keep, gain)
    right = lax.ppermute(west, "lon", [(i + 1, i) for i in range(lons - 1)])

    parcel = pl.pallas_call(
        functools.partial(give_gauges, height, width, blocks, samples, coast_count),
        out_shape=f32(tiles, gauge_rows(owned)[0], LANES),
        in_specs=vmem(1) + [pl.BlockSpec(memory_space=pl.ANY)],
        out_specs=vmem(1)[0],
        scratch_shapes=[pltpu.VMEM((24, LANES), jnp.float32)],
        compiler_params=params,
        cost_estimate=hint(10),
        name="give_gauges",
    )(gauges, west)

    def exchange(array, axes, groups=None):
        return lax.all_to_all(array, axes, split_axis=0, concat_axis=0, axis_index_groups=groups, tiled=True)

    rank = {row_tiles - 1: 1, 0: 2}
    group = sorted(range(tiles), key=lambda tile: (rank.get(tile % row_tiles, 0), -(tile // row_tiles)))
    parcel = exchange(parcel, GRID_AXES, [group])

    to_far, to_near = pl.pallas_call(
        functools.partial(give_rows, halo), out_shape=(f32(2, halo, planes * LANES),) * 2, in_specs=vmem(3),
        out_specs=tuple(vmem(2)), compiler_params=params, cost_estimate=hint(40), name="give_rows",
    )(keep, gain, right)
    far = lax.ppermute(to_far, ROW_AXES, [pair for i in range(1, row_tiles - 1, 2) for pair in ((i, i + 1), (i + 1, i))])
    near = lax.ppermute(to_near, ROW_AXES, [pair for i in range(0, row_tiles, 2) for pair in ((i, i + 1), (i + 1, i))])

    deal, own, weights = pl.pallas_call(
        functools.partial(deal_own, 2 * halo),
        out_shape=(
            jax.ShapeDtypeStruct((planes * LANES, planes * LANES), jnp.bfloat16), f32(2, planes, height, LANES),
            jax.ShapeDtypeStruct((16 + halo, 3 * planes * LANES), jnp.bfloat16),
        ),
        in_specs=vmem(3) + [pl.BlockSpec(memory_space=pl.ANY)],
        out_specs=tuple(vmem(3)),
        compiler_params=params,
        cost_estimate=hint(4),
        name="deal_own",
    )(keep, gain, right, to_far)

    wide = max(2 * LANES, owned)
    pushes = pl.pallas_call(
        functools.partial(force, steps, halo, height, width),
        out_shape=f32(steps + 1, planes, spaced(rows_all), LANES),
        in_specs=vmem(1) + [pl.BlockSpec(memory_space=pl.ANY)],
        out_specs=vmem(1)[0],
        scratch_shapes=[
            pltpu.VMEM((steps, wide), jnp.float32),
            pltpu.VMEM((rows_all, wide), jnp.bfloat16),
            pltpu.VMEM((2 * wide, planes * LANES), jnp.bfloat16),
        ],
        compiler_params=params,
        cost_estimate=pl.CostEstimate(
            flops=4 * steps * rows_all * wide * planes * LANES, bytes_accessed=4 * steps * planes * rows_all * LANES,
            transcendentals=0,
        ),
        name="force",
    )(parcel, deal)

    plane = pltpu.VMEM((planes, spaced(rows_all), LANES), jnp.float32)
    grad, sums = pl.pallas_call(
        functools.partial(sweep, steps),
        out_shape=(f32(height, planes * LANES), f32(lons, 8 + halo, height)),
        in_specs=vmem(6),
        out_specs=tuple(vmem(2)),
        scratch_shapes=[plane] * 3 + [
            pltpu.VMEM((planes + 1, spaced(rows_all + 8), LANES), jnp.float32),
            pltpu.VMEM((planes + 1, spaced(rows_all + 8), LANES), jnp.float32),
            pltpu.VMEM((2, planes, spaced(rows_all), LANES), jnp.float32),
        ],
        compiler_params=params,
        name="sweep",
    )(deal, own, weights, far, near, pushes)

    order = list(range(lons // 2, lons)) + list(range(lons // 2))[::-1]
    sums = exchange(sums, "lon", [order])
    own, weights = pl.pallas_call(
        functools.partial(smooth, halo, order),
        out_shape=(f32(height, width), jax.ShapeDtypeStruct((3 * lons * (8 + halo), width), jnp.bfloat16)),
        in_specs=vmem(1),
        out_specs=tuple(vmem(2)),
        scratch_shapes=[pltpu.VMEM((lons * (8 + halo), width), jnp.float32)],
        compiler_params=params,
        cost_estimate=pl.CostEstimate(
            flops=6 * 2 * height * width * width, bytes_accessed=2 * 4 * height * width, transcendentals=width * width
        ),
        name="smooth",
    )(grad)
    return pl.pallas_call(
        finish, out_shape=f32(height, width), in_specs=vmem(3), out_specs=vmem(1)[0], compiler_params=params, name="finish",
    )(own, weights, sums.reshape(lons * (8 + halo), height))


def solution(mesh):
    in_specs = (
        P(("lat", "gau"), "lon"),
        P(("scen", "lat", "gau"), "lon"),
        P(("lat", "gau"), "lon"),
        P(("lat", "gau"), "lon"),
        P(),
        P(("scen", "lon", "lat", "gau"), None),
        P(("scen", "lon", "lat", "gau")),
        P(("scen", "lon", "lat", "gau"), None, None),
        P(("scen", "lon", "lat", "gau"), None, None),
    )
    out_specs = P(("scen", "lat", "gau"), "lon")
    return jax.shard_map(local, mesh=mesh, in_specs=in_specs, out_specs=out_specs, check_vma=False)
```

```python
import functools
import math

import jax
import jax.numpy as jnp
from jax import lax
from jax.experimental import pallas as pl
from jax.experimental.pallas import tpu as pltpu
from jax.sharding import PartitionSpec as P

STEPS_BLOCK = 8
LANES = 128
SEG = 32
LEVELS = 16

courant = 0.45
depth_floor = 0.1

GRID_AXES = ("lon", "lat", "gau")
ROW_AXES = ("lat", "gau")
VMEM_LIMIT = 16 * 1024 * 1024


def roll_lanes(x, shift):
    shift = shift % LANES
    return x if shift == 0 else pltpu.roll(x, shift, 1)


def lane_iota(rows):
    return lax.broadcasted_iota(jnp.int32, (rows, LANES), 1)


def gauge_rows(owned):
    if 3 * owned <= LANES:
        return STEPS_BLOCK, owned
    assert owned <= LANES
    return 3 * STEPS_BLOCK, 0


def my_place():
    row = lax.axis_index("lat") * lax.axis_size("gau") + lax.axis_index("gau")
    return row, lax.axis_index("lon"), lax.axis_size("lat") * lax.axis_size("gau"), lax.axis_size("lon")


def give_west(reach, keep_ref, gain_ref, west_ref):
    height = keep_ref.shape[0]
    lower = lane_iota(height) < reach
    west_ref[:height] = jnp.where(lower, keep_ref[:, :LANES], roll_lanes(gain_ref[:, :LANES], reach))
    west_ref[height:] = jnp.zeros((west_ref.shape[0] - height, LANES), jnp.float32)


def give_rows(halo, keep_ref, gain_ref, right_ref, far_ref, near_ref):
    height, width = keep_ref.shape
    lower = lane_iota(halo) < 2 * halo
    odd = my_place()[0] & 1
    for goal, south in ((far_ref, odd), (near_ref, 1 - odd)):
        rows = pl.ds(pl.multiple_of(south * (height - halo), halo), halo)
        for kind, source in enumerate((keep_ref, gain_ref)):
            goal[kind, :, :width] = source[rows, :]
            goal[kind, :, width:] = jnp.where(lower, roll_lanes(right_ref[rows, :], -2 * halo * kind), 0.0)


def give_gauges(height, width, blocks, samples, coast_count, gauge_ref, after_ref, parcel_ref, block_ref):
    row_tiles = lax.axis_size("lat") * lax.axis_size("gau")
    owned = gauge_ref.shape[2]
    assert blocks == 2
    route, cell, coast = (gauge_ref[2 * blocks, i : i + 1, :].astype(jnp.int32) for i in range(3))
    target = jnp.zeros_like(route)
    for entry in range(coast_count):
        target = jnp.where(route == entry, jnp.broadcast_to(coast[:, entry : entry + 1], route.shape), target)
    row_bits, width_bits = int(math.log2(row_tiles)), int(math.log2(width))
    assert row_tiles == 1 << row_bits and width == 1 << width_bits
    grid_row = (target & (row_tiles - 1)) * height + (cell >> width_bits)
    grid_col = (target >> row_bits) * width + (cell & (width - 1))
    block_ref[...] = jnp.zeros_like(block_ref)
    levels = lax.broadcasted_iota(jnp.int32, (STEPS_BLOCK, owned), 0).astype(jnp.float32)
    for block in range(blocks):
        series = jnp.zeros((STEPS_BLOCK, owned), jnp.float32)
        for sample in range(samples):
            times = gauge_ref[block, sample : sample + 1, :]
            resid = gauge_ref[blocks + block, sample : sample + 1, :]
            series = series + jnp.where(times == levels, resid, 0.0)
        block_ref[block * STEPS_BLOCK : (block + 1) * STEPS_BLOCK, :owned] = series
    at = blocks * STEPS_BLOCK
    block_ref[at : at + 1, :owned] = grid_row.astype(jnp.float32)
    block_ref[at + 1 : at + 2, :owned] = grid_col.astype(jnp.float32)
    size, apart = gauge_rows(owned)
    gauges = block_ref[...]
    if size == STEPS_BLOCK:
        gauges = sum(
            roll_lanes(gauges[i * STEPS_BLOCK : (i + 1) * STEPS_BLOCK], i * apart) for i in range(3)
        )
    tiles = parcel_ref.shape[0]

    def put(tile, carry):
        parcel_ref[tile, 0:size, :] = gauges
        return carry

    lax.fori_loop(0, tiles, put, 0, unroll=tiles <= 16)


def halves(value):
    high = value.astype(jnp.bfloat16)
    return high, (value - high.astype(jnp.float32)).astype(jnp.bfloat16)


def dealt_column(place, planes):
    return (place & (LANES - 1)) * planes + place // LANES


def force(steps, halo, height, width, parcel_ref, after_ref, force_ref, series_ref, rows_hot, cols_hot):
    planes, rows_all = force_ref.shape[1], height + 2 * halo
    my_row, my_lon, row_tiles, lons = my_place()
    wide = rows_hot.shape[1]
    tiles, parcel_rows = parcel_ref.shape[:2]
    size = parcel_rows
    apart = wide // tiles if size == STEPS_BLOCK else 0
    owned = apart if apart else LANES
    group = wide // owned
    groups = tiles // group
    per_plane = LANES // owned
    blocks = rows_all // 8
    row_shift = (halo - my_row * height).astype(jnp.float32)
    col_shift = (-my_lon * width).astype(jnp.float32)
    place = lax.broadcasted_iota(jnp.int32, (rows_all, LANES), 0)
    at = ((place & 7) * blocks + (place >> 3)).astype(jnp.float32)

    def gather_gauges(index):
        lanes = lane_iota(STEPS_BLOCK)
        for part in range(wide // LANES):
            cols = slice(part * LANES, (part + 1) * LANES)
            fields = []
            for field in range(3):
                total = jnp.zeros((STEPS_BLOCK, LANES), jnp.float32)
                rows = slice(0, 8) if apart else slice(8 * field, 8 * field + 8)
                for i in range(per_plane):
                    source = index * group + part * per_plane + i
                    block = roll_lanes(parcel_ref[source, rows, :], i * owned - field * apart)
                    total = jnp.where((lanes >= i * owned) & (lanes < (i + 1) * owned), block, total)
                fields.append(total)
            series_ref[0:8, cols] = fields[0]
            series_ref[8:16, cols] = fields[1]
            row = fields[2][0:1] + row_shift
            col = fields[2][1:2] + col_shift
            col = jnp.where(col < width + 2 * halo, col, -1.0)
            rows_hot[:, cols] = (at == row).astype(jnp.float32).astype(jnp.bfloat16)
            by_gauge = jnp.transpose(jnp.broadcast_to(col, (LANES, LANES)))
            for c in range(planes):
                spot = (lane_iota(LANES) * planes + c).astype(jnp.float32)
                hot = (by_gauge == spot).astype(jnp.float32).astype(jnp.bfloat16)
                cols_hot[part * LANES : (part + 1) * LANES, c * LANES : (c + 1) * LANES] = hot
                cols_hot[wide + part * LANES : wide + (part + 1) * LANES, c * LANES : (c + 1) * LANES] = hot

    def levels_of(start, add):
        hot = rows_hot[...]
        both = []
        for level in range(LEVELS):
            value = series_ref[pl.ds(start + level, 1), :]
            high, low = halves(value)
            both.append(jnp.concatenate([hot * high, hot * low], axis=1))
        both = jnp.concatenate(both, axis=0)
        for first in range(0, planes, 2):
            count = min(2, planes - first)
            total = jnp.dot(
                both, cols_hot[:, first * LANES : (first + count) * LANES], preferred_element_type=jnp.float32
            )
            for level in range(LEVELS):
                for c in range(count):
                    part = total[level * rows_all : (level + 1) * rows_all, c * LANES : (c + 1) * LANES]
                    goal = (start + level, first + c, slice(0, rows_all))
                    force_ref[goal] = force_ref[goal] + part if add else part

    def levels(add):
        def one(index, carry):
            levels_of(index * LEVELS, add)
            return carry

        if steps == LEVELS:
            levels_of(0, add)
        else:
            lax.fori_loop(0, steps // LEVELS, one, 0)

    force_ref[steps] = jnp.zeros_like(force_ref[steps])
    gather_gauges(0)
    levels(False)
    if groups > 1:

        def more(index, carry):
            gather_gauges(index)
            levels(True)
            return carry

        lax.fori_loop(1, groups, more, 0)


def deal_own(reach, keep_ref, gain_ref, right_ref, after_ref, deal_ref, own_ref, weights_ref):
    height, width = keep_ref.shape
    planes = own_ref.shape[1]
    columns = planes * LANES
    parts = []
    for kind, source in enumerate((keep_ref, gain_ref)):
        beside = jnp.where(lane_iota(height) < reach, roll_lanes(right_ref[:height], -reach * kind), 0.0)
        parts += halves(jnp.concatenate([source[...], beside], axis=1))
    parts = jnp.concatenate(parts, axis=0)
    shape = (columns, LANES)
    ahead = lax.broadcasted_iota(jnp.int32, shape, 0) - lax.broadcasted_iota(jnp.int32, shape, 1) * planes
    for first in range(0, planes, 2):
        pair = range(first, min(first + 2, planes))
        deal = jnp.concatenate([(ahead == c).astype(jnp.float32).astype(jnp.bfloat16) for c in pair], axis=1)
        deal_ref[:, first * LANES : (first + len(pair)) * LANES] = deal
        dealt = jnp.dot(parts, deal, preferred_element_type=jnp.float32)
        for i, c in enumerate(pair):
            piece = dealt[:, i * LANES : (i + 1) * LANES]
            for kind in range(2):
                at = 2 * kind * height
                own_ref[kind, c] = piece[at : at + height] + piece[at + height : at + 2 * height]

    halo = reach // 2
    length = 2.0 * width
    shape = (planes * LANES, LANES)
    kind = lax.broadcasted_iota(jnp.int32, shape, 1)
    column = dealt_column(lax.broadcasted_iota(jnp.int32, shape, 0), planes)
    beyond = column - width
    off = jnp.where(kind == 0, column, jnp.where(kind == 1, -1 - beyond, jnp.where(kind == 2, beyond, width - 1 - beyond)))
    mine = ((kind < 2) & (beyond < 0)) | ((kind >= 2) & (kind < 4) & (beyond >= 0))
    weights = jnp.where(mine, jnp.exp(-jnp.maximum(off, 0).astype(jnp.float32) / length), 0.0)
    weights = jnp.where((kind >= 8) & (beyond == kind - 8), 1.0, weights)
    high, low = halves(weights)
    weights_ref[...] = jnp.concatenate([high, high, low], axis=0)


def sweep(
    steps, deal_ref, own_ref, weights_ref, far_ref, near_ref, force_ref,
    grad_ref, sums_ref,
    a, fx, fy, keeps, gains, plain,
):
    planes, height = own_ref.shape[1:3]
    width = (planes - 1) * LANES
    halo = 2 * steps
    rows_all = height + 2 * halo
    blocks = rows_all // 8
    my_row, my_lon, row_tiles, lons = my_place()
    has_top, has_bottom = my_row > 0, my_row < row_tiles - 1
    has_right = my_lon < lons - 1
    odd = (jnp.zeros((halo, planes * LANES), jnp.int32) + (my_row & 1)) == 1
    lanes8 = lane_iota(8)

    def up(value):
        return pltpu.roll(value, 7, 0)

    def down(value):
        return pltpu.roll(value, 1, 0)

    every = range(planes)
    columns = planes * LANES

    parts = []
    for kind in range(2):
        far, near = far_ref[kind], near_ref[kind]
        parts += halves(jnp.concatenate([jnp.where(odd, near, far), jnp.where(odd, far, near)], axis=0))
    parts = jnp.concatenate(parts, axis=0)
    for first in range(0, planes, 2):
        pair = range(first, min(first + 2, planes))
        dealt = jnp.dot(
            parts, deal_ref[:, first * LANES : (first + len(pair)) * LANES], preferred_element_type=jnp.float32
        )
        for i, c in enumerate(pair):
            piece = dealt[:, i * LANES : (i + 1) * LANES]
            for kind in range(2):
                at = 4 * kind * halo
                value = piece[at : at + 2 * halo] + piece[at + 2 * halo : at + 4 * halo]
                plain[kind, c, 0:halo, :] = value[:halo]
                plain[kind, c, halo : halo + height, :] = own_ref[kind, c]
                plain[kind, c, halo + height : rows_all, :] = value[halo:]
    for kind, goal in enumerate((keeps, gains)):
        for q in range(blocks):
            for c in every:
                value = plain[kind, c, pl.ds(q, 8, stride=blocks), :]
                goal[c, 8 * q : 8 * q + 8, :] = value
                if q == 0:
                    goal[c, 8 * blocks : 8 * blocks + 8, :] = up(value)
                if c == 0:
                    goal[planes, 8 * q : 8 * q + 8, :] = roll_lanes(value, -1)

    def cell_mask(column, there):
        lane, plane = column // planes, column % planes
        return plane, jnp.where(lanes8 == lane, there, 1.0)

    column_mask = dict([cell_mask(width, jnp.where(has_right, 1.0, 0.0)), cell_mask(columns - 1, 0.0)])
    assert len(column_mask) == 2
    sublane = lax.broadcasted_iota(jnp.int32, (8, LANES), 0)
    row_mask = {}
    for row, there in ((halo - 1, has_top), (halo + height, has_bottom)):
        row_mask[row % blocks] = jnp.where(sublane == row // blocks, jnp.where(there, 1.0, 0.0), 1.0)

    def step(index, carry, opening=False):
        level = jnp.where(index < steps - 1, steps - 2 - index, steps)
        near, ahead, new_y, beside, total, behind = {}, {}, {}, {}, {}, {}

        def rows(q):
            return slice(8 * q, 8 * q + 8)

        def first(q):
            source = force_ref.at[steps - 1] if opening else a
            near[q] = [source[c, rows(q % blocks), :] for c in every]
            if q < blocks:
                ahead[q] = near[q][2:] + [roll_lanes(value, -1) for value in near[q][:2]]
            else:
                near[q] = [up(value) for value in near[q]]

        def coefficients(q):
            return [[ref[c, rows(q), :] for c in range(planes + 1)] for ref in (keeps, gains)]

        def second_y(q):
            beside[q + 1] = keep, gain = coefficients(q + 1)
            new_y[q] = [gain[c] * (near[q + 2][c] - near[q][c]) for c in every]
            if not opening:
                new_y[q] = [new_y[q][c] + keep[c] * fy[c, rows(q), :] for c in every]
            for c in every:
                fy[c, rows(q), :] = new_y[q][c]

        def second_x(q):
            keep, gain = beside[q]
            new_x = [gain[c + 1] * (ahead[q][c] - near[q][c]) for c in every]
            if not opening:
                new_x = [new_x[c] + keep[c + 1] * fx[c, rows(q), :] for c in every]
            behind[q] = [roll_lanes(value, 1) for value in new_x[-2:]] + new_x[:-2]
            before = new_y[q - 2] if q >= 2 else [down(fy[c, rows(q - 2 + blocks), :]) for c in every]
            push = [force_ref[level, c, rows(q), :] for c in every]
            total[q] = [(near[q][c] + push[c]) + (new_y[q][c] - before[c]) + new_x[c] for c in every]
            for c in every:
                fx[c, rows(q), :] = new_x[c]

        def third(q):
            for c in every:
                value = total[q][c] - behind[q][c]
                if c in column_mask:
                    value = value * column_mask[c]
                if q in row_mask:
                    value = value * row_mask[q]
                a[c, rows(q), :] = value

        for q in range(4):
            first(q)
        second_y(0)
        second_y(1)
        for q in range(2, blocks):
            first(q + 2)
            second_y(q)
            second_x(q)
            if q > 2:
                third(q - 1)
        for q in range(2):
            first(q)
            new_y[q] = [fy[c, rows(q), :] for c in every]
            beside[q] = coefficients(q)
        for q in range(2):
            second_x(q)
            third(q - 1 if q else blocks - 1)
        third(1)
        return carry

    step(0, 0, opening=True)
    lax.fori_loop(1, steps, step, 0)

    start = jnp.where(my_lon > 0, halo, 0)
    for c in every:
        column = lanes8 * planes + c
        known = (column >= start) & (column < width + halo)
        for r in range(0, height, 8):
            s, q = divmod(halo + r, blocks)
            strided = pl.ds(8 * q + s, 8, stride=8)
            value = jnp.where(known & (keeps[c, strided, :] > 0.0), a[c, strided, :], 0.0)
            grad_ref[r : r + 8, c * LANES : (c + 1) * LANES] = value
    high, low = halves(grad_ref[...])
    sums = jnp.dot(
        jnp.concatenate([high, low, high], axis=1), weights_ref[...], preferred_element_type=jnp.float32
    )
    sums = jnp.transpose(sums)[: 8 + halo]
    for i in range(sums_ref.shape[0]):
        sums_ref[i] = sums


def smooth(halo, order, grad_ref, out_ref, weights_ref, exact_ref):
    width = out_ref.shape[1]
    length = 2.0 * width
    planes = grad_ref.shape[1] // LANES
    column = lax.broadcasted_iota(jnp.int32, (LANES, width), 1)
    lane = lax.broadcasted_iota(jnp.int32, (LANES, width), 0)
    sources = [lane * planes + c for c in range(planes)]
    kernel = jnp.concatenate(
        [jnp.where(x < width, jnp.exp(-jnp.abs(x - column).astype(jnp.float32) / length), 0.0) for x in sources], axis=0
    )
    out_ref[...] = jnp.dot(
        grad_ref[...], kernel, precision=lax.Precision.HIGHEST, preferred_element_type=jnp.float32
    )
    me = lax.axis_index("lon")
    shape = (8 + halo, width)
    kind, column = lax.broadcasted_iota(jnp.int32, shape, 0), lax.broadcasted_iota(jnp.int32, shape, 1)
    for place, source in enumerate(order):
        strip = jnp.where(kind < 2, source, source + 1)
        left = ((kind == 0) | (kind == 2)) & (strip > me)
        right = ((kind == 1) | (kind == 3)) & (strip < me)
        near = (kind >= 8) & (source + 1 == me)
        away = jnp.where(left, (strip - me) * width - column, (me - strip - 1) * width + column + 1)
        away = jnp.where(near, jnp.abs(kind - 8 - column), away)
        weights = jnp.where(left | right | near, jnp.exp(-jnp.maximum(away, 0).astype(jnp.float32) / length), 0.0)
        exact_ref[place * shape[0] : (place + 1) * shape[0], :] = weights
    high, low = halves(exact_ref[...])
    count = high.shape[0]
    for place, part in enumerate((high, high, low)):
        weights_ref[place * count : (place + 1) * count, :] = part


def finish(own_ref, weights_ref, sums_ref, out_ref):
    high, low = halves(sums_ref[...])
    out_ref[...] = own_ref[...] + lax.dot_general(
        jnp.concatenate([high, low, high], axis=0), weights_ref[...], (((0,), (0,)), ((), ())),
        preferred_element_type=jnp.float32,
    )


def f32(*shape):
    return jax.ShapeDtypeStruct(shape, jnp.float32)


def hint(megabytes):
    return pl.CostEstimate(flops=0, bytes_accessed=megabytes * 1000 * 1000, transcendentals=0)


def spaced(rows):
    return 8 * (rows // 8 | 1)


def vmem(count):
    return [pl.BlockSpec(memory_space=pltpu.VMEM)] * count


def local(depth, surface, friction, wet, coastal_tiles, gauge_route, gauge_cell, gauge_times, gauge_resid):
    height, width = depth.shape
    owned = gauge_route.shape[0]
    blocks = gauge_resid.shape[1]
    steps = blocks * STEPS_BLOCK
    halo = 2 * steps
    assert halo == SEG and height == LANES
    tiles = lax.axis_size(GRID_AXES)
    lons = lax.axis_size("lon")
    row_tiles = lax.axis_size(ROW_AXES)
    planes = width // LANES + 1
    rows_all = height + 2 * halo
    params = pltpu.CompilerParams(vmem_limit_bytes=VMEM_LIMIT)

    keep = (1.0 - friction) * wet.astype(jnp.float32)
    gain = ((courant * 0.5) ** 2 * jnp.maximum(depth + surface, depth_floor)) * keep
    samples, coast_count = gauge_resid.shape[2], coastal_tiles.shape[0]
    assert coast_count <= owned

    assert samples >= 3

    def put(array, group, row):
        groups, rows, lanes = array.shape
        return jnp.pad(array, ((group, 2 * blocks + 1 - group - groups), (row, samples - row - rows), (0, owned - lanes)))

    gauges = (
        put(jnp.transpose(gauge_times, (1, 2, 0)), 0, 0)
        + put(gauge_route.reshape(1, 1, owned), 2 * blocks, 0)
        + put(gauge_cell.reshape(1, 1, owned), 2 * blocks, 1)
        + put(coastal_tiles.reshape(1, 1, coast_count), 2 * blocks, 2)
    ).astype(jnp.float32) + put(jnp.transpose(gauge_resid, (1, 2, 0)), blocks, 0)
    west = pl.pallas_call(
        functools.partial(give_west, 2 * halo), out_shape=f32(2 * height, LANES), in_specs=vmem(2), out_specs=vmem(1)[0],
        compiler_params=params, name="give_west",
    )(keep, gain)
    right = lax.ppermute(west, "lon", [(i + 1, i) for i in range(lons - 1)])

    parcel = pl.pallas_call(
        functools.partial(give_gauges, height, width, blocks, samples, coast_count),
        out_shape=f32(tiles, gauge_rows(owned)[0], LANES),
        in_specs=vmem(1) + [pl.BlockSpec(memory_space=pl.ANY)],
        out_specs=vmem(1)[0],
        scratch_shapes=[pltpu.VMEM((24, LANES), jnp.float32)],
        compiler_params=params,
        cost_estimate=hint(10),
        name="give_gauges",
    )(gauges, west)

    def exchange(array, axes, groups=None):
        return lax.all_to_all(array, axes, split_axis=0, concat_axis=0, axis_index_groups=groups, tiled=True)

    rank = {row_tiles - 1: 1, 0: 2}
    group = sorted(range(tiles), key=lambda tile: (rank.get(tile % row_tiles, 0), -(tile // row_tiles)))
    parcel = exchange(parcel, GRID_AXES, [group])

    to_far, to_near = pl.pallas_call(
        functools.partial(give_rows, halo), out_shape=(f32(2, halo, planes * LANES),) * 2, in_specs=vmem(3),
        out_specs=tuple(vmem(2)), compiler_params=params, cost_estimate=hint(40), name="give_rows",
    )(keep, gain, right)
    far = lax.ppermute(to_far, ROW_AXES, [pair for i in range(1, row_tiles - 1, 2) for pair in ((i, i + 1), (i + 1, i))])
    near = lax.ppermute(to_near, ROW_AXES, [pair for i in range(0, row_tiles, 2) for pair in ((i, i + 1), (i + 1, i))])

    deal, own, weights = pl.pallas_call(
        functools.partial(deal_own, 2 * halo),
        out_shape=(
            jax.ShapeDtypeStruct((planes * LANES, planes * LANES), jnp.bfloat16), f32(2, planes, height, LANES),
            jax.ShapeDtypeStruct((3 * planes * LANES, LANES), jnp.bfloat16),
        ),
        in_specs=vmem(3) + [pl.BlockSpec(memory_space=pl.ANY)],
        out_specs=tuple(vmem(3)),
        compiler_params=params,
        cost_estimate=hint(4),
        name="deal_own",
    )(keep, gain, right, to_far)

    wide = max(2 * LANES, owned)
    pushes = pl.pallas_call(
        functools.partial(force, steps, halo, height, width),
        out_shape=f32(steps + 1, planes, spaced(rows_all), LANES),
        in_specs=vmem(1) + [pl.BlockSpec(memory_space=pl.ANY)],
        out_specs=vmem(1)[0],
        scratch_shapes=[
            pltpu.VMEM((steps, wide), jnp.float32),
            pltpu.VMEM((rows_all, wide), jnp.bfloat16),
            pltpu.VMEM((2 * wide, planes * LANES), jnp.bfloat16),
        ],
        compiler_params=params,
        cost_estimate=pl.CostEstimate(
            flops=4 * steps * rows_all * wide * planes * LANES, bytes_accessed=4 * steps * planes * rows_all * LANES,
            transcendentals=0,
        ),
        name="force",
    )(parcel, deal)

    plane = pltpu.VMEM((planes, spaced(rows_all), LANES), jnp.float32)
    grad, sums = pl.pallas_call(
        functools.partial(sweep, steps),
        out_shape=(f32(height, planes * LANES), f32(lons, 8 + halo, height)),
        in_specs=vmem(6),
        out_specs=tuple(vmem(2)),
        scratch_shapes=[plane] * 3 + [
            pltpu.VMEM((planes + 1, spaced(rows_all + 8), LANES), jnp.float32),
            pltpu.VMEM((planes + 1, spaced(rows_all + 8), LANES), jnp.float32),
            pltpu.VMEM((2, planes, spaced(rows_all), LANES), jnp.float32),
        ],
        compiler_params=params,
        name="sweep",
    )(deal, own, weights, far, near, pushes)

    order = list(range(lons // 2, lons)) + list(range(lons // 2))[::-1]
    sums = exchange(sums, "lon", [order])
    own, weights = pl.pallas_call(
        functools.partial(smooth, halo, order),
        out_shape=(f32(height, width), jax.ShapeDtypeStruct((3 * lons * (8 + halo), width), jnp.bfloat16)),
        in_specs=vmem(1),
        out_specs=tuple(vmem(2)),
        scratch_shapes=[pltpu.VMEM((lons * (8 + halo), width), jnp.float32)],
        compiler_params=params,
        cost_estimate=pl.CostEstimate(
            flops=6 * 2 * height * width * width, bytes_accessed=2 * 4 * height * width, transcendentals=width * width
        ),
        name="smooth",
    )(grad)
    return pl.pallas_call(
        finish, out_shape=f32(height, width), in_specs=vmem(3), out_specs=vmem(1)[0], compiler_params=params, name="finish",
    )(own, weights, sums.reshape(lons * (8 + halo), height))


def solution(mesh):
    in_specs = (
        P(("lat", "gau"), "lon"),
        P(("scen", "lat", "gau"), "lon"),
        P(("lat", "gau"), "lon"),
        P(("lat", "gau"), "lon"),
        P(),
        P(("scen", "lon", "lat", "gau"), None),
        P(("scen", "lon", "lat", "gau")),
        P(("scen", "lon", "lat", "gau"), None, None),
        P(("scen", "lon", "lat", "gau"), None, None),
    )
    out_specs = P(("scen", "lat", "gau"), "lon")
    return jax.shard_map(local, mesh=mesh, in_specs=in_specs, out_specs=out_specs, check_vma=False)
```

```python
import functools
import math

import jax
import jax.numpy as jnp
from jax import lax
from jax.experimental import pallas as pl
from jax.experimental.pallas import tpu as pltpu
from jax.sharding import PartitionSpec as P

STEPS_BLOCK = 8
LANES = 128
SEG = 32
LEVELS = 16

courant = 0.45
depth_floor = 0.1

GRID_AXES = ("lon", "lat", "gau")
ROW_AXES = ("lat", "gau")
VMEM_LIMIT = 16 * 1024 * 1024


def roll_lanes(x, shift):
    shift = shift % LANES
    return x if shift == 0 else pltpu.roll(x, shift, 1)


def lane_iota(rows):
    return lax.broadcasted_iota(jnp.int32, (rows, LANES), 1)


def gauge_rows(owned):
    if 3 * owned <= LANES:
        return STEPS_BLOCK, owned
    assert owned <= LANES
    return 3 * STEPS_BLOCK, 0


def my_place():
    row = lax.axis_index("lat") * lax.axis_size("gau") + lax.axis_index("gau")
    return row, lax.axis_index("lon"), lax.axis_size("lat") * lax.axis_size("gau"), lax.axis_size("lon")


def give_west(reach, keep_ref, gain_ref, west_ref):
    height = keep_ref.shape[0]
    lower = lane_iota(height) < reach
    west_ref[:height] = jnp.where(lower, keep_ref[:, :LANES], roll_lanes(gain_ref[:, :LANES], reach))
    west_ref[height:] = jnp.zeros((west_ref.shape[0] - height, LANES), jnp.float32)


def give_rows(halo, keep_ref, gain_ref, right_ref, far_ref, near_ref):
    height, width = keep_ref.shape
    lower = lane_iota(halo) < 2 * halo
    odd = my_place()[0] & 1
    for goal, south in ((far_ref, odd), (near_ref, 1 - odd)):
        rows = pl.ds(pl.multiple_of(south * (height - halo), halo), halo)
        for kind, source in enumerate((keep_ref, gain_ref)):
            goal[kind, :, :width] = source[rows, :]
            goal[kind, :, width:] = jnp.where(lower, roll_lanes(right_ref[rows, :], -2 * halo * kind), 0.0)


def give_gauges(height, width, blocks, samples, coast_count, gauge_ref, after_ref, parcel_ref, block_ref):
    row_tiles = lax.axis_size("lat") * lax.axis_size("gau")
    owned = gauge_ref.shape[2]
    assert blocks == 2
    route, cell, coast = (gauge_ref[2 * blocks, i : i + 1, :].astype(jnp.int32) for i in range(3))
    target = jnp.zeros_like(route)
    for entry in range(coast_count):
        target = jnp.where(route == entry, jnp.broadcast_to(coast[:, entry : entry + 1], route.shape), target)
    row_bits, width_bits = int(math.log2(row_tiles)), int(math.log2(width))
    assert row_tiles == 1 << row_bits and width == 1 << width_bits
    grid_row = (target & (row_tiles - 1)) * height + (cell >> width_bits)
    grid_col = (target >> row_bits) * width + (cell & (width - 1))
    block_ref[...] = jnp.zeros_like(block_ref)
    levels = lax.broadcasted_iota(jnp.int32, (STEPS_BLOCK, owned), 0).astype(jnp.float32)
    for block in range(blocks):
        series = jnp.zeros((STEPS_BLOCK, owned), jnp.float32)
        for sample in range(samples):
            times = gauge_ref[block, sample : sample + 1, :]
            resid = gauge_ref[blocks + block, sample : sample + 1, :]
            series = series + jnp.where(times == levels, resid, 0.0)
        block_ref[block * STEPS_BLOCK : (block + 1) * STEPS_BLOCK, :owned] = series
    at = blocks * STEPS_BLOCK
    block_ref[at : at + 1, :owned] = grid_row.astype(jnp.float32)
    block_ref[at + 1 : at + 2, :owned] = grid_col.astype(jnp.float32)
    size, apart = gauge_rows(owned)
    gauges = block_ref[...]
    if size == STEPS_BLOCK:
        gauges = sum(
            roll_lanes(gauges[i * STEPS_BLOCK : (i + 1) * STEPS_BLOCK], i * apart) for i in range(3)
        )
    tiles = parcel_ref.shape[0]

    def put(tile, carry):
        parcel_ref[tile, 0:size, :] = gauges
        return carry

    lax.fori_loop(0, tiles, put, 0, unroll=tiles <= 16)


def halves(value):
    high = value.astype(jnp.bfloat16)
    return high, (value - high.astype(jnp.float32)).astype(jnp.bfloat16)


def dealt_column(place, planes):
    return (place & (LANES - 1)) * planes + place // LANES


def force(steps, halo, height, width, parcel_ref, after_ref, force_ref, series_ref, rows_hot, cols_hot):
    planes, rows_all = force_ref.shape[1], height + 2 * halo
    my_row, my_lon, row_tiles, lons = my_place()
    wide = rows_hot.shape[1]
    tiles, parcel_rows = parcel_ref.shape[:2]
    size = parcel_rows
    apart = wide // tiles if size == STEPS_BLOCK else 0
    owned = apart if apart else LANES
    group = wide // owned
    groups = tiles // group
    per_plane = LANES // owned
    blocks = rows_all // 8
    row_shift = (halo - my_row * height).astype(jnp.float32)
    col_shift = (-my_lon * width).astype(jnp.float32)
    place = lax.broadcasted_iota(jnp.int32, (rows_all, LANES), 0)
    at = ((place & 7) * blocks + (place >> 3)).astype(jnp.float32)

    def gather_gauges(index):
        lanes = lane_iota(STEPS_BLOCK)
        for part in range(wide // LANES):
            cols = slice(part * LANES, (part + 1) * LANES)
            fields = []
            for field in range(3):
                total = jnp.zeros((STEPS_BLOCK, LANES), jnp.float32)
                rows = slice(0, 8) if apart else slice(8 * field, 8 * field + 8)
                for i in range(per_plane):
                    source = index * group + part * per_plane + i
                    block = roll_lanes(parcel_ref[source, rows, :], i * owned - field * apart)
                    total = jnp.where((lanes >= i * owned) & (lanes < (i + 1) * owned), block, total)
                fields.append(total)
            series_ref[0:8, cols] = fields[0]
            series_ref[8:16, cols] = fields[1]
            row = fields[2][0:1] + row_shift
            col = fields[2][1:2] + col_shift
            col = jnp.where(col < width + 2 * halo, col, -1.0)
            rows_hot[:, cols] = (at == row).astype(jnp.float32).astype(jnp.bfloat16)
            by_gauge = jnp.transpose(jnp.broadcast_to(col, (LANES, LANES)))
            for c in range(planes):
                spot = (lane_iota(LANES) * planes + c).astype(jnp.float32)
                hot = (by_gauge == spot).astype(jnp.float32).astype(jnp.bfloat16)
                cols_hot[part * LANES : (part + 1) * LANES, c * LANES : (c + 1) * LANES] = hot
                cols_hot[wide + part * LANES : wide + (part + 1) * LANES, c * LANES : (c + 1) * LANES] = hot

    def levels_of(start, add):
        hot = rows_hot[...]
        both = []
        for level in range(LEVELS):
            value = series_ref[pl.ds(start + level, 1), :]
            high, low = halves(value)
            both.append(jnp.concatenate([hot * high, hot * low], axis=1))
        both = jnp.concatenate(both, axis=0)
        for first in range(0, planes, 2):
            count = min(2, planes - first)
            total = jnp.dot(
                both, cols_hot[:, first * LANES : (first + count) * LANES], preferred_element_type=jnp.float32
            )
            for level in range(LEVELS):
                for c in range(count):
                    part = total[level * rows_all : (level + 1) * rows_all, c * LANES : (c + 1) * LANES]
                    goal = (start + level, first + c, slice(0, rows_all))
                    force_ref[goal] = force_ref[goal] + part if add else part

    def levels(add):
        def one(index, carry):
            levels_of(index * LEVELS, add)
            return carry

        if steps == LEVELS:
            levels_of(0, add)
        else:
            lax.fori_loop(0, steps // LEVELS, one, 0)

    force_ref[steps] = jnp.zeros_like(force_ref[steps])
    gather_gauges(0)
    levels(False)
    if groups > 1:

        def more(index, carry):
            gather_gauges(index)
            levels(True)
            return carry

        lax.fori_loop(1, groups, more, 0)


def deal_own(reach, keep_ref, gain_ref, right_ref, after_ref, deal_ref, own_ref, weights_ref):
    height, width = keep_ref.shape
    planes = own_ref.shape[1]
    columns = planes * LANES
    parts = []
    for kind, source in enumerate((keep_ref, gain_ref)):
        beside = jnp.where(lane_iota(height) < reach, roll_lanes(right_ref[:height], -reach * kind), 0.0)
        parts += halves(jnp.concatenate([source[...], beside], axis=1))
    parts = jnp.concatenate(parts, axis=0)
    shape = (columns, LANES)
    ahead = lax.broadcasted_iota(jnp.int32, shape, 0) - lax.broadcasted_iota(jnp.int32, shape, 1) * planes
    for first in range(0, planes, 2):
        pair = range(first, min(first + 2, planes))
        deal = jnp.concatenate([(ahead == c).astype(jnp.float32).astype(jnp.bfloat16) for c in pair], axis=1)
        deal_ref[:, first * LANES : (first + len(pair)) * LANES] = deal
        dealt = jnp.dot(parts, deal, preferred_element_type=jnp.float32)
        for i, c in enumerate(pair):
            piece = dealt[:, i * LANES : (i + 1) * LANES]
            for kind in range(2):
                at = 2 * kind * height
                own_ref[kind, c] = piece[at : at + height] + piece[at + height : at + 2 * height]

    halo = reach // 2
    length = 2.0 * width
    shape = (planes * LANES, LANES)
    kind = lax.broadcasted_iota(jnp.int32, shape, 1)
    column = dealt_column(lax.broadcasted_iota(jnp.int32, shape, 0), planes)
    beyond = column - width
    off = jnp.where(kind == 0, column, jnp.where(kind == 1, -1 - beyond, jnp.where(kind == 2, beyond, width - 1 - beyond)))
    mine = ((kind < 2) & (beyond < 0)) | ((kind >= 2) & (kind < 4) & (beyond >= 0))
    weights = jnp.where(mine, jnp.exp(-jnp.maximum(off, 0).astype(jnp.float32) / length), 0.0)
    weights = jnp.where((kind >= 8) & (beyond == kind - 8), 1.0, weights)
    high, low = halves(weights)
    weights_ref[...] = jnp.concatenate([high, high, low], axis=0)


def sweep(
    steps, deal_ref, own_ref, weights_ref, far_ref, near_ref, force_ref,
    grad_ref, sums_ref,
    a, fx, fy, keeps, gains, plain,
):
    planes, height = own_ref.shape[1:3]
    width = (planes - 1) * LANES
    halo = 2 * steps
    rows_all = height + 2 * halo
    blocks = rows_all // 8
    my_row, my_lon, row_tiles, lons = my_place()
    has_top, has_bottom = my_row > 0, my_row < row_tiles - 1
    has_right = my_lon < lons - 1
    odd = (jnp.zeros((halo, planes * LANES), jnp.int32) + (my_row & 1)) == 1
    lanes8 = lane_iota(8)

    def up(value):
        return pltpu.roll(value, 7, 0)

    def down(value):
        return pltpu.roll(value, 1, 0)

    every = range(planes)
    columns = planes * LANES

    parts = []
    for kind in range(2):
        far, near = far_ref[kind], near_ref[kind]
        parts += halves(jnp.concatenate([jnp.where(odd, near, far), jnp.where(odd, far, near)], axis=0))
    parts = jnp.concatenate(parts, axis=0)
    for first in range(0, planes, 2):
        pair = range(first, min(first + 2, planes))
        dealt = jnp.dot(
            parts, deal_ref[:, first * LANES : (first + len(pair)) * LANES], preferred_element_type=jnp.float32
        )
        for i, c in enumerate(pair):
            piece = dealt[:, i * LANES : (i + 1) * LANES]
            for kind in range(2):
                at = 4 * kind * halo
                value = piece[at : at + 2 * halo] + piece[at + 2 * halo : at + 4 * halo]
                plain[kind, c, 0:halo, :] = value[:halo]
                plain[kind, c, halo : halo + height, :] = own_ref[kind, c]
                plain[kind, c, halo + height : rows_all, :] = value[halo:]
    for kind, goal in enumerate((keeps, gains)):
        for q in range(blocks):
            for c in every:
                value = plain[kind, c, pl.ds(q, 8, stride=blocks), :]
                goal[c, 8 * q : 8 * q + 8, :] = value
                if q == 0:
                    goal[c, 8 * blocks : 8 * blocks + 8, :] = up(value)
                if c == 0:
                    goal[planes, 8 * q : 8 * q + 8, :] = roll_lanes(value, -1)

    def cell_mask(column, there):
        lane, plane = column // planes, column % planes
        return plane, jnp.where(lanes8 == lane, there, 1.0)

    column_mask = dict([cell_mask(width, jnp.where(has_right, 1.0, 0.0)), cell_mask(columns - 1, 0.0)])
    assert len(column_mask) == 2
    sublane = lax.broadcasted_iota(jnp.int32, (8, LANES), 0)
    row_mask = {}
    for row, there in ((halo - 1, has_top), (halo + height, has_bottom)):
        row_mask[row % blocks] = jnp.where(sublane == row // blocks, jnp.where(there, 1.0, 0.0), 1.0)

    def step(index, carry, opening=False):
        level = jnp.where(index < steps - 1, steps - 2 - index, steps)
        near, ahead, new_y, beside, total, behind = {}, {}, {}, {}, {}, {}

        def rows(q):
            return slice(8 * q, 8 * q + 8)

        def first(q):
            source = force_ref.at[steps - 1] if opening else a
            near[q] = [source[c, rows(q % blocks), :] for c in every]
            if q < blocks:
                ahead[q] = near[q][2:] + [roll_lanes(value, -1) for value in near[q][:2]]
            else:
                near[q] = [up(value) for value in near[q]]

        def coefficients(q):
            return [[ref[c, rows(q), :] for c in range(planes + 1)] for ref in (keeps, gains)]

        def second_y(q):
            beside[q + 1] = keep, gain = coefficients(q + 1)
            new_y[q] = [gain[c] * (near[q + 2][c] - near[q][c]) for c in every]
            if not opening:
                new_y[q] = [new_y[q][c] + keep[c] * fy[c, rows(q), :] for c in every]
            for c in every:
                fy[c, rows(q), :] = new_y[q][c]

        def second_x(q):
            keep, gain = beside[q]
            new_x = [gain[c + 1] * (ahead[q][c] - near[q][c]) for c in every]
            if not opening:
                new_x = [new_x[c] + keep[c + 1] * fx[c, rows(q), :] for c in every]
            behind[q] = [roll_lanes(value, 1) for value in new_x[-2:]] + new_x[:-2]
            before = new_y[q - 2] if q >= 2 else [down(fy[c, rows(q - 2 + blocks), :]) for c in every]
            push = [force_ref[level, c, rows(q), :] for c in every]
            total[q] = [(near[q][c] + push[c]) + (new_y[q][c] - before[c]) + new_x[c] for c in every]
            for c in every:
                fx[c, rows(q), :] = new_x[c]

        def third(q):
            for c in every:
                value = total[q][c] - behind[q][c]
                if c in column_mask:
                    value = value * column_mask[c]
                if q in row_mask:
                    value = value * row_mask[q]
                a[c, rows(q), :] = value

        for q in range(4):
            first(q)
        second_y(0)
        second_y(1)
        for q in range(2, blocks):
            first(q + 2)
            second_y(q)
            second_x(q)
            if q > 2:
                third(q - 1)
        for q in range(2):
            first(q)
            new_y[q] = [fy[c, rows(q), :] for c in every]
            beside[q] = coefficients(q)
        for q in range(2):
            second_x(q)
            third(q - 1 if q else blocks - 1)
        third(1)
        return carry

    step(0, 0, opening=True)
    lax.fori_loop(1, steps, step, 0)

    start = jnp.where(my_lon > 0, halo, 0)
    for c in every:
        column = lanes8 * planes + c
        known = (column >= start) & (column < width + halo)
        for r in range(0, height, 8):
            s, q = divmod(halo + r, blocks)
            strided = pl.ds(8 * q + s, 8, stride=8)
            value = jnp.where(known & (keeps[c, strided, :] > 0.0), a[c, strided, :], 0.0)
            grad_ref[r : r + 8, c * LANES : (c + 1) * LANES] = value
    high, low = halves(grad_ref[...])
    sums = jnp.dot(
        jnp.concatenate([high, low, high], axis=1), weights_ref[...], preferred_element_type=jnp.float32
    )
    sums = jnp.transpose(sums)[: 8 + halo]
    for i in range(sums_ref.shape[0]):
        sums_ref[i] = sums


def smooth(halo, order, grad_ref, out_ref, weights_ref, exact_ref):
    width = out_ref.shape[1]
    length = 2.0 * width
    planes = grad_ref.shape[1] // LANES
    column = lax.broadcasted_iota(jnp.int32, (LANES, width), 1)
    lane = lax.broadcasted_iota(jnp.int32, (LANES, width), 0)
    sources = [lane * planes + c for c in range(planes)]
    kernel = jnp.concatenate(
        [jnp.where(x < width, jnp.exp(-jnp.abs(x - column).astype(jnp.float32) / length), 0.0) for x in sources], axis=0
    )
    out_ref[...] = jnp.dot(
        grad_ref[...], kernel, precision=lax.Precision.HIGHEST, preferred_element_type=jnp.float32
    )
    me = lax.axis_index("lon")
    shape = (8 + halo, width)
    kind, column = lax.broadcasted_iota(jnp.int32, shape, 0), lax.broadcasted_iota(jnp.int32, shape, 1)
    for place, source in enumerate(order):
        strip = jnp.where(kind < 2, source, source + 1)
        left = ((kind == 0) | (kind == 2)) & (strip > me)
        right = ((kind == 1) | (kind == 3)) & (strip < me)
        near = (kind >= 8) & (source + 1 == me)
        away = jnp.where(left, (strip - me) * width - column, (me - strip - 1) * width + column + 1)
        away = jnp.where(near, jnp.abs(kind - 8 - column), away)
        weights = jnp.where(left | right | near, jnp.exp(-jnp.maximum(away, 0).astype(jnp.float32) / length), 0.0)
        exact_ref[place * shape[0] : (place + 1) * shape[0], :] = weights
    high, low = halves(exact_ref[...])
    count = high.shape[0]
    for place, part in enumerate((high, high, low)):
        weights_ref[place * count : (place + 1) * count, :] = part


def finish(own_ref, weights_ref, sums_ref, out_ref):
    high, low = halves(sums_ref[...])
    out_ref[...] = own_ref[...] + lax.dot_general(
        jnp.concatenate([high, low, high], axis=0), weights_ref[...], (((0,), (0,)), ((), ())),
        preferred_element_type=jnp.float32,
    )


def f32(*shape):
    return jax.ShapeDtypeStruct(shape, jnp.float32)


def hint(megabytes):
    return pl.CostEstimate(flops=0, bytes_accessed=megabytes * 1000 * 1000, transcendentals=0)


def spaced(rows):
    return 8 * (rows // 8 | 1)


def vmem(count):
    return [pl.BlockSpec(memory_space=pltpu.VMEM)] * count


def local(depth, surface, friction, wet, coastal_tiles, gauge_route, gauge_cell, gauge_times, gauge_resid):
    height, width = depth.shape
    owned = gauge_route.shape[0]
    blocks = gauge_resid.shape[1]
    steps = blocks * STEPS_BLOCK
    halo = 2 * steps
    assert halo == SEG and height == LANES
    tiles = lax.axis_size(GRID_AXES)
    lons = lax.axis_size("lon")
    row_tiles = lax.axis_size(ROW_AXES)
    planes = width // LANES + 1
    rows_all = height + 2 * halo
    params = pltpu.CompilerParams(vmem_limit_bytes=VMEM_LIMIT)

    keep = (1.0 - friction) * wet.astype(jnp.float32)
    gain = ((courant * 0.5) ** 2 * jnp.maximum(depth + surface, depth_floor)) * keep
    samples, coast_count = gauge_resid.shape[2], coastal_tiles.shape[0]
    assert coast_count <= owned

    assert samples >= 3

    def put(array, group, row):
        groups, rows, lanes = array.shape
        return jnp.pad(array, ((group, 2 * blocks + 1 - group - groups), (row, samples - row - rows), (0, owned - lanes)))

    gauges = (
        put(jnp.transpose(gauge_times, (1, 2, 0)), 0, 0)
        + put(gauge_route.reshape(1, 1, owned), 2 * blocks, 0)
        + put(gauge_cell.reshape(1, 1, owned), 2 * blocks, 1)
        + put(coastal_tiles.reshape(1, 1, coast_count), 2 * blocks, 2)
    ).astype(jnp.float32) + put(jnp.transpose(gauge_resid, (1, 2, 0)), blocks, 0)
    west = pl.pallas_call(
        functools.partial(give_west, 2 * halo), out_shape=f32(2 * height, LANES), in_specs=vmem(2), out_specs=vmem(1)[0],
        compiler_params=params, name="give_west",
    )(keep, gain)
    right = lax.ppermute(west, "lon", [(i + 1, i) for i in range(lons - 1)])

    parcel = pl.pallas_call(
        functools.partial(give_gauges, height, width, blocks, samples, coast_count),
        out_shape=f32(tiles, gauge_rows(owned)[0], LANES),
        in_specs=vmem(1) + [pl.BlockSpec(memory_space=pl.ANY)],
        out_specs=vmem(1)[0],
        scratch_shapes=[pltpu.VMEM((24, LANES), jnp.float32)],
        compiler_params=params,
        cost_estimate=hint(10),
        name="give_gauges",
    )(gauges, west)

    def exchange(array, axes, groups=None):
        return lax.all_to_all(array, axes, split_axis=0, concat_axis=0, axis_index_groups=groups, tiled=True)

    rank = {row_tiles - 1: 1, 0: 2}
    inside = list(range(lons))[::-1]
    ends = list(range(1, lons - 1))[::-1] + [lons - 1, 0]

    def place(tile):
        row, lon = tile % row_tiles, tile // row_tiles
        return rank.get(row, 0), (ends if row in rank else inside).index(lon)

    group = sorted(range(tiles), key=place)
    parcel = exchange(parcel, GRID_AXES, [group])

    to_far, to_near = pl.pallas_call(
        functools.partial(give_rows, halo), out_shape=(f32(2, halo, planes * LANES),) * 2, in_specs=vmem(3),
        out_specs=tuple(vmem(2)), compiler_params=params, cost_estimate=hint(40), name="give_rows",
    )(keep, gain, right)
    far = lax.ppermute(to_far, ROW_AXES, [pair for i in range(1, row_tiles - 1, 2) for pair in ((i, i + 1), (i + 1, i))])
    near = lax.ppermute(to_near, ROW_AXES, [pair for i in range(0, row_tiles, 2) for pair in ((i, i + 1), (i + 1, i))])

    deal, own, weights = pl.pallas_call(
        functools.partial(deal_own, 2 * halo),
        out_shape=(
            jax.ShapeDtypeStruct((planes * LANES, planes * LANES), jnp.bfloat16), f32(2, planes, height, LANES),
            jax.ShapeDtypeStruct((3 * planes * LANES, LANES), jnp.bfloat16),
        ),
        in_specs=vmem(3) + [pl.BlockSpec(memory_space=pl.ANY)],
        out_specs=tuple(vmem(3)),
        compiler_params=params,
        cost_estimate=hint(4),
        name="deal_own",
    )(keep, gain, right, to_far)

    wide = max(2 * LANES, owned)
    pushes = pl.pallas_call(
        functools.partial(force, steps, halo, height, width),
        out_shape=f32(steps + 1, planes, spaced(rows_all), LANES),
        in_specs=vmem(1) + [pl.BlockSpec(memory_space=pl.ANY)],
        out_specs=vmem(1)[0],
        scratch_shapes=[
            pltpu.VMEM((steps, wide), jnp.float32),
            pltpu.VMEM((rows_all, wide), jnp.bfloat16),
            pltpu.VMEM((2 * wide, planes * LANES), jnp.bfloat16),
        ],
        compiler_params=params,
        cost_estimate=pl.CostEstimate(
            flops=4 * steps * rows_all * wide * planes * LANES, bytes_accessed=4 * steps * planes * rows_all * LANES,
            transcendentals=0,
        ),
        name="force",
    )(parcel, deal)

    plane = pltpu.VMEM((planes, spaced(rows_all), LANES), jnp.float32)
    grad, sums = pl.pallas_call(
        functools.partial(sweep, steps),
        out_shape=(f32(height, planes * LANES), f32(lons, 8 + halo, height)),
        in_specs=vmem(6),
        out_specs=tuple(vmem(2)),
        scratch_shapes=[plane] * 3 + [
            pltpu.VMEM((planes + 1, spaced(rows_all + 8), LANES), jnp.float32),
            pltpu.VMEM((planes + 1, spaced(rows_all + 8), LANES), jnp.float32),
            pltpu.VMEM((2, planes, spaced(rows_all), LANES), jnp.float32),
        ],
        compiler_params=params,
        name="sweep",
    )(deal, own, weights, far, near, pushes)

    order = list(range(lons // 2, lons)) + list(range(lons // 2))[::-1]
    sums = exchange(sums, "lon", [order])
    own, weights = pl.pallas_call(
        functools.partial(smooth, halo, order),
        out_shape=(f32(height, width), jax.ShapeDtypeStruct((3 * lons * (8 + halo), width), jnp.bfloat16)),
        in_specs=vmem(1),
        out_specs=tuple(vmem(2)),
        scratch_shapes=[pltpu.VMEM((lons * (8 + halo), width), jnp.float32)],
        compiler_params=params,
        cost_estimate=pl.CostEstimate(
            flops=6 * 2 * height * width * width, bytes_accessed=2 * 4 * height * width, transcendentals=width * width
        ),
        name="smooth",
    )(grad)
    return pl.pallas_call(
        finish, out_shape=f32(height, width), in_specs=vmem(3), out_specs=vmem(1)[0], compiler_params=params, name="finish",
    )(own, weights, sums.reshape(lons * (8 + halo), height))


def solution(mesh):
    in_specs = (
        P(("lat", "gau"), "lon"),
        P(("scen", "lat", "gau"), "lon"),
        P(("lat", "gau"), "lon"),
        P(("lat", "gau"), "lon"),
        P(),
        P(("scen", "lon", "lat", "gau"), None),
        P(("scen", "lon", "lat", "gau")),
        P(("scen", "lon", "lat", "gau"), None, None),
        P(("scen", "lon", "lat", "gau"), None, None),
    )
    out_specs = P(("scen", "lat", "gau"), "lon")
    return jax.shard_map(local, mesh=mesh, in_specs=in_specs, out_specs=out_specs, check_vma=False)
```

```python
import functools
import math

import jax
import jax.numpy as jnp
from jax import lax
from jax.experimental import pallas as pl
from jax.experimental.pallas import tpu as pltpu
from jax.sharding import PartitionSpec as P

STEPS_BLOCK = 8
LANES = 128
SEG = 32
LEVELS = 16

courant = 0.45
depth_floor = 0.1

GRID_AXES = ("lon", "lat", "gau")
ROW_AXES = ("lat", "gau")
VMEM_LIMIT = 16 * 1024 * 1024


def roll_lanes(x, shift):
    shift = shift % LANES
    return x if shift == 0 else pltpu.roll(x, shift, 1)


def lane_iota(rows):
    return lax.broadcasted_iota(jnp.int32, (rows, LANES), 1)


def gauge_rows(owned):
    if 3 * owned <= LANES:
        return STEPS_BLOCK, owned
    assert owned <= LANES
    return 3 * STEPS_BLOCK, 0


def my_place():
    row = lax.axis_index("lat") * lax.axis_size("gau") + lax.axis_index("gau")
    return row, lax.axis_index("lon"), lax.axis_size("lat") * lax.axis_size("gau"), lax.axis_size("lon")


def give_west(reach, keep_ref, gain_ref, west_ref):
    height = keep_ref.shape[0]
    lower = lane_iota(height) < reach
    west_ref[:height] = jnp.where(lower, keep_ref[:, :LANES], roll_lanes(gain_ref[:, :LANES], reach))
    west_ref[height:] = jnp.zeros((west_ref.shape[0] - height, LANES), jnp.float32)


def give_rows(halo, keep_ref, gain_ref, right_ref, far_ref, near_ref):
    height, width = keep_ref.shape
    lower = lane_iota(halo) < 2 * halo
    odd = my_place()[0] & 1
    for goal, south in ((far_ref, odd), (near_ref, 1 - odd)):
        rows = pl.ds(pl.multiple_of(south * (height - halo), halo), halo)
        for kind, source in enumerate((keep_ref, gain_ref)):
            goal[kind, :, :width] = source[rows, :]
            goal[kind, :, width:] = jnp.where(lower, roll_lanes(right_ref[rows, :], -2 * halo * kind), 0.0)


def give_gauges(height, width, blocks, samples, coast_count, gauge_ref, after_ref, parcel_ref, block_ref):
    row_tiles = lax.axis_size("lat") * lax.axis_size("gau")
    owned = gauge_ref.shape[2]
    assert blocks == 2
    route, cell, coast = (gauge_ref[2 * blocks, i : i + 1, :].astype(jnp.int32) for i in range(3))
    target = jnp.zeros_like(route)
    for entry in range(coast_count):
        target = jnp.where(route == entry, jnp.broadcast_to(coast[:, entry : entry + 1], route.shape), target)
    row_bits, width_bits = int(math.log2(row_tiles)), int(math.log2(width))
    assert row_tiles == 1 << row_bits and width == 1 << width_bits
    grid_row = (target & (row_tiles - 1)) * height + (cell >> width_bits)
    grid_col = (target >> row_bits) * width + (cell & (width - 1))
    block_ref[...] = jnp.zeros_like(block_ref)
    levels = lax.broadcasted_iota(jnp.int32, (STEPS_BLOCK, owned), 0).astype(jnp.float32)
    for block in range(blocks):
        series = jnp.zeros((STEPS_BLOCK, owned), jnp.float32)
        for sample in range(samples):
            times = gauge_ref[block, sample : sample + 1, :]
            resid = gauge_ref[blocks + block, sample : sample + 1, :]
            series = series + jnp.where(times == levels, resid, 0.0)
        block_ref[block * STEPS_BLOCK : (block + 1) * STEPS_BLOCK, :owned] = series
    at = blocks * STEPS_BLOCK
    block_ref[at : at + 1, :owned] = grid_row.astype(jnp.float32)
    block_ref[at + 1 : at + 2, :owned] = grid_col.astype(jnp.float32)
    size, apart = gauge_rows(owned)
    gauges = block_ref[...]
    if size == STEPS_BLOCK:
        gauges = sum(
            roll_lanes(gauges[i * STEPS_BLOCK : (i + 1) * STEPS_BLOCK], i * apart) for i in range(3)
        )
    tiles = parcel_ref.shape[0]

    def put(tile, carry):
        parcel_ref[tile, 0:size, :] = gauges
        return carry

    lax.fori_loop(0, tiles, put, 0, unroll=tiles <= 16)


def halves(value):
    high = value.astype(jnp.bfloat16)
    return high, (value - high.astype(jnp.float32)).astype(jnp.bfloat16)


def dealt_column(place, planes):
    return (place & (LANES - 1)) * planes + place // LANES


def force(steps, halo, height, width, parcel_ref, after_ref, force_ref, series_ref, rows_hot, cols_hot):
    planes, rows_all = force_ref.shape[1], height + 2 * halo
    my_row, my_lon, row_tiles, lons = my_place()
    wide = rows_hot.shape[1]
    tiles, parcel_rows = parcel_ref.shape[:2]
    size = parcel_rows
    apart = wide // tiles if size == STEPS_BLOCK else 0
    owned = apart if apart else LANES
    group = wide // owned
    groups = tiles // group
    per_plane = LANES // owned
    blocks = rows_all // 8
    row_shift = (halo - my_row * height).astype(jnp.float32)
    col_shift = (-my_lon * width).astype(jnp.float32)
    place = lax.broadcasted_iota(jnp.int32, (rows_all, LANES), 0)
    at = ((place & 7) * blocks + (place >> 3)).astype(jnp.float32)

    def gather_gauges(index):
        lanes = lane_iota(STEPS_BLOCK)
        for part in range(wide // LANES):
            cols = slice(part * LANES, (part + 1) * LANES)
            fields = []
            for field in range(3):
                total = jnp.zeros((STEPS_BLOCK, LANES), jnp.float32)
                rows = slice(0, 8) if apart else slice(8 * field, 8 * field + 8)
                for i in range(per_plane):
                    source = index * group + part * per_plane + i
                    block = roll_lanes(parcel_ref[source, rows, :], i * owned - field * apart)
                    total = jnp.where((lanes >= i * owned) & (lanes < (i + 1) * owned), block, total)
                fields.append(total)
            series_ref[0:8, cols] = fields[0]
            series_ref[8:16, cols] = fields[1]
            row = fields[2][0:1] + row_shift
            col = fields[2][1:2] + col_shift
            col = jnp.where(col < width + 2 * halo, col, -1.0)
            rows_hot[:, cols] = (at == row).astype(jnp.float32).astype(jnp.bfloat16)
            by_gauge = jnp.transpose(jnp.broadcast_to(col, (LANES, LANES)))
            for c in range(planes):
                spot = (lane_iota(LANES) * planes + c).astype(jnp.float32)
                hot = (by_gauge == spot).astype(jnp.float32).astype(jnp.bfloat16)
                cols_hot[part * LANES : (part + 1) * LANES, c * LANES : (c + 1) * LANES] = hot
                cols_hot[wide + part * LANES : wide + (part + 1) * LANES, c * LANES : (c + 1) * LANES] = hot

    def levels_of(start, add):
        hot = rows_hot[...]
        both = []
        for level in range(LEVELS):
            value = series_ref[pl.ds(start + level, 1), :]
            high, low = halves(value)
            both.append(jnp.concatenate([hot * high, hot * low], axis=1))
        both = jnp.concatenate(both, axis=0)
        for first in range(0, planes, 2):
            count = min(2, planes - first)
            total = jnp.dot(
                both, cols_hot[:, first * LANES : (first + count) * LANES], preferred_element_type=jnp.float32
            )
            for level in range(LEVELS):
                for c in range(count):
                    part = total[level * rows_all : (level + 1) * rows_all, c * LANES : (c + 1) * LANES]
                    goal = (start + level, first + c, slice(0, rows_all))
                    force_ref[goal] = force_ref[goal] + part if add else part

    def levels(add):
        def one(index, carry):
            levels_of(index * LEVELS, add)
            return carry

        if steps == LEVELS:
            levels_of(0, add)
        else:
            lax.fori_loop(0, steps // LEVELS, one, 0)

    force_ref[steps] = jnp.zeros_like(force_ref[steps])
    gather_gauges(0)
    levels(False)
    if groups > 1:

        def more(index, carry):
            gather_gauges(index)
            levels(True)
            return carry

        lax.fori_loop(1, groups, more, 0)


def deal_own(reach, keep_ref, gain_ref, right_ref, after_ref, deal_ref, own_ref, weights_ref):
    height, width = keep_ref.shape
    planes = own_ref.shape[1]
    columns = planes * LANES
    parts = []
    for kind, source in enumerate((keep_ref, gain_ref)):
        beside = jnp.where(lane_iota(height) < reach, roll_lanes(right_ref[:height], -reach * kind), 0.0)
        parts += halves(jnp.concatenate([source[...], beside], axis=1))
    parts = jnp.concatenate(parts, axis=0)
    shape = (columns, LANES)
    ahead = lax.broadcasted_iota(jnp.int32, shape, 0) - lax.broadcasted_iota(jnp.int32, shape, 1) * planes
    for first in range(0, planes, 2):
        pair = range(first, min(first + 2, planes))
        deal = jnp.concatenate([(ahead == c).astype(jnp.float32).astype(jnp.bfloat16) for c in pair], axis=1)
        deal_ref[:, first * LANES : (first + len(pair)) * LANES] = deal
        dealt = jnp.dot(parts, deal, preferred_element_type=jnp.float32)
        for i, c in enumerate(pair):
            piece = dealt[:, i * LANES : (i + 1) * LANES]
            for kind in range(2):
                at = 2 * kind * height
                own_ref[kind, c] = piece[at : at + height] + piece[at + height : at + 2 * height]

    halo = reach // 2
    length = 2.0 * width
    shape = (planes * LANES, LANES)
    kind = lax.broadcasted_iota(jnp.int32, shape, 1)
    column = dealt_column(lax.broadcasted_iota(jnp.int32, shape, 0), planes)
    beyond = column - width
    off = jnp.where(kind == 0, column, jnp.where(kind == 1, -1 - beyond, jnp.where(kind == 2, beyond, width - 1 - beyond)))
    mine = ((kind < 2) & (beyond < 0)) | ((kind >= 2) & (kind < 4) & (beyond >= 0))
    weights = jnp.where(mine, jnp.exp(-jnp.maximum(off, 0).astype(jnp.float32) / length), 0.0)
    weights = jnp.where((kind >= 8) & (beyond == kind - 8), 1.0, weights)
    high, low = halves(weights)
    weights_ref[...] = jnp.concatenate([high, high, low], axis=0)


def sweep(
    steps, deal_ref, own_ref, weights_ref, far_ref, near_ref, force_ref,
    grad_ref, sums_ref,
    a, fx, fy, keeps, gains, plain,
):
    planes, height = own_ref.shape[1:3]
    width = (planes - 1) * LANES
    halo = 2 * steps
    rows_all = height + 2 * halo
    blocks = rows_all // 8
    my_row, my_lon, row_tiles, lons = my_place()
    has_top, has_bottom = my_row > 0, my_row < row_tiles - 1
    has_right = my_lon < lons - 1
    odd = (jnp.zeros((halo, planes * LANES), jnp.int32) + (my_row & 1)) == 1
    lanes8 = lane_iota(8)

    def up(value):
        return pltpu.roll(value, 7, 0)

    def down(value):
        return pltpu.roll(value, 1, 0)

    every = range(planes)
    columns = planes * LANES

    parts = []
    for kind in range(2):
        far, near = far_ref[kind], near_ref[kind]
        parts += halves(jnp.concatenate([jnp.where(odd, near, far), jnp.where(odd, far, near)], axis=0))
    parts = jnp.concatenate(parts, axis=0)
    for first in range(0, planes, 2):
        pair = range(first, min(first + 2, planes))
        dealt = jnp.dot(
            parts, deal_ref[:, first * LANES : (first + len(pair)) * LANES], preferred_element_type=jnp.float32
        )
        for i, c in enumerate(pair):
            piece = dealt[:, i * LANES : (i + 1) * LANES]
            for kind in range(2):
                at = 4 * kind * halo
                value = piece[at : at + 2 * halo] + piece[at + 2 * halo : at + 4 * halo]
                plain[kind, c, 0:halo, :] = value[:halo]
                plain[kind, c, halo : halo + height, :] = own_ref[kind, c]
                plain[kind, c, halo + height : rows_all, :] = value[halo:]
    for kind, goal in enumerate((keeps, gains)):
        for q in range(blocks):
            for c in every:
                value = plain[kind, c, pl.ds(q, 8, stride=blocks), :]
                goal[c, 8 * q : 8 * q + 8, :] = value
                if q == 0:
                    goal[c, 8 * blocks : 8 * blocks + 8, :] = up(value)
                if c == 0:
                    goal[planes, 8 * q : 8 * q + 8, :] = roll_lanes(value, -1)

    def cell_mask(column, there):
        lane, plane = column // planes, column % planes
        return plane, jnp.where(lanes8 == lane, there, 1.0)

    column_mask = dict([cell_mask(width, jnp.where(has_right, 1.0, 0.0)), cell_mask(columns - 1, 0.0)])
    assert len(column_mask) == 2
    sublane = lax.broadcasted_iota(jnp.int32, (8, LANES), 0)
    row_mask = {}
    for row, there in ((halo - 1, has_top), (halo + height, has_bottom)):
        row_mask[row % blocks] = jnp.where(sublane == row // blocks, jnp.where(there, 1.0, 0.0), 1.0)

    def step(index, carry, opening=False):
        level = jnp.where(index < steps - 1, steps - 2 - index, steps)
        near, ahead, new_y, beside, total, behind = {}, {}, {}, {}, {}, {}

        def rows(q):
            return slice(8 * q, 8 * q + 8)

        def first(q):
            source = force_ref.at[steps - 1] if opening else a
            near[q] = [source[c, rows(q % blocks), :] for c in every]
            if q < blocks:
                ahead[q] = near[q][2:] + [roll_lanes(value, -1) for value in near[q][:2]]
            else:
                near[q] = [up(value) for value in near[q]]

        def coefficients(q):
            return [[ref[c, rows(q), :] for c in range(planes + 1)] for ref in (keeps, gains)]

        def second_y(q):
            beside[q + 1] = keep, gain = coefficients(q + 1)
            new_y[q] = [gain[c] * (near[q + 2][c] - near[q][c]) for c in every]
            if not opening:
                new_y[q] = [new_y[q][c] + keep[c] * fy[c, rows(q), :] for c in every]
            for c in every:
                fy[c, rows(q), :] = new_y[q][c]

        def second_x(q):
            keep, gain = beside[q]
            new_x = [gain[c + 1] * (ahead[q][c] - near[q][c]) for c in every]
            if not opening:
                new_x = [new_x[c] + keep[c + 1] * fx[c, rows(q), :] for c in every]
            behind[q] = [roll_lanes(value, 1) for value in new_x[-2:]] + new_x[:-2]
            before = new_y[q - 2] if q >= 2 else [down(fy[c, rows(q - 2 + blocks), :]) for c in every]
            push = [force_ref[level, c, rows(q), :] for c in every]
            total[q] = [(near[q][c] + push[c]) + (new_y[q][c] - before[c]) + new_x[c] for c in every]
            for c in every:
                fx[c, rows(q), :] = new_x[c]

        def third(q):
            for c in every:
                value = total[q][c] - behind[q][c]
                if c in column_mask:
                    value = value * column_mask[c]
                if q in row_mask:
                    value = value * row_mask[q]
                a[c, rows(q), :] = value

        for q in range(4):
            first(q)
        second_y(0)
        second_y(1)
        for q in range(2, blocks):
            first(q + 2)
            second_y(q)
            second_x(q)
            if q > 2:
                third(q - 1)
        for q in range(2):
            first(q)
            new_y[q] = [fy[c, rows(q), :] for c in every]
            beside[q] = coefficients(q)
        for q in range(2):
            second_x(q)
            third(q - 1 if q else blocks - 1)
        third(1)
        return carry

    step(0, 0, opening=True)
    lax.fori_loop(1, steps, step, 0)

    start = jnp.where(my_lon > 0, halo, 0)
    for c in every:
        column = lanes8 * planes + c
        known = (column >= start) & (column < width + halo)
        for r in range(0, height, 8):
            s, q = divmod(halo + r, blocks)
            strided = pl.ds(8 * q + s, 8, stride=8)
            value = jnp.where(known & (keeps[c, strided, :] > 0.0), a[c, strided, :], 0.0)
            grad_ref[r : r + 8, c * LANES : (c + 1) * LANES] = value
    high, low = halves(grad_ref[...])
    sums = jnp.dot(
        jnp.concatenate([high, low, high], axis=1), weights_ref[...], preferred_element_type=jnp.float32
    )
    sums = jnp.transpose(sums)[: 8 + halo]
    for i in range(sums_ref.shape[0]):
        sums_ref[i] = sums


def smooth(halo, order, grad_ref, out_ref, weights_ref, exact_ref):
    width = out_ref.shape[1]
    length = 2.0 * width
    planes = grad_ref.shape[1] // LANES
    column = lax.broadcasted_iota(jnp.int32, (LANES, width), 1)
    lane = lax.broadcasted_iota(jnp.int32, (LANES, width), 0)
    sources = [lane * planes + c for c in range(planes)]
    kernel = jnp.concatenate(
        [jnp.where(x < width, jnp.exp(-jnp.abs(x - column).astype(jnp.float32) / length), 0.0) for x in sources], axis=0
    )
    out_ref[...] = jnp.dot(
        grad_ref[...], kernel, precision=lax.Precision.HIGHEST, preferred_element_type=jnp.float32
    )
    me = lax.axis_index("lon")
    shape = (8 + halo, width)
    kind, column = lax.broadcasted_iota(jnp.int32, shape, 0), lax.broadcasted_iota(jnp.int32, shape, 1)
    for place, source in enumerate(order):
        strip = jnp.where(kind < 2, source, source + 1)
        left = ((kind == 0) | (kind == 2)) & (strip > me)
        right = ((kind == 1) | (kind == 3)) & (strip < me)
        near = (kind >= 8) & (source + 1 == me)
        away = jnp.where(left, (strip - me) * width - column, (me - strip - 1) * width + column + 1)
        away = jnp.where(near, jnp.abs(kind - 8 - column), away)
        weights = jnp.where(left | right | near, jnp.exp(-jnp.maximum(away, 0).astype(jnp.float32) / length), 0.0)
        exact_ref[place * shape[0] : (place + 1) * shape[0], :] = weights
    high, low = halves(exact_ref[...])
    count = high.shape[0]
    for place, part in enumerate((high, high, low)):
        weights_ref[place * count : (place + 1) * count, :] = part


def finish(own_ref, weights_ref, sums_ref, out_ref):
    high, low = halves(sums_ref[...])
    out_ref[...] = own_ref[...] + lax.dot_general(
        jnp.concatenate([high, low, high], axis=0), weights_ref[...], (((0,), (0,)), ((), ())),
        preferred_element_type=jnp.float32,
    )


def f32(*shape):
    return jax.ShapeDtypeStruct(shape, jnp.float32)


def hint(megabytes):
    return pl.CostEstimate(flops=0, bytes_accessed=megabytes * 1000 * 1000, transcendentals=0)


def spaced(rows):
    return 8 * (rows // 8 | 1)


def vmem(count):
    return [pl.BlockSpec(memory_space=pltpu.VMEM)] * count


def local(depth, surface, friction, wet, coastal_tiles, gauge_route, gauge_cell, gauge_times, gauge_resid):
    height, width = depth.shape
    owned = gauge_route.shape[0]
    blocks = gauge_resid.shape[1]
    steps = blocks * STEPS_BLOCK
    halo = 2 * steps
    assert halo == SEG and height == LANES
    tiles = lax.axis_size(GRID_AXES)
    lons = lax.axis_size("lon")
    row_tiles = lax.axis_size(ROW_AXES)
    planes = width // LANES + 1
    rows_all = height + 2 * halo
    params = pltpu.CompilerParams(vmem_limit_bytes=VMEM_LIMIT)

    keep = (1.0 - friction) * wet.astype(jnp.float32)
    gain = ((courant * 0.5) ** 2 * jnp.maximum(depth + surface, depth_floor)) * keep
    samples, coast_count = gauge_resid.shape[2], coastal_tiles.shape[0]
    assert coast_count <= owned

    assert samples >= 3

    def put(array, group, row):
        groups, rows, lanes = array.shape
        return jnp.pad(array, ((group, 2 * blocks + 1 - group - groups), (row, samples - row - rows), (0, owned - lanes)))

    gauges = (
        put(jnp.transpose(gauge_times, (1, 2, 0)), 0, 0)
        + put(gauge_route.reshape(1, 1, owned), 2 * blocks, 0)
        + put(gauge_cell.reshape(1, 1, owned), 2 * blocks, 1)
        + put(coastal_tiles.reshape(1, 1, coast_count), 2 * blocks, 2)
    ).astype(jnp.float32) + put(jnp.transpose(gauge_resid, (1, 2, 0)), blocks, 0)
    west = pl.pallas_call(
        functools.partial(give_west, 2 * halo), out_shape=f32(height + 64, LANES), in_specs=vmem(2), out_specs=vmem(1)[0],
        compiler_params=params, name="give_west",
    )(keep, gain)
    right = lax.ppermute(west, "lon", [(i + 1, i) for i in range(lons - 1)])

    parcel = pl.pallas_call(
        functools.partial(give_gauges, height, width, blocks, samples, coast_count),
        out_shape=f32(tiles, gauge_rows(owned)[0], LANES),
        in_specs=vmem(1) + [pl.BlockSpec(memory_space=pl.ANY)],
        out_specs=vmem(1)[0],
        scratch_shapes=[pltpu.VMEM((24, LANES), jnp.float32)],
        compiler_params=params,
        cost_estimate=hint(10),
        name="give_gauges",
    )(gauges, west)

    def exchange(array, axes, groups=None):
        return lax.all_to_all(array, axes, split_axis=0, concat_axis=0, axis_index_groups=groups, tiled=True)

    rank = {row_tiles - 1: 1, 0: 2}
    group = sorted(range(tiles), key=lambda tile: (rank.get(tile % row_tiles, 0), -(tile // row_tiles)))
    parcel = exchange(parcel, GRID_AXES, [group])

    to_far, to_near = pl.pallas_call(
        functools.partial(give_rows, halo), out_shape=(f32(2, halo, planes * LANES),) * 2, in_specs=vmem(3),
        out_specs=tuple(vmem(2)), compiler_params=params, cost_estimate=hint(40), name="give_rows",
    )(keep, gain, right)
    far = lax.ppermute(to_far, ROW_AXES, [pair for i in range(1, row_tiles - 1, 2) for pair in ((i, i + 1), (i + 1, i))])
    near = lax.ppermute(to_near, ROW_AXES, [pair for i in range(0, row_tiles, 2) for pair in ((i, i + 1), (i + 1, i))])

    deal, own, weights = pl.pallas_call(
        functools.partial(deal_own, 2 * halo),
        out_shape=(
            jax.ShapeDtypeStruct((planes * LANES, planes * LANES), jnp.bfloat16), f32(2, planes, height, LANES),
            jax.ShapeDtypeStruct((3 * planes * LANES, LANES), jnp.bfloat16),
        ),
        in_specs=vmem(3) + [pl.BlockSpec(memory_space=pl.ANY)],
        out_specs=tuple(vmem(3)),
        compiler_params=params,
        cost_estimate=hint(4),
        name="deal_own",
    )(keep, gain, right, to_far)

    wide = max(2 * LANES, owned)
    pushes = pl.pallas_call(
        functools.partial(force, steps, halo, height, width),
        out_shape=f32(steps + 1, planes, spaced(rows_all), LANES),
        in_specs=vmem(1) + [pl.BlockSpec(memory_space=pl.ANY)],
        out_specs=vmem(1)[0],
        scratch_shapes=[
            pltpu.VMEM((steps, wide), jnp.float32),
            pltpu.VMEM((rows_all, wide), jnp.bfloat16),
            pltpu.VMEM((2 * wide, planes * LANES), jnp.bfloat16),
        ],
        compiler_params=params,
        cost_estimate=pl.CostEstimate(
            flops=4 * steps * rows_all * wide * planes * LANES, bytes_accessed=4 * steps * planes * rows_all * LANES,
            transcendentals=0,
        ),
        name="force",
    )(parcel, deal)

    plane = pltpu.VMEM((planes, spaced(rows_all), LANES), jnp.float32)
    grad, sums = pl.pallas_call(
        functools.partial(sweep, steps),
        out_shape=(f32(height, planes * LANES), f32(lons, 8 + halo, height)),
        in_specs=vmem(6),
        out_specs=tuple(vmem(2)),
        scratch_shapes=[plane] * 3 + [
            pltpu.VMEM((planes + 1, spaced(rows_all + 8), LANES), jnp.float32),
            pltpu.VMEM((planes + 1, spaced(rows_all + 8), LANES), jnp.float32),
            pltpu.VMEM((2, planes, spaced(rows_all), LANES), jnp.float32),
        ],
        compiler_params=params,
        name="sweep",
    )(deal, own, weights, far, near, pushes)

    order = list(range(lons // 2, lons)) + list(range(lons // 2))[::-1]
    sums = exchange(sums, "lon", [order])
    own, weights = pl.pallas_call(
        functools.partial(smooth, halo, order),
        out_shape=(f32(height, width), jax.ShapeDtypeStruct((3 * lons * (8 + halo), width), jnp.bfloat16)),
        in_specs=vmem(1),
        out_specs=tuple(vmem(2)),
        scratch_shapes=[pltpu.VMEM((lons * (8 + halo), width), jnp.float32)],
        compiler_params=params,
        cost_estimate=pl.CostEstimate(
            flops=6 * 2 * height * width * width, bytes_accessed=2 * 4 * height * width, transcendentals=width * width
        ),
        name="smooth",
    )(grad)
    return pl.pallas_call(
        finish, out_shape=f32(height, width), in_specs=vmem(3), out_specs=vmem(1)[0], compiler_params=params, name="finish",
    )(own, weights, sums.reshape(lons * (8 + halo), height))


def solution(mesh):
    in_specs = (
        P(("lat", "gau"), "lon"),
        P(("scen", "lat", "gau"), "lon"),
        P(("lat", "gau"), "lon"),
        P(("lat", "gau"), "lon"),
        P(),
        P(("scen", "lon", "lat", "gau"), None),
        P(("scen", "lon", "lat", "gau")),
        P(("scen", "lon", "lat", "gau"), None, None),
        P(("scen", "lon", "lat", "gau"), None, None),
    )
    out_specs = P(("scen", "lat", "gau"), "lon")
    return jax.shard_map(local, mesh=mesh, in_specs=in_specs, out_specs=out_specs, check_vma=False)
```

```python
import functools
import math

import jax
import jax.numpy as jnp
from jax import lax
from jax.experimental import pallas as pl
from jax.experimental.pallas import tpu as pltpu
from jax.sharding import PartitionSpec as P

STEPS_BLOCK = 8
LANES = 128
SEG = 32
LEVELS = 16

courant = 0.45
depth_floor = 0.1

GRID_AXES = ("lon", "lat", "gau")
ROW_AXES = ("lat", "gau")
VMEM_LIMIT = 16 * 1024 * 1024


def roll_lanes(x, shift):
    shift = shift % LANES
    return x if shift == 0 else pltpu.roll(x, shift, 1)


def lane_iota(rows):
    return lax.broadcasted_iota(jnp.int32, (rows, LANES), 1)


def gauge_rows(owned):
    if 3 * owned <= LANES:
        return STEPS_BLOCK, owned
    assert owned <= LANES
    return 3 * STEPS_BLOCK, 0


def my_place():
    row = lax.axis_index("lat") * lax.axis_size("gau") + lax.axis_index("gau")
    return row, lax.axis_index("lon"), lax.axis_size("lat") * lax.axis_size("gau"), lax.axis_size("lon")


def give_west(reach, keep_ref, gain_ref, west_ref):
    height = keep_ref.shape[0]
    lower = lane_iota(height) < reach
    west_ref[:height] = jnp.where(lower, keep_ref[:, :LANES], roll_lanes(gain_ref[:, :LANES], reach))
    west_ref[height:] = jnp.zeros((west_ref.shape[0] - height, LANES), jnp.float32)


def give_rows(halo, keep_ref, gain_ref, right_ref, far_ref, near_ref):
    height, width = keep_ref.shape
    lower = lane_iota(halo) < 2 * halo
    odd = my_place()[0] & 1
    for goal, south in ((far_ref, odd), (near_ref, 1 - odd)):
        rows = pl.ds(pl.multiple_of(south * (height - halo), halo), halo)
        for kind, source in enumerate((keep_ref, gain_ref)):
            goal[kind, :, :width] = source[rows, :]
            goal[kind, :, width:] = jnp.where(lower, roll_lanes(right_ref[rows, :], -2 * halo * kind), 0.0)


def give_gauges(height, width, blocks, samples, coast_count, gauge_ref, after_ref, parcel_ref, block_ref):
    row_tiles = lax.axis_size("lat") * lax.axis_size("gau")
    owned = gauge_ref.shape[2]
    assert blocks == 2
    route, cell, coast = (gauge_ref[2 * blocks, i : i + 1, :].astype(jnp.int32) for i in range(3))
    target = jnp.zeros_like(route)
    for entry in range(coast_count):
        target = jnp.where(route == entry, jnp.broadcast_to(coast[:, entry : entry + 1], route.shape), target)
    row_bits, width_bits = int(math.log2(row_tiles)), int(math.log2(width))
    assert row_tiles == 1 << row_bits and width == 1 << width_bits
    grid_row = (target & (row_tiles - 1)) * height + (cell >> width_bits)
    grid_col = (target >> row_bits) * width + (cell & (width - 1))
    block_ref[...] = jnp.zeros_like(block_ref)
    levels = lax.broadcasted_iota(jnp.int32, (STEPS_BLOCK, owned), 0).astype(jnp.float32)
    for block in range(blocks):
        series = jnp.zeros((STEPS_BLOCK, owned), jnp.float32)
        for sample in range(samples):
            times = gauge_ref[block, sample : sample + 1, :]
            resid = gauge_ref[blocks + block, sample : sample + 1, :]
            series = series + jnp.where(times == levels, resid, 0.0)
        block_ref[block * STEPS_BLOCK : (block + 1) * STEPS_BLOCK, :owned] = series
    at = blocks * STEPS_BLOCK
    block_ref[at : at + 1, :owned] = grid_row.astype(jnp.float32)
    block_ref[at + 1 : at + 2, :owned] = grid_col.astype(jnp.float32)
    size, apart = gauge_rows(owned)
    gauges = block_ref[...]
    if size == STEPS_BLOCK:
        gauges = sum(
            roll_lanes(gauges[i * STEPS_BLOCK : (i + 1) * STEPS_BLOCK], i * apart) for i in range(3)
        )
    tiles = parcel_ref.shape[0]

    def put(tile, carry):
        parcel_ref[tile, 0:size, :] = gauges
        return carry

    lax.fori_loop(0, tiles, put, 0, unroll=tiles <= 16)


def halves(value):
    high = value.astype(jnp.bfloat16)
    return high, (value - high.astype(jnp.float32)).astype(jnp.bfloat16)


def dealt_column(place, planes):
    return (place & (LANES - 1)) * planes + place // LANES


def force(steps, halo, height, width, parcel_ref, after_ref, force_ref, series_ref, rows_hot, cols_hot):
    planes, rows_all = force_ref.shape[1], height + 2 * halo
    my_row, my_lon, row_tiles, lons = my_place()
    wide = rows_hot.shape[1]
    tiles, parcel_rows = parcel_ref.shape[:2]
    size = parcel_rows
    apart = wide // tiles if size == STEPS_BLOCK else 0
    owned = apart if apart else LANES
    group = wide // owned
    groups = tiles // group
    per_plane = LANES // owned
    blocks = rows_all // 8
    row_shift = (halo - my_row * height).astype(jnp.float32)
    col_shift = (-my_lon * width).astype(jnp.float32)
    place = lax.broadcasted_iota(jnp.int32, (rows_all, LANES), 0)
    at = ((place & 7) * blocks + (place >> 3)).astype(jnp.float32)

    def gather_gauges(index):
        lanes = lane_iota(STEPS_BLOCK)
        for part in range(wide // LANES):
            cols = slice(part * LANES, (part + 1) * LANES)
            fields = []
            for field in range(3):
                total = jnp.zeros((STEPS_BLOCK, LANES), jnp.float32)
                rows = slice(0, 8) if apart else slice(8 * field, 8 * field + 8)
                for i in range(per_plane):
                    source = index * group + part * per_plane + i
                    block = roll_lanes(parcel_ref[source, rows, :], i * owned - field * apart)
                    total = jnp.where((lanes >= i * owned) & (lanes < (i + 1) * owned), block, total)
                fields.append(total)
            series_ref[0:8, cols] = fields[0]
            series_ref[8:16, cols] = fields[1]
            row = fields[2][0:1] + row_shift
            col = fields[2][1:2] + col_shift
            col = jnp.where(col < width + 2 * halo, col, -1.0)
            rows_hot[:, cols] = (at == row).astype(jnp.float32).astype(jnp.bfloat16)
            by_gauge = jnp.transpose(jnp.broadcast_to(col, (LANES, LANES)))
            for c in range(planes):
                spot = (lane_iota(LANES) * planes + c).astype(jnp.float32)
                hot = (by_gauge == spot).astype(jnp.float32).astype(jnp.bfloat16)
                cols_hot[part * LANES : (part + 1) * LANES, c * LANES : (c + 1) * LANES] = hot
                cols_hot[wide + part * LANES : wide + (part + 1) * LANES, c * LANES : (c + 1) * LANES] = hot

    def levels_of(start, add):
        hot = rows_hot[...]
        both = []
        for level in range(LEVELS):
            value = series_ref[pl.ds(start + level, 1), :]
            high, low = halves(value)
            both.append(jnp.concatenate([hot * high, hot * low], axis=1))
        both = jnp.concatenate(both, axis=0)
        for first in range(0, planes, 2):
            count = min(2, planes - first)
            total = jnp.dot(
                both, cols_hot[:, first * LANES : (first + count) * LANES], preferred_element_type=jnp.float32
            )
            for level in range(LEVELS):
                for c in range(count):
                    part = total[level * rows_all : (level + 1) * rows_all, c * LANES : (c + 1) * LANES]
                    goal = (start + level, first + c, slice(0, rows_all))
                    force_ref[goal] = force_ref[goal] + part if add else part

    def levels(add):
        def one(index, carry):
            levels_of(index * LEVELS, add)
            return carry

        if steps == LEVELS:
            levels_of(0, add)
        else:
            lax.fori_loop(0, steps // LEVELS, one, 0)

    gather_gauges(0)
    levels(False)
    if groups > 1:

        def more(index, carry):
            gather_gauges(index)
            levels(True)
            return carry

        lax.fori_loop(1, groups, more, 0)


def deal_own(reach, keep_ref, gain_ref, right_ref, after_ref, deal_ref, own_ref, weights_ref):
    height, width = keep_ref.shape
    planes = own_ref.shape[1]
    columns = planes * LANES
    parts = []
    for kind, source in enumerate((keep_ref, gain_ref)):
        beside = jnp.where(lane_iota(height) < reach, roll_lanes(right_ref[:height], -reach * kind), 0.0)
        parts += halves(jnp.concatenate([source[...], beside], axis=1))
    parts = jnp.concatenate(parts, axis=0)
    shape = (columns, LANES)
    ahead = lax.broadcasted_iota(jnp.int32, shape, 0) - lax.broadcasted_iota(jnp.int32, shape, 1) * planes
    for first in range(0, planes, 2):
        pair = range(first, min(first + 2, planes))
        deal = jnp.concatenate([(ahead == c).astype(jnp.float32).astype(jnp.bfloat16) for c in pair], axis=1)
        deal_ref[:, first * LANES : (first + len(pair)) * LANES] = deal
        dealt = jnp.dot(parts, deal, preferred_element_type=jnp.float32)
        for i, c in enumerate(pair):
            piece = dealt[:, i * LANES : (i + 1) * LANES]
            for kind in range(2):
                at = 2 * kind * height
                own_ref[kind, c] = piece[at : at + height] + piece[at + height : at + 2 * height]

    halo = reach // 2
    length = 2.0 * width
    shape = (planes * LANES, LANES)
    kind = lax.broadcasted_iota(jnp.int32, shape, 1)
    column = dealt_column(lax.broadcasted_iota(jnp.int32, shape, 0), planes)
    beyond = column - width
    off = jnp.where(kind == 0, column, jnp.where(kind == 1, -1 - beyond, jnp.where(kind == 2, beyond, width - 1 - beyond)))
    mine = ((kind < 2) & (beyond < 0)) | ((kind >= 2) & (kind < 4) & (beyond >= 0))
    weights = jnp.where(mine, jnp.exp(-jnp.maximum(off, 0).astype(jnp.float32) / length), 0.0)
    weights = jnp.where((kind >= 8) & (beyond == kind - 8), 1.0, weights)
    high, low = halves(weights)
    weights_ref[...] = jnp.concatenate([high, high, low], axis=0)


def sweep(
    steps, deal_ref, own_ref, weights_ref, far_ref, near_ref, force_ref,
    grad_ref, sums_ref,
    a, fx, fy, keeps, gains, plain,
):
    planes, height = own_ref.shape[1:3]
    width = (planes - 1) * LANES
    halo = 2 * steps
    rows_all = height + 2 * halo
    blocks = rows_all // 8
    my_row, my_lon, row_tiles, lons = my_place()
    has_top, has_bottom = my_row > 0, my_row < row_tiles - 1
    has_right = my_lon < lons - 1
    odd = (jnp.zeros((halo, planes * LANES), jnp.int32) + (my_row & 1)) == 1
    lanes8 = lane_iota(8)

    def up(value):
        return pltpu.roll(value, 7, 0)

    def down(value):
        return pltpu.roll(value, 1, 0)

    every = range(planes)
    columns = planes * LANES

    parts = []
    for kind in range(2):
        far, near = far_ref[kind], near_ref[kind]
        parts += halves(jnp.concatenate([jnp.where(odd, near, far), jnp.where(odd, far, near)], axis=0))
    parts = jnp.concatenate(parts, axis=0)
    for first in range(0, planes, 2):
        pair = range(first, min(first + 2, planes))
        dealt = jnp.dot(
            parts, deal_ref[:, first * LANES : (first + len(pair)) * LANES], preferred_element_type=jnp.float32
        )
        for i, c in enumerate(pair):
            piece = dealt[:, i * LANES : (i + 1) * LANES]
            for kind in range(2):
                at = 4 * kind * halo
                value = piece[at : at + 2 * halo] + piece[at + 2 * halo : at + 4 * halo]
                plain[kind, c, 0:halo, :] = value[:halo]
                plain[kind, c, halo : halo + height, :] = own_ref[kind, c]
                plain[kind, c, halo + height : rows_all, :] = value[halo:]
    for kind, goal in enumerate((keeps, gains)):
        for q in range(blocks):
            for c in every:
                value = plain[kind, c, pl.ds(q, 8, stride=blocks), :]
                goal[c, 8 * q : 8 * q + 8, :] = value
                if q == 0:
                    goal[c, 8 * blocks : 8 * blocks + 8, :] = up(value)
                if c == 0:
                    goal[planes, 8 * q : 8 * q + 8, :] = roll_lanes(value, -1)

    def cell_mask(column, there):
        lane, plane = column // planes, column % planes
        return plane, jnp.where(lanes8 == lane, there, 1.0)

    column_mask = dict([cell_mask(width, jnp.where(has_right, 1.0, 0.0)), cell_mask(columns - 1, 0.0)])
    assert len(column_mask) == 2
    sublane = lax.broadcasted_iota(jnp.int32, (8, LANES), 0)
    row_mask = {}
    for row, there in ((halo - 1, has_top), (halo + height, has_bottom)):
        row_mask[row % blocks] = jnp.where(sublane == row // blocks, jnp.where(there, 1.0, 0.0), 1.0)

    def step(index, carry, opening=False, closing=False):
        level = steps - 2 - index
        near, ahead, new_y, beside, total, behind = {}, {}, {}, {}, {}, {}

        def rows(q):
            return slice(8 * q, 8 * q + 8)

        def first(q):
            source = force_ref.at[steps - 1] if opening else a
            near[q] = [source[c, rows(q % blocks), :] for c in every]
            if q < blocks:
                ahead[q] = near[q][2:] + [roll_lanes(value, -1) for value in near[q][:2]]
            else:
                near[q] = [up(value) for value in near[q]]

        def coefficients(q):
            return [[ref[c, rows(q), :] for c in range(planes + 1)] for ref in (keeps, gains)]

        def second_y(q):
            beside[q + 1] = keep, gain = coefficients(q + 1)
            new_y[q] = [gain[c] * (near[q + 2][c] - near[q][c]) for c in every]
            if not opening:
                new_y[q] = [new_y[q][c] + keep[c] * fy[c, rows(q), :] for c in every]
            for c in every:
                fy[c, rows(q), :] = new_y[q][c]

        def second_x(q):
            keep, gain = beside[q]
            new_x = [gain[c + 1] * (ahead[q][c] - near[q][c]) for c in every]
            if not opening:
                new_x = [new_x[c] + keep[c + 1] * fx[c, rows(q), :] for c in every]
            behind[q] = [roll_lanes(value, 1) for value in new_x[-2:]] + new_x[:-2]
            before = new_y[q - 2] if q >= 2 else [down(fy[c, rows(q - 2 + blocks), :]) for c in every]
            total[q] = near[q] if closing else [near[q][c] + force_ref[level, c, rows(q), :] for c in every]
            total[q] = [total[q][c] + (new_y[q][c] - before[c]) + new_x[c] for c in every]
            for c in every:
                fx[c, rows(q), :] = new_x[c]

        def third(q):
            for c in every:
                value = total[q][c] - behind[q][c]
                if c in column_mask:
                    value = value * column_mask[c]
                if q in row_mask:
                    value = value * row_mask[q]
                a[c, rows(q), :] = value

        for q in range(4):
            first(q)
        second_y(0)
        second_y(1)
        for q in range(2, blocks):
            first(q + 2)
            second_y(q)
            second_x(q)
            if q > 2:
                third(q - 1)
        for q in range(2):
            first(q)
            new_y[q] = [fy[c, rows(q), :] for c in every]
            beside[q] = coefficients(q)
        for q in range(2):
            second_x(q)
            third(q - 1 if q else blocks - 1)
        third(1)
        return carry

    step(0, 0, opening=True)
    lax.fori_loop(1, steps - 1, step, 0)
    step(steps - 1, 0, closing=True)

    start = jnp.where(my_lon > 0, halo, 0)
    for c in every:
        column = lanes8 * planes + c
        known = (column >= start) & (column < width + halo)
        for r in range(0, height, 8):
            s, q = divmod(halo + r, blocks)
            strided = pl.ds(8 * q + s, 8, stride=8)
            value = jnp.where(known & (keeps[c, strided, :] > 0.0), a[c, strided, :], 0.0)
            grad_ref[r : r + 8, c * LANES : (c + 1) * LANES] = value
    high, low = halves(grad_ref[...])
    sums = jnp.dot(
        jnp.concatenate([high, low, high], axis=1), weights_ref[...], preferred_element_type=jnp.float32
    )
    sums = jnp.transpose(sums)[: 8 + halo]
    for i in range(sums_ref.shape[0]):
        sums_ref[i] = sums


def smooth(halo, order, grad_ref, out_ref, weights_ref, exact_ref):
    width = out_ref.shape[1]
    length = 2.0 * width
    planes = grad_ref.shape[1] // LANES
    column = lax.broadcasted_iota(jnp.int32, (LANES, width), 1)
    lane = lax.broadcasted_iota(jnp.int32, (LANES, width), 0)
    sources = [lane * planes + c for c in range(planes)]
    kernel = jnp.concatenate(
        [jnp.where(x < width, jnp.exp(-jnp.abs(x - column).astype(jnp.float32) / length), 0.0) for x in sources], axis=0
    )
    out_ref[...] = jnp.dot(
        grad_ref[...], kernel, precision=lax.Precision.HIGHEST, preferred_element_type=jnp.float32
    )
    me = lax.axis_index("lon")
    shape = (8 + halo, width)
    kind, column = lax.broadcasted_iota(jnp.int32, shape, 0), lax.broadcasted_iota(jnp.int32, shape, 1)
    for place, source in enumerate(order):
        strip = jnp.where(kind < 2, source, source + 1)
        left = ((kind == 0) | (kind == 2)) & (strip > me)
        right = ((kind == 1) | (kind == 3)) & (strip < me)
        near = (kind >= 8) & (source + 1 == me)
        away = jnp.where(left, (strip - me) * width - column, (me - strip - 1) * width + column + 1)
        away = jnp.where(near, jnp.abs(kind - 8 - column), away)
        weights = jnp.where(left | right | near, jnp.exp(-jnp.maximum(away, 0).astype(jnp.float32) / length), 0.0)
        exact_ref[place * shape[0] : (place + 1) * shape[0], :] = weights
    high, low = halves(exact_ref[...])
    count = high.shape[0]
    for place, part in enumerate((high, high, low)):
        weights_ref[place * count : (place + 1) * count, :] = part


def finish(own_ref, weights_ref, sums_ref, out_ref):
    high, low = halves(sums_ref[...])
    out_ref[...] = own_ref[...] + lax.dot_general(
        jnp.concatenate([high, low, high], axis=0), weights_ref[...], (((0,), (0,)), ((), ())),
        preferred_element_type=jnp.float32,
    )


def f32(*shape):
    return jax.ShapeDtypeStruct(shape, jnp.float32)


def hint(megabytes):
    return pl.CostEstimate(flops=0, bytes_accessed=megabytes * 1000 * 1000, transcendentals=0)


def spaced(rows):
    return 8 * (rows // 8 | 1)


def vmem(count):
    return [pl.BlockSpec(memory_space=pltpu.VMEM)] * count


def local(depth, surface, friction, wet, coastal_tiles, gauge_route, gauge_cell, gauge_times, gauge_resid):
    height, width = depth.shape
    owned = gauge_route.shape[0]
    blocks = gauge_resid.shape[1]
    steps = blocks * STEPS_BLOCK
    halo = 2 * steps
    assert halo == SEG and height == LANES
    tiles = lax.axis_size(GRID_AXES)
    lons = lax.axis_size("lon")
    row_tiles = lax.axis_size(ROW_AXES)
    planes = width // LANES + 1
    rows_all = height + 2 * halo
    params = pltpu.CompilerParams(vmem_limit_bytes=VMEM_LIMIT)

    keep = (1.0 - friction) * wet.astype(jnp.float32)
    gain = ((courant * 0.5) ** 2 * jnp.maximum(depth + surface, depth_floor)) * keep
    samples, coast_count = gauge_resid.shape[2], coastal_tiles.shape[0]
    assert coast_count <= owned

    assert samples >= 3

    def put(array, group, row):
        groups, rows, lanes = array.shape
        return jnp.pad(array, ((group, 2 * blocks + 1 - group - groups), (row, samples - row - rows), (0, owned - lanes)))

    gauges = (
        put(jnp.transpose(gauge_times, (1, 2, 0)), 0, 0)
        + put(gauge_route.reshape(1, 1, owned), 2 * blocks, 0)
        + put(gauge_cell.reshape(1, 1, owned), 2 * blocks, 1)
        + put(coastal_tiles.reshape(1, 1, coast_count), 2 * blocks, 2)
    ).astype(jnp.float32) + put(jnp.transpose(gauge_resid, (1, 2, 0)), blocks, 0)
    west = pl.pallas_call(
        functools.partial(give_west, 2 * halo), out_shape=f32(2 * height, LANES), in_specs=vmem(2), out_specs=vmem(1)[0],
        compiler_params=params, name="give_west",
    )(keep, gain)
    right = lax.ppermute(west, "lon", [(i + 1, i) for i in range(lons - 1)])

    parcel = pl.pallas_call(
        functools.partial(give_gauges, height, width, blocks, samples, coast_count),
        out_shape=f32(tiles, gauge_rows(owned)[0], LANES),
        in_specs=vmem(1) + [pl.BlockSpec(memory_space=pl.ANY)],
        out_specs=vmem(1)[0],
        scratch_shapes=[pltpu.VMEM((24, LANES), jnp.float32)],
        compiler_params=params,
        cost_estimate=hint(10),
        name="give_gauges",
    )(gauges, west)

    def exchange(array, axes, groups=None):
        return lax.all_to_all(array, axes, split_axis=0, concat_axis=0, axis_index_groups=groups, tiled=True)

    rank = {row_tiles - 1: 1, 0: 2}
    group = sorted(range(tiles), key=lambda tile: (rank.get(tile % row_tiles, 0), -(tile // row_tiles)))
    parcel = exchange(parcel, GRID_AXES, [group])

    to_far, to_near = pl.pallas_call(
        functools.partial(give_rows, halo), out_shape=(f32(2, halo, planes * LANES),) * 2, in_specs=vmem(3),
        out_specs=tuple(vmem(2)), compiler_params=params, cost_estimate=hint(40), name="give_rows",
    )(keep, gain, right)
    far = lax.ppermute(to_far, ROW_AXES, [pair for i in range(1, row_tiles - 1, 2) for pair in ((i, i + 1), (i + 1, i))])
    near = lax.ppermute(to_near, ROW_AXES, [pair for i in range(0, row_tiles, 2) for pair in ((i, i + 1), (i + 1, i))])

    deal, own, weights = pl.pallas_call(
        functools.partial(deal_own, 2 * halo),
        out_shape=(
            jax.ShapeDtypeStruct((planes * LANES, planes * LANES), jnp.bfloat16), f32(2, planes, height, LANES),
            jax.ShapeDtypeStruct((3 * planes * LANES, LANES), jnp.bfloat16),
        ),
        in_specs=vmem(3) + [pl.BlockSpec(memory_space=pl.ANY)],
        out_specs=tuple(vmem(3)),
        compiler_params=params,
        cost_estimate=hint(4),
        name="deal_own",
    )(keep, gain, right, to_far)

    wide = max(2 * LANES, owned)
    pushes = pl.pallas_call(
        functools.partial(force, steps, halo, height, width),
        out_shape=f32(steps, planes, spaced(rows_all), LANES),
        in_specs=vmem(1) + [pl.BlockSpec(memory_space=pl.ANY)],
        out_specs=vmem(1)[0],
        scratch_shapes=[
            pltpu.VMEM((steps, wide), jnp.float32),
            pltpu.VMEM((rows_all, wide), jnp.bfloat16),
            pltpu.VMEM((2 * wide, planes * LANES), jnp.bfloat16),
        ],
        compiler_params=params,
        cost_estimate=pl.CostEstimate(
            flops=4 * steps * rows_all * wide * planes * LANES, bytes_accessed=4 * steps * planes * rows_all * LANES,
            transcendentals=0,
        ),
        name="force",
    )(parcel, deal)

    plane = pltpu.VMEM((planes, spaced(rows_all), LANES), jnp.float32)
    grad, sums = pl.pallas_call(
        functools.partial(sweep, steps),
        out_shape=(f32(height, planes * LANES), f32(lons, 8 + halo, height)),
        in_specs=vmem(6),
        out_specs=tuple(vmem(2)),
        scratch_shapes=[plane] * 3 + [
            pltpu.VMEM((planes + 1, spaced(rows_all + 8), LANES), jnp.float32),
            pltpu.VMEM((planes + 1, spaced(rows_all + 8), LANES), jnp.float32),
            pltpu.VMEM((2, planes, spaced(rows_all), LANES), jnp.float32),
        ],
        compiler_params=params,
        name="sweep",
    )(deal, own, weights, far, near, pushes)

    order = list(range(lons // 2, lons)) + list(range(lons // 2))[::-1]
    sums = exchange(sums, "lon", [order])
    own, weights = pl.pallas_call(
        functools.partial(smooth, halo, order),
        out_shape=(f32(height, width), jax.ShapeDtypeStruct((3 * lons * (8 + halo), width), jnp.bfloat16)),
        in_specs=vmem(1),
        out_specs=tuple(vmem(2)),
        scratch_shapes=[pltpu.VMEM((lons * (8 + halo), width), jnp.float32)],
        compiler_params=params,
        cost_estimate=pl.CostEstimate(
            flops=6 * 2 * height * width * width, bytes_accessed=2 * 4 * height * width, transcendentals=width * width
        ),
        name="smooth",
    )(grad)
    return pl.pallas_call(
        finish, out_shape=f32(height, width), in_specs=vmem(3), out_specs=vmem(1)[0], compiler_params=params, name="finish",
    )(own, weights, sums.reshape(lons * (8 + halo), height))


def solution(mesh):
    in_specs = (
        P(("lat", "gau"), "lon"),
        P(("scen", "lat", "gau"), "lon"),
        P(("lat", "gau"), "lon"),
        P(("lat", "gau"), "lon"),
        P(),
        P(("scen", "lon", "lat", "gau"), None),
        P(("scen", "lon", "lat", "gau")),
        P(("scen", "lon", "lat", "gau"), None, None),
        P(("scen", "lon", "lat", "gau"), None, None),
    )
    out_specs = P(("scen", "lat", "gau"), "lon")
    return jax.shard_map(local, mesh=mesh, in_specs=in_specs, out_specs=out_specs, check_vma=False)
```
